128 devices in a mesh: ctx: 16 (over x, z_hi, core), head: 8 (over z_lo, y).
Axes of the slice: x: 4, y: 4, z: 4 (z_hi: 2, z_lo: 2; z = z_hi * 2 + z_lo), core: 2. Of those that a mesh axis runs over, the one named last changes fastest.
Arguments:
- prefill_query: bfloat16 [4096, 8192], P('ctx', 'head'), may hold values from -96 to 96
- prefill_key: bfloat16 [4096, 1024], P('ctx', 'head'), may hold values from -4 to 4
- prefill_value: bfloat16 [4096, 1024], P('ctx', 'head'), may hold values from -5 to 5
- tree_mask: int32 [64, 64], replicated, may hold values from 0 to 1, as said below
- pages: int32 [256, 8], replicated, may hold values from 0 to 63, as said below
- cache_len: int32 [256], replicated, may hold values from 256 to 512, as said below
- dec_in: bfloat16 [4, 256, 8192], P(None, None, 'ctx'), may hold values from -4 to 4
- norm_gain: bfloat16 [8192], P('ctx'), may hold values from 0.25 to 1.75
- w_query: bfloat16 [8192, 8192], P('ctx', 'head'), may hold values from -1 to 1
- w_keyval: bfloat16 [8192, 2, 1024], P('ctx', None, 'head'), may hold values from -0.0625 to 0.0625
- w_out: bfloat16 [8192, 8192], P('head', 'ctx'), may hold values from -0.125 to 0.125
Outputs:
- prefill_out: bfloat16 [4096, 8192], P('ctx', 'head')
- dec_out: bfloat16 [4, 256, 8192], P(None, None, 'ctx')
The draws below stay inside these ranges and needn't reach their ends.
Inputs may be any that keep to these rules, and one draw needn't show every extreme that they name: `tree_mask`: entry [a, b] is 1 exactly when node b is node a or an ancestor of a in the prompt tree, where every node but node 0 has one earlier node as parent. Page k holds prompt positions k * 64 to (k + 1) * 64 - 1; each row names 8 distinct pages; the 128 entries of each aligned block of 16 rows name exactly 2 distinct pages among pages k * 4 to (k + 1) * 4 - 1, for every k, each such page named equally often. `cache_len`: some row reads all 512 cached positions.
All inputs are finite; a program needn't handle non-finite values.
Results may differ from the reference program's by a relative error of at most 0.034.
Values may be sent and summed in bfloat16 or wider, within the bound.
A program may use at most 64 MiB of HBM per device.

```python
import jax
import jax.numpy as jnp
from jax import lax

D = 8192
HEADS = 64
KV = 8
HD = 128
GRP = 8
TOK_DEV = 256
LEN = 4096
PAGE = 64
PD = 4
NODES = 64
CAP = 2
P_SIZE = 8
POOL = 32
ROW_GRP = 16
ROWS = 256
STEPS = 4
N_CTX = 16


def shared_keys(key):
    return jnp.clip(jax.random.normal(key, (LEN, KV * HD), jnp.float32), -4.0, 4.0)


def draw_prefill_key(key, part):
    values = shared_keys(key)
    return values.astype(jnp.bfloat16)


def draw_prefill_query(key, part):
    key = jax.random.fold_in(key, 11)
    noise_key = jax.random.fold_in(key, 0)
    values = jnp.clip(jax.random.normal(noise_key, (LEN, HEADS * HD), jnp.float32), -4.0, 4.0)
    return values.astype(jnp.bfloat16)


def draw_w_query(key, part):
    key = jax.random.fold_in(key, 13)
    weight_key = jax.random.fold_in(key, 0)
    values = jnp.clip(jax.random.normal(weight_key, (D, HEADS * HD), jnp.float32), -4.0, 4.0) * D ** (-0.5)
    return jnp.clip(values, -1.0, 1.0).astype(jnp.bfloat16)


def draw_tree_mask(key, part):
    key = jax.random.fold_in(key, 5)
    nodes = jnp.arange(NODES, dtype=jnp.int32)
    parent = jax.random.randint(key, (NODES,), 0, 1 << 20, dtype=jnp.int32) % jnp.maximum(nodes, 1)
    linked = (parent[:, None] == nodes[None, :]).astype(jnp.int32)
    reach = jnp.maximum(linked, jnp.eye(NODES, dtype=jnp.int32))
    for turn in range(int(NODES).bit_length() + 1):
        reach = jnp.minimum(jnp.dot(reach, reach), 1)
    return reach.astype(jnp.int32)


def draw_pages(key, part):
    key = jax.random.fold_in(key, 7)
    group_key, page_key = jax.random.split(key)
    order = jax.vmap(lambda one: jax.random.permutation(one, POOL))(jax.random.split(group_key, N_CTX))
    picks = jax.vmap(lambda one: jax.random.permutation(one, PD))(jax.random.split(page_key, N_CTX * N_CTX))
    picks = picks.reshape(N_CTX, N_CTX, PD)[:, :, :CAP]
    pool = (jnp.arange(N_CTX, dtype=jnp.int32)[None, :, None] * PD + picks).reshape(N_CTX, POOL)
    slots = (jnp.arange(ROW_GRP, dtype=jnp.int32)[:, None] * P_SIZE + jnp.arange(P_SIZE, dtype=jnp.int32)[None, :]) % POOL
    where_in_pool = order[:, slots].reshape(N_CTX, ROW_GRP * P_SIZE)
    chosen = jnp.take_along_axis(pool, where_in_pool, axis=1)
    return chosen.reshape(ROWS, P_SIZE).astype(jnp.int32)


def draw_cache_len(key, part):
    key = jax.random.fold_in(key, 9)
    len_key, row_key = jax.random.split(key)
    lengths = jax.random.randint(len_key, (ROWS,), P_SIZE * PAGE // 2, P_SIZE * PAGE + 1, dtype=jnp.int32)
    fullrow = jax.random.randint(row_key, (), 0, ROWS, dtype=jnp.int32)
    return jnp.where(jnp.arange(ROWS, dtype=jnp.int32) == fullrow, P_SIZE * PAGE, lengths).astype(jnp.int32)


def block_levels(stream_key, dims, cuts, low, high):
    level = 1.0
    for dim, parts in cuts:
        draws = jax.random.uniform(jax.random.fold_in(jax.random.fold_in(stream_key, 6), dim), (parts,), jnp.float32, low / len(cuts), high / len(cuts))
        level = level * jnp.repeat(jnp.exp(draws), dims[dim] // parts).reshape((-1,) + (1,) * (len(dims) - 1 - dim))
    return level


def scatter_about(own_key, shape, width, bound, shards=(), kind=jnp.bfloat16):
    result = jax.random.normal(own_key, shape, jnp.float32) * width
    if len(shards) > 0:
        result = block_levels(own_key, shape, shards, -0.22, 0.18) * result
    return jnp.clip(result, min=-bound, max=bound).astype(kind)


def setup_inputs(seed: int = 0) -> dict:
    keys = jax.random.split(jax.random.key(seed), 12)
    prefill_query = draw_prefill_query(jax.random.fold_in(keys[11], 71), 0)
    prefill_key = draw_prefill_key(jax.random.fold_in(keys[11], 71), 0)
    prefill_value = scatter_about(keys[2], (LEN, KV * HD), 1.0, 5.0, ((0, 16), (1, 8)))
    tree_mask = draw_tree_mask(jax.random.fold_in(keys[11], 71), 0)
    pages = draw_pages(jax.random.fold_in(keys[11], 71), 0)
    cache_len = draw_cache_len(jax.random.fold_in(keys[11], 71), 0)
    dec_in = scatter_about(keys[6], (STEPS, ROWS, D), 0.5, 4.0, ((2, 16),))
    norm_gain = jnp.clip(1.0 + 0.15 * jax.random.normal(keys[7], (D,), jnp.float32), 0.25, 1.75).astype(jnp.bfloat16)
    w_query = draw_w_query(jax.random.fold_in(keys[11], 71), 0)
    w_keyval = scatter_about(keys[9], (D, 2, KV * HD), D ** -0.5, 0.0625, ((0, 16), (2, 8)))
    w_out = scatter_about(keys[10], (HEADS * HD, D), (HEADS * HD // 4) ** -0.5, 0.125, ((0, 8), (1, 16)))
    return dict(prefill_query=prefill_query, prefill_key=prefill_key, prefill_value=prefill_value, tree_mask=tree_mask, pages=pages, cache_len=cache_len, dec_in=dec_in, norm_gain=norm_gain, w_query=w_query, w_keyval=w_keyval, w_out=w_out)


def reference(prefill_query, prefill_key, prefill_value, tree_mask, pages, cache_len, dec_in, norm_gain, w_query, w_keyval, w_out):
    scale = HD ** (-0.5)
    positions = jnp.arange(LEN, dtype=jnp.int32)
    nodes = positions // PAGE
    queries = prefill_query.reshape(LEN // TOK_DEV, TOK_DEV, KV, GRP, HD)
    keys_all = prefill_key.reshape(LEN, KV, HD).astype(jnp.float32)
    values_all = prefill_value.reshape(LEN, KV, HD).astype(jnp.float32)

    def one_block(index):
        qblock = queries[index].astype(jnp.float32)
        qpos = index * TOK_DEV + jnp.arange(TOK_DEV, dtype=jnp.int32)
        allowed = (tree_mask[qpos // PAGE][:, nodes] > 0) & (qpos[:, None] >= positions[None, :])

        def one_head(kv_index):
            qhead = qblock[:, kv_index]
            scores = jnp.einsum('tgd,sd->gts', qhead, keys_all[:, kv_index]) * scale
            scores = jnp.where(allowed[None], scores, -1e+30)
            top = lax.optimization_barrier(jnp.max(scores, axis=-1, keepdims=True))
            weights = jnp.where(allowed[None], jnp.exp(scores - top), 0.0)
            total = lax.optimization_barrier(jnp.sum(weights, axis=-1))
            rounded = weights.astype(jnp.bfloat16).astype(jnp.float32)
            mixed = jnp.einsum('gts,sd->gtd', rounded, values_all[:, kv_index])
            return (mixed / total[..., None]).astype(jnp.bfloat16)
        heads_out = lax.map(one_head, jnp.arange(KV, dtype=jnp.int32))
        return heads_out.transpose(2, 0, 1, 3).reshape(TOK_DEV, HEADS * HD)
    prefill_out = lax.map(one_block, jnp.arange(LEN // TOK_DEV, dtype=jnp.int32)).reshape(LEN, HEADS * HD)
    cache_keys = prefill_key.reshape(NODES, PAGE, KV, HD)[pages].reshape(ROWS, P_SIZE * PAGE, KV, HD).astype(jnp.float32)
    cache_values = prefill_value.reshape(NODES, PAGE, KV, HD)[pages].reshape(ROWS, P_SIZE * PAGE, KV, HD).astype(jnp.float32)
    live = jnp.arange(P_SIZE * PAGE, dtype=jnp.int32)[None, :] < cache_len[:, None]
    gain = norm_gain.astype(jnp.float32)
    new_keys = jnp.zeros((ROWS, STEPS, KV, HD), jnp.float32)
    new_values = jnp.zeros((ROWS, STEPS, KV, HD), jnp.float32)
    outputs = []
    for step in range(STEPS):
        hidden = dec_in[step].astype(jnp.float32)
        row_sq = lax.optimization_barrier(jnp.sum(hidden * hidden, axis=1))
        inverse = lax.rsqrt(row_sq / D + 1e-05)
        scaled = (hidden * gain).astype(jnp.bfloat16)
        query_raw = jnp.dot(scaled, w_query, preferred_element_type=jnp.float32)
        keyval_raw = jnp.dot(scaled, w_keyval.reshape(D, 2 * KV * HD), preferred_element_type=jnp.float32)
        query_now = (query_raw * inverse[:, None]).astype(jnp.bfloat16).astype(jnp.float32).reshape(ROWS, KV, GRP, HD)
        keyval_now = (keyval_raw * inverse[:, None]).astype(jnp.bfloat16).astype(jnp.float32).reshape(ROWS, 2, KV, HD)
        new_keys = new_keys.at[:, step].set(keyval_now[:, 0])
        new_values = new_values.at[:, step].set(keyval_now[:, 1])
        score_cache = jnp.einsum('rkgd,rskd->rkgs', query_now, cache_keys) * scale
        score_cache = jnp.where(live[:, None, None, :], score_cache, -1e+30)
        score_new = jnp.einsum('rkgd,rskd->rkgs', query_now, new_keys) * scale
        score_new = jnp.where((jnp.arange(STEPS) <= step)[None, None, None, :], score_new, -1e+30)
        scores = jnp.concatenate([score_cache, score_new], axis=-1)
        top = lax.optimization_barrier(jnp.max(scores, axis=-1, keepdims=True))
        weights = jnp.exp(scores - top)
        total = lax.optimization_barrier(jnp.sum(weights, axis=-1, keepdims=True))
        rounded = weights.astype(jnp.bfloat16).astype(jnp.float32)
        mixed = jnp.einsum('rkgs,rskd->rkgd', rounded[..., :P_SIZE * PAGE], cache_values)
        mixed = mixed + jnp.einsum('rkgs,rskd->rkgd', rounded[..., P_SIZE * PAGE:], new_values)
        head_out = (mixed / total).reshape(ROWS, HEADS * HD).astype(jnp.bfloat16)
        added = jnp.dot(head_out, w_out, preferred_element_type=jnp.float32)
        outputs.append((hidden + added).astype(jnp.bfloat16))
    return (prefill_out, jnp.stack(outputs))
```

```python
import jax
import jax.numpy as jnp
from jax import lax
from jax.experimental import pallas as pl
from jax.experimental.pallas import tpu as pltpu
from jax.sharding import PartitionSpec as P

D = 8192
HD = 128
PAGE = 64
STEPS = 4
SCALE = HD ** (-0.5)
NEG = -1e30
F32 = jnp.float32
BF16 = jnp.bfloat16
MESH = pl.DeviceIdType.MESH

NCH = 2
TS = STEPS // NCH
RB = 16 * TS

KV0 = 0
SQ0 = 17
PART0 = 33
M_CORE, M_X, M_Z, M_HO, M_Y, M_ZL, M_FO = 0, 1, 7, 8, 25, 31, 32
PART_MSGS = 41
NMSG = PART0 + NCH * PART_MSGS


def rdot(a, b):
    return lax.dot_general(a, b, (((1,), (1,)), ((), ())), preferred_element_type=F32)


def mdot(a, b):
    return lax.dot_general(a, b, (((1,), (0,)), ((), ())), preferred_element_type=F32)


def layer_kernel(
    q_ref, key_ref, val_ref, mask_ref, pages_ref, clen_ref, x_ref, gain_ref, wq_ref, wkv_ref,
    wo_ref,
    pout, out,
    kv, qb, xb, wb, wkvb, wkvf, wob, xs, sqs, sqr, gs, gr, g, prelay, pleft, pright, zs, zr, rf,
    pr, nk, nv, bias, marks, sb, lsum, acc, psb, plsum, pacc, ho, o, of, orelay, oleft, oright,
    ozs, ozr, lsem, ssem, rsem,
):
    c = lax.axis_index("ctx")
    h = lax.axis_index("head")
    core = lax.rem(c, 2)
    zh = lax.rem(c // 2, 2)
    x = c // 4
    y = lax.rem(h, 4)
    zl = h // 4

    def cidx(xi, zi, ci):
        return xi * 4 + zi * 2 + ci

    def hidx(yi, zi):
        return zi * 4 + yi

    xr, xl, xo = lax.rem(x + 1, 4), lax.rem(x + 3, 4), lax.rem(x + 2, 4)
    yr, yl, yo = lax.rem(y + 1, 4), lax.rem(y + 3, 4), lax.rem(y + 2, 4)
    d_xr = (cidx(xr, zh, core), h)
    d_xl = (cidx(xl, zh, core), h)
    d_z = (cidx(x, 1 - zh, core), h)
    d_c = (cidx(x, zh, 1 - core), h)
    d_yr = (c, hidx(yr, zl))
    d_yl = (c, hidx(yl, zl))
    d_zl = (c, hidx(y, 1 - zl))

    def msg(i, src, dst, dev):
        return pltpu.make_async_remote_copy(
            src_ref=src, dst_ref=dst, send_sem=ssem.at[i], recv_sem=rsem.at[i],
            device_id=dev, device_id_type=MESH,
        )

    loads = [
        pltpu.make_async_copy(key_ref, kv.at[0, c], lsem.at[0]),
        pltpu.make_async_copy(val_ref, kv.at[1, c], lsem.at[1]),
        pltpu.make_async_copy(x_ref, xb, lsem.at[2]),
        pltpu.make_async_copy(wkv_ref, wkvb, lsem.at[3]),
    ]
    for j in range(4):
        loads.append(
            pltpu.make_async_copy(wq_ref.at[:, pl.ds(256 * j, 256)], wb.at[j], lsem.at[4 + j])
        )
    for j in range(2):
        loads.append(
            pltpu.make_async_copy(wo_ref.at[:, pl.ds(256 * j, 256)], wob.at[j], lsem.at[8 + j])
        )
    loads.append(pltpu.make_async_copy(q_ref, qb, lsem.at[10]))
    for copy in loads:
        copy.start()

    barrier = pltpu.get_barrier_semaphore()

    def greet(d, carry):
        pl.semaphore_signal(
            barrier, inc=1, device_id=(lax.rem(c + d, 16), h), device_id_type=MESH
        )
        return carry

    lax.fori_loop(1, 16, greet, 0)
    for dev in (d_yr, d_yl, d_zl):
        pl.semaphore_signal(barrier, inc=1, device_id=dev, device_id_type=MESH)
    pl.semaphore_wait(barrier, 18)

    sent = []

    def send(i, src, dst, dev):
        m = msg(i, src, dst, dev)
        m.start()
        sent.append(m)
        return m

    class Gather:
        def __init__(self, base, blk, half, p, q, right, left, far_p, d_r, d_l, d_q, share):
            self.base, self.blk, self.half, self.p, self.q = base, blk, half, p, q
            self.right, self.left, self.far_p = right, left, far_p
            self.d_r, self.d_l, self.d_q, self.share = d_r, d_l, d_q, share
            self.m = {}

        def put(self, k, ref, dev):
            self.m[k] = send(self.base + k, ref, ref, dev)

        def to_core(self, k, p_, q_):
            if self.share:
                ref = self.blk(p_, q_)
                self.m[9 + k] = send(self.base + 9 + k, ref, ref, d_c)

        def start(self):
            own = self.blk(self.p, self.q)
            self.put(0, own, self.d_q)
            self.put(1, own, self.d_r)
            self.put(2, own, self.d_l)
            self.to_core(0, self.p, self.q)

        def near(self):
            q2 = 1 - self.q
            self.m[0].wait_recv()
            other = self.blk(self.p, q2)
            self.put(3, other, self.d_r)
            self.put(4, other, self.d_l)
            self.to_core(1, self.p, q2)
            self.m[1].wait_recv()
            self.put(5, self.half(self.left, self.q, 0), self.d_r)
            self.to_core(2, self.left, self.q)
            self.m[2].wait_recv()
            self.put(6, self.half(self.right, self.q, 1), self.d_l)
            self.to_core(3, self.right, self.q)

        def far(self):
            q2 = 1 - self.q
            self.m[3].wait_recv()
            self.put(7, self.half(self.left, q2, 0), self.d_r)
            self.to_core(4, self.left, q2)
            self.m[4].wait_recv()
            self.put(8, self.half(self.right, q2, 1), self.d_l)
            self.to_core(5, self.right, q2)

        def last(self):
            q2 = 1 - self.q
            self.m[5].wait_recv()
            self.m[6].wait_recv()
            self.to_core(6, self.far_p, self.q)
            self.m[7].wait_recv()
            self.m[8].wait_recv()
            self.to_core(7, self.far_p, q2)

        def finish(self):
            if self.share:
                for k in range(8):
                    self.m[9 + k].wait_recv()

    kvg = Gather(
        KV0, lambda a, b: kv.at[:, cidx(a, b, core)], lambda a, b, k: kv.at[k, cidx(a, b, core)],
        x, zh, xr, xl, xo, d_xr, d_xl, d_z, True,
    )
    loads[0].wait()
    loads[1].wait()
    kvg.start()

    loads[2].wait()
    row_id = lax.broadcasted_iota(jnp.int32, (64, 128), 0)
    lane_id = lax.broadcasted_iota(jnp.int32, (64, 128), 1)
    eye = row_id == lane_id
    gain4 = gain_ref[...].astype(F32)
    gain = jnp.concatenate([gain4[i : i + 1] for i in range(4)], axis=1)

    def prepare(d, carry):
        raw = xb[:, d].astype(F32).reshape(64, 512)
        scaled = (raw * gain).astype(BF16).reshape(NCH, RB, 512)
        for k in range(NCH):
            xs[k, lax.rem(d, 2), d // 2] = scaled[k]
        part = jnp.sum(raw * raw, axis=1, keepdims=True)
        flat = jnp.sum(jnp.where(eye, part, 0.0), axis=0, keepdims=True)
        sqs[d] = jnp.broadcast_to(flat, (8, 128))
        return carry

    lax.fori_loop(0, 16, prepare, 0)

    def sq_msg(d):
        to = lax.rem(c + d, 16)
        return msg(SQ0 + d, sqs.at[to], sqr.at[c], (to, h))

    loads[3].wait()
    wkvf[...] = wkvb[...].astype(F32)
    wb[4, :, 0:128] = wkvf[pl.ds(0, 512, stride=2), :].astype(BF16)
    wb[4, :, 128:256] = wkvf[pl.ds(1, 512, stride=2), :].astype(BF16)
    for k in range(4, 8):
        loads[k].wait()

    first = pl.ds(0, 5)
    second = pl.ds(5, 5)

    class Part:
        pass

    parts = []
    for k in range(NCH):
        p = Part()
        p.k = k
        p.base = PART0 + k * PART_MSGS
        p.px, p.oy = {}, {}
        p.hog = Gather(
            p.base + M_HO, lambda a, b, k=k: ho.at[k, cidx(a, b, core)],
            lambda a, b, f, k=k: ho.at[k, cidx(a, b, core), f],
            x, zh, xr, xl, xo, d_xr, d_xl, d_z, True,
        )
        steps = pl.ds(k * TS, TS)
        p.fog = Gather(
            p.base + M_FO, lambda a, b, s=steps: out.at[s, 2 * a + b],
            lambda a, b, f, s=steps: out.at[s, 2 * a + b, pl.ds(16 * f, 16)],
            y, zl, yr, yl, yo, d_yr, d_yl, d_zl, False,
        )
        parts.append(p)

    def other_rows(p):
        k = p.k

        def body(j, carry):
            res = mdot(xs[k, 1 - core].reshape(8 * RB, 512), wb[j]).astype(BF16)
            gs[k, 2 * j] = res[:, :128].reshape(4, 2, RB, 128)
            gs[k, 2 * j + 1] = res[:, 128:].reshape(4, 2, RB, 128)
            return carry

        lax.fori_loop(0, 5, body, 0)
        p.core = send(p.base + M_CORE, gs.at[k], gr.at[k], d_c)

    def own_rows(p):
        k, px = p.k, p.px
        p.core.wait_recv()

        def body(j, carry):
            res = mdot(xs[k, core].reshape(8 * RB, 512), wb[j])
            for i in range(2):
                both = res[:, 128 * i : 128 * i + 128].reshape(4, 2, RB, 128) + gr[
                    k, 2 * j + i
                ].astype(F32)
                g[k, 2 * j + i] = both.astype(BF16)
            return carry

        lax.fori_loop(0, 3, body, 0)
        px[0] = send(p.base + M_X + 0, g.at[k, first, xo], prelay.at[k, 0], d_xr)
        px[3] = send(p.base + M_X + 3, g.at[k, first, xl], pright.at[k, 0], d_xl)
        lax.fori_loop(3, 5, body, 0)
        px[2] = send(p.base + M_X + 2, g.at[k, second, xo], prelay.at[k, 1], d_xl)
        px[1] = send(p.base + M_X + 1, g.at[k, second, xr], pleft.at[k, 1], d_xr)

    def x_relay(p):
        k, px = p.k, p.px
        px[0].wait_recv()
        g[k, first, xr] = (g[k, first, xr].astype(F32) + prelay[k, 0].astype(F32)).astype(BF16)
        px[4] = send(p.base + M_X + 4, g.at[k, first, xr], pleft.at[k, 0], d_xr)
        px[2].wait_recv()
        g[k, second, xl] = (g[k, second, xl].astype(F32) + prelay[k, 1].astype(F32)).astype(BF16)
        px[5] = send(p.base + M_X + 5, g.at[k, second, xl], pright.at[k, 1], d_xl)

    def x_sum(p):
        k, px = p.k, p.px
        for i in (1, 3, 4, 5):
            px[i].wait_recv()

        def three(half, s, z):
            return (
                g[k, 5 * half + s, x, z].astype(F32)
                + pleft[k, half, s, z].astype(F32)
                + pright[k, half, s, z].astype(F32)
            )

        def gone(s, carry):
            for half in range(2):
                zs[k, 5 * half + s] = three(half, s, 1 - zh).astype(BF16)
            return carry

        lax.fori_loop(0, 5, gone, 0)
        p.zp = send(p.base + M_Z, zs.at[k], zr.at[k], d_z)

        def kept(s, carry):
            for half in range(2):
                rf[k, 5 * half + s] = three(half, s, zh)
            return carry

        lax.fori_loop(0, 5, kept, 0)

    def attend(p, inverse):
        k = p.k
        nrow = 8 * RB
        nnew = (k + 1) * RB
        inv = inverse[k * RB : (k + 1) * RB]
        p.zp.wait_recv()

        def projected(s, carry):
            pr[k, s] = ((rf[k, s] + zr[k, s].astype(F32)) * inv).astype(BF16)
            return carry

        lax.fori_loop(0, 10, projected, 0)
        nk[k * RB : (k + 1) * RB] = pr[k, 8]
        nv[k * RB : (k + 1) * RB] = pr[k, 9]

        def queries():
            return pr[k, 0:8].reshape(nrow, HD)

        i_id = lax.broadcasted_iota(jnp.int32, (nrow, nnew), 0)
        j_id = lax.broadcasted_iota(jnp.int32, (nrow, nnew), 1)
        seen = (lax.rem(i_id, 16) == lax.rem(j_id, 16)) & (
            j_id // 16 <= k * TS + lax.rem(i_id // 16, TS)
        )
        s_new = jnp.where(seen, rdot(queries(), nk[0:nnew]) * SCALE, NEG)
        lsum[...] = jnp.full((nrow, 128), NEG, F32)

        def score(b, carry):
            s = rdot(queries(), kv[0, b]) * SCALE
            s = (s.reshape(nrow // 16, 16, 256) + bias[b][None]).reshape(nrow, 256)
            sb[b] = s
            lsum[...] = jnp.maximum(lsum[...], jnp.maximum(s[:, :128], s[:, 128:]))
            return carry

        lax.fori_loop(0, 16, score, 0)
        top = jnp.maximum(
            jnp.max(lsum[...], axis=1, keepdims=True), jnp.max(s_new, axis=1, keepdims=True)
        )
        w_new = jnp.exp(s_new - top)
        new_total = jnp.sum(w_new, axis=1, keepdims=True)
        acc[...] = mdot(w_new.astype(BF16), nv[0:nnew])
        lsum[...] = jnp.zeros((nrow, 128), F32)

        def mix(b, carry):
            w = jnp.exp(sb[b] - top)
            lsum[...] += w[:, :128] + w[:, 128:]
            acc[...] += mdot(w.astype(BF16), kv[1, b])
            return carry

        lax.fori_loop(0, 16, mix, 0)
        total = jnp.sum(lsum[...], axis=1, keepdims=True) + new_total
        head_out = (acc[...] / total).astype(BF16)
        for s in range(8):
            ho[k, c, s // 4, :, (s % 4) * HD : (s % 4 + 1) * HD] = head_out[s * RB : (s + 1) * RB]
        p.hog.start()

    def out_rows(p):
        k, oy = p.k, p.oy
        p.hog.finish()
        lhs = [ho[k, :, f].reshape(16 * RB, 512) for f in range(2)]
        for n in range(2):
            res = mdot(lhs[0], wob[n, 0:512]) + mdot(lhs[1], wob[n, 512:1024])
            o[k, :, :, :, n * 256 : (n + 1) * 256] = res.astype(BF16).reshape(4, 2, 2 * RB, 256)
        oy[0] = send(p.base + M_Y + 0, o.at[k, yo, 0], orelay.at[k, 0], d_yr)
        oy[2] = send(p.base + M_Y + 2, o.at[k, yo, 1], orelay.at[k, 1], d_yl)
        oy[1] = send(p.base + M_Y + 1, o.at[k, yr, 1], oleft.at[k, 1], d_yr)
        oy[3] = send(p.base + M_Y + 3, o.at[k, yl, 0], oright.at[k, 0], d_yl)

    def y_relay(p):
        k, oy = p.k, p.oy
        oy[0].wait_recv()
        o[k, yr, 0] = (o[k, yr, 0].astype(F32) + orelay[k, 0].astype(F32)).astype(BF16)
        oy[4] = send(p.base + M_Y + 4, o.at[k, yr, 0], oleft.at[k, 0], d_yr)
        oy[2].wait_recv()
        o[k, yl, 1] = (o[k, yl, 1].astype(F32) + orelay[k, 1].astype(F32)).astype(BF16)
        oy[5] = send(p.base + M_Y + 5, o.at[k, yl, 1], oright.at[k, 1], d_yl)

    def y_sum(p):
        k, oy = p.k, p.oy
        for i in (1, 3, 4, 5):
            oy[i].wait_recv()

        def three(z):
            return (
                o[k, y, z].astype(F32) + oleft[k, z].astype(F32) + oright[k, z].astype(F32)
            )

        ozs[k] = three(1 - zl).astype(BF16)
        p.oz = send(p.base + M_ZL, ozs.at[k], ozr.at[k], d_zl)
        of[k] = three(zl)

    def add_input(p):
        k = p.k
        p.oz.wait_recv()
        steps = pl.ds(k * TS, TS)
        mine = 2 * y + zl
        for i in range(2):
            rows = pl.ds(i * RB, RB)
            full = (of[k, rows] + ozr[k, rows].astype(F32)).reshape(TS, 16, 512)
            hidden = xb[steps, cidx(y, zl, i)].astype(F32)
            out[steps, mine, pl.ds(16 * i, 16), :] = (hidden + full).astype(BF16)
        p.fog.start()

    def prefill_head(s):
        lanes = slice(s * HD, (s + 1) * HD)

        def score_block(b):
            t = rdot(qb[:, lanes], kv[0, b])
            rows = [
                t[64 * n : 64 * n + 64] * SCALE + marks[b, pl.ds(4 * c + n, 1), :]
                for n in range(4)
            ]
            return jnp.concatenate(rows, axis=0)

        q_id = lax.broadcasted_iota(jnp.int32, (256, 256), 0)
        k_id = lax.broadcasted_iota(jnp.int32, (256, 256), 1)
        own = jnp.where(q_id >= k_id, score_block(c), NEG)
        plsum[...] = jnp.maximum(own[:, :128], own[:, 128:])

        def score(b, carry):
            t = score_block(b)
            psb[b] = t
            plsum[...] = jnp.maximum(plsum[...], jnp.maximum(t[:, :128], t[:, 128:]))
            return carry

        lax.fori_loop(0, c, score, 0)
        psb[c] = own
        top = jnp.max(plsum[...], axis=1, keepdims=True)
        plsum[...] = jnp.zeros((256, 128), F32)
        pacc[...] = jnp.zeros((256, HD), F32)

        def mix(b, carry):
            w = jnp.exp(psb[b] - top)
            plsum[...] += w[:, :128] + w[:, 128:]
            pacc[...] += mdot(w.astype(BF16), kv[1, b])
            return carry

        lax.fori_loop(0, c + 1, mix, 0)
        total = jnp.sum(plsum[...], axis=1, keepdims=True)
        pout[:, lanes] = (pacc[...] / total).astype(BF16)

    todo = list(range(8))

    def fill(count=1):
        for _ in range(count):
            if todo:
                prefill_head(todo.pop(0))

    pa, pb = parts
    other_rows(pa)
    other_rows(pb)

    def sq_send(d, carry):
        sq_msg(d).start()
        return carry

    lax.fori_loop(1, 16, sq_send, 0)
    own_rows(pa)
    own_rows(pb)
    kvg.near()
    x_relay(pa)

    pick = (
        lax.broadcasted_iota(jnp.int32, (16, 256), 1)
        == lax.broadcasted_iota(jnp.int32, (16, 256), 0) + 16 * c
    )
    own_pages = rdot(pick.astype(BF16), pages_ref[...].astype(BF16)).astype(jnp.int32)
    r_id = lax.broadcasted_iota(jnp.int32, (16, 256), 0)
    s_id = lax.broadcasted_iota(jnp.int32, (16, 256), 1)
    lens = jnp.zeros((16, 256), jnp.int32)
    for r in range(16):
        lens = jnp.where(r_id == r, clen_ref[c * 16 + r], lens)
    in_page = lax.rem(s_id, PAGE)
    node_marks = mask_ref[...].astype(BF16)
    node_id = lax.broadcasted_iota(jnp.int32, (64, 256), 0)
    node_of = lax.broadcasted_iota(jnp.int32, (64, 256), 1) // PAGE

    def masks(b, carry):
        page = b * 4 + s_id // PAGE
        live = jnp.zeros((16, 256), F32)
        for slot in range(8):
            hit = (own_pages[:, slot : slot + 1] == page) & (in_page + slot * PAGE < lens)
            live = jnp.where(hit, 1.0, live)
        bias[b] = jnp.where(live > 0.0, 0.0, NEG)
        spread = mdot(node_marks, (node_id == node_of + 4 * b).astype(BF16))
        marks[b] = jnp.where(spread > 0.5, 0.0, NEG)
        return carry

    lax.fori_loop(0, 16, masks, 0)

    def sq_wait(d, carry):
        sq_msg(d).wait_recv()
        return carry

    lax.fori_loop(1, 16, sq_wait, 0)
    sqr[c] = sqs[c]
    flat = jnp.sum(sqr[...], axis=0)[0:1, :]
    row_sq = jnp.sum(jnp.where(eye, flat, 0.0), axis=1, keepdims=True)
    inverse = lax.rsqrt(row_sq / D + 1e-05)

    kvg.far()
    x_relay(pb)
    x_sum(pa)
    kvg.last()
    x_sum(pb)
    kvg.finish()
    attend(pa, inverse)
    attend(pb, inverse)
    loads[10].wait()
    fill()
    pa.hog.near()
    fill()
    pb.hog.near()
    pa.hog.far()
    fill()
    pa.hog.last()
    pb.hog.far()
    loads[8].wait()
    loads[9].wait()
    out_rows(pa)
    pb.hog.last()
    fill()
    out_rows(pb)
    y_relay(pa)
    fill()
    y_relay(pb)
    y_sum(pa)
    fill()
    y_sum(pb)
    add_input(pa)
    fill()
    add_input(pb)
    pa.fog.near()
    fill()
    pb.fog.near()
    pa.fog.far()
    pb.fog.far()
    pa.fog.last()
    pb.fog.last()

    for m in sent:
        m.wait_send()

    def sq_done(d, carry):
        sq_msg(d).wait_send()
        return carry

    lax.fori_loop(1, 16, sq_done, 0)


def layer_call(*args):
    hbm = pl.BlockSpec(memory_space=pl.ANY)
    vmem = pl.BlockSpec(memory_space=pltpu.VMEM)
    smem = pl.BlockSpec(memory_space=pltpu.SMEM)
    return pl.pallas_call(
        layer_kernel,
        out_shape=(
            jax.ShapeDtypeStruct((256, 1024), BF16),
            jax.ShapeDtypeStruct((4, 8, 32, 512), BF16),
        ),
        in_specs=[hbm, hbm, hbm, vmem, vmem, smem, hbm, vmem, hbm, hbm, hbm],
        out_specs=(vmem, vmem),
        scratch_shapes=[
            pltpu.VMEM((2, 16, 256, HD), BF16),
            pltpu.VMEM((256, 1024), BF16),
            pltpu.VMEM((4, 16, 16, 512), BF16),
            pltpu.VMEM((5, 512, 256), BF16),
            pltpu.VMEM((1024, 128), BF16),
            pltpu.VMEM((1024, 128), F32),
            pltpu.VMEM((2, 1024, 256), BF16),
            pltpu.VMEM((NCH, 2, 8, RB, 512), BF16),
            pltpu.VMEM((16, 8, 128), F32),
            pltpu.VMEM((16, 8, 128), F32),
            pltpu.VMEM((NCH, 10, 4, 2, RB, 128), BF16),
            pltpu.VMEM((NCH, 10, 4, 2, RB, 128), BF16),
            pltpu.VMEM((NCH, 10, 4, 2, RB, 128), BF16),
            pltpu.VMEM((NCH, 2, 5, 2, RB, 128), BF16),
            pltpu.VMEM((NCH, 2, 5, 2, RB, 128), BF16),
            pltpu.VMEM((NCH, 2, 5, 2, RB, 128), BF16),
            pltpu.VMEM((NCH, 10, RB, 128), BF16),
            pltpu.VMEM((NCH, 10, RB, 128), BF16),
            pltpu.VMEM((NCH, 10, RB, 128), F32),
            pltpu.VMEM((NCH, 10, RB, 128), BF16),
            pltpu.VMEM((64, 128), BF16),
            pltpu.VMEM((64, 128), BF16),
            pltpu.VMEM((16, 16, 256), F32),
            pltpu.VMEM((16, 64, 256), F32),
            pltpu.VMEM((16, 8 * RB, 256), F32),
            pltpu.VMEM((8 * RB, 128), F32),
            pltpu.VMEM((8 * RB, 128), F32),
            pltpu.VMEM((16, 256, 256), F32),
            pltpu.VMEM((256, 128), F32),
            pltpu.VMEM((256, 128), F32),
            pltpu.VMEM((NCH, 16, 2, RB, 512), BF16),
            pltpu.VMEM((NCH, 4, 2, 2 * RB, 512), BF16),
            pltpu.VMEM((NCH, 2 * RB, 512), F32),
            pltpu.VMEM((NCH, 2, 2 * RB, 512), BF16),
            pltpu.VMEM((NCH, 2, 2 * RB, 512), BF16),
            pltpu.VMEM((NCH, 2, 2 * RB, 512), BF16),
            pltpu.VMEM((NCH, 2 * RB, 512), BF16),
            pltpu.VMEM((NCH, 2 * RB, 512), BF16),
            pltpu.SemaphoreType.DMA((11,)),
            pltpu.SemaphoreType.DMA((NMSG,)),
            pltpu.SemaphoreType.DMA((NMSG,)),
        ],
        compiler_params=pltpu.CompilerParams(
            collective_id=0, has_side_effects=True, vmem_limit_bytes=56 * 1024 * 1024
        ),
        name="layer",
    )(*args)


def per_device(
    prefill_query, prefill_key, prefill_value, tree_mask, pages, cache_len,
    dec_in, norm_gain, w_query, w_keyval, w_out,
):
    prefill_out, dec_out = layer_call(
        prefill_query, prefill_key, prefill_value, tree_mask, pages.T, cache_len,
        dec_in.reshape(4, 16, 16, 512), norm_gain.reshape(4, 128), w_query,
        w_keyval.reshape(1024, 128), w_out,
    )
    return prefill_out, dec_out.reshape(4, 256, 512)


def solution(mesh):
    return jax.shard_map(
        per_device,
        mesh=mesh,
        in_specs=(
            P("ctx", "head"), P("ctx", "head"), P("ctx", "head"), P(), P(), P(),
            P(None, None, "ctx"), P("ctx"), P("ctx", "head"), P("ctx", None, "head"),
            P("head", "ctx"),
        ),
        out_specs=(P("ctx", "head"), P(None, None, "ctx")),
        check_vma=False,
    )
```

```python
import jax
import jax.numpy as jnp
from jax import lax
from jax.experimental import pallas as pl
from jax.experimental.pallas import tpu as pltpu
from jax.sharding import PartitionSpec as P

D = 8192
HD = 128
PAGE = 64
STEPS = 4
SCALE = HD ** (-0.5)
NEG = -1e30
F32 = jnp.float32
BF16 = jnp.bfloat16
MESH = pl.DeviceIdType.MESH

NCH = 2
TS = STEPS // NCH
RB = 16 * TS

KV0 = 0
SQ0 = 17
PART0 = 33
M_CORE, M_X, M_Z, M_HO, M_Y, M_ZL, M_FO = 0, 1, 7, 8, 25, 31, 32
PART_MSGS = 36
NMSG = PART0 + NCH * PART_MSGS


ORDER = (
    "p0.other", "p1.other", "kv.r1", "kv.r2", "p0.own", "all.sq", "kv.r5", "kv.r0", "p0.xr0",
    "p0.xr2", "p1.own", "all.mask", "kv.r3", "kv.r4", "p1.xr0", "p1.xr2", "p0.xsum", "all.list",
    "kv.r7", "p1.xsum", "kv.fin", "all.take", "p0.att", "p1.att", "p0.h0", "p0.h1", "p0.h2",
    "p1.h1", "p1.h2", "p0.h3", "p0.h4", "p1.h0", "p0.h5", "p1.h5", "p0.h7", "p1.h3", "p1.h4",
    "p0.out", "p1.h7", "p0.yr0", "p0.yr2", "p1.out", "p0.ysum", "p1.yr0", "p1.yr2", "p0.add",
    "p1.ysum", "p1.add", "p0.f1", "p0.f2", "p1.f1", "p1.f2", "p0.f5", "p1.f5",
)


def rdot(a, b):
    return lax.dot_general(a, b, (((1,), (1,)), ((), ())), preferred_element_type=F32)


def mdot(a, b):
    return lax.dot_general(a, b, (((1,), (0,)), ((), ())), preferred_element_type=F32)


def layer_kernel(
    key_ref, val_ref, mask_ref, pages_ref, clen_ref, x_ref, gain_ref, wq_ref, wkv_ref, wo_ref,
    kv_out, picks, out,
    kv, xb, wb, wkvb, wkvf, wob, xs, sqs, sqr, gs, gr, g, prelay, pleft, pright, zs, zr, rf,
    pr, nk, nv, bias, chosen, pool, sb, ho, o, orelay, oleft, oright, ozs, ozr,
    lsem, ssem, rsem,
):
    c = lax.axis_index("ctx")
    h = lax.axis_index("head")
    core = lax.rem(c, 2)
    zh = lax.rem(c // 2, 2)
    x = c // 4
    y = lax.rem(h, 4)
    zl = h // 4

    def cidx(xi, zi, ci):
        return xi * 4 + zi * 2 + ci

    def hidx(yi, zi):
        return zi * 4 + yi

    xr, xl, xo = lax.rem(x + 1, 4), lax.rem(x + 3, 4), lax.rem(x + 2, 4)
    yr, yl, yo = lax.rem(y + 1, 4), lax.rem(y + 3, 4), lax.rem(y + 2, 4)
    d_xr = (cidx(xr, zh, core), h)
    d_xl = (cidx(xl, zh, core), h)
    d_z = (cidx(x, 1 - zh, core), h)
    d_c = (cidx(x, zh, 1 - core), h)
    d_yr = (c, hidx(yr, zl))
    d_yl = (c, hidx(yl, zl))
    d_zl = (c, hidx(y, 1 - zl))

    def msg(i, src, dst, dev):
        return pltpu.make_async_remote_copy(
            src_ref=src, dst_ref=dst, send_sem=ssem.at[i], recv_sem=rsem.at[i],
            device_id=dev, device_id_type=MESH,
        )

    loads = [
        pltpu.make_async_copy(key_ref, kv.at[0, c], lsem.at[0]),
        pltpu.make_async_copy(val_ref, kv.at[1, c], lsem.at[1]),
        pltpu.make_async_copy(x_ref, xb, lsem.at[2]),
        pltpu.make_async_copy(wkv_ref, wkvb, lsem.at[3]),
    ]
    for j in range(4):
        loads.append(
            pltpu.make_async_copy(wq_ref.at[:, pl.ds(256 * j, 256)], wb.at[j], lsem.at[4 + j])
        )
    for j in range(2):
        loads.append(
            pltpu.make_async_copy(wo_ref.at[:, pl.ds(256 * j, 256)], wob.at[j], lsem.at[8 + j])
        )
    for copy in loads:
        copy.start()

    barrier = pltpu.get_barrier_semaphore()

    def greet(d, carry):
        pl.semaphore_signal(
            barrier, inc=1, device_id=(lax.rem(c + d, 16), h), device_id_type=MESH
        )
        return carry

    lax.fori_loop(1, 16, greet, 0)
    for dev in (d_yr, d_yl, d_zl):
        pl.semaphore_signal(barrier, inc=1, device_id=dev, device_id_type=MESH)
    pl.semaphore_wait(barrier, 18)

    sent = []

    def send(i, src, dst, dev):
        m = msg(i, src, dst, dev)
        m.start()
        sent.append(m)
        return m

    class Gather:
        def __init__(self, base, blk, half):
            self.base, self.blk, self.half = base, blk, half
            self.m = {}

        def put(self, k, ref, dev):
            self.m[k] = send(self.base + k, ref, ref, dev)

        def share(self, k, xi, zi):
            ref = self.blk(xi, zi)
            self.m[9 + k] = send(self.base + 9 + k, ref, ref, d_c)

        def start(self):
            own = self.blk(x, zh)
            self.put(0, own, d_z)
            self.put(1, own, d_xr)
            self.put(2, own, d_xl)
            self.share(0, x, zh)

        def take(self, k):
            z2 = 1 - zh
            self.m[k].wait_recv()
            if k == 0:
                other = self.blk(x, z2)
                self.put(3, other, d_xr)
                self.put(4, other, d_xl)
                self.share(1, x, z2)
            elif k == 1:
                self.put(5, self.half(xl, zh, 0), d_xr)
                self.share(2, xl, zh)
            elif k == 2:
                self.put(6, self.half(xr, zh, 1), d_xl)
                self.share(3, xr, zh)
            elif k == 3:
                self.put(7, self.half(xl, z2, 0), d_xr)
                self.share(4, xl, z2)
            elif k == 4:
                self.put(8, self.half(xr, z2, 1), d_xl)
                self.share(5, xr, z2)
            elif k == 5:
                self.m[6].wait_recv()
                self.share(6, xo, zh)
            else:
                self.m[8].wait_recv()
                self.share(7, xo, z2)

        def finish(self):
            for k in range(8):
                self.m[9 + k].wait_recv()

    kvg = Gather(
        KV0, lambda a, b: kv.at[:, cidx(a, b, core)], lambda a, b, k: kv.at[k, cidx(a, b, core)]
    )
    loads[0].wait()
    loads[1].wait()
    kvg.start()

    loads[2].wait()
    row_id = lax.broadcasted_iota(jnp.int32, (64, 128), 0)
    lane_id = lax.broadcasted_iota(jnp.int32, (64, 128), 1)
    eye = row_id == lane_id
    gain4 = gain_ref[...].astype(F32)
    gain = jnp.concatenate([gain4[i : i + 1] for i in range(4)], axis=1)

    def scale_rows(p, side):
        steps = pl.ds(p.k * TS, TS)

        def body(i, carry):
            raw = xb[steps, 2 * i + side].astype(F32).reshape(RB, 512)
            xs[p.k, side, i] = (raw * gain).astype(BF16)
            return carry

        lax.fori_loop(0, 8, body, 0, unroll=True)

    def squares(d, carry):
        raw = xb[:, d].astype(F32).reshape(64, 512)
        part = jnp.sum(raw * raw, axis=1, keepdims=True)
        flat = jnp.sum(jnp.where(eye, part, 0.0), axis=0, keepdims=True)
        sqs[d] = jnp.broadcast_to(flat, (8, 128))
        return carry

    def sq_msg(d):
        to = lax.rem(c + d, 16)
        return msg(SQ0 + d, sqs.at[to], sqr.at[c], (to, h))

    first = pl.ds(0, 5)
    second = pl.ds(5, 5)

    class Part:
        pass

    parts = []
    for k in range(NCH):
        p = Part()
        p.k = k
        p.base = PART0 + k * PART_MSGS
        p.px, p.oy = {}, {}
        p.hog = Gather(
            p.base + M_HO, lambda a, b, k=k: ho.at[k, cidx(a, b, core)],
            lambda a, b, f, k=k: ho.at[k, cidx(a, b, core), f],
        )
        parts.append(p)

    def other_rows(p):
        k = p.k

        rows = xs[k, 1 - core].reshape(8 * RB, 512)
        for j in range(5):
            res = mdot(rows, wb[j]).astype(BF16)
            gs[k, 2 * j] = res[:, :128].reshape(4, 2, RB, 128)
            gs[k, 2 * j + 1] = res[:, 128:].reshape(4, 2, RB, 128)
        p.core = send(p.base + M_CORE, gs.at[k], gr.at[k], d_c)

    def own_rows(p):
        k, px = p.k, p.px
        p.core.wait_recv()
        rows = xs[k, core].reshape(8 * RB, 512)

        def body(j):
            res = mdot(rows, wb[j])
            for i in range(2):
                both = res[:, 128 * i : 128 * i + 128].reshape(4, 2, RB, 128) + gr[
                    k, 2 * j + i
                ].astype(F32)
                g[k, 2 * j + i] = both.astype(BF16)

        for j in range(3):
            body(j)
        px[0] = send(p.base + M_X + 0, g.at[k, first, xo], prelay.at[k, 0], d_xr)
        px[3] = send(p.base + M_X + 3, g.at[k, first, xl], pright.at[k, 0], d_xl)
        for j in range(3, 5):
            body(j)
        px[2] = send(p.base + M_X + 2, g.at[k, second, xo], prelay.at[k, 1], d_xl)
        px[1] = send(p.base + M_X + 1, g.at[k, second, xr], pleft.at[k, 1], d_xr)

    def x_relay(p, half):
        k, px = p.k, p.px
        which, to, dev, into = ((first, xr, d_xr, pleft), (second, xl, d_xl, pright))[half]
        px[2 * half].wait_recv()
        g[k, which, to] = (g[k, which, to].astype(F32) + prelay[k, half].astype(F32)).astype(BF16)
        px[4 + half] = send(p.base + M_X + 4 + half, g.at[k, which, to], into.at[k, half], dev)

    def x_sum(p):
        k, px = p.k, p.px
        for i in (1, 3, 4, 5):
            px[i].wait_recv()

        def three(half, s, z):
            return (
                g[k, 5 * half + s, x, z].astype(F32)
                + pleft[k, half, s, z].astype(F32)
                + pright[k, half, s, z].astype(F32)
            )

        for s in range(10):
            zs[k, s] = three(s // 5, s % 5, 1 - zh).astype(BF16)
        p.zp = send(p.base + M_Z, zs.at[k], zr.at[k], d_z)

        for s in range(10):
            rf[k, s] = three(s // 5, s % 5, zh)

    def attend(p, inverse):
        k = p.k
        nrow = 8 * RB
        nnew = (k + 1) * RB
        inv = inverse[k * RB : (k + 1) * RB]
        p.zp.wait_recv()

        for s in range(10):
            pr[k, s] = ((rf[k, s] + zr[k, s].astype(F32)) * inv).astype(BF16)
        nk[k * RB : (k + 1) * RB] = pr[k, 8]
        nv[k * RB : (k + 1) * RB] = pr[k, 9]

        q = pr[k, 0:8].reshape(nrow, HD)
        i_id = lax.broadcasted_iota(jnp.int32, (nrow, nnew), 0)
        j_id = lax.broadcasted_iota(jnp.int32, (nrow, nnew), 1)
        seen = (lax.rem(i_id, 16) == lax.rem(j_id, 16)) & (
            j_id // 16 <= k * TS + lax.rem(i_id // 16, TS)
        )
        s_new = jnp.where(seen, rdot(q, nk[0:nnew]) * SCALE, NEG)
        peak = None
        for b in range(8):
            s = rdot(q, pool[0, 256 * b : 256 * b + 256]) * SCALE
            s = (s.reshape(nrow // 16, 16, 256) + bias[b][None]).reshape(nrow, 256)
            sb[b] = s
            here = jnp.maximum(s[:, :128], s[:, 128:])
            peak = here if peak is None else jnp.maximum(peak, here)
        top = jnp.maximum(
            jnp.max(peak, axis=1, keepdims=True), jnp.max(s_new, axis=1, keepdims=True)
        )
        w_new = jnp.exp(s_new - top)
        mixed = mdot(w_new.astype(BF16), nv[0:nnew])
        part = None
        for b in range(8):
            w = jnp.exp(sb[b] - top)
            here = w[:, :128] + w[:, 128:]
            part = here if part is None else part + here
            mixed = mixed + mdot(w.astype(BF16), pool[1, 256 * b : 256 * b + 256])
        total = jnp.sum(part, axis=1, keepdims=True) + jnp.sum(w_new, axis=1, keepdims=True)
        head_out = (mixed / total).astype(BF16)
        for s in range(8):
            ho[k, c, s // 4, :, (s % 4) * HD : (s % 4 + 1) * HD] = head_out[s * RB : (s + 1) * RB]
        p.hog.start()

    def out_rows(p):
        k, oy = p.k, p.oy
        p.hog.finish()
        lhs = [ho[k, :, f].reshape(16 * RB, 512) for f in range(2)]
        for n in range(2):
            res = mdot(lhs[0], wob[n, 0:512]) + mdot(lhs[1], wob[n, 512:1024])
            o[k, :, :, :, n * 256 : (n + 1) * 256] = res.astype(BF16).reshape(4, 2, 2 * RB, 256)
        oy[0] = send(p.base + M_Y + 0, o.at[k, yo, 0], orelay.at[k, 0], d_yr)
        oy[2] = send(p.base + M_Y + 2, o.at[k, yo, 1], orelay.at[k, 1], d_yl)
        oy[1] = send(p.base + M_Y + 1, o.at[k, yr, 1], oleft.at[k, 1], d_yr)
        oy[3] = send(p.base + M_Y + 3, o.at[k, yl, 0], oright.at[k, 0], d_yl)

    def y_relay(p, half):
        k, oy = p.k, p.oy
        to, dev, into = ((yr, d_yr, oleft), (yl, d_yl, oright))[half]
        oy[2 * half].wait_recv()
        o[k, to, half] = (o[k, to, half].astype(F32) + orelay[k, half].astype(F32)).astype(BF16)
        oy[4 + half] = send(p.base + M_Y + 4 + half, o.at[k, to, half], into.at[k, half], dev)

    def y_sum(p):
        k, oy = p.k, p.oy
        for i in (1, 3, 4, 5):
            oy[i].wait_recv()

        for z in range(2):
            ozs[k, z] = (
                o[k, y, z].astype(F32) + oleft[k, z].astype(F32) + oright[k, z].astype(F32)
            ).astype(BF16)
        p.oz = send(p.base + M_ZL, ozs.at[k], ozr.at[k], d_zl)

    def add_input(p):
        k = p.k
        p.oz.wait_recv()
        steps = pl.ds(k * TS, TS)
        for z in range(2):
            for i in range(2):
                rows = pl.ds(i * RB, RB)
                full = ozs[k, z, rows].astype(F32) + ozr[k, z, rows].astype(F32)
                hidden = xb[steps, cidx(y, z, i)].astype(F32)
                out[steps, 2 * y + z, pl.ds(16 * i, 16), :] = (
                    hidden + full.reshape(TS, 16, 512)
                ).astype(BF16)
        own = out.at[steps, pl.ds(2 * y, 2)]
        p.fo = {
            1: send(p.base + M_FO, own, own, d_yr),
            2: send(p.base + M_FO + 1, own, own, d_yl),
        }

    def pass_on(p, k):
        steps = pl.ds(p.k * TS, TS)
        p.fo[k].wait_recv()
        if k == 1:
            part = out.at[steps, 2 * yl]
            p.fo[5] = send(p.base + M_FO + 2, part, part, d_yr)
        elif k == 2:
            part = out.at[steps, 2 * yr + 1]
            p.fo[6] = send(p.base + M_FO + 3, part, part, d_yl)
        else:
            p.fo[6].wait_recv()

    def load_weights():
        for k in range(3, 8):
            loads[k].wait()
        wkvf[...] = wkvb[...].astype(F32)
        wb[4, :, 0:128] = wkvf[pl.ds(0, 512, stride=2), :].astype(BF16)
        wb[4, :, 128:256] = wkvf[pl.ds(1, 512, stride=2), :].astype(BF16)

    def sum_squares():
        lax.fori_loop(0, 16, squares, 0, unroll=4)

        def sq_send(d, carry):
            sq_msg(d).start()
            return carry

        lax.fori_loop(1, 16, sq_send, 0)

    def inverse_rms():
        def sq_wait(d, carry):
            sq_msg(d).wait_recv()
            return carry

        lax.fori_loop(1, 16, sq_wait, 0)
        sqr[c] = sqs[c]
        flat = jnp.sum(sqr[...], axis=0)[0:1, :]
        row_sq = jnp.sum(jnp.where(eye, flat, 0.0), axis=1, keepdims=True)
        return lax.rsqrt(row_sq / D + 1e-05)

    def choose_pages():
        pick = (
            lax.broadcasted_iota(jnp.int32, (16, 256), 1)
            == lax.broadcasted_iota(jnp.int32, (16, 256), 0) + 16 * c
        )
        own_pages = rdot(pick.astype(BF16), pages_ref[...].astype(BF16)).astype(jnp.int32)
        r_id = lax.broadcasted_iota(jnp.int32, (16, 256), 0)
        s_id = lax.broadcasted_iota(jnp.int32, (16, 256), 1)
        lens = jnp.zeros((16, 256), jnp.int32)
        for r in range(16):
            lens = jnp.where(r_id == r, clen_ref[c * 16 + r], lens)
        in_page = lax.rem(s_id, PAGE)
        page_id = lax.broadcasted_iota(jnp.int32, (16, 64), 1)
        named = jnp.zeros((16, 64), F32)
        for slot in range(8):
            named = jnp.where(own_pages[:, slot : slot + 1] == page_id, 1.0, named)
        present = jnp.broadcast_to(jnp.max(named, axis=0, keepdims=True), (16, 64))
        a_id = lax.broadcasted_iota(jnp.int32, (64, 64), 0)
        b_id = lax.broadcasted_iota(jnp.int32, (64, 64), 1)
        ahead = (a_id // 4 == b_id // 4) & (a_id < b_id)
        rank = mdot(present.astype(BF16), ahead.astype(BF16))
        code = jnp.where(present > 0.5, rank + 1.0, 0.0).astype(BF16)
        node_id = lax.broadcasted_iota(jnp.int32, (64, 256), 0)
        node_of = lax.broadcasted_iota(jnp.int32, (64, 256), 1) // PAGE
        to_id = lax.broadcasted_iota(jnp.int32, (128, 256), 0)
        from_id = lax.broadcasted_iota(jnp.int32, (128, 256), 1)
        same = lax.rem(to_id, PAGE) == lax.rem(from_id, PAGE)
        want = jnp.where(same, (to_id // PAGE + 1).astype(F32), -1.0)
        last = [
            (own_pages[:, slot : slot + 1], lens - slot * PAGE, s_id // PAGE)
            for slot in range(8)
        ]

        def choose(b):
            live = jnp.zeros((16, 256), F32)
            for named_page, upto, page in last:
                hit = (named_page - 4 * b == page) & (in_page < upto)
                live = jnp.where(hit, 1.0, live)
            spread = mdot(code, (node_id == node_of + 4 * b).astype(BF16))
            sel = jnp.where(spread[0:1] == want, 1.0, 0.0).astype(BF16)
            chosen[b] = sel
            return jnp.where(rdot(live.astype(BF16), sel) > 0.5, 0.0, NEG)

        def choose_two(i, carry):
            bias[i, :, 0:128] = choose(2 * i)
            bias[i, :, 128:256] = choose(2 * i + 1)
            return carry

        lax.fori_loop(0, 8, choose_two, 0, unroll=2)

    def take_pages():
        def take(b, carry):
            for f in range(2):
                rows = pl.ds(pl.multiple_of(128 * b, 128), 128)
                pool[f, rows] = mdot(chosen[b], kv[f, b]).astype(BF16)
            return carry

        lax.fori_loop(0, 16, take, 0, unroll=8)

    def list_pages():
        a_id = lax.broadcasted_iota(jnp.int32, (64, 64), 0)
        b_id = lax.broadcasted_iota(jnp.int32, (64, 64), 1)
        col_id = lax.broadcasted_iota(jnp.int32, (64, 128), 1)
        p_id = lax.broadcasted_iota(jnp.int32, (64, 128), 0)
        rows = []
        for n in range(4):
            a = 4 * c + n
            line = mask_ref[pl.ds(a, 1), :].astype(F32)
            readable = jnp.sum(jnp.where(a_id == b_id, line, 0.0), axis=1, keepdims=True)
            readable = jnp.where((readable > 0.5) & (p_id < a), 1.0, 0.0)
            before = mdot((b_id < a_id).astype(BF16), readable.astype(BF16))
            place = jnp.where(p_id == a, 0.0, before + 1.0).astype(jnp.int32)
            hit = (place == col_id) & ((readable > 0.5) | (p_id == a))
            line = jnp.sum(jnp.where(hit, p_id.astype(F32), 0.0), axis=0, keepdims=True)
            count = jnp.sum(readable, axis=0, keepdims=True) + 1.0
            rows.append(jnp.where(col_id[0:1] == 127, count, line))
        picks[...] = jnp.concatenate(rows + rows, axis=0).astype(jnp.int32)

    keep = pltpu.make_async_copy(kv, kv_out, lsem.at[10])
    rms = []

    def step(event):
        who, what = event.split(".")
        if who == "kv":
            if what == "fin":
                kvg.finish()
                keep.start()
            else:
                kvg.take(int(what[1]))
            return
        if who == "all":
            {"sq": sum_squares, "mask": choose_pages, "take": take_pages, "list": list_pages}[
                what
            ]()
            return
        p = parts[int(who[1])]
        if what == "other":
            scale_rows(p, 1 - core)
            if p.k == 0:
                load_weights()
            other_rows(p)
        elif what == "own":
            scale_rows(p, core)
            own_rows(p)
        elif what[0] == "x":
            if what == "xsum":
                x_sum(p)
            else:
                x_relay(p, int(what[2]) // 2)
        elif what == "att":
            if not rms:
                rms.append(inverse_rms())
            attend(p, rms[0])
        elif what[0] == "h":
            p.hog.take(int(what[1]))
        elif what == "out":
            if p.k == 0:
                loads[8].wait()
                loads[9].wait()
            out_rows(p)
        elif what == "ysum":
            y_sum(p)
        elif what[0] == "y":
            y_relay(p, int(what[2]) // 2)
        elif what == "add":
            add_input(p)
        else:
            pass_on(p, int(what[1]))

    for event in ORDER:
        step(event)
    keep.wait()

    for m in sent:
        m.wait_send()

    def sq_done(d, carry):
        sq_msg(d).wait_send()
        return carry

    lax.fori_loop(1, 16, sq_done, 0)


def layer_call(*args):
    hbm = pl.BlockSpec(memory_space=pl.ANY)
    vmem = pl.BlockSpec(memory_space=pltpu.VMEM)
    smem = pl.BlockSpec(memory_space=pltpu.SMEM)
    return pl.pallas_call(
        layer_kernel,
        out_shape=(
            jax.ShapeDtypeStruct((2, 16, 256, HD), BF16),
            jax.ShapeDtypeStruct((8, 128), jnp.int32),
            jax.ShapeDtypeStruct((4, 8, 32, 512), BF16),
        ),
        in_specs=[hbm, hbm, vmem, vmem, smem, hbm, vmem, hbm, hbm, hbm],
        out_specs=(hbm, vmem, vmem),
        scratch_shapes=[
            pltpu.VMEM((2, 16, 256, HD), BF16),
            pltpu.VMEM((4, 16, 16, 512), BF16),
            pltpu.VMEM((5, 512, 256), BF16),
            pltpu.VMEM((1024, 128), BF16),
            pltpu.VMEM((1024, 128), F32),
            pltpu.VMEM((2, 1024, 256), BF16),
            pltpu.VMEM((NCH, 2, 8, RB, 512), BF16),
            pltpu.VMEM((16, 8, 128), F32),
            pltpu.VMEM((16, 8, 128), F32),
            pltpu.VMEM((NCH, 10, 4, 2, RB, 128), BF16),
            pltpu.VMEM((NCH, 10, 4, 2, RB, 128), BF16),
            pltpu.VMEM((NCH, 10, 4, 2, RB, 128), BF16),
            pltpu.VMEM((NCH, 2, 5, 2, RB, 128), BF16),
            pltpu.VMEM((NCH, 2, 5, 2, RB, 128), BF16),
            pltpu.VMEM((NCH, 2, 5, 2, RB, 128), BF16),
            pltpu.VMEM((NCH, 10, RB, 128), BF16),
            pltpu.VMEM((NCH, 10, RB, 128), BF16),
            pltpu.VMEM((NCH, 10, RB, 128), F32),
            pltpu.VMEM((NCH, 10, RB, 128), BF16),
            pltpu.VMEM((64, 128), BF16),
            pltpu.VMEM((64, 128), BF16),
            pltpu.VMEM((8, 16, 256), F32),
            pltpu.VMEM((16, 128, 256), BF16),
            pltpu.VMEM((2, 2048, HD), BF16),
            pltpu.VMEM((8, 8 * RB, 256), F32),
            pltpu.VMEM((NCH, 16, 2, RB, 512), BF16),
            pltpu.VMEM((NCH, 4, 2, 2 * RB, 512), BF16),
            pltpu.VMEM((NCH, 2, 2 * RB, 512), BF16),
            pltpu.VMEM((NCH, 2, 2 * RB, 512), BF16),
            pltpu.VMEM((NCH, 2, 2 * RB, 512), BF16),
            pltpu.VMEM((NCH, 2, 2 * RB, 512), BF16),
            pltpu.VMEM((NCH, 2, 2 * RB, 512), BF16),
            pltpu.SemaphoreType.DMA((11,)),
            pltpu.SemaphoreType.DMA((NMSG,)),
            pltpu.SemaphoreType.DMA((NMSG,)),
        ],
        compiler_params=pltpu.CompilerParams(
            collective_id=0, has_side_effects=True, vmem_limit_bytes=56 * 1024 * 1024
        ),
        name="layer",
    )(*args)


def prefill_kernel(
    q_ref, kv_ref, picks, dec_ref, out, dec_out, kv, stage, mixes, peaks, totals, sem
):
    fetched = pltpu.make_async_copy(dec_ref, stage, sem.at[0])
    moved = pltpu.make_async_copy(stage, dec_out, sem.at[3])
    loads = [pltpu.make_async_copy(kv_ref.at[i], kv.at[i], sem.at[1 + i]) for i in range(2)]
    for copy in loads:
        copy.start()
    fetched.start()
    for copy in loads:
        copy.wait()
    fetched.wait()
    moved.start()

    def attend(n, start, pages, state):
        keys = jnp.concatenate([kv[0, picks[n, start + k]] for k in range(pages)], axis=0)
        values = jnp.concatenate([kv[1, picks[n, start + k]] for k in range(pages)], axis=0)
        q = jnp.concatenate([q_ref[n, :, s * HD : (s + 1) * HD] for s in range(8)], axis=0)
        i_id = lax.broadcasted_iota(jnp.int32, (512, pages * PAGE), 0)
        j_id = lax.broadcasted_iota(jnp.int32, (512, pages * PAGE), 1)
        allowed = j_id < (picks[n, 127] - start) * PAGE
        if state is None:
            allowed = allowed & ((j_id >= PAGE) | (j_id <= lax.rem(i_id, PAGE)))
        s = jnp.where(allowed, rdot(q, keys) * SCALE, NEG)
        peak = jnp.max(s, axis=1, keepdims=True)
        if state is not None:
            peak = jnp.maximum(peak, state[0])
        w = jnp.exp(s - peak)
        total = jnp.sum(w, axis=1, keepdims=True)
        mixed = mdot(w.astype(BF16), values)
        if state is not None:
            factor = jnp.exp(state[0] - peak)
            total = total + state[1] * factor
            mixed = mixed + state[2] * factor
        return peak, total, mixed

    for n in range(4):
        peak, total, mixed = attend(n, 0, 8, None)
        peaks[n] = jnp.broadcast_to(peak, (512, 128))
        totals[n] = jnp.broadcast_to(total, (512, 128))
        mixes[n] = mixed

    def deep(n, carry):
        def more(t, inner):
            state = (peaks[n][:, 0:1], totals[n][:, 0:1], mixes[n])
            peak, total, mixed = attend(n, 8 + 4 * t, 4, state)
            peaks[n] = jnp.broadcast_to(peak, (512, 128))
            totals[n] = jnp.broadcast_to(total, (512, 128))
            mixes[n] = mixed
            return inner

        return lax.fori_loop(0, jnp.maximum(picks[n, 127] - 5, 0) // 4, more, carry)

    lax.fori_loop(0, 4, deep, 0)
    for n in range(4):
        result = (mixes[n] / totals[n]).astype(BF16)
        for s in range(8):
            out[n, :, s * HD : (s + 1) * HD] = result[s * 64 : (s + 1) * 64]
    moved.wait()


def prefill_call(q, kv, picks, dec):
    hbm = pl.BlockSpec(memory_space=pl.ANY)
    vmem = pl.BlockSpec(memory_space=pltpu.VMEM)
    smem = pl.BlockSpec(memory_space=pltpu.SMEM)
    return pl.pallas_call(
        prefill_kernel,
        out_shape=(
            jax.ShapeDtypeStruct((4, PAGE, 1024), BF16),
            jax.ShapeDtypeStruct(dec.shape, BF16),
        ),
        in_specs=[vmem, hbm, smem, hbm],
        out_specs=(vmem, hbm),
        scratch_shapes=[
            pltpu.VMEM((2, 64, PAGE, HD), BF16),
            pltpu.VMEM(dec.shape, BF16),
            pltpu.VMEM((4, 512, HD), F32),
            pltpu.VMEM((4, 512, 128), F32),
            pltpu.VMEM((4, 512, 128), F32),
            pltpu.SemaphoreType.DMA((4,)),
        ],
        compiler_params=pltpu.CompilerParams(vmem_limit_bytes=62 * 1024 * 1024),
        name="prefill",
    )(q, kv, picks, dec)


def per_device(
    prefill_query, prefill_key, prefill_value, tree_mask, pages, cache_len,
    dec_in, norm_gain, w_query, w_keyval, w_out,
):
    kv, picks, dec = layer_call(
        prefill_key, prefill_value, tree_mask, pages.T, cache_len,
        dec_in.reshape(4, 16, 16, 512), norm_gain.reshape(4, 128), w_query,
        w_keyval.reshape(1024, 128), w_out,
    )
    prefill_out, dec_out = prefill_call(
        prefill_query.reshape(4, PAGE, 1024), kv.reshape(2, 64, PAGE, HD), picks, dec
    )
    return prefill_out.reshape(256, 1024), dec_out.reshape(4, 256, 512)


def solution(mesh):
    return jax.shard_map(
        per_device,
        mesh=mesh,
        in_specs=(
            P("ctx", "head"), P("ctx", "head"), P("ctx", "head"), P(), P(), P(),
            P(None, None, "ctx"), P("ctx"), P("ctx", "head"), P("ctx", None, "head"),
            P("head", "ctx"),
        ),
        out_specs=(P("ctx", "head"), P(None, None, "ctx")),
        check_vma=False,
    )
```

```python
import jax
import jax.numpy as jnp
from jax import lax
from jax.experimental import pallas as pl
from jax.experimental.pallas import tpu as pltpu
from jax.sharding import PartitionSpec as P

D = 8192
HD = 128
PAGE = 64
STEPS = 4
SCALE = HD ** (-0.5)
NEG = -1e30
F32 = jnp.float32
BF16 = jnp.bfloat16
MESH = pl.DeviceIdType.MESH

NCH = 4
TS = STEPS // NCH
RB = 16 * TS

KV0 = 0
SQ0 = 17
PART0 = 33
M_CORE, M_X, M_Z, M_HO, M_Y, M_ZL, M_FO = 0, 1, 7, 8, 25, 31, 32
PART_MSGS = 36
NMSG = PART0 + NCH * PART_MSGS


ORDER = (
    "p0.other", "p0.own", "all.sq", "kv.r2", "kv.r1", "p0.xr0", "p0.xr2", "p1.other", "kv.r0",
    "p2.other", "kv.r5", "p1.own", "all.mask", "kv.r3", "kv.r4", "p3.other", "p1.xr0", "p1.xr2",
    "p0.xsum", "p2.own", "kv.r7", "p3.own", "p1.xsum", "kv.fin", "all.take", "p2.xr2", "p2.xr0",
    "p0.att", "p3.xr2", "p2.xsum", "p3.xr0", "p1.att", "p3.xsum", "p0.h1", "p0.h2", "p0.h0",
    "p1.h1", "p2.att", "p0.h3", "p1.h0", "p0.h4", "p0.h5", "p3.att", "p2.h0", "p1.h4", "p0.h7",
    "p1.h3", "p2.h2", "p2.h1", "p1.h2", "p2.h3", "p2.h4", "p0.out", "p2.h5", "p1.h7", "p1.h5",
    "p2.h7", "p3.h0", "p3.h2", "p3.h1", "p2.out", "p0.yr2", "p3.h4", "p3.h3", "p0.yr0",
    "p1.out", "p3.h5", "p2.yr0", "p2.yr2", "p3.h7", "p0.ysum", "p1.yr0", "p1.yr2", "p3.out",
    "p1.ysum", "p2.ysum", "p3.yr0", "p3.yr2", "p0.add", "p1.add", "p3.ysum", "p2.add", "p0.f1",
    "all.list", "p1.f2", "p3.add", "p1.f1", "p2.f2", "p2.f1", "p0.f2", "p3.f1", "p3.f2",
    "p2.f5", "p1.f5", "p0.f5", "p3.f5",
)


def rdot(a, b):
    return lax.dot_general(a, b, (((1,), (1,)), ((), ())), preferred_element_type=F32)


def mdot(a, b):
    return lax.dot_general(a, b, (((1,), (0,)), ((), ())), preferred_element_type=F32)


def layer_kernel(
    key_ref, val_ref, mask_hbm, pages_hbm, clen_hbm, x_ref, gain_hbm, wq_ref, wkv_ref, wo_ref,
    kv_out, picks, out,
    mask_ref, pages_ref, clen_ref, gain_ref,
    kv, xb, wb, wkvb, wkvf, wob, xs, sqs, sqr, gs, gr, g, prelay, pleft, pright, zs, zr, rf,
    pr, nk, nv, bias, chosen, pool_k, pool_v, sb, ho, o, orelay, oleft, oright, ozs, ozr,
    lsem, ssem, rsem,
):
    c = lax.axis_index("ctx")
    h = lax.axis_index("head")
    core = lax.rem(c, 2)
    zh = lax.rem(c // 2, 2)
    x = c // 4
    y = lax.rem(h, 4)
    zl = h // 4

    def cidx(xi, zi, ci):
        return xi * 4 + zi * 2 + ci

    def hidx(yi, zi):
        return zi * 4 + yi

    xr, xl, xo = lax.rem(x + 1, 4), lax.rem(x + 3, 4), lax.rem(x + 2, 4)
    yr, yl, yo = lax.rem(y + 1, 4), lax.rem(y + 3, 4), lax.rem(y + 2, 4)
    d_xr = (cidx(xr, zh, core), h)
    d_xl = (cidx(xl, zh, core), h)
    d_z = (cidx(x, 1 - zh, core), h)
    d_c = (cidx(x, zh, 1 - core), h)
    d_yr = (c, hidx(yr, zl))
    d_yl = (c, hidx(yl, zl))
    d_zl = (c, hidx(y, 1 - zl))

    def msg(i, src, dst, dev):
        return pltpu.make_async_remote_copy(
            src_ref=src, dst_ref=dst, send_sem=ssem.at[i], recv_sem=rsem.at[i],
            device_id=dev, device_id_type=MESH,
        )

    barrier = pltpu.get_barrier_semaphore()

    def greet(d, carry):
        pl.semaphore_signal(
            barrier, inc=1, device_id=(lax.rem(c + d, 16), h), device_id_type=MESH
        )
        return carry

    for dev in (d_yr, d_yl, d_zl):
        pl.semaphore_signal(barrier, inc=1, device_id=dev, device_id_type=MESH)
    lax.fori_loop(1, 16, greet, 0)

    loads = [
        pltpu.make_async_copy(key_ref, kv.at[0, c], lsem.at[0]),
        pltpu.make_async_copy(val_ref, kv.at[1, c], lsem.at[1]),
        pltpu.make_async_copy(x_ref, xb, lsem.at[2]),
        pltpu.make_async_copy(wkv_ref, wkvb, lsem.at[3]),
    ]
    for j in range(4):
        loads.append(
            pltpu.make_async_copy(wq_ref.at[:, pl.ds(256 * j, 256)], wb.at[j], lsem.at[4 + j])
        )
    for j in range(2):
        loads.append(
            pltpu.make_async_copy(wo_ref.at[:, pl.ds(256 * j, 256)], wob.at[j], lsem.at[8 + j])
        )
    for i, (src, dst) in enumerate(
        ((gain_hbm, gain_ref), (mask_hbm, mask_ref), (pages_hbm, pages_ref), (clen_hbm, clen_ref))
    ):
        loads.append(pltpu.make_async_copy(src, dst, lsem.at[11 + i]))
    for copy in loads:
        copy.start()

    pl.semaphore_wait(barrier, 18)

    sent = []

    def send(i, src, dst, dev):
        m = msg(i, src, dst, dev)
        m.start()
        sent.append(m)
        return m

    class Gather:
        def __init__(self, base, blk, half):
            self.base, self.blk, self.half = base, blk, half
            self.m = {}

        def put(self, k, ref, dev):
            self.m[k] = send(self.base + k, ref, ref, dev)

        def share(self, k, xi, zi):
            ref = self.blk(xi, zi)
            self.m[9 + k] = send(self.base + 9 + k, ref, ref, d_c)

        def start(self):
            own = self.blk(x, zh)
            self.put(0, own, d_z)
            self.put(1, own, d_xr)
            self.put(2, own, d_xl)
            self.share(0, x, zh)

        def take(self, k):
            z2 = 1 - zh
            self.m[k].wait_recv()
            if k == 0:
                other = self.blk(x, z2)
                self.put(3, other, d_xr)
                self.put(4, other, d_xl)
                self.share(1, x, z2)
            elif k == 1:
                self.put(5, self.half(xl, zh, 0), d_xr)
                self.share(2, xl, zh)
            elif k == 2:
                self.put(6, self.half(xr, zh, 1), d_xl)
                self.share(3, xr, zh)
            elif k == 3:
                self.put(7, self.half(xl, z2, 0), d_xr)
                self.share(4, xl, z2)
            elif k == 4:
                self.put(8, self.half(xr, z2, 1), d_xl)
                self.share(5, xr, z2)
            elif k == 5:
                self.m[6].wait_recv()
                self.share(6, xo, zh)
            else:
                self.m[8].wait_recv()
                self.share(7, xo, z2)

        def finish(self):
            for k in range(8):
                self.m[9 + k].wait_recv()

    kvg = Gather(
        KV0, lambda a, b: kv.at[:, cidx(a, b, core)], lambda a, b, k: kv.at[k, cidx(a, b, core)]
    )
    loads[0].wait()
    loads[1].wait()
    kvg.start()

    loads[2].wait()
    loads[10].wait()
    row_id = lax.broadcasted_iota(jnp.int32, (64, 128), 0)
    lane_id = lax.broadcasted_iota(jnp.int32, (64, 128), 1)
    eye = row_id == lane_id
    gain4 = gain_ref[...].astype(F32)
    gain = jnp.concatenate([gain4[i : i + 1] for i in range(4)], axis=1)

    def scale_rows(p, side):
        steps = pl.ds(p.k * TS, TS)

        def body(i, carry):
            raw = xb[steps, 2 * i + side].astype(F32).reshape(RB, 512)
            xs[p.k, side, i] = (raw * gain).astype(BF16)
            return carry

        lax.fori_loop(0, 8, body, 0, unroll=True)

    def squares(d, carry):
        raw = xb[:, d].astype(F32).reshape(64, 512)
        part = jnp.sum(raw * raw, axis=1, keepdims=True)
        flat = jnp.sum(jnp.where(eye, part, 0.0), axis=0, keepdims=True)
        sqs[d] = jnp.broadcast_to(flat, (8, 128))
        return carry

    def sq_msg(d):
        to = lax.rem(c + d, 16)
        return msg(SQ0 + d, sqs.at[to], sqr.at[c], (to, h))

    first = pl.ds(0, 5)
    second = pl.ds(5, 5)

    class Part:
        pass

    parts = []
    for k in range(NCH):
        p = Part()
        p.k = k
        p.base = PART0 + k * PART_MSGS
        p.px, p.oy = {}, {}
        p.hog = Gather(
            p.base + M_HO, lambda a, b, k=k: ho.at[k, cidx(a, b, core)],
            lambda a, b, f, k=k: ho.at[k, cidx(a, b, core), f],
        )
        parts.append(p)

    def other_rows(p):
        k = p.k

        rows = xs[k, 1 - core].reshape(8 * RB, 512)
        for j in range(5):
            res = mdot(rows, wb[j]).astype(BF16)
            gs[k, 2 * j] = res[:, :128].reshape(4, 2, RB, 128)
            gs[k, 2 * j + 1] = res[:, 128:].reshape(4, 2, RB, 128)
        p.core = send(p.base + M_CORE, gs.at[k], gr.at[k], d_c)

    def own_rows(p):
        k, px = p.k, p.px
        p.core.wait_recv()
        rows = xs[k, core].reshape(8 * RB, 512)

        def body(j):
            res = mdot(rows, wb[j])
            for i in range(2):
                both = res[:, 128 * i : 128 * i + 128].reshape(4, 2, RB, 128) + gr[
                    k, 2 * j + i
                ].astype(F32)
                g[k, 2 * j + i] = both.astype(BF16)

        for j in range(3):
            body(j)
        px[0] = send(p.base + M_X + 0, g.at[k, first, xo], prelay.at[k, 0], d_xr)
        px[3] = send(p.base + M_X + 3, g.at[k, first, xl], pright.at[k, 0], d_xl)
        for j in range(3, 5):
            body(j)
        px[2] = send(p.base + M_X + 2, g.at[k, second, xo], prelay.at[k, 1], d_xl)
        px[1] = send(p.base + M_X + 1, g.at[k, second, xr], pleft.at[k, 1], d_xr)

    def x_relay(p, half):
        k, px = p.k, p.px
        which, to, dev, into = ((first, xr, d_xr, pleft), (second, xl, d_xl, pright))[half]
        px[2 * half].wait_recv()
        g[k, which, to] = (g[k, which, to].astype(F32) + prelay[k, half].astype(F32)).astype(BF16)
        px[4 + half] = send(p.base + M_X + 4 + half, g.at[k, which, to], into.at[k, half], dev)

    def x_sum(p):
        k, px = p.k, p.px
        for i in (1, 3, 4, 5):
            px[i].wait_recv()

        def three(half, s, z):
            return (
                g[k, 5 * half + s, x, z].astype(F32)
                + pleft[k, half, s, z].astype(F32)
                + pright[k, half, s, z].astype(F32)
            )

        for s in range(10):
            zs[k, s] = three(s // 5, s % 5, 1 - zh).astype(BF16)
        p.zp = send(p.base + M_Z, zs.at[k], zr.at[k], d_z)

        for s in range(10):
            rf[k, s] = three(s // 5, s % 5, zh)

    def attend(p, inverse):
        k = p.k
        nrow = 8 * RB
        nnew = (k + 1) * RB
        inv = inverse[k * RB : (k + 1) * RB]
        p.zp.wait_recv()

        for s in range(10):
            pr[k, s] = ((rf[k, s] + zr[k, s].astype(F32)) * inv).astype(BF16)
        nk[k * RB : (k + 1) * RB] = pr[k, 8]
        nv[k * RB : (k + 1) * RB, 0:128] = pr[k, 9]

        q = pr[k, 0:8].reshape(nrow, HD)
        i_id = lax.broadcasted_iota(jnp.int32, (nrow, nnew), 0)
        j_id = lax.broadcasted_iota(jnp.int32, (nrow, nnew), 1)
        seen = (lax.rem(i_id, 16) == lax.rem(j_id, 16)) & (
            j_id // 16 <= k * TS + lax.rem(i_id // 16, TS)
        )
        s_new = jnp.where(seen, rdot(q, nk[0:nnew]) * SCALE, NEG)
        peak = None
        for b in range(8):
            s = rdot(q, pool_k[256 * b : 256 * b + 256]) * SCALE
            s = (s.reshape(nrow // 16, 16, 256) + bias[b][None]).reshape(nrow, 256)
            sb[b] = s
            here = jnp.maximum(s[:, :128], s[:, 128:])
            peak = here if peak is None else jnp.maximum(peak, here)
        top = jnp.maximum(
            jnp.max(peak, axis=1, keepdims=True), jnp.max(s_new, axis=1, keepdims=True)
        )
        w_new = jnp.exp(s_new - top)
        mixed = mdot(w_new.astype(BF16), nv[0:nnew])
        for b in range(8):
            w = jnp.exp(sb[b] - top).astype(BF16)
            mixed = mixed + mdot(w, pool_v[256 * b : 256 * b + 256])
        head_out = (mixed[:, 0:128] / mixed[:, 128:256]).astype(BF16)
        for s in range(8):
            ho[k, c, s // 4, :, (s % 4) * HD : (s % 4 + 1) * HD] = head_out[s * RB : (s + 1) * RB]
        p.hog.start()

    def out_rows(p):
        k, oy = p.k, p.oy
        p.hog.finish()
        lhs = [ho[k, :, f].reshape(16 * RB, 512) for f in range(2)]
        for n in range(2):
            res = mdot(lhs[0], wob[n, 0:512]) + mdot(lhs[1], wob[n, 512:1024])
            o[k, :, :, :, n * 256 : (n + 1) * 256] = res.astype(BF16).reshape(4, 2, 2 * RB, 256)
        oy[0] = send(p.base + M_Y + 0, o.at[k, yo, 0], orelay.at[k, 0], d_yr)
        oy[2] = send(p.base + M_Y + 2, o.at[k, yo, 1], orelay.at[k, 1], d_yl)
        oy[1] = send(p.base + M_Y + 1, o.at[k, yr, 1], oleft.at[k, 1], d_yr)
        oy[3] = send(p.base + M_Y + 3, o.at[k, yl, 0], oright.at[k, 0], d_yl)

    def y_relay(p, half):
        k, oy = p.k, p.oy
        to, dev, into = ((yr, d_yr, oleft), (yl, d_yl, oright))[half]
        oy[2 * half].wait_recv()
        o[k, to, half] = (o[k, to, half].astype(F32) + orelay[k, half].astype(F32)).astype(BF16)
        oy[4 + half] = send(p.base + M_Y + 4 + half, o.at[k, to, half], into.at[k, half], dev)

    def y_sum(p):
        k, oy = p.k, p.oy
        for i in (1, 3, 4, 5):
            oy[i].wait_recv()

        for z in range(2):
            ozs[k, z] = (
                o[k, y, z].astype(F32) + oleft[k, z].astype(F32) + oright[k, z].astype(F32)
            ).astype(BF16)
        p.oz = send(p.base + M_ZL, ozs.at[k], ozr.at[k], d_zl)

    def add_input(p):
        k = p.k
        p.oz.wait_recv()
        steps = pl.ds(k * TS, TS)
        for z in range(2):
            for i in range(2):
                rows = pl.ds(i * RB, RB)
                full = ozs[k, z, rows].astype(F32) + ozr[k, z, rows].astype(F32)
                hidden = xb[steps, cidx(y, z, i)].astype(F32)
                out[steps, 2 * y + z, pl.ds(16 * i, 16), :] = (
                    hidden + full.reshape(TS, 16, 512)
                ).astype(BF16)
        own = out.at[steps, pl.ds(2 * y, 2)]
        p.fo = {
            1: send(p.base + M_FO, own, own, d_yr),
            2: send(p.base + M_FO + 1, own, own, d_yl),
        }

    def pass_on(p, k):
        steps = pl.ds(p.k * TS, TS)
        p.fo[k].wait_recv()
        if k == 1:
            part = out.at[steps, 2 * yl]
            p.fo[5] = send(p.base + M_FO + 2, part, part, d_yr)
        elif k == 2:
            part = out.at[steps, 2 * yr + 1]
            p.fo[6] = send(p.base + M_FO + 3, part, part, d_yl)
        else:
            p.fo[6].wait_recv()

    def load_weights():
        for k in range(3, 8):
            loads[k].wait()
        wkvf[...] = wkvb[...].astype(F32)
        wb[4, :, 0:128] = wkvf[pl.ds(0, 512, stride=2), :].astype(BF16)
        wb[4, :, 128:256] = wkvf[pl.ds(1, 512, stride=2), :].astype(BF16)

    def sum_squares():
        lax.fori_loop(0, 16, squares, 0, unroll=4)

        def sq_send(d, carry):
            sq_msg(d).start()
            return carry

        lax.fori_loop(1, 16, sq_send, 0)

    def inverse_rms():
        def sq_wait(d, carry):
            sq_msg(d).wait_recv()
            return carry

        lax.fori_loop(1, 16, sq_wait, 0)
        sqr[c] = sqs[c]
        flat = jnp.sum(sqr[...], axis=0)[0:1, :]
        row_sq = jnp.sum(jnp.where(eye, flat, 0.0), axis=1, keepdims=True)
        return lax.rsqrt(row_sq / D + 1e-05)

    def choose_pages():
        loads[12].wait()
        loads[13].wait()
        pick = (
            lax.broadcasted_iota(jnp.int32, (16, 256), 1)
            == lax.broadcasted_iota(jnp.int32, (16, 256), 0) + 16 * c
        )
        own_pages = rdot(pick.astype(BF16), pages_ref[...].astype(BF16)).astype(jnp.int32)
        r_id = lax.broadcasted_iota(jnp.int32, (16, 256), 0)
        s_id = lax.broadcasted_iota(jnp.int32, (16, 256), 1)
        lens = jnp.zeros((16, 256), jnp.int32)
        for r in range(16):
            lens = jnp.where(r_id == r, clen_ref[c * 16 + r], lens)
        in_page = lax.rem(s_id, PAGE)
        page_id = lax.broadcasted_iota(jnp.int32, (16, 64), 1)
        named = jnp.zeros((16, 64), F32)
        for slot in range(8):
            named = jnp.where(own_pages[:, slot : slot + 1] == page_id, 1.0, named)
        present = jnp.broadcast_to(jnp.max(named, axis=0, keepdims=True), (16, 64))
        a_id = lax.broadcasted_iota(jnp.int32, (64, 64), 0)
        b_id = lax.broadcasted_iota(jnp.int32, (64, 64), 1)
        ahead = (a_id // 4 == b_id // 4) & (a_id < b_id)
        rank = mdot(present.astype(BF16), ahead.astype(BF16))
        code = jnp.where(present > 0.5, rank + 1.0, 0.0).astype(BF16)
        node_id = lax.broadcasted_iota(jnp.int32, (64, 256), 0)
        node_of = lax.broadcasted_iota(jnp.int32, (64, 256), 1) // PAGE
        to_id = lax.broadcasted_iota(jnp.int32, (128, 256), 0)
        from_id = lax.broadcasted_iota(jnp.int32, (128, 256), 1)
        same = lax.rem(to_id, PAGE) == lax.rem(from_id, PAGE)
        want = jnp.where(same, (to_id // PAGE + 1).astype(F32), -1.0)
        last = [
            (own_pages[:, slot : slot + 1], lens - slot * PAGE, s_id // PAGE)
            for slot in range(8)
        ]

        def choose(b):
            live = jnp.zeros((16, 256), F32)
            for named_page, upto, page in last:
                hit = (named_page - 4 * b == page) & (in_page < upto)
                live = jnp.where(hit, 1.0, live)
            spread = mdot(code, (node_id == node_of + 4 * b).astype(BF16))
            sel = jnp.where(spread[0:1] == want, 1.0, 0.0).astype(BF16)
            chosen[b] = sel
            return jnp.where(rdot(live.astype(BF16), sel) > 0.5, 0.0, NEG)

        def choose_two(i, carry):
            bias[i, :, 0:128] = choose(2 * i)
            bias[i, :, 128:256] = choose(2 * i + 1)
            return carry

        lax.fori_loop(0, 8, choose_two, 0, unroll=2)

    def take_pages():
        pool_v[:, 128:256] = jnp.ones((2048, 128), BF16)
        nv[:, 128:256] = jnp.ones((64, 128), BF16)

        def take(b, carry):
            rows = pl.ds(pl.multiple_of(128 * b, 128), 128)
            pool_k[rows] = mdot(chosen[b], kv[0, b]).astype(BF16)
            pool_v[rows, 0:128] = mdot(chosen[b], kv[1, b]).astype(BF16)
            return carry

        lax.fori_loop(0, 16, take, 0, unroll=8)

    def list_pages():
        loads[11].wait()
        a_id = lax.broadcasted_iota(jnp.int32, (64, 64), 0)
        b_id = lax.broadcasted_iota(jnp.int32, (64, 64), 1)
        col_id = lax.broadcasted_iota(jnp.int32, (64, 128), 1)
        p_id = lax.broadcasted_iota(jnp.int32, (64, 128), 0)
        rows = []
        for n in range(4):
            a = 4 * c + n
            line = mask_ref[pl.ds(a, 1), :].astype(F32)
            readable = jnp.sum(jnp.where(a_id == b_id, line, 0.0), axis=1, keepdims=True)
            readable = jnp.where((readable > 0.5) & (p_id < a), 1.0, 0.0)
            before = mdot((b_id < a_id).astype(BF16), readable.astype(BF16))
            place = jnp.where(p_id == a, 0.0, before + 1.0).astype(jnp.int32)
            hit = (place == col_id) & ((readable > 0.5) | (p_id == a))
            line = jnp.sum(jnp.where(hit, p_id.astype(F32), 0.0), axis=0, keepdims=True)
            count = jnp.sum(readable, axis=0, keepdims=True) + 1.0
            rows.append(jnp.where(col_id[0:1] == 127, count, line))
        picks[...] = jnp.concatenate(rows + rows, axis=0).astype(jnp.int32)

    keep = pltpu.make_async_copy(kv, kv_out, lsem.at[10])
    rms = []
    late = [loads[8], loads[9]]

    def step(event):
        who, what = event.split(".")
        if who == "kv":
            if what == "fin":
                kvg.finish()
                keep.start()
            else:
                kvg.take(int(what[1]))
            return
        if who == "all":
            {"sq": sum_squares, "mask": choose_pages, "take": take_pages, "list": list_pages}[
                what
            ]()
            return
        p = parts[int(who[1])]
        if what == "other":
            scale_rows(p, 1 - core)
            if p.k == 0:
                load_weights()
            other_rows(p)
        elif what == "own":
            scale_rows(p, core)
            own_rows(p)
        elif what[0] == "x":
            if what == "xsum":
                x_sum(p)
            else:
                x_relay(p, int(what[2]) // 2)
        elif what == "att":
            if not rms:
                rms.append(inverse_rms())
            attend(p, rms[0])
        elif what[0] == "h":
            p.hog.take(int(what[1]))
        elif what == "out":
            while late:
                late.pop().wait()
            out_rows(p)
        elif what == "ysum":
            y_sum(p)
        elif what[0] == "y":
            y_relay(p, int(what[2]) // 2)
        elif what == "add":
            add_input(p)
        else:
            pass_on(p, int(what[1]))

    for event in ORDER:
        step(event)
    keep.wait()

    for m in sent:
        m.wait_send()

    def sq_done(d, carry):
        sq_msg(d).wait_send()
        return carry

    lax.fori_loop(1, 16, sq_done, 0)


def layer_call(*args):
    hbm = pl.BlockSpec(memory_space=pl.ANY)
    vmem = pl.BlockSpec(memory_space=pltpu.VMEM)
    return pl.pallas_call(
        layer_kernel,
        out_shape=(
            jax.ShapeDtypeStruct((2, 16, 256, HD), BF16),
            jax.ShapeDtypeStruct((8, 128), jnp.int32),
            jax.ShapeDtypeStruct((4, 8, 32, 512), BF16),
        ),
        in_specs=[hbm] * 10,
        out_specs=(hbm, vmem, vmem),
        scratch_shapes=[
            pltpu.VMEM((64, 64), jnp.int32),
            pltpu.VMEM((8, 256), jnp.int32),
            pltpu.SMEM((256,), jnp.int32),
            pltpu.VMEM((4, 128), BF16),
            pltpu.VMEM((2, 16, 256, HD), BF16),
            pltpu.VMEM((4, 16, 16, 512), BF16),
            pltpu.VMEM((5, 512, 256), BF16),
            pltpu.VMEM((1024, 128), BF16),
            pltpu.VMEM((1024, 128), F32),
            pltpu.VMEM((2, 1024, 256), BF16),
            pltpu.VMEM((NCH, 2, 8, RB, 512), BF16),
            pltpu.VMEM((16, 8, 128), F32),
            pltpu.VMEM((16, 8, 128), F32),
            pltpu.VMEM((NCH, 10, 4, 2, RB, 128), BF16),
            pltpu.VMEM((NCH, 10, 4, 2, RB, 128), BF16),
            pltpu.VMEM((NCH, 10, 4, 2, RB, 128), BF16),
            pltpu.VMEM((NCH, 2, 5, 2, RB, 128), BF16),
            pltpu.VMEM((NCH, 2, 5, 2, RB, 128), BF16),
            pltpu.VMEM((NCH, 2, 5, 2, RB, 128), BF16),
            pltpu.VMEM((NCH, 10, RB, 128), BF16),
            pltpu.VMEM((NCH, 10, RB, 128), BF16),
            pltpu.VMEM((NCH, 10, RB, 128), F32),
            pltpu.VMEM((NCH, 10, RB, 128), BF16),
            pltpu.VMEM((64, 128), BF16),
            pltpu.VMEM((64, 256), BF16),
            pltpu.VMEM((8, 16, 256), F32),
            pltpu.VMEM((16, 128, 256), BF16),
            pltpu.VMEM((2048, HD), BF16),
            pltpu.VMEM((2048, 2 * HD), BF16),
            pltpu.VMEM((8, 8 * RB, 256), F32),
            pltpu.VMEM((NCH, 16, 2, RB, 512), BF16),
            pltpu.VMEM((NCH, 4, 2, 2 * RB, 512), BF16),
            pltpu.VMEM((NCH, 2, 2 * RB, 512), BF16),
            pltpu.VMEM((NCH, 2, 2 * RB, 512), BF16),
            pltpu.VMEM((NCH, 2, 2 * RB, 512), BF16),
            pltpu.VMEM((NCH, 2, 2 * RB, 512), BF16),
            pltpu.VMEM((NCH, 2, 2 * RB, 512), BF16),
            pltpu.SemaphoreType.DMA((15,)),
            pltpu.SemaphoreType.DMA((NMSG,)),
            pltpu.SemaphoreType.DMA((NMSG,)),
        ],
        compiler_params=pltpu.CompilerParams(
            collective_id=0, has_side_effects=True, vmem_limit_bytes=56 * 1024 * 1024
        ),
        name="layer",
    )(*args)


def prefill_kernel(
    q_hbm, kv_ref, picks, dec_ref, out_hbm, dec_out, q_ref, kv, stage, out, peaks, mixes, sem
):
    loads = [pltpu.make_async_copy(kv_ref.at[i], kv.at[i], sem.at[i]) for i in range(2)]
    loads.append(pltpu.make_async_copy(q_hbm, q_ref, sem.at[2]))
    fetched = pltpu.make_async_copy(dec_ref, stage, sem.at[3])
    moved = pltpu.make_async_copy(stage, dec_out, sem.at[4])
    for copy in loads:
        copy.start()
    fetched.start()

    def attend(n, start, pages, state):
        keys = jnp.concatenate([kv[0, picks[n, start + k]] for k in range(pages)], axis=0)
        values = jnp.concatenate([kv[1, picks[n, start + k]] for k in range(pages)], axis=0)
        values = jnp.concatenate([values, jnp.ones((pages * PAGE, 128), BF16)], axis=1)
        q = jnp.concatenate([q_ref[n, :, s * HD : (s + 1) * HD] for s in range(8)], axis=0)
        i_id = lax.broadcasted_iota(jnp.int32, (512, pages * PAGE), 0)
        j_id = lax.broadcasted_iota(jnp.int32, (512, pages * PAGE), 1)
        allowed = j_id < (picks[n, 127] - start) * PAGE
        if state is None:
            allowed = allowed & ((j_id >= PAGE) | (j_id <= lax.rem(i_id, PAGE)))
        s = jnp.where(allowed, rdot(q, keys) * SCALE, NEG)
        peak = jnp.max(s, axis=1, keepdims=True)
        if state is not None:
            peak = jnp.maximum(peak, state[0])
        mixed = mdot(jnp.exp(s - peak).astype(BF16), values)
        if state is not None:
            mixed = mixed + state[1] * jnp.exp(state[0] - peak)
        return peak, mixed

    def write(n, mixed):
        result = (mixed[:, 0:128] / mixed[:, 128:256]).astype(BF16)
        for s in range(8):
            out[n, :, s * HD : (s + 1) * HD] = result[s * 64 : (s + 1) * 64]

    for copy in loads:
        copy.wait()
    fetched.wait()
    moved.start()
    for n in range(4):
        peak, mixed = attend(n, 0, 8, None)
        peaks[n] = jnp.broadcast_to(peak, (512, 128))
        mixes[n] = mixed
        write(n, mixed)

    def deep(n, carry):
        @pl.when(picks[n, 127] > 8)
        def _():
            def more(t, inner):
                peak, mixed = attend(n, 8 + 4 * t, 4, (peaks[n][:, 0:1], mixes[n]))
                peaks[n] = jnp.broadcast_to(peak, (512, 128))
                mixes[n] = mixed
                return inner

            lax.fori_loop(0, (picks[n, 127] - 5) // 4, more, 0)
            write(n, mixes[n])

        return carry

    lax.fori_loop(0, 4, deep, 0)
    done = pltpu.make_async_copy(out, out_hbm, sem.at[5])
    done.start()
    done.wait()
    moved.wait()


def prefill_call(q, kv, picks, dec):
    hbm = pl.BlockSpec(memory_space=pl.ANY)
    smem = pl.BlockSpec(memory_space=pltpu.SMEM)
    return pl.pallas_call(
        prefill_kernel,
        out_shape=(
            jax.ShapeDtypeStruct((4, PAGE, 1024), BF16),
            jax.ShapeDtypeStruct(dec.shape, BF16),
        ),
        in_specs=[hbm, hbm, smem, hbm],
        out_specs=(hbm, hbm),
        scratch_shapes=[
            pltpu.VMEM((4, PAGE, 1024), BF16),
            pltpu.VMEM((2, 64, PAGE, HD), BF16),
            pltpu.VMEM(dec.shape, BF16),
            pltpu.VMEM((4, PAGE, 1024), BF16),
            pltpu.VMEM((4, 512, 128), F32),
            pltpu.VMEM((4, 512, 256), F32),
            pltpu.SemaphoreType.DMA((6,)),
        ],
        compiler_params=pltpu.CompilerParams(vmem_limit_bytes=62 * 1024 * 1024),
        name="prefill",
    )(q, kv, picks, dec)


def per_device(
    prefill_query, prefill_key, prefill_value, tree_mask, pages, cache_len,
    dec_in, norm_gain, w_query, w_keyval, w_out,
):
    kv, picks, dec = layer_call(
        prefill_key, prefill_value, tree_mask, pages.T, cache_len,
        dec_in.reshape(4, 16, 16, 512), norm_gain.reshape(4, 128), w_query,
        w_keyval.reshape(1024, 128), w_out,
    )
    prefill_out, dec_out = prefill_call(
        prefill_query.reshape(4, PAGE, 1024), kv.reshape(2, 64, PAGE, HD), picks, dec
    )
    return prefill_out.reshape(256, 1024), dec_out.reshape(4, 256, 512)


def solution(mesh):
    return jax.shard_map(
        per_device,
        mesh=mesh,
        in_specs=(
            P("ctx", "head"), P("ctx", "head"), P("ctx", "head"), P(), P(), P(),
            P(None, None, "ctx"), P("ctx"), P("ctx", "head"), P("ctx", None, "head"),
            P("head", "ctx"),
        ),
        out_specs=(P("ctx", "head"), P(None, None, "ctx")),
        check_vma=False,
    )
```

```python
import jax
import jax.numpy as jnp
from jax import lax
from jax.experimental import pallas as pl
from jax.experimental.pallas import tpu as pltpu
from jax.sharding import PartitionSpec as P

D = 8192
HD = 128
PAGE = 64
STEPS = 4
SCALE = HD ** (-0.5)
NEG = -1e30
F32 = jnp.float32
BF16 = jnp.bfloat16
MESH = pl.DeviceIdType.MESH

NCH = 4
TS = STEPS // NCH
RB = 16 * TS

KV0 = 0
SQ0 = 11
PART0 = 16
M_CORE, M_X, M_Z, M_HO, M_Y, M_ZL, M_FO = 0, 1, 7, 8, 17, 23, 24
PART_MSGS = 28
NMSG = PART0 + NCH * PART_MSGS


ORDER = (
    "p0.other", "all.sq", "p1.other", "p0.own", "kv.z", "p1.own", "p0.xr2", "all.sq1", "p0.xr0",
    "p2.other", "p3.other", "kv.l", "kv.r", "p1.xr0", "p2.own", "p1.xr2", "p0.xsum", "p3.own",
    "all.mask", "kv.f", "all.sq2", "p2.xr2", "p1.xsum", "p2.xr0", "kv.fin", "all.take",
    "p0.att", "p2.xsum", "p3.xr0", "p3.xr2", "p1.att", "p0.hz", "p2.att", "p3.xsum", "p0.hl",
    "p0.hr", "p1.hz", "p2.hz", "p0.hf", "p3.att", "p1.hl", "p1.hr", "p2.hl", "p2.hr", "p0.out",
    "p1.hf", "p3.hz", "all.list", "p2.hf", "p1.out", "p3.hl", "p3.hr", "p2.out", "p0.yr0",
    "p3.hf", "p0.yr2", "p1.yr2", "p1.yr0", "p3.out", "p0.ysum", "p2.yr0", "p2.yr2", "p1.ysum",
    "p3.yr0", "p3.yr2", "p2.ysum", "p0.add", "p3.ysum", "p1.add", "p2.add", "p3.add", "p0.f2",
    "p1.f1", "p1.f2", "p0.f1", "p2.f1", "p2.f2", "p3.f2", "p3.f1", "p0.f5", "p1.f5", "p2.f5",
    "p3.f5",
)


def rdot(a, b):
    return lax.dot_general(a, b, (((1,), (1,)), ((), ())), preferred_element_type=F32)


def mdot(a, b):
    return lax.dot_general(a, b, (((1,), (0,)), ((), ())), preferred_element_type=F32)


def layer_kernel(
    key_ref, val_ref, mask_hbm, pages_hbm, clen_hbm, x_ref, gain_hbm, wq_ref, wkv_ref, wo_ref,
    kv_out, picks, out,
    ob, mask_ref, pages_ref, clen_ref, gain_ref,
    kv, xb, wb, wkvb, wkvf, wob, xs, sqs, sqc, sqx, sqn, sqz, sqr, gs, gr, g, prelay, pleft, pright, zs, zr, rf,
    pr, nk, nv, bias, chosen, pool_k, pool_v, sb, ho, o, orelay, oleft, oright, ozs, ozr,
    lsem, ssem, rsem,
):
    c = lax.axis_index("ctx")
    h = lax.axis_index("head")
    core = lax.rem(c, 2)
    zh = lax.rem(c // 2, 2)
    x = c // 4
    y = lax.rem(h, 4)
    zl = h // 4

    def cidx(xi, zi, ci):
        return xi * 4 + zi * 2 + ci

    def hidx(yi, zi):
        return zi * 4 + yi

    xr, xl, xo = lax.rem(x + 1, 4), lax.rem(x + 3, 4), lax.rem(x + 2, 4)
    yr, yl, yo = lax.rem(y + 1, 4), lax.rem(y + 3, 4), lax.rem(y + 2, 4)
    d_xr = (cidx(xr, zh, core), h)
    d_xl = (cidx(xl, zh, core), h)
    d_z = (cidx(x, 1 - zh, core), h)
    d_c = (cidx(x, zh, 1 - core), h)
    d_yr = (c, hidx(yr, zl))
    d_yl = (c, hidx(yl, zl))
    d_zl = (c, hidx(y, 1 - zl))
    d_xo = (cidx(xo, zh, core), h)

    def msg(i, src, dst, dev):
        return pltpu.make_async_remote_copy(
            src_ref=src, dst_ref=dst, send_sem=ssem.at[i], recv_sem=rsem.at[i],
            device_id=dev, device_id_type=MESH,
        )

    barrier = pltpu.get_barrier_semaphore()

    for dev in (d_xr, d_xl, d_z, d_c, d_yr, d_yl, d_zl, d_xo):
        pl.semaphore_signal(barrier, inc=1, device_id=dev, device_id_type=MESH)

    loads = [
        pltpu.make_async_copy(key_ref, kv.at[x, core, zh, 0], lsem.at[0]),
        pltpu.make_async_copy(val_ref, kv.at[x, core, zh, 1], lsem.at[1]),
        pltpu.make_async_copy(x_ref, xb, lsem.at[2]),
        pltpu.make_async_copy(wkv_ref, wkvb, lsem.at[3]),
    ]
    for j in range(4):
        loads.append(
            pltpu.make_async_copy(wq_ref.at[:, pl.ds(256 * j, 256)], wb.at[j], lsem.at[4 + j])
        )
    for j in range(2):
        loads.append(
            pltpu.make_async_copy(wo_ref.at[:, pl.ds(256 * j, 256)], wob.at[j], lsem.at[8 + j])
        )
    for i, (src, dst) in enumerate(
        ((gain_hbm, gain_ref), (mask_hbm, mask_ref), (pages_hbm, pages_ref), (clen_hbm, clen_ref))
    ):
        loads.append(pltpu.make_async_copy(src, dst, lsem.at[11 + i]))
    for copy in loads:
        copy.start()

    pl.semaphore_wait(barrier, 8)

    sent = []

    def send(i, src, dst, dev):
        m = msg(i, src, dst, dev)
        m.start()
        sent.append(m)
        return m

    def drain(left):
        while len(sent) > left:
            sent.pop(0).wait_send()

    class Gather:
        def __init__(self, base, pair, early):
            self.base, self.pair, self.early = base, pair, early
            self.m = {}

        def put(self, k, ref, dev):
            self.m[k] = send(self.base + k, ref, ref, dev)

        def start(self):
            own = self.pair(x).at[zh]
            self.put(0, own, d_z)
            if self.early:
                self.put(9, own, d_xr)
                self.put(10, own, d_xl)

        def take(self, which):
            if which == "z":
                self.m[0].wait_recv()
                ref = self.pair(x)
                part = ref.at[1 - zh] if self.early else ref
                self.put(1, part, d_xr)
                self.put(2, part, d_xl)
                self.put(5, ref, d_c)
            elif which == "l":
                if self.early:
                    self.m[9].wait_recv()
                self.m[1].wait_recv()
                self.put(3, self.pair(xl).at[0], d_xr)
                self.put(6, self.pair(xl), d_c)
            elif which == "r":
                if self.early:
                    self.m[10].wait_recv()
                self.m[2].wait_recv()
                self.put(4, self.pair(xr).at[1], d_xl)
                self.put(7, self.pair(xr), d_c)
            else:
                self.m[3].wait_recv()
                self.m[4].wait_recv()
                self.put(8, self.pair(xo), d_c)

        def finish(self):
            for k in range(5, 9):
                self.m[k].wait_recv()

    kvg = Gather(KV0, lambda a: kv.at[a, core], True)
    loads[0].wait()
    loads[1].wait()
    kvg.start()

    loads[2].wait()
    loads[10].wait()
    row_id = lax.broadcasted_iota(jnp.int32, (64, 128), 0)
    lane_id = lax.broadcasted_iota(jnp.int32, (64, 128), 1)
    eye = row_id == lane_id
    gain4 = gain_ref[...].astype(F32)
    gain = jnp.concatenate([gain4[i : i + 1] for i in range(4)], axis=1)

    def scale_rows(p, side):
        steps = pl.ds(p.k * TS, TS)

        def body(i, carry):
            raw = xb[steps, 2 * i + side].astype(F32).reshape(RB, 512)
            xs[p.k, side, i] = (raw * gain).astype(BF16)
            return carry

        lax.fori_loop(0, 8, body, 0, unroll=True)

    def squares(d, carry):
        raw = xb[:, d].astype(F32).reshape(64, 512)
        part = jnp.sum(raw * raw, axis=1, keepdims=True)
        flat = jnp.sum(jnp.where(eye, part, 0.0), axis=0, keepdims=True)
        sqs[lax.rem(d, 2), d // 4, lax.rem(d // 2, 2)] = jnp.broadcast_to(flat, (8, 128))
        return carry

    first = pl.ds(0, 5)
    second = pl.ds(5, 5)

    class Part:
        pass

    parts = []
    for k in range(NCH):
        p = Part()
        p.k = k
        p.base = PART0 + k * PART_MSGS
        p.px, p.oy = {}, {}
        p.hog = Gather(p.base + M_HO, lambda a, k=k: ho.at[k, a, core], False)
        parts.append(p)

    def other_rows(p):
        k = p.k

        rows = xs[k, 1 - core].reshape(8 * RB, 512)
        for j in range(5):
            res = mdot(rows, wb[j]).astype(BF16)
            gs[k, 2 * j] = res[:, :128].reshape(4, 2, RB, 128)
            gs[k, 2 * j + 1] = res[:, 128:].reshape(4, 2, RB, 128)
        p.core = send(p.base + M_CORE, gs.at[k], gr.at[k], d_c)

    def own_rows(p):
        k, px = p.k, p.px
        p.core.wait_recv()
        rows = xs[k, core].reshape(8 * RB, 512)

        def body(j):
            res = mdot(rows, wb[j])
            for i in range(2):
                both = res[:, 128 * i : 128 * i + 128].reshape(4, 2, RB, 128) + gr[
                    k, 2 * j + i
                ].astype(F32)
                g[k, :, 2 * j + i] = both.astype(BF16)

        for j in range(3):
            body(j)
        px[0] = send(p.base + M_X + 0, g.at[k, xo, first], prelay.at[k, 0], d_xr)
        px[3] = send(p.base + M_X + 3, g.at[k, xl, first], pright.at[k, 0], d_xl)
        for j in range(3, 5):
            body(j)
        px[2] = send(p.base + M_X + 2, g.at[k, xo, second], prelay.at[k, 1], d_xl)
        px[1] = send(p.base + M_X + 1, g.at[k, xr, second], pleft.at[k, 1], d_xr)

    def x_relay(p, half):
        k, px = p.k, p.px
        which, to, dev, into = ((first, xr, d_xr, pleft), (second, xl, d_xl, pright))[half]
        px[2 * half].wait_recv()
        g[k, to, which] = (g[k, to, which].astype(F32) + prelay[k, half].astype(F32)).astype(BF16)
        px[4 + half] = send(p.base + M_X + 4 + half, g.at[k, to, which], into.at[k, half], dev)

    def x_sum(p):
        k, px = p.k, p.px
        for i in (1, 3, 4, 5):
            px[i].wait_recv()

        def three(half, s, z):
            return (
                g[k, x, 5 * half + s, z].astype(F32)
                + pleft[k, half, s, z].astype(F32)
                + pright[k, half, s, z].astype(F32)
            )

        for s in range(10):
            zs[k, s] = three(s // 5, s % 5, 1 - zh).astype(BF16)
        p.zp = send(p.base + M_Z, zs.at[k], zr.at[k], d_z)

        for s in range(10):
            rf[k, s] = three(s // 5, s % 5, zh)

    def attend(p, inverse):
        k = p.k
        nrow = 8 * RB
        nnew = (k + 1) * RB
        inv = inverse[k * RB : (k + 1) * RB]
        p.zp.wait_recv()

        for s in range(10):
            pr[k, s] = ((rf[k, s] + zr[k, s].astype(F32)) * inv).astype(BF16)
        nk[k * RB : (k + 1) * RB] = pr[k, 8]
        nv[k * RB : (k + 1) * RB, 0:128] = pr[k, 9]

        q = pr[k, 0:8].reshape(nrow, HD)
        i_id = lax.broadcasted_iota(jnp.int32, (nrow, nnew), 0)
        j_id = lax.broadcasted_iota(jnp.int32, (nrow, nnew), 1)
        seen = (lax.rem(i_id, 16) == lax.rem(j_id, 16)) & (
            j_id // 16 <= k * TS + lax.rem(i_id // 16, TS)
        )
        s_new = jnp.where(seen, rdot(q, nk[0:nnew]) * SCALE, NEG)
        peak = None
        for b in range(8):
            s = rdot(q, pool_k[256 * b : 256 * b + 256]) * SCALE
            s = (s.reshape(nrow // 16, 16, 256) + bias[b][None]).reshape(nrow, 256)
            sb[b] = s
            here = jnp.maximum(s[:, :128], s[:, 128:])
            peak = here if peak is None else jnp.maximum(peak, here)
        top = jnp.maximum(
            jnp.max(peak, axis=1, keepdims=True), jnp.max(s_new, axis=1, keepdims=True)
        )
        w_new = jnp.exp(s_new - top)
        mixed = mdot(w_new.astype(BF16), nv[0:nnew])
        for b in range(8):
            w = jnp.exp(sb[b] - top).astype(BF16)
            mixed = mixed + mdot(w, pool_v[256 * b : 256 * b + 256])
        head_out = (mixed[:, 0:128] / mixed[:, 128:256]).astype(BF16)
        for s in range(8):
            ho[k, x, core, zh, s // 4, :, (s % 4) * HD : (s % 4 + 1) * HD] = head_out[s * RB : (s + 1) * RB]
        p.hog.start()

    def out_rows(p):
        k, oy = p.k, p.oy
        p.hog.finish()
        lhs = [ho[k, :, :, :, f].reshape(16 * RB, 512) for f in range(2)]
        for n in range(2):
            res = mdot(lhs[0], wob[n, 0:512]) + mdot(lhs[1], wob[n, 512:1024])
            o[k, :, :, :, :, n * 256 : (n + 1) * 256] = res.astype(BF16).reshape(4, 2, 2, RB, 256)
        oy[0] = send(p.base + M_Y + 0, o.at[k, yo, 0], orelay.at[k, 0], d_yr)
        oy[2] = send(p.base + M_Y + 2, o.at[k, yo, 1], orelay.at[k, 1], d_yl)
        oy[1] = send(p.base + M_Y + 1, o.at[k, yr, 1], oleft.at[k, 1], d_yr)
        oy[3] = send(p.base + M_Y + 3, o.at[k, yl, 0], oright.at[k, 0], d_yl)

    def y_relay(p, half):
        k, oy = p.k, p.oy
        to, dev, into = ((yr, d_yr, oleft), (yl, d_yl, oright))[half]
        oy[2 * half].wait_recv()
        o[k, to, half] = (o[k, to, half].astype(F32) + orelay[k, half].astype(F32)).astype(BF16)
        oy[4 + half] = send(p.base + M_Y + 4 + half, o.at[k, to, half], into.at[k, half], dev)

    def y_sum(p):
        k, oy = p.k, p.oy
        for i in (1, 3, 4, 5):
            oy[i].wait_recv()

        for i in range(2):
            ozs[k, i] = (
                o[k, y, i].astype(F32) + oleft[k, i].astype(F32) + oright[k, i].astype(F32)
            ).astype(BF16)
        p.oz = send(p.base + M_ZL, ozs.at[k], ozr.at[k], d_zl)

    def add_input(p):
        k = p.k
        p.oz.wait_recv()
        steps = pl.ds(k * TS, TS)
        for z in range(2):
            for i in range(2):
                full = ozs[k, i, z].astype(F32) + ozr[k, i, z].astype(F32)
                hidden = xb[steps, cidx(y, z, i)].astype(F32)
                ob[steps, 2 * y + z, pl.ds(16 * i, 16), :] = (
                    hidden + full.reshape(TS, 16, 512)
                ).astype(BF16)
        own = ob.at[steps, pl.ds(2 * y, 2)]
        p.fo = {
            1: send(p.base + M_FO, own, own, d_yr),
            2: send(p.base + M_FO + 1, own, own, d_yl),
        }

    def pass_on(p, k):
        steps = pl.ds(p.k * TS, TS)
        if k == 1:
            p.fo[1].wait_recv()
            part = ob.at[steps, 2 * yl]
            p.fo[5] = send(p.base + M_FO + 2, part, part, d_yr)
        elif k == 2:
            p.fo[2].wait_recv()
            part = ob.at[steps, 2 * yr + 1]
            p.fo[6] = send(p.base + M_FO + 3, part, part, d_yl)
        else:
            p.fo[5].wait_recv()
            p.fo[6].wait_recv()
            p.done = pltpu.make_async_copy(ob.at[steps], out.at[steps], lsem.at[15 + p.k])
            p.done.start()

    def load_weights():
        for k in range(3, 8):
            loads[k].wait()
        wkvf[...] = wkvb[...].astype(F32)
        wb[4, :, 0:128] = wkvf[pl.ds(0, 512, stride=2), :].astype(BF16)
        wb[4, :, 128:256] = wkvf[pl.ds(1, 512, stride=2), :].astype(BF16)

    def sum_squares():
        lax.fori_loop(0, 16, squares, 0, unroll=4)
        return [send(SQ0, sqs.at[1 - core], sqc, d_c)]

    def sum_squares_x(before):
        before[0].wait_recv()
        sqx[...] = sqs[core] + sqc[...]
        return [
            send(SQ0 + 1, sqx.at[xr], sqn.at[0], d_xr),
            send(SQ0 + 2, sqx.at[xl], sqn.at[1], d_xl),
            send(SQ0 + 3, sqx.at[xo], sqn.at[2], d_xo),
        ]

    def sum_squares_z(before):
        for m in before:
            m.wait_recv()
        sqz[...] = sqx[x] + sqn[0] + sqn[1] + sqn[2]
        return [send(SQ0 + 4, sqz.at[1 - zh], sqr, d_z)]

    def inverse_rms(before):
        before[0].wait_recv()
        flat = (sqz[zh] + sqr[...])[0:1, :]
        row_sq = jnp.sum(jnp.where(eye, flat, 0.0), axis=1, keepdims=True)
        return lax.rsqrt(row_sq / D + 1e-05)

    def choose_pages():
        loads[12].wait()
        loads[13].wait()
        pick = (
            lax.broadcasted_iota(jnp.int32, (16, 256), 1)
            == lax.broadcasted_iota(jnp.int32, (16, 256), 0) + 16 * c
        )
        own_pages = rdot(pick.astype(BF16), pages_ref[...].astype(BF16)).astype(jnp.int32)
        r_id = lax.broadcasted_iota(jnp.int32, (16, 256), 0)
        s_id = lax.broadcasted_iota(jnp.int32, (16, 256), 1)
        lens = jnp.zeros((16, 256), jnp.int32)
        for r in range(16):
            lens = jnp.where(r_id == r, clen_ref[c * 16 + r], lens)
        in_page = lax.rem(s_id, PAGE)
        page_id = lax.broadcasted_iota(jnp.int32, (16, 64), 1)
        named = jnp.zeros((16, 64), F32)
        for slot in range(8):
            named = jnp.where(own_pages[:, slot : slot + 1] == page_id, 1.0, named)
        present = jnp.broadcast_to(jnp.max(named, axis=0, keepdims=True), (16, 64))
        a_id = lax.broadcasted_iota(jnp.int32, (64, 64), 0)
        b_id = lax.broadcasted_iota(jnp.int32, (64, 64), 1)
        ahead = (a_id // 4 == b_id // 4) & (a_id < b_id)
        rank = mdot(present.astype(BF16), ahead.astype(BF16))
        code = jnp.where(present > 0.5, rank + 1.0, 0.0).astype(BF16)
        node_id = lax.broadcasted_iota(jnp.int32, (64, 256), 0)
        node_of = lax.broadcasted_iota(jnp.int32, (64, 256), 1) // PAGE
        to_id = lax.broadcasted_iota(jnp.int32, (128, 256), 0)
        from_id = lax.broadcasted_iota(jnp.int32, (128, 256), 1)
        same = lax.rem(to_id, PAGE) == lax.rem(from_id, PAGE)
        want = jnp.where(same, (to_id // PAGE + 1).astype(F32), -1.0)
        last = [
            (own_pages[:, slot : slot + 1], lens - slot * PAGE, s_id // PAGE)
            for slot in range(8)
        ]

        def choose(b):
            live = jnp.zeros((16, 256), F32)
            for named_page, upto, page in last:
                hit = (named_page - 4 * b == page) & (in_page < upto)
                live = jnp.where(hit, 1.0, live)
            spread = mdot(code, (node_id == node_of + 4 * b).astype(BF16))
            sel = jnp.where(spread[0:1] == want, 1.0, 0.0).astype(BF16)
            chosen[b] = sel
            return jnp.where(rdot(live.astype(BF16), sel) > 0.5, 0.0, NEG)

        def choose_two(i, carry):
            bias[i, :, 0:128] = choose(2 * i)
            bias[i, :, 128:256] = choose(2 * i + 1)
            return carry

        lax.fori_loop(0, 8, choose_two, 0, unroll=2)

    def take_pages():
        pool_v[:, 128:256] = jnp.ones((2048, 128), BF16)
        nv[:, 128:256] = jnp.ones((64, 128), BF16)

        def take(b, carry):
            rows = pl.ds(pl.multiple_of(128 * b, 128), 128)
            block = (b // 4, lax.rem(b, 2), lax.rem(b // 2, 2))
            pool_k[rows] = mdot(chosen[b], kv[block + (0,)]).astype(BF16)
            pool_v[rows, 0:128] = mdot(chosen[b], kv[block + (1,)]).astype(BF16)
            return carry

        lax.fori_loop(0, 16, take, 0, unroll=8)

    def list_pages():
        loads[11].wait()
        a_id = lax.broadcasted_iota(jnp.int32, (64, 64), 0)
        b_id = lax.broadcasted_iota(jnp.int32, (64, 64), 1)
        col_id = lax.broadcasted_iota(jnp.int32, (64, 128), 1)
        p_id = lax.broadcasted_iota(jnp.int32, (64, 128), 0)
        spot = (p_id // 16) * 16 + lax.rem(p_id // 4, 2) * 8 + lax.rem(p_id // 8, 2) * 4
        spot = (spot + lax.rem(p_id, 4)).astype(F32)
        rows = []
        for n in range(4):
            a = 4 * c + n
            line = mask_ref[pl.ds(a, 1), :].astype(F32)
            readable = jnp.sum(jnp.where(a_id == b_id, line, 0.0), axis=1, keepdims=True)
            readable = jnp.where((readable > 0.5) & (p_id < a), 1.0, 0.0)
            before = mdot((b_id < a_id).astype(BF16), readable.astype(BF16))
            place = jnp.where(p_id == a, 0.0, before + 1.0).astype(jnp.int32)
            hit = (place == col_id) & ((readable > 0.5) | (p_id == a))
            line = jnp.sum(jnp.where(hit, spot, 0.0), axis=0, keepdims=True)
            count = jnp.sum(readable, axis=0, keepdims=True) + 1.0
            rows.append(jnp.where(col_id[0:1] == 127, count, line))
        picks[...] = jnp.concatenate(rows + rows, axis=0).astype(jnp.int32)

    keep = pltpu.make_async_copy(kv, kv_out, lsem.at[10])
    rms, squared = [], []
    late = [loads[8], loads[9]]

    def step(event):
        who, what = event.split(".")
        if who == "kv":
            if what == "fin":
                kvg.finish()
                keep.start()
            else:
                kvg.take(what)
            return
        if who == "all":
            if what[:2] == "sq":
                stage = {"sq": sum_squares, "sq1": sum_squares_x, "sq2": sum_squares_z}[what]
                squared[:] = stage(squared) if squared else stage()
            else:
                {"mask": choose_pages, "take": take_pages, "list": list_pages}[what]()
            return
        p = parts[int(who[1])]
        if what == "other":
            scale_rows(p, 1 - core)
            if p.k == 0:
                load_weights()
            other_rows(p)
        elif what == "own":
            scale_rows(p, core)
            own_rows(p)
        elif what[0] == "x":
            if what == "xsum":
                x_sum(p)
            else:
                x_relay(p, int(what[2]) // 2)
        elif what == "att":
            if not rms:
                rms.append(inverse_rms(squared))
            attend(p, rms[0])
        elif what[0] == "h":
            p.hog.take(what[1])
        elif what == "out":
            while late:
                late.pop().wait()
            out_rows(p)
        elif what == "ysum":
            drain(10)
            y_sum(p)
        elif what[0] == "y":
            y_relay(p, int(what[2]) // 2)
        elif what == "add":
            add_input(p)
        else:
            drain(6)
            pass_on(p, int(what[1]))

    for event in ORDER:
        step(event)
    keep.wait()
    drain(0)
    for p in parts:
        p.done.wait()


def layer_call(*args):
    hbm = pl.BlockSpec(memory_space=pl.ANY)
    vmem = pl.BlockSpec(memory_space=pltpu.VMEM)
    return pl.pallas_call(
        layer_kernel,
        out_shape=(
            jax.ShapeDtypeStruct((4, 2, 2, 2, 256, HD), BF16),
            jax.ShapeDtypeStruct((8, 128), jnp.int32),
            jax.ShapeDtypeStruct((4, 8, 32, 512), BF16),
        ),
        in_specs=[hbm] * 10,
        out_specs=(hbm, vmem, hbm),
        scratch_shapes=[
            pltpu.VMEM((4, 8, 32, 512), BF16),
            pltpu.VMEM((64, 64), jnp.int32),
            pltpu.VMEM((8, 256), jnp.int32),
            pltpu.SMEM((256,), jnp.int32),
            pltpu.VMEM((4, 128), BF16),
            pltpu.VMEM((4, 2, 2, 2, 256, HD), BF16),
            pltpu.VMEM((4, 16, 16, 512), BF16),
            pltpu.VMEM((5, 512, 256), BF16),
            pltpu.VMEM((1024, 128), BF16),
            pltpu.VMEM((1024, 128), F32),
            pltpu.VMEM((2, 1024, 256), BF16),
            pltpu.VMEM((NCH, 2, 8, RB, 512), BF16),
            pltpu.VMEM((2, 4, 2, 8, 128), F32),
            pltpu.VMEM((4, 2, 8, 128), F32),
            pltpu.VMEM((4, 2, 8, 128), F32),
            pltpu.VMEM((3, 2, 8, 128), F32),
            pltpu.VMEM((2, 8, 128), F32),
            pltpu.VMEM((8, 128), F32),
            pltpu.VMEM((NCH, 10, 4, 2, RB, 128), BF16),
            pltpu.VMEM((NCH, 10, 4, 2, RB, 128), BF16),
            pltpu.VMEM((NCH, 4, 10, 2, RB, 128), BF16),
            pltpu.VMEM((NCH, 2, 5, 2, RB, 128), BF16),
            pltpu.VMEM((NCH, 2, 5, 2, RB, 128), BF16),
            pltpu.VMEM((NCH, 2, 5, 2, RB, 128), BF16),
            pltpu.VMEM((NCH, 10, RB, 128), BF16),
            pltpu.VMEM((NCH, 10, RB, 128), BF16),
            pltpu.VMEM((NCH, 10, RB, 128), F32),
            pltpu.VMEM((NCH, 10, RB, 128), BF16),
            pltpu.VMEM((64, 128), BF16),
            pltpu.VMEM((64, 256), BF16),
            pltpu.VMEM((8, 16, 256), F32),
            pltpu.VMEM((16, 128, 256), BF16),
            pltpu.VMEM((2048, HD), BF16),
            pltpu.VMEM((2048, 2 * HD), BF16),
            pltpu.VMEM((8, 8 * RB, 256), F32),
            pltpu.VMEM((NCH, 4, 2, 2, 2, RB, 512), BF16),
            pltpu.VMEM((NCH, 4, 2, 2, RB, 512), BF16),
            pltpu.VMEM((NCH, 2, 2, RB, 512), BF16),
            pltpu.VMEM((NCH, 2, 2, RB, 512), BF16),
            pltpu.VMEM((NCH, 2, 2, RB, 512), BF16),
            pltpu.VMEM((NCH, 2, 2, RB, 512), BF16),
            pltpu.VMEM((NCH, 2, 2, RB, 512), BF16),
            pltpu.SemaphoreType.DMA((15 + NCH,)),
            pltpu.SemaphoreType.DMA((NMSG,)),
            pltpu.SemaphoreType.DMA((NMSG,)),
        ],
        compiler_params=pltpu.CompilerParams(
            collective_id=0, has_side_effects=True, vmem_limit_bytes=56 * 1024 * 1024
        ),
        name="layer",
    )(*args)


def prefill_kernel(
    q_hbm, kv_ref, picks, dec_ref, out_hbm, dec_out, q_ref, kv, stage, out, peaks, mixes, sem
):
    loads = [pltpu.make_async_copy(kv_ref, kv, sem.at[0])]
    loads.append(pltpu.make_async_copy(q_hbm, q_ref, sem.at[2]))
    fetched = pltpu.make_async_copy(dec_ref, stage, sem.at[3])
    moved = pltpu.make_async_copy(stage, dec_out, sem.at[4])
    for copy in loads:
        copy.start()
    fetched.start()

    def attend(n, start, pages, state):
        spots = [picks[n, start + k] for k in range(pages)]
        keys = jnp.concatenate([kv[p // 4, 0, lax.rem(p, 4)] for p in spots], axis=0)
        values = jnp.concatenate([kv[p // 4, 1, lax.rem(p, 4)] for p in spots], axis=0)
        values = jnp.concatenate([values, jnp.ones((pages * PAGE, 128), BF16)], axis=1)
        q = jnp.concatenate([q_ref[n, :, s * HD : (s + 1) * HD] for s in range(8)], axis=0)
        i_id = lax.broadcasted_iota(jnp.int32, (512, pages * PAGE), 0)
        j_id = lax.broadcasted_iota(jnp.int32, (512, pages * PAGE), 1)
        allowed = j_id < (picks[n, 127] - start) * PAGE
        if state is None:
            allowed = allowed & ((j_id >= PAGE) | (j_id <= lax.rem(i_id, PAGE)))
        s = jnp.where(allowed, rdot(q, keys) * SCALE, NEG)
        peak = jnp.max(s, axis=1, keepdims=True)
        if state is not None:
            peak = jnp.maximum(peak, state[0])
        mixed = mdot(jnp.exp(s - peak).astype(BF16), values)
        if state is not None:
            mixed = mixed + state[1] * jnp.exp(state[0] - peak)
        return peak, mixed

    def write(n, mixed):
        result = (mixed[:, 0:128] / mixed[:, 128:256]).astype(BF16)
        for s in range(8):
            out[n, :, s * HD : (s + 1) * HD] = result[s * 64 : (s + 1) * 64]

    for copy in loads:
        copy.wait()
    fetched.wait()
    moved.start()
    for n in range(4):
        peak, mixed = attend(n, 0, 8, None)
        peaks[n] = jnp.broadcast_to(peak, (512, 128))
        mixes[n] = mixed
        write(n, mixed)

    def deep(n, carry):
        @pl.when(picks[n, 127] > 8)
        def _():
            def more(t, inner):
                peak, mixed = attend(n, 8 + 4 * t, 4, (peaks[n][:, 0:1], mixes[n]))
                peaks[n] = jnp.broadcast_to(peak, (512, 128))
                mixes[n] = mixed
                return inner

            lax.fori_loop(0, (picks[n, 127] - 5) // 4, more, 0)
            write(n, mixes[n])

        return carry

    lax.fori_loop(0, 4, deep, 0)
    done = pltpu.make_async_copy(out, out_hbm, sem.at[5])
    done.start()
    done.wait()
    moved.wait()


def prefill_call(q, kv, picks, dec):
    hbm = pl.BlockSpec(memory_space=pl.ANY)
    smem = pl.BlockSpec(memory_space=pltpu.SMEM)
    return pl.pallas_call(
        prefill_kernel,
        out_shape=(
            jax.ShapeDtypeStruct((4, PAGE, 1024), BF16),
            jax.ShapeDtypeStruct(dec.shape, BF16),
        ),
        in_specs=[hbm, hbm, smem, hbm],
        out_specs=(hbm, hbm),
        scratch_shapes=[
            pltpu.VMEM((4, PAGE, 1024), BF16),
            pltpu.VMEM((16, 2, 4, PAGE, HD), BF16),
            pltpu.VMEM(dec.shape, BF16),
            pltpu.VMEM((4, PAGE, 1024), BF16),
            pltpu.VMEM((4, 512, 128), F32),
            pltpu.VMEM((4, 512, 256), F32),
            pltpu.SemaphoreType.DMA((6,)),
        ],
        compiler_params=pltpu.CompilerParams(vmem_limit_bytes=62 * 1024 * 1024),
        name="prefill",
    )(q, kv, picks, dec)


def per_device(
    prefill_query, prefill_key, prefill_value, tree_mask, pages, cache_len,
    dec_in, norm_gain, w_query, w_keyval, w_out,
):
    kv, picks, dec = layer_call(
        prefill_key, prefill_value, tree_mask, pages.T, cache_len,
        dec_in.reshape(4, 16, 16, 512), norm_gain.reshape(4, 128), w_query,
        w_keyval.reshape(1024, 128), w_out,
    )
    prefill_out, dec_out = prefill_call(
        prefill_query.reshape(4, PAGE, 1024), kv.reshape(16, 2, 4, PAGE, HD), picks, dec
    )
    return prefill_out.reshape(256, 1024), dec_out.reshape(4, 256, 512)


def solution(mesh):
    return jax.shard_map(
        per_device,
        mesh=mesh,
        in_specs=(
            P("ctx", "head"), P("ctx", "head"), P("ctx", "head"), P(), P(), P(),
            P(None, None, "ctx"), P("ctx"), P("ctx", "head"), P("ctx", None, "head"),
            P("head", "ctx"),
        ),
        out_specs=(P("ctx", "head"), P(None, None, "ctx")),
        check_vma=False,
    )
```

```python
import jax
import jax.numpy as jnp
from jax import lax
from jax.experimental import pallas as pl
from jax.experimental.pallas import tpu as pltpu
from jax.sharding import PartitionSpec as P

D = 8192
HD = 128
PAGE = 64
STEPS = 4
SCALE = HD ** (-0.5)
NEG = -1e30
F32 = jnp.float32
BF16 = jnp.bfloat16
MESH = pl.DeviceIdType.MESH

NCH = 4
TS = STEPS // NCH
RB = 16 * TS

KV0 = 0
SQ0 = 12
PART0 = 17
M_CORE, M_X, M_Z, M_HO, M_Y, M_ZL, M_FO = 0, 1, 5, 6, 15, 19, 20
PART_MSGS = 24
NMSG = PART0 + NCH * PART_MSGS


ORDER = (
    "p0.other", "p1.other", "all.sq", "p0.own", "kv.r", "p2.other", "kv.l", "p3.other",
    "p0.xr0", "p0.xr2", "p1.own", "kv.f", "p2.own", "p3.own", "kv.s", "all.sq1", "p1.xr0",
    "kv.z", "p0.xsum", "kv.m", "p1.xr2", "all.sq2", "p3.xr0", "p3.xr2", "p2.xr2", "p2.xr0",
    "kv.o", "all.mask", "kv.fin", "p1.xsum", "all.take", "p0.att", "p2.xsum", "p3.xsum",
    "p1.att", "p0.hz", "p2.att", "p1.hz", "p0.hl", "p0.hr", "p3.att", "p2.hz", "p0.hf", "p1.hr",
    "p1.hl", "p0.out", "p3.hz", "p1.hf", "p2.hr", "p2.hl", "p1.out", "p3.hl", "p2.hf", "p3.hr",
    "p0.yr2", "p0.yr0", "p2.out", "p3.hf", "p1.yr2", "p1.yr0", "p3.out", "p0.ysum", "p2.yr2",
    "p2.yr0", "p1.ysum", "p3.yr0", "p3.yr2", "p0.add", "p2.ysum", "p1.add", "p3.ysum", "p0.f1",
    "p0.f2", "p2.add", "p3.add", "p1.f1", "p1.f2", "p2.f1", "p2.f2", "p3.f1", "p3.f2", "p1.f5",
    "p2.f5", "all.list", "p0.f5", "p3.f5",
)


def rdot(a, b):
    return lax.dot_general(a, b, (((1,), (1,)), ((), ())), preferred_element_type=F32)


def mdot(a, b):
    return lax.dot_general(a, b, (((1,), (0,)), ((), ())), preferred_element_type=F32)


def layer_kernel(
    key_ref, val_ref, mask_hbm, pages_hbm, clen_hbm, x_ref, gain_hbm, wq_ref, wkv_ref, wo_ref,
    kv_out, picks, out,
    ob, mask_ref, pages_ref, clen_ref, gain_ref,
    kv, xb, wb, wkvb, wkvf, wob, xs, sqs, sqc, sqx, sqn, sqz, sqr, gs, gr, g, prelay, pleft, pright, zs, zr, rf,
    pr, nk, nv, bias, chosen, pool_k, pool_v, sb, ho, o, orelay, oleft, oright, ozs, ozr,
    lsem, ssem, rsem,
):
    c = lax.axis_index("ctx")
    h = lax.axis_index("head")
    core = lax.rem(c, 2)
    zh = lax.rem(c // 2, 2)
    x = c // 4
    y = lax.rem(h, 4)
    zl = h // 4

    def cidx(xi, zi, ci):
        return xi * 4 + zi * 2 + ci

    def hidx(yi, zi):
        return zi * 4 + yi

    xr, xl, xo = lax.rem(x + 1, 4), lax.rem(x + 3, 4), lax.rem(x + 2, 4)
    yr, yl, yo = lax.rem(y + 1, 4), lax.rem(y + 3, 4), lax.rem(y + 2, 4)
    d_xr = (cidx(xr, zh, core), h)
    d_xl = (cidx(xl, zh, core), h)
    d_z = (cidx(x, 1 - zh, core), h)
    d_c = (cidx(x, zh, 1 - core), h)
    d_yr = (c, hidx(yr, zl))
    d_yl = (c, hidx(yl, zl))
    d_zl = (c, hidx(y, 1 - zl))
    d_xo = (cidx(xo, zh, core), h)

    def msg(i, src, dst, dev):
        return pltpu.make_async_remote_copy(
            src_ref=src, dst_ref=dst, send_sem=ssem.at[i], recv_sem=rsem.at[i],
            device_id=dev, device_id_type=MESH,
        )

    barrier = pltpu.get_barrier_semaphore()

    for dev in (d_xr, d_xl, d_z, d_c, d_yr, d_yl, d_zl, d_xo):
        pl.semaphore_signal(barrier, inc=1, device_id=dev, device_id_type=MESH)

    loads = [
        pltpu.make_async_copy(key_ref, kv.at[x, core, zh, 0], lsem.at[0]),
        pltpu.make_async_copy(val_ref, kv.at[x, core, zh, 1], lsem.at[1]),
        pltpu.make_async_copy(x_ref, xb, lsem.at[2]),
        pltpu.make_async_copy(wkv_ref, wkvb, lsem.at[3]),
    ]
    for j in range(4):
        loads.append(
            pltpu.make_async_copy(wq_ref.at[:, pl.ds(256 * j, 256)], wb.at[j], lsem.at[4 + j])
        )
    for j in range(2):
        loads.append(
            pltpu.make_async_copy(wo_ref.at[:, pl.ds(256 * j, 256)], wob.at[j], lsem.at[8 + j])
        )
    for i, (src, dst) in enumerate(
        ((gain_hbm, gain_ref), (mask_hbm, mask_ref), (pages_hbm, pages_ref), (clen_hbm, clen_ref))
    ):
        loads.append(pltpu.make_async_copy(src, dst, lsem.at[11 + i]))
    for copy in loads:
        copy.start()

    pl.semaphore_wait(barrier, 8)

    sent = []

    def send(i, src, dst, dev):
        m = msg(i, src, dst, dev)
        m.start()
        sent.append(m)
        return m

    def drain(left):
        while len(sent) > left:
            sent.pop(0).wait_send()

    def pass_to(msgs, base, k, ref, dev):
        msgs[k] = send(base + k, ref, ref, dev)

    kvm = {}

    def kv_start():
        own = kv.at[x, core, zh]
        pass_to(kvm, KV0, 1, own, d_xr)
        pass_to(kvm, KV0, 2, own, d_xl)
        pass_to(kvm, KV0, 0, own, d_z)

    def kv_pass(what):
        if what == "l":
            kvm[1].wait_recv()
            pass_to(kvm, KV0, 3, kv.at[xl, core, zh, 0], d_xr)
            pass_to(kvm, KV0, 5, kv.at[xl, core, zh], d_z)
        elif what == "r":
            kvm[2].wait_recv()
            pass_to(kvm, KV0, 4, kv.at[xr, core, zh, 1], d_xl)
            pass_to(kvm, KV0, 6, kv.at[xr, core, zh], d_z)
        elif what == "f":
            kvm[3].wait_recv()
            kvm[4].wait_recv()
            pass_to(kvm, KV0, 7, kv.at[xo, core, zh], d_z)
        else:
            waited, given, place = {"z": (0, 8, x), "m": (5, 9, xl), "s": (6, 10, xr), "o": (7, 11, xo)}[
                what
            ]
            kvm[waited].wait_recv()
            pass_to(kvm, KV0, given, kv.at[place, core], d_c)

    class Gather:
        def __init__(self, base, pair):
            self.base, self.pair, self.m = base, pair, {}

        def put(self, k, ref, dev):
            pass_to(self.m, self.base, k, ref, dev)

        def start(self):
            self.put(0, self.pair(x).at[zh], d_z)

        def take(self, which):
            if which == "z":
                self.m[0].wait_recv()
                self.put(1, self.pair(x), d_xr)
                self.put(2, self.pair(x), d_xl)
                self.put(5, self.pair(x), d_c)
            elif which == "l":
                self.m[1].wait_recv()
                self.put(3, self.pair(xl).at[0], d_xr)
                self.put(6, self.pair(xl), d_c)
            elif which == "r":
                self.m[2].wait_recv()
                self.put(4, self.pair(xr).at[1], d_xl)
                self.put(7, self.pair(xr), d_c)
            else:
                self.m[3].wait_recv()
                self.m[4].wait_recv()
                self.put(8, self.pair(xo), d_c)

        def finish(self):
            for k in range(5, 9):
                self.m[k].wait_recv()

    loads[0].wait()
    loads[1].wait()
    kv_start()

    loads[2].wait()
    loads[10].wait()
    row_id = lax.broadcasted_iota(jnp.int32, (64, 128), 0)
    lane_id = lax.broadcasted_iota(jnp.int32, (64, 128), 1)
    eye = row_id == lane_id
    gain4 = gain_ref[...].astype(F32)
    gain = jnp.concatenate([gain4[i : i + 1] for i in range(4)], axis=1)

    def scale_rows(p, side):
        steps = pl.ds(p.k * TS, TS)

        def body(i, carry):
            raw = xb[steps, 2 * i + side].astype(F32).reshape(RB, 512)
            xs[p.k, side, i] = (raw * gain).astype(BF16)
            return carry

        lax.fori_loop(0, 8, body, 0, unroll=True)

    def squares(d, carry):
        raw = xb[:, d].astype(F32).reshape(64, 512)
        part = jnp.sum(raw * raw, axis=1, keepdims=True)
        flat = jnp.sum(jnp.where(eye, part, 0.0), axis=0, keepdims=True)
        sqs[lax.rem(d, 2), d // 4, lax.rem(d // 2, 2)] = jnp.broadcast_to(flat, (8, 128))
        return carry

    first = pl.ds(0, 5)
    second = pl.ds(5, 5)

    class Part:
        pass

    parts = []
    for k in range(NCH):
        p = Part()
        p.k = k
        p.base = PART0 + k * PART_MSGS
        p.px, p.oy = {}, {}
        p.hog = Gather(p.base + M_HO, lambda a, k=k: ho.at[k, a, core])
        parts.append(p)

    def other_rows(p):
        k = p.k

        rows = xs[k, 1 - core].reshape(8 * RB, 512)
        for j in range(5):
            res = mdot(rows, wb[j]).astype(BF16)
            gs[k, 2 * j] = res[:, :128].reshape(4, 2, RB, 128)
            gs[k, 2 * j + 1] = res[:, 128:].reshape(4, 2, RB, 128)
        p.core = send(p.base + M_CORE, gs.at[k], gr.at[k], d_c)

    def own_rows(p):
        k, px = p.k, p.px
        p.core.wait_recv()
        rows = xs[k, core].reshape(8 * RB, 512)

        def body(j):
            res = mdot(rows, wb[j])
            for i in range(2):
                both = res[:, 128 * i : 128 * i + 128].reshape(4, 2, RB, 128) + gr[
                    k, 2 * j + i
                ].astype(F32)
                g[k, :, 2 * j + i] = both.astype(BF16)

        for j in range(3):
            body(j)
        px[0] = send(p.base + M_X, g.at[k, xo, first], prelay.at[k, 0], d_xr)
        for j in range(3, 5):
            body(j)
        px[1] = send(p.base + M_X + 1, g.at[k, xo, second], prelay.at[k, 1], d_xl)

    def x_relay(p, side):
        k, px = p.k, p.px
        which, to, dev, into = ((first, xr, d_xr, pleft), (second, xl, d_xl, pright))[side]
        px[side].wait_recv()
        g[k, to, which] = (g[k, to, which].astype(F32) + prelay[k, side].astype(F32)).astype(BF16)
        px[2 + side] = send(p.base + M_X + 2 + side, g.at[k, to], into.at[k], dev)

    def x_sum(p):
        k, px = p.k, p.px
        px[2].wait_recv()
        px[3].wait_recv()

        def three(s, z):
            return (
                g[k, x, s, z].astype(F32)
                + pleft[k, s, z].astype(F32)
                + pright[k, s, z].astype(F32)
            )

        for s in range(10):
            zs[k, s] = three(s, 1 - zh).astype(BF16)
        p.zp = send(p.base + M_Z, zs.at[k], zr.at[k], d_z)

        for s in range(10):
            rf[k, s] = three(s, zh)

    def attend(p, inverse):
        k = p.k
        nrow = 8 * RB
        nnew = (k + 1) * RB
        inv = inverse[k * RB : (k + 1) * RB]
        p.zp.wait_recv()

        for s in range(10):
            pr[k, s] = ((rf[k, s] + zr[k, s].astype(F32)) * inv).astype(BF16)
        nk[k * RB : (k + 1) * RB] = pr[k, 8]
        nv[k * RB : (k + 1) * RB, 0:128] = pr[k, 9]

        q = pr[k, 0:8].reshape(nrow, HD)
        i_id = lax.broadcasted_iota(jnp.int32, (nrow, nnew), 0)
        j_id = lax.broadcasted_iota(jnp.int32, (nrow, nnew), 1)
        seen = (lax.rem(i_id, 16) == lax.rem(j_id, 16)) & (
            j_id // 16 <= k * TS + lax.rem(i_id // 16, TS)
        )
        s_new = jnp.where(seen, rdot(q, nk[0:nnew]) * SCALE, NEG)
        peak = None
        for b in range(8):
            s = rdot(q, pool_k[256 * b : 256 * b + 256]) * SCALE
            s = (s.reshape(nrow // 16, 16, 256) + bias[b][None]).reshape(nrow, 256)
            sb[b] = s
            here = jnp.maximum(s[:, :128], s[:, 128:])
            peak = here if peak is None else jnp.maximum(peak, here)
        top = jnp.maximum(
            jnp.max(peak, axis=1, keepdims=True), jnp.max(s_new, axis=1, keepdims=True)
        )
        w_new = jnp.exp(s_new - top)
        mixed = mdot(w_new.astype(BF16), nv[0:nnew])
        for b in range(8):
            w = jnp.exp(sb[b] - top).astype(BF16)
            mixed = mixed + mdot(w, pool_v[256 * b : 256 * b + 256])
        head_out = (mixed[:, 0:128] / mixed[:, 128:256]).astype(BF16)
        for s in range(8):
            ho[k, x, core, zh, s // 4, :, (s % 4) * HD : (s % 4 + 1) * HD] = head_out[s * RB : (s + 1) * RB]
        p.hog.start()

    def out_rows(p):
        k, oy = p.k, p.oy
        p.hog.finish()
        lhs = [ho[k, :, :, :, f].reshape(16 * RB, 512) for f in range(2)]
        for n in range(2):
            res = mdot(lhs[0], wob[n, 0:512]) + mdot(lhs[1], wob[n, 512:1024])
            o[k, :, :, :, :, n * 256 : (n + 1) * 256] = res.astype(BF16).reshape(4, 2, 2, RB, 256)
        oy[0] = send(p.base + M_Y, o.at[k, yo, 0], orelay.at[k, 0], d_yr)
        oy[1] = send(p.base + M_Y + 1, o.at[k, yo, 1], orelay.at[k, 1], d_yl)

    def y_relay(p, side):
        k, oy = p.k, p.oy
        to, dev, into = ((yr, d_yr, oleft), (yl, d_yl, oright))[side]
        oy[side].wait_recv()
        o[k, to, side] = (o[k, to, side].astype(F32) + orelay[k, side].astype(F32)).astype(BF16)
        oy[2 + side] = send(p.base + M_Y + 2 + side, o.at[k, to], into.at[k], dev)

    def y_sum(p):
        k, oy = p.k, p.oy
        oy[2].wait_recv()
        oy[3].wait_recv()

        for i in range(2):
            ozs[k, i] = (
                o[k, y, i].astype(F32) + oleft[k, i].astype(F32) + oright[k, i].astype(F32)
            ).astype(BF16)
        p.oz = send(p.base + M_ZL, ozs.at[k], ozr.at[k], d_zl)

    def add_input(p):
        k = p.k
        p.oz.wait_recv()
        steps = pl.ds(k * TS, TS)
        for z in range(2):
            for i in range(2):
                full = ozs[k, i, z].astype(F32) + ozr[k, i, z].astype(F32)
                hidden = xb[steps, cidx(y, z, i)].astype(F32)
                ob[steps, 2 * y + z, pl.ds(16 * i, 16), :] = (
                    hidden + full.reshape(TS, 16, 512)
                ).astype(BF16)
        own = ob.at[steps, pl.ds(2 * y, 2)]
        p.fo = {
            1: send(p.base + M_FO, own, own, d_yr),
            2: send(p.base + M_FO + 1, own, own, d_yl),
        }

    def pass_on(p, k):
        steps = pl.ds(p.k * TS, TS)
        if k == 1:
            p.fo[1].wait_recv()
            part = ob.at[steps, 2 * yl]
            p.fo[5] = send(p.base + M_FO + 2, part, part, d_yr)
        elif k == 2:
            p.fo[2].wait_recv()
            part = ob.at[steps, 2 * yr + 1]
            p.fo[6] = send(p.base + M_FO + 3, part, part, d_yl)
        else:
            p.fo[5].wait_recv()
            p.fo[6].wait_recv()
            p.done = pltpu.make_async_copy(ob.at[steps], out.at[steps], lsem.at[15 + p.k])
            p.done.start()

    def load_weights():
        for k in range(3, 8):
            loads[k].wait()
        wkvf[...] = wkvb[...].astype(F32)
        wb[4, :, 0:128] = wkvf[pl.ds(0, 512, stride=2), :].astype(BF16)
        wb[4, :, 128:256] = wkvf[pl.ds(1, 512, stride=2), :].astype(BF16)

    def sum_squares():
        lax.fori_loop(0, 16, squares, 0, unroll=4)
        return [send(SQ0, sqs.at[1 - core], sqc, d_c)]

    def sum_squares_x(before):
        before[0].wait_recv()
        sqx[...] = sqs[core] + sqc[...]
        return [
            send(SQ0 + 1, sqx.at[xr], sqn.at[0], d_xr),
            send(SQ0 + 2, sqx.at[xl], sqn.at[1], d_xl),
            send(SQ0 + 3, sqx.at[xo], sqn.at[2], d_xo),
        ]

    def sum_squares_z(before):
        for m in before:
            m.wait_recv()
        sqz[...] = sqx[x] + sqn[0] + sqn[1] + sqn[2]
        return [send(SQ0 + 4, sqz.at[1 - zh], sqr, d_z)]

    def inverse_rms(before):
        before[0].wait_recv()
        flat = (sqz[zh] + sqr[...])[0:1, :]
        row_sq = jnp.sum(jnp.where(eye, flat, 0.0), axis=1, keepdims=True)
        return lax.rsqrt(row_sq / D + 1e-05)

    def choose_pages():
        loads[12].wait()
        loads[13].wait()
        pick = (
            lax.broadcasted_iota(jnp.int32, (16, 256), 1)
            == lax.broadcasted_iota(jnp.int32, (16, 256), 0) + 16 * c
        )
        own_pages = rdot(pick.astype(BF16), pages_ref[...].astype(BF16)).astype(jnp.int32)
        r_id = lax.broadcasted_iota(jnp.int32, (16, 256), 0)
        s_id = lax.broadcasted_iota(jnp.int32, (16, 256), 1)
        lens = jnp.zeros((16, 256), jnp.int32)
        for r in range(16):
            lens = jnp.where(r_id == r, clen_ref[c * 16 + r], lens)
        in_page = lax.rem(s_id, PAGE)
        page_id = lax.broadcasted_iota(jnp.int32, (16, 64), 1)
        named = jnp.zeros((16, 64), F32)
        for slot in range(8):
            named = jnp.where(own_pages[:, slot : slot + 1] == page_id, 1.0, named)
        present = jnp.broadcast_to(jnp.max(named, axis=0, keepdims=True), (16, 64))
        a_id = lax.broadcasted_iota(jnp.int32, (64, 64), 0)
        b_id = lax.broadcasted_iota(jnp.int32, (64, 64), 1)
        ahead = (a_id // 4 == b_id // 4) & (a_id < b_id)
        rank = mdot(present.astype(BF16), ahead.astype(BF16))
        code = jnp.where(present > 0.5, rank + 1.0, 0.0).astype(BF16)
        node_id = lax.broadcasted_iota(jnp.int32, (64, 256), 0)
        node_of = lax.broadcasted_iota(jnp.int32, (64, 256), 1) // PAGE
        to_id = lax.broadcasted_iota(jnp.int32, (128, 256), 0)
        from_id = lax.broadcasted_iota(jnp.int32, (128, 256), 1)
        same = lax.rem(to_id, PAGE) == lax.rem(from_id, PAGE)
        want = jnp.where(same, (to_id // PAGE + 1).astype(F32), -1.0)
        last = [
            (own_pages[:, slot : slot + 1], lens - slot * PAGE, s_id // PAGE)
            for slot in range(8)
        ]

        def choose(b):
            live = jnp.zeros((16, 256), F32)
            for named_page, upto, page in last:
                hit = (named_page - 4 * b == page) & (in_page < upto)
                live = jnp.where(hit, 1.0, live)
            spread = mdot(code, (node_id == node_of + 4 * b).astype(BF16))
            sel = jnp.where(spread[0:1] == want, 1.0, 0.0).astype(BF16)
            chosen[b] = sel
            return jnp.where(rdot(live.astype(BF16), sel) > 0.5, 0.0, NEG)

        def choose_two(i, carry):
            bias[i, :, 0:128] = choose(2 * i)
            bias[i, :, 128:256] = choose(2 * i + 1)
            return carry

        lax.fori_loop(0, 8, choose_two, 0, unroll=2)

    def take_pages():
        pool_v[:, 128:256] = jnp.ones((2048, 128), BF16)
        nv[:, 128:256] = jnp.ones((64, 128), BF16)

        def take(b, carry):
            rows = pl.ds(pl.multiple_of(128 * b, 128), 128)
            block = (b // 4, lax.rem(b, 2), lax.rem(b // 2, 2))
            pool_k[rows] = mdot(chosen[b], kv[block + (0,)]).astype(BF16)
            pool_v[rows, 0:128] = mdot(chosen[b], kv[block + (1,)]).astype(BF16)
            return carry

        lax.fori_loop(0, 16, take, 0, unroll=8)

    def list_pages():
        loads[11].wait()
        a_id = lax.broadcasted_iota(jnp.int32, (64, 64), 0)
        b_id = lax.broadcasted_iota(jnp.int32, (64, 64), 1)
        col_id = lax.broadcasted_iota(jnp.int32, (64, 128), 1)
        p_id = lax.broadcasted_iota(jnp.int32, (64, 128), 0)
        spot = (p_id // 16) * 16 + lax.rem(p_id // 4, 2) * 8 + lax.rem(p_id // 8, 2) * 4
        spot = (spot + lax.rem(p_id, 4)).astype(F32)
        rows = []
        for n in range(4):
            a = 4 * c + n
            line = mask_ref[pl.ds(a, 1), :].astype(F32)
            readable = jnp.sum(jnp.where(a_id == b_id, line, 0.0), axis=1, keepdims=True)
            readable = jnp.where((readable > 0.5) & (p_id < a), 1.0, 0.0)
            before = mdot((b_id < a_id).astype(BF16), readable.astype(BF16))
            place = jnp.where(p_id == a, 0.0, before + 1.0).astype(jnp.int32)
            hit = (place == col_id) & ((readable > 0.5) | (p_id == a))
            line = jnp.sum(jnp.where(hit, spot, 0.0), axis=0, keepdims=True)
            count = jnp.sum(readable, axis=0, keepdims=True) + 1.0
            rows.append(jnp.where(col_id[0:1] == 127, count, line))
        picks[...] = jnp.concatenate(rows + rows, axis=0).astype(jnp.int32)

    keep = pltpu.make_async_copy(kv, kv_out, lsem.at[10])
    rms, squared = [], []
    late = [loads[8], loads[9]]

    def step(event):
        who, what = event.split(".")
        if who == "kv":
            if what == "fin":
                for k in range(8, 12):
                    kvm[k].wait_recv()
                keep.start()
            else:
                kv_pass(what)
            return
        if who == "all":
            if what[:2] == "sq":
                stage = {"sq": sum_squares, "sq1": sum_squares_x, "sq2": sum_squares_z}[what]
                squared[:] = stage(squared) if squared else stage()
            else:
                {"mask": choose_pages, "take": take_pages, "list": list_pages}[what]()
            return
        p = parts[int(who[1])]
        if what == "other":
            scale_rows(p, 1 - core)
            if p.k == 0:
                load_weights()
            other_rows(p)
        elif what == "own":
            scale_rows(p, core)
            own_rows(p)
        elif what[0] == "x":
            if what == "xsum":
                x_sum(p)
            else:
                x_relay(p, int(what[2]) // 2)
        elif what == "att":
            if not rms:
                rms.append(inverse_rms(squared))
            attend(p, rms[0])
        elif what[0] == "h":
            p.hog.take(what[1])
        elif what == "out":
            while late:
                late.pop().wait()
            out_rows(p)
        elif what == "ysum":
            drain(10)
            y_sum(p)
        elif what[0] == "y":
            y_relay(p, int(what[2]) // 2)
        elif what == "add":
            add_input(p)
        else:
            drain(6)
            pass_on(p, int(what[1]))

    for event in ORDER:
        step(event)
    keep.wait()
    drain(0)
    for p in parts:
        p.done.wait()


def layer_call(*args):
    hbm = pl.BlockSpec(memory_space=pl.ANY)
    vmem = pl.BlockSpec(memory_space=pltpu.VMEM)
    return pl.pallas_call(
        layer_kernel,
        out_shape=(
            jax.ShapeDtypeStruct((4, 2, 2, 2, 256, HD), BF16),
            jax.ShapeDtypeStruct((8, 128), jnp.int32),
            jax.ShapeDtypeStruct((4, 8, 32, 512), BF16),
        ),
        in_specs=[hbm] * 10,
        out_specs=(hbm, vmem, hbm),
        scratch_shapes=[
            pltpu.VMEM((4, 8, 32, 512), BF16),
            pltpu.VMEM((64, 64), jnp.int32),
            pltpu.VMEM((8, 256), jnp.int32),
            pltpu.SMEM((256,), jnp.int32),
            pltpu.VMEM((4, 128), BF16),
            pltpu.VMEM((4, 2, 2, 2, 256, HD), BF16),
            pltpu.VMEM((4, 16, 16, 512), BF16),
            pltpu.VMEM((5, 512, 256), BF16),
            pltpu.VMEM((1024, 128), BF16),
            pltpu.VMEM((1024, 128), F32),
            pltpu.VMEM((2, 1024, 256), BF16),
            pltpu.VMEM((NCH, 2, 8, RB, 512), BF16),
            pltpu.VMEM((2, 4, 2, 8, 128), F32),
            pltpu.VMEM((4, 2, 8, 128), F32),
            pltpu.VMEM((4, 2, 8, 128), F32),
            pltpu.VMEM((3, 2, 8, 128), F32),
            pltpu.VMEM((2, 8, 128), F32),
            pltpu.VMEM((8, 128), F32),
            pltpu.VMEM((NCH, 10, 4, 2, RB, 128), BF16),
            pltpu.VMEM((NCH, 10, 4, 2, RB, 128), BF16),
            pltpu.VMEM((NCH, 4, 10, 2, RB, 128), BF16),
            pltpu.VMEM((NCH, 2, 5, 2, RB, 128), BF16),
            pltpu.VMEM((NCH, 10, 2, RB, 128), BF16),
            pltpu.VMEM((NCH, 10, 2, RB, 128), BF16),
            pltpu.VMEM((NCH, 10, RB, 128), BF16),
            pltpu.VMEM((NCH, 10, RB, 128), BF16),
            pltpu.VMEM((NCH, 10, RB, 128), F32),
            pltpu.VMEM((NCH, 10, RB, 128), BF16),
            pltpu.VMEM((64, 128), BF16),
            pltpu.VMEM((64, 256), BF16),
            pltpu.VMEM((8, 16, 256), F32),
            pltpu.VMEM((16, 128, 256), BF16),
            pltpu.VMEM((2048, HD), BF16),
            pltpu.VMEM((2048, 2 * HD), BF16),
            pltpu.VMEM((8, 8 * RB, 256), F32),
            pltpu.VMEM((NCH, 4, 2, 2, 2, RB, 512), BF16),
            pltpu.VMEM((NCH, 4, 2, 2, RB, 512), BF16),
            pltpu.VMEM((NCH, 2, 2, RB, 512), BF16),
            pltpu.VMEM((NCH, 2, 2, RB, 512), BF16),
            pltpu.VMEM((NCH, 2, 2, RB, 512), BF16),
            pltpu.VMEM((NCH, 2, 2, RB, 512), BF16),
            pltpu.VMEM((NCH, 2, 2, RB, 512), BF16),
            pltpu.SemaphoreType.DMA((15 + NCH,)),
            pltpu.SemaphoreType.DMA((NMSG,)),
            pltpu.SemaphoreType.DMA((NMSG,)),
        ],
        compiler_params=pltpu.CompilerParams(
            collective_id=0, has_side_effects=True, vmem_limit_bytes=56 * 1024 * 1024
        ),
        name="layer",
    )(*args)


def prefill_kernel(
    q_hbm, kv_ref, picks, dec_ref, out_hbm, dec_out, q_ref, kv, stage, out, peaks, mixes, sem
):
    loads = [pltpu.make_async_copy(kv_ref, kv, sem.at[0])]
    loads.append(pltpu.make_async_copy(q_hbm, q_ref, sem.at[2]))
    fetched = pltpu.make_async_copy(dec_ref, stage, sem.at[3])
    moved = pltpu.make_async_copy(stage, dec_out, sem.at[4])
    for copy in loads:
        copy.start()
    fetched.start()

    def attend(n, start, pages, state):
        spots = [picks[n, start + k] for k in range(pages)]
        keys = jnp.concatenate([kv[p // 4, 0, lax.rem(p, 4)] for p in spots], axis=0)
        values = jnp.concatenate([kv[p // 4, 1, lax.rem(p, 4)] for p in spots], axis=0)
        values = jnp.concatenate([values, jnp.ones((pages * PAGE, 128), BF16)], axis=1)
        q = jnp.concatenate([q_ref[n, :, s * HD : (s + 1) * HD] for s in range(8)], axis=0)
        j_id = lax.broadcasted_iota(jnp.int32, (1, pages * PAGE), 1)
        hidden = jnp.where(j_id < (picks[n, 127] - start) * PAGE, 0.0, NEG)
        s = rdot(q, keys) * SCALE + hidden
        if state is None:
            i_id = lax.broadcasted_iota(jnp.int32, (512, 128), 0)
            j_id = lax.broadcasted_iota(jnp.int32, (512, 128), 1)
            seen = (j_id >= PAGE) | (j_id <= lax.rem(i_id, PAGE))
            s = jnp.concatenate([jnp.where(seen, s[:, :128], NEG), s[:, 128:]], axis=1)
        peak = jnp.max(s, axis=1, keepdims=True)
        if state is not None:
            peak = jnp.maximum(peak, state[0])
        mixed = mdot(jnp.exp(s - peak).astype(BF16), values)
        if state is not None:
            mixed = mixed + state[1] * jnp.exp(state[0] - peak)
        return peak, mixed

    def write(n, mixed):
        result = (mixed[:, 0:128] / mixed[:, 128:256]).astype(BF16)
        for s in range(8):
            out[n, :, s * HD : (s + 1) * HD] = result[s * 64 : (s + 1) * 64]

    def leave(n):
        return pltpu.make_async_copy(out.at[n], out_hbm.at[n], sem.at[5 + n])

    for copy in loads:
        copy.wait()
    for n in range(4):
        peak, mixed = attend(n, 0, 8, None)
        peaks[n] = jnp.broadcast_to(peak, (512, 128))
        mixes[n] = mixed
        write(n, mixed)
        leave(n).start()
        if n == 0:
            fetched.wait()
            moved.start()

    def deep(n, carry):
        @pl.when(picks[n, 127] > 8)
        def _():
            def more(t, inner):
                peak, mixed = attend(n, 8 + 4 * t, 4, (peaks[n][:, 0:1], mixes[n]))
                peaks[n] = jnp.broadcast_to(peak, (512, 128))
                mixes[n] = mixed
                return inner

            lax.fori_loop(0, (picks[n, 127] - 5) // 4, more, 0)
            leave(n).wait()
            write(n, mixes[n])
            leave(n).start()

        return carry

    lax.fori_loop(0, 4, deep, 0)
    for n in range(4):
        leave(n).wait()
    moved.wait()


def prefill_call(q, kv, picks, dec):
    hbm = pl.BlockSpec(memory_space=pl.ANY)
    smem = pl.BlockSpec(memory_space=pltpu.SMEM)
    return pl.pallas_call(
        prefill_kernel,
        out_shape=(
            jax.ShapeDtypeStruct((4, PAGE, 1024), BF16),
            jax.ShapeDtypeStruct(dec.shape, BF16),
        ),
        in_specs=[hbm, hbm, smem, hbm],
        out_specs=(hbm, hbm),
        scratch_shapes=[
            pltpu.VMEM((4, PAGE, 1024), BF16),
            pltpu.VMEM((16, 2, 4, PAGE, HD), BF16),
            pltpu.VMEM(dec.shape, BF16),
            pltpu.VMEM((4, PAGE, 1024), BF16),
            pltpu.VMEM((4, 512, 128), F32),
            pltpu.VMEM((4, 512, 256), F32),
            pltpu.SemaphoreType.DMA((9,)),
        ],
        compiler_params=pltpu.CompilerParams(vmem_limit_bytes=62 * 1024 * 1024),
        name="prefill",
    )(q, kv, picks, dec)


def per_device(
    prefill_query, prefill_key, prefill_value, tree_mask, pages, cache_len,
    dec_in, norm_gain, w_query, w_keyval, w_out,
):
    kv, picks, dec = layer_call(
        prefill_key, prefill_value, tree_mask, pages.T, cache_len,
        dec_in.reshape(4, 16, 16, 512), norm_gain.reshape(4, 128), w_query,
        w_keyval.reshape(1024, 128), w_out,
    )
    prefill_out, dec_out = prefill_call(
        prefill_query.reshape(4, PAGE, 1024), kv.reshape(16, 2, 4, PAGE, HD), picks, dec
    )
    return prefill_out.reshape(256, 1024), dec_out.reshape(4, 256, 512)


def solution(mesh):
    return jax.shard_map(
        per_device,
        mesh=mesh,
        in_specs=(
            P("ctx", "head"), P("ctx", "head"), P("ctx", "head"), P(), P(), P(),
            P(None, None, "ctx"), P("ctx"), P("ctx", "head"), P("ctx", None, "head"),
            P("head", "ctx"),
        ),
        out_specs=(P("ctx", "head"), P(None, None, "ctx")),
        check_vma=False,
    )
```

```python
import jax
import jax.numpy as jnp
from jax import lax
from jax.experimental import pallas as pl
from jax.experimental.pallas import tpu as pltpu
from jax.sharding import PartitionSpec as P

D = 8192
HD = 128
PAGE = 64
STEPS = 4
SCALE = HD ** (-0.5)
NEG = -1e30
F32 = jnp.float32
BF16 = jnp.bfloat16
MESH = pl.DeviceIdType.MESH

NCH = 4
TS = STEPS // NCH
RB = 16 * TS

KV0 = 0
SQ0 = 12
PART0 = 17
M_CORE, M_X, M_Z, M_HO, M_Y, M_ZL, M_FO = 0, 1, 5, 6, 15, 19, 20
PART_MSGS = 24
NMSG = PART0 + NCH * PART_MSGS


ORDER = (
    "p0.other", "p1.other", "all.sq", "p0.own", "kv.r", "p2.other", "kv.l", "p3.other",
    "p0.xr0", "p0.xr2", "p1.own", "kv.f", "p2.own", "p3.own", "kv.s", "all.sq1", "p1.xr0",
    "kv.z", "p0.xsum", "kv.m", "p1.xr2", "all.sq2", "p3.xr0", "p3.xr2", "p2.xr2", "p2.xr0",
    "kv.o", "all.mask", "kv.fin", "p1.xsum", "all.take", "p0.att", "p2.xsum", "p3.xsum",
    "p1.att", "p0.hz", "p2.att", "p1.hz", "p0.hl", "p0.hr", "p3.att", "p2.hz", "p0.hf", "p1.hr",
    "p1.hl", "p0.out", "p3.hz", "p1.hf", "p2.hr", "p2.hl", "p1.out", "p3.hl", "p2.hf", "p3.hr",
    "p0.yr2", "p0.yr0", "p2.out", "p3.hf", "p1.yr2", "p1.yr0", "p3.out", "p0.ysum", "p2.yr2",
    "p2.yr0", "p1.ysum", "p3.yr0", "p3.yr2", "p0.add", "p2.ysum", "p1.add", "p3.ysum", "p0.f1",
    "p0.f2", "p2.add", "p3.add", "p1.f1", "p1.f2", "p2.f1", "p2.f2", "p3.f1", "p3.f2", "p1.f5",
    "p2.f5", "all.list", "p0.f5", "p3.f5",
)


def rdot(a, b):
    return lax.dot_general(a, b, (((1,), (1,)), ((), ())), preferred_element_type=F32)


def mdot(a, b):
    return lax.dot_general(a, b, (((1,), (0,)), ((), ())), preferred_element_type=F32)


def layer_kernel(
    key_ref, val_ref, mask_hbm, pages_hbm, clen_hbm, x_ref, gain_hbm, wq_ref, wkv_ref, wo_ref,
    kv_out, picks, out,
    ob, mask_ref, pages_ref, clen_ref, gain_ref,
    kv, xb, wb, wkvb, wkvf, wob, xs, sqs, sqc, sqx, sqn, sqz, sqr, gs, gr, g, prelay, pleft, pright, zs, zr, rf,
    pr, nk, nv, bias, chosen, pool_k, pool_v, sb, ho, o, orelay, oleft, oright, ozs, ozr,
    lsem, ssem, rsem,
):
    c = lax.axis_index("ctx")
    h = lax.axis_index("head")
    core = lax.rem(c, 2)
    zh = lax.rem(c // 2, 2)
    x = c // 4
    y = lax.rem(h, 4)
    zl = h // 4

    def cidx(xi, zi, ci):
        return xi * 4 + zi * 2 + ci

    def hidx(yi, zi):
        return zi * 4 + yi

    xr, xl, xo = lax.rem(x + 1, 4), lax.rem(x + 3, 4), lax.rem(x + 2, 4)
    yr, yl, yo = lax.rem(y + 1, 4), lax.rem(y + 3, 4), lax.rem(y + 2, 4)
    d_xr = (cidx(xr, zh, core), h)
    d_xl = (cidx(xl, zh, core), h)
    d_z = (cidx(x, 1 - zh, core), h)
    d_c = (cidx(x, zh, 1 - core), h)
    d_yr = (c, hidx(yr, zl))
    d_yl = (c, hidx(yl, zl))
    d_zl = (c, hidx(y, 1 - zl))
    d_xo = (cidx(xo, zh, core), h)

    def msg(i, src, dst, dev):
        return pltpu.make_async_remote_copy(
            src_ref=src, dst_ref=dst, send_sem=ssem.at[i], recv_sem=rsem.at[i],
            device_id=dev, device_id_type=MESH,
        )

    barrier = pltpu.get_barrier_semaphore()

    for dev in (d_xr, d_xl, d_z, d_c, d_yr, d_yl, d_zl, d_xo):
        pl.semaphore_signal(barrier, inc=1, device_id=dev, device_id_type=MESH)

    loads = [
        pltpu.make_async_copy(key_ref, kv.at[x, core, zh, 0], lsem.at[0]),
        pltpu.make_async_copy(val_ref, kv.at[x, core, zh, 1], lsem.at[1]),
        pltpu.make_async_copy(x_ref, xb, lsem.at[2]),
        pltpu.make_async_copy(wkv_ref, wkvb, lsem.at[3]),
    ]
    for j in range(4):
        loads.append(
            pltpu.make_async_copy(wq_ref.at[:, pl.ds(256 * j, 256)], wb.at[j], lsem.at[4 + j])
        )
    for j in range(2):
        loads.append(
            pltpu.make_async_copy(wo_ref.at[:, pl.ds(256 * j, 256)], wob.at[j], lsem.at[8 + j])
        )
    for i, (src, dst) in enumerate(
        ((gain_hbm, gain_ref), (mask_hbm, mask_ref), (pages_hbm, pages_ref), (clen_hbm, clen_ref))
    ):
        loads.append(pltpu.make_async_copy(src, dst, lsem.at[11 + i]))
    for copy in loads:
        copy.start()

    pl.semaphore_wait(barrier, 8)

    sent = []

    def send(i, src, dst, dev):
        m = msg(i, src, dst, dev)
        m.start()
        sent.append(m)
        return m

    def drain(left):
        while len(sent) > left:
            sent.pop(0).wait_send()

    def pass_to(msgs, base, k, ref, dev):
        msgs[k] = send(base + k, ref, ref, dev)

    kvm = {}

    def kv_start():
        own = kv.at[x, core, zh]
        pass_to(kvm, KV0, 1, own, d_xr)
        pass_to(kvm, KV0, 2, own, d_xl)
        pass_to(kvm, KV0, 0, own, d_z)

    def kv_pass(what):
        if what == "l":
            kvm[1].wait_recv()
            pass_to(kvm, KV0, 3, kv.at[xl, core, zh, 0], d_xr)
            pass_to(kvm, KV0, 5, kv.at[xl, core, zh], d_z)
        elif what == "r":
            kvm[2].wait_recv()
            pass_to(kvm, KV0, 4, kv.at[xr, core, zh, 1], d_xl)
            pass_to(kvm, KV0, 6, kv.at[xr, core, zh], d_z)
        elif what == "f":
            kvm[3].wait_recv()
            kvm[4].wait_recv()
            pass_to(kvm, KV0, 7, kv.at[xo, core, zh], d_z)
        else:
            waited, given, place = {"z": (0, 8, x), "m": (5, 9, xl), "s": (6, 10, xr), "o": (7, 11, xo)}[
                what
            ]
            kvm[waited].wait_recv()
            pass_to(kvm, KV0, given, kv.at[place, core], d_c)

    class Gather:
        def __init__(self, base, pair):
            self.base, self.pair, self.m = base, pair, {}

        def put(self, k, ref, dev):
            pass_to(self.m, self.base, k, ref, dev)

        def start(self):
            self.put(0, self.pair(x).at[zh], d_z)

        def take(self, which):
            if which == "z":
                self.m[0].wait_recv()
                self.put(1, self.pair(x), d_xr)
                self.put(2, self.pair(x), d_xl)
                self.put(5, self.pair(x), d_c)
            elif which == "l":
                self.m[1].wait_recv()
                self.put(3, self.pair(xl).at[0], d_xr)
                self.put(6, self.pair(xl), d_c)
            elif which == "r":
                self.m[2].wait_recv()
                self.put(4, self.pair(xr).at[1], d_xl)
                self.put(7, self.pair(xr), d_c)
            else:
                self.m[3].wait_recv()
                self.m[4].wait_recv()
                self.put(8, self.pair(xo), d_c)

        def finish(self):
            for k in range(5, 9):
                self.m[k].wait_recv()

    loads[0].wait()
    loads[1].wait()
    kv_start()

    loads[2].wait()
    loads[10].wait()
    row_id = lax.broadcasted_iota(jnp.int32, (64, 128), 0)
    lane_id = lax.broadcasted_iota(jnp.int32, (64, 128), 1)
    eye = row_id == lane_id
    gain4 = gain_ref[...].astype(F32)
    gain = jnp.concatenate([gain4[i : i + 1] for i in range(4)], axis=1)

    def scale_rows(p, side):
        steps = pl.ds(p.k * TS, TS)

        def body(i, carry):
            raw = xb[steps, 2 * i + side].astype(F32).reshape(RB, 512)
            xs[p.k, side, i] = (raw * gain).astype(BF16)
            return carry

        lax.fori_loop(0, 8, body, 0, unroll=True)

    def squares(d, carry):
        raw = xb[:, d].astype(F32).reshape(64, 512)
        part = jnp.sum(raw * raw, axis=1, keepdims=True)
        flat = jnp.sum(jnp.where(eye, part, 0.0), axis=0, keepdims=True)
        sqs[lax.rem(d, 2), d // 4, lax.rem(d // 2, 2)] = jnp.broadcast_to(flat, (8, 128))
        return carry

    first = pl.ds(0, 5)
    second = pl.ds(5, 5)

    class Part:
        pass

    parts = []
    for k in range(NCH):
        p = Part()
        p.k = k
        p.base = PART0 + k * PART_MSGS
        p.px, p.oy = {}, {}
        p.hog = Gather(p.base + M_HO, lambda a, k=k: ho.at[k, a, core])
        parts.append(p)

    def other_rows(p):
        k = p.k

        rows = xs[k, 1 - core].reshape(8 * RB, 512)
        for j in range(5):
            res = mdot(rows, wb[j]).astype(BF16)
            gs[k, 2 * j] = res[:, :128].reshape(4, 2, RB, 128)
            gs[k, 2 * j + 1] = res[:, 128:].reshape(4, 2, RB, 128)
        p.core = send(p.base + M_CORE, gs.at[k], gr.at[k], d_c)

    def own_rows(p):
        k, px = p.k, p.px
        p.core.wait_recv()
        rows = xs[k, core].reshape(8 * RB, 512)

        def body(j):
            res = mdot(rows, wb[j])
            for i in range(2):
                both = res[:, 128 * i : 128 * i + 128].reshape(4, 2, RB, 128) + gr[
                    k, 2 * j + i
                ].astype(F32)
                g[k, :, 2 * j + i] = both.astype(BF16)

        for j in range(3):
            body(j)
        px[0] = send(p.base + M_X, g.at[k, xo, first], prelay.at[k, 0], d_xr)
        for j in range(3, 5):
            body(j)
        px[1] = send(p.base + M_X + 1, g.at[k, xo, second], prelay.at[k, 1], d_xl)

    def x_relay(p, side):
        k, px = p.k, p.px
        which, to, dev, into = ((first, xr, d_xr, pleft), (second, xl, d_xl, pright))[side]
        px[side].wait_recv()
        g[k, to, which] = (g[k, to, which].astype(F32) + prelay[k, side].astype(F32)).astype(BF16)
        px[2 + side] = send(p.base + M_X + 2 + side, g.at[k, to], into.at[k], dev)

    def x_sum(p):
        k, px = p.k, p.px
        px[2].wait_recv()
        px[3].wait_recv()

        def three(s, z):
            return (
                g[k, x, s, z].astype(F32)
                + pleft[k, s, z].astype(F32)
                + pright[k, s, z].astype(F32)
            )

        for s in range(10):
            zs[k, s] = three(s, 1 - zh).astype(BF16)
        p.zp = send(p.base + M_Z, zs.at[k], zr.at[k], d_z)

        for s in range(10):
            rf[k, s] = three(s, zh)

    def attend(p, inverse):
        k = p.k
        nrow = 8 * RB
        nnew = (k + 1) * RB
        inv = inverse[k * RB : (k + 1) * RB]
        p.zp.wait_recv()

        for s in range(10):
            pr[k, s] = ((rf[k, s] + zr[k, s].astype(F32)) * inv).astype(BF16)
        nk[k * RB : (k + 1) * RB] = pr[k, 8]
        nv[k * RB : (k + 1) * RB, 0:128] = pr[k, 9]

        q = pr[k, 0:8].reshape(nrow, HD)
        i_id = lax.broadcasted_iota(jnp.int32, (nrow, nnew), 0)
        j_id = lax.broadcasted_iota(jnp.int32, (nrow, nnew), 1)
        seen = (lax.rem(i_id, 16) == lax.rem(j_id, 16)) & (
            j_id // 16 <= k * TS + lax.rem(i_id // 16, TS)
        )
        s_new = jnp.where(seen, rdot(q, nk[0:nnew]) * SCALE, NEG)
        peak = None
        for b in range(8):
            s = rdot(q, pool_k[256 * b : 256 * b + 256]) * SCALE
            s = (s.reshape(nrow // 16, 16, 256) + bias[b][None]).reshape(nrow, 256)
            sb[b] = s
            here = jnp.maximum(s[:, :128], s[:, 128:])
            peak = here if peak is None else jnp.maximum(peak, here)
        top = jnp.maximum(
            jnp.max(peak, axis=1, keepdims=True), jnp.max(s_new, axis=1, keepdims=True)
        )
        w_new = jnp.exp(s_new - top)
        mixed = mdot(w_new.astype(BF16), nv[0:nnew])
        for b in range(8):
            w = jnp.exp(sb[b] - top).astype(BF16)
            mixed = mixed + mdot(w, pool_v[256 * b : 256 * b + 256])
        head_out = (mixed[:, 0:128] / mixed[:, 128:256]).astype(BF16)
        for s in range(8):
            ho[k, x, core, zh, s // 4, :, (s % 4) * HD : (s % 4 + 1) * HD] = head_out[s * RB : (s + 1) * RB]
        p.hog.start()

    def out_rows(p):
        k, oy = p.k, p.oy
        p.hog.finish()
        lhs = [ho[k, :, :, :, f].reshape(16 * RB, 512) for f in range(2)]
        for n in range(2):
            res = mdot(lhs[0], wob[n, 0:512]) + mdot(lhs[1], wob[n, 512:1024])
            o[k, :, :, :, :, n * 256 : (n + 1) * 256] = res.astype(BF16).reshape(4, 2, 2, RB, 256)
        oy[0] = send(p.base + M_Y, o.at[k, yo, 0], orelay.at[k, 0], d_yr)
        oy[1] = send(p.base + M_Y + 1, o.at[k, yo, 1], orelay.at[k, 1], d_yl)

    def y_relay(p, side):
        k, oy = p.k, p.oy
        to, dev, into = ((yr, d_yr, oleft), (yl, d_yl, oright))[side]
        oy[side].wait_recv()
        o[k, to, side] = (o[k, to, side].astype(F32) + orelay[k, side].astype(F32)).astype(BF16)
        oy[2 + side] = send(p.base + M_Y + 2 + side, o.at[k, to], into.at[k], dev)

    def y_sum(p):
        k, oy = p.k, p.oy
        oy[2].wait_recv()
        oy[3].wait_recv()

        for i in range(2):
            ozs[k, i] = (
                o[k, y, i].astype(F32) + oleft[k, i].astype(F32) + oright[k, i].astype(F32)
            ).astype(BF16)
        p.oz = send(p.base + M_ZL, ozs.at[k], ozr.at[k], d_zl)

    def add_input(p):
        k = p.k
        p.oz.wait_recv()
        steps = pl.ds(k * TS, TS)
        for z in range(2):
            for i in range(2):
                full = ozs[k, i, z].astype(F32) + ozr[k, i, z].astype(F32)
                hidden = xb[steps, cidx(y, z, i)].astype(F32)
                ob[steps, 2 * y + z, pl.ds(16 * i, 16), :] = (
                    hidden + full.reshape(TS, 16, 512)
                ).astype(BF16)
        own = ob.at[steps, pl.ds(2 * y, 2)]
        p.fo = {
            1: send(p.base + M_FO, own, own, d_yr),
            2: send(p.base + M_FO + 1, own, own, d_yl),
        }

    def pass_on(p, k):
        steps = pl.ds(p.k * TS, TS)
        if k == 1:
            p.fo[1].wait_recv()
            part = ob.at[steps, 2 * yl]
            p.fo[5] = send(p.base + M_FO + 2, part, part, d_yr)
        elif k == 2:
            p.fo[2].wait_recv()
            part = ob.at[steps, 2 * yr + 1]
            p.fo[6] = send(p.base + M_FO + 3, part, part, d_yl)
        else:
            p.fo[5].wait_recv()
            p.fo[6].wait_recv()
            p.done = pltpu.make_async_copy(ob.at[steps], out.at[steps], lsem.at[15 + p.k])
            p.done.start()

    def load_weights():
        for k in range(3, 8):
            loads[k].wait()
        wkvf[...] = wkvb[...].astype(F32)
        wb[4, :, 0:128] = wkvf[pl.ds(0, 512, stride=2), :].astype(BF16)
        wb[4, :, 128:256] = wkvf[pl.ds(1, 512, stride=2), :].astype(BF16)

    def sum_squares():
        lax.fori_loop(0, 16, squares, 0, unroll=4)
        return [send(SQ0, sqs.at[1 - core], sqc, d_c)]

    def sum_squares_x(before):
        before[0].wait_recv()
        sqx[...] = sqs[core] + sqc[...]
        return [
            send(SQ0 + 1, sqx.at[xr], sqn.at[0], d_xr),
            send(SQ0 + 2, sqx.at[xl], sqn.at[1], d_xl),
            send(SQ0 + 3, sqx.at[xo], sqn.at[2], d_xo),
        ]

    def sum_squares_z(before):
        for m in before:
            m.wait_recv()
        sqz[...] = sqx[x] + sqn[0] + sqn[1] + sqn[2]
        return [send(SQ0 + 4, sqz.at[1 - zh], sqr, d_z)]

    def inverse_rms(before):
        before[0].wait_recv()
        flat = (sqz[zh] + sqr[...])[0:1, :]
        row_sq = jnp.sum(jnp.where(eye, flat, 0.0), axis=1, keepdims=True)
        return lax.rsqrt(row_sq / D + 1e-05)

    def choose_pages():
        loads[12].wait()
        loads[13].wait()
        pick = (
            lax.broadcasted_iota(jnp.int32, (16, 256), 1)
            == lax.broadcasted_iota(jnp.int32, (16, 256), 0) + 16 * c
        )
        own_pages = rdot(pick.astype(BF16), pages_ref[...].astype(BF16)).astype(jnp.int32)
        r_id = lax.broadcasted_iota(jnp.int32, (16, 256), 0)
        s_id = lax.broadcasted_iota(jnp.int32, (16, 256), 1)
        lens = jnp.zeros((16, 256), jnp.int32)
        for r in range(16):
            lens = jnp.where(r_id == r, clen_ref[c * 16 + r], lens)
        in_page = lax.rem(s_id, PAGE)
        page_id = lax.broadcasted_iota(jnp.int32, (16, 64), 1)
        named = jnp.zeros((16, 64), F32)
        for slot in range(8):
            named = jnp.where(own_pages[:, slot : slot + 1] == page_id, 1.0, named)
        present = jnp.broadcast_to(jnp.max(named, axis=0, keepdims=True), (16, 64))
        a_id = lax.broadcasted_iota(jnp.int32, (64, 64), 0)
        b_id = lax.broadcasted_iota(jnp.int32, (64, 64), 1)
        ahead = (a_id // 4 == b_id // 4) & (a_id < b_id)
        rank = mdot(present.astype(BF16), ahead.astype(BF16))
        code = jnp.where(present > 0.5, rank + 1.0, 0.0).astype(BF16)
        node_id = lax.broadcasted_iota(jnp.int32, (64, 256), 0)
        node_of = lax.broadcasted_iota(jnp.int32, (64, 256), 1) // PAGE
        to_id = lax.broadcasted_iota(jnp.int32, (128, 256), 0)
        from_id = lax.broadcasted_iota(jnp.int32, (128, 256), 1)
        same = lax.rem(to_id, PAGE) == lax.rem(from_id, PAGE)
        want = jnp.where(same, (to_id // PAGE + 1).astype(F32), -1.0)
        last = [
            (own_pages[:, slot : slot + 1], lens - slot * PAGE, s_id // PAGE)
            for slot in range(8)
        ]

        def choose(b):
            live = jnp.zeros((16, 256), F32)
            for named_page, upto, page in last:
                hit = (named_page - 4 * b == page) & (in_page < upto)
                live = jnp.where(hit, 1.0, live)
            spread = mdot(code, (node_id == node_of + 4 * b).astype(BF16))
            sel = jnp.where(spread[0:1] == want, 1.0, 0.0).astype(BF16)
            chosen[b] = sel
            return jnp.where(rdot(live.astype(BF16), sel) > 0.5, 0.0, NEG)

        def choose_two(i, carry):
            bias[i, :, 0:128] = choose(2 * i)
            bias[i, :, 128:256] = choose(2 * i + 1)
            return carry

        lax.fori_loop(0, 8, choose_two, 0, unroll=2)

    def take_pages():
        pool_v[:, 128:256] = jnp.ones((2048, 128), BF16)
        nv[:, 128:256] = jnp.ones((64, 128), BF16)

        def take(b, carry):
            rows = pl.ds(pl.multiple_of(128 * b, 128), 128)
            block = (b // 4, lax.rem(b, 2), lax.rem(b // 2, 2))
            pool_k[rows] = mdot(chosen[b], kv[block + (0,)]).astype(BF16)
            pool_v[rows, 0:128] = mdot(chosen[b], kv[block + (1,)]).astype(BF16)
            return carry

        lax.fori_loop(0, 16, take, 0, unroll=8)

    def list_pages():
        loads[11].wait()
        a_id = lax.broadcasted_iota(jnp.int32, (64, 64), 0)
        b_id = lax.broadcasted_iota(jnp.int32, (64, 64), 1)
        col_id = lax.broadcasted_iota(jnp.int32, (64, 128), 1)
        p_id = lax.broadcasted_iota(jnp.int32, (64, 128), 0)
        spot = (p_id // 16) * 16 + lax.rem(p_id // 4, 2) * 8 + lax.rem(p_id // 8, 2) * 4
        spot = (spot + lax.rem(p_id, 4)).astype(F32)
        rows = []
        for n in range(4):
            a = 4 * c + n
            line = mask_ref[pl.ds(a, 1), :].astype(F32)
            readable = jnp.sum(jnp.where(a_id == b_id, line, 0.0), axis=1, keepdims=True)
            readable = jnp.where((readable > 0.5) & (p_id < a), 1.0, 0.0)
            before = mdot((b_id < a_id).astype(BF16), readable.astype(BF16))
            place = jnp.where(p_id == a, 0.0, before + 1.0).astype(jnp.int32)
            hit = (place == col_id) & ((readable > 0.5) | (p_id == a))
            line = jnp.sum(jnp.where(hit, spot, 0.0), axis=0, keepdims=True)
            count = jnp.sum(readable, axis=0, keepdims=True) + 1.0
            rows.append(jnp.where(col_id[0:1] == 127, count, line))
        picks[...] = jnp.concatenate(rows + rows, axis=0).astype(jnp.int32)

    keep = pltpu.make_async_copy(kv, kv_out, lsem.at[10])
    rms, squared = [], []
    late = [loads[8], loads[9]]

    def step(event):
        who, what = event.split(".")
        if who == "kv":
            if what == "fin":
                for k in range(8, 12):
                    kvm[k].wait_recv()
                keep.start()
            else:
                kv_pass(what)
            return
        if who == "all":
            if what[:2] == "sq":
                stage = {"sq": sum_squares, "sq1": sum_squares_x, "sq2": sum_squares_z}[what]
                squared[:] = stage(squared) if squared else stage()
            else:
                {"mask": choose_pages, "take": take_pages, "list": list_pages}[what]()
            return
        p = parts[int(who[1])]
        if what == "other":
            scale_rows(p, 1 - core)
            if p.k == 0:
                load_weights()
            other_rows(p)
        elif what == "own":
            scale_rows(p, core)
            own_rows(p)
        elif what[0] == "x":
            if what == "xsum":
                x_sum(p)
            else:
                x_relay(p, int(what[2]) // 2)
        elif what == "att":
            if not rms:
                rms.append(inverse_rms(squared))
            attend(p, rms[0])
        elif what[0] == "h":
            p.hog.take(what[1])
        elif what == "out":
            while late:
                late.pop().wait()
            out_rows(p)
        elif what == "ysum":
            drain(10)
            y_sum(p)
        elif what[0] == "y":
            y_relay(p, int(what[2]) // 2)
        elif what == "add":
            add_input(p)
        else:
            drain(6)
            pass_on(p, int(what[1]))

    for event in ORDER:
        step(event)
    keep.wait()
    drain(0)
    for p in parts:
        p.done.wait()


def layer_call(*args):
    hbm = pl.BlockSpec(memory_space=pl.ANY)
    vmem = pl.BlockSpec(memory_space=pltpu.VMEM)
    return pl.pallas_call(
        layer_kernel,
        out_shape=(
            jax.ShapeDtypeStruct((4, 2, 2, 2, 256, HD), BF16),
            jax.ShapeDtypeStruct((8, 128), jnp.int32),
            jax.ShapeDtypeStruct((4, 8, 32, 512), BF16),
        ),
        in_specs=[hbm] * 10,
        out_specs=(hbm, vmem, hbm),
        scratch_shapes=[
            pltpu.VMEM((4, 8, 32, 512), BF16),
            pltpu.VMEM((64, 64), jnp.int32),
            pltpu.VMEM((8, 256), jnp.int32),
            pltpu.SMEM((256,), jnp.int32),
            pltpu.VMEM((4, 128), BF16),
            pltpu.VMEM((4, 2, 2, 2, 256, HD), BF16),
            pltpu.VMEM((4, 16, 16, 512), BF16),
            pltpu.VMEM((5, 512, 256), BF16),
            pltpu.VMEM((1024, 128), BF16),
            pltpu.VMEM((1024, 128), F32),
            pltpu.VMEM((2, 1024, 256), BF16),
            pltpu.VMEM((NCH, 2, 8, RB, 512), BF16),
            pltpu.VMEM((2, 4, 2, 8, 128), F32),
            pltpu.VMEM((4, 2, 8, 128), F32),
            pltpu.VMEM((4, 2, 8, 128), F32),
            pltpu.VMEM((3, 2, 8, 128), F32),
            pltpu.VMEM((2, 8, 128), F32),
            pltpu.VMEM((8, 128), F32),
            pltpu.VMEM((NCH, 10, 4, 2, RB, 128), BF16),
            pltpu.VMEM((NCH, 10, 4, 2, RB, 128), BF16),
            pltpu.VMEM((NCH, 4, 10, 2, RB, 128), BF16),
            pltpu.VMEM((NCH, 2, 5, 2, RB, 128), BF16),
            pltpu.VMEM((NCH, 10, 2, RB, 128), BF16),
            pltpu.VMEM((NCH, 10, 2, RB, 128), BF16),
            pltpu.VMEM((NCH, 10, RB, 128), BF16),
            pltpu.VMEM((NCH, 10, RB, 128), BF16),
            pltpu.VMEM((NCH, 10, RB, 128), F32),
            pltpu.VMEM((NCH, 10, RB, 128), BF16),
            pltpu.VMEM((64, 128), BF16),
            pltpu.VMEM((64, 256), BF16),
            pltpu.VMEM((8, 16, 256), F32),
            pltpu.VMEM((16, 128, 256), BF16),
            pltpu.VMEM((2048, HD), BF16),
            pltpu.VMEM((2048, 2 * HD), BF16),
            pltpu.VMEM((8, 8 * RB, 256), F32),
            pltpu.VMEM((NCH, 4, 2, 2, 2, RB, 512), BF16),
            pltpu.VMEM((NCH, 4, 2, 2, RB, 512), BF16),
            pltpu.VMEM((NCH, 2, 2, RB, 512), BF16),
            pltpu.VMEM((NCH, 2, 2, RB, 512), BF16),
            pltpu.VMEM((NCH, 2, 2, RB, 512), BF16),
            pltpu.VMEM((NCH, 2, 2, RB, 512), BF16),
            pltpu.VMEM((NCH, 2, 2, RB, 512), BF16),
            pltpu.SemaphoreType.DMA((15 + NCH,)),
            pltpu.SemaphoreType.DMA((NMSG,)),
            pltpu.SemaphoreType.DMA((NMSG,)),
        ],
        compiler_params=pltpu.CompilerParams(
            collective_id=0, has_side_effects=True, vmem_limit_bytes=56 * 1024 * 1024
        ),
        name="layer",
    )(*args)


def prefill_kernel(
    q_hbm, kv_ref, picks, dec_ref, out_hbm, dec_out, q_ref, kv, extra, stage, out, peaks, mixes, sem
):
    def page(n, k):
        spot = picks[n, k]
        return kv_ref.at[spot // 4, :, lax.rem(spot, 4)]

    get_q = pltpu.make_async_copy(q_hbm, q_ref, sem.at[0])
    fetched = pltpu.make_async_copy(dec_ref, stage, sem.at[1])
    moved = pltpu.make_async_copy(stage, dec_out, sem.at[2])
    get_q.start()
    for n in range(4):
        for k in range(8):
            pltpu.make_async_copy(page(n, k), kv.at[n, k], sem.at[7 + n]).start()
    fetched.start()

    def attend(n, start, pages, state):
        block = kv[n] if state is None else extra[...]
        keys = block[:, 0].reshape(pages * PAGE, HD)
        values = jnp.concatenate(
            [block[:, 1].reshape(pages * PAGE, HD), jnp.ones((pages * PAGE, 128), BF16)], axis=1
        )
        q = jnp.concatenate([q_ref[n, :, s * HD : (s + 1) * HD] for s in range(8)], axis=0)
        j_id = lax.broadcasted_iota(jnp.int32, (1, pages * PAGE), 1)
        hidden = jnp.where(j_id < (picks[n, 127] - start) * PAGE, 0.0, NEG)
        s = rdot(q, keys) * SCALE + hidden
        if state is None:
            i_id = lax.broadcasted_iota(jnp.int32, (512, 128), 0)
            j_id = lax.broadcasted_iota(jnp.int32, (512, 128), 1)
            seen = (j_id >= PAGE) | (j_id <= lax.rem(i_id, PAGE))
            s = jnp.concatenate([jnp.where(seen, s[:, :128], NEG), s[:, 128:]], axis=1)
        peak = jnp.max(s, axis=1, keepdims=True)
        if state is not None:
            peak = jnp.maximum(peak, state[0])
        mixed = mdot(jnp.exp(s - peak).astype(BF16), values)
        if state is not None:
            mixed = mixed + state[1] * jnp.exp(state[0] - peak)
        return peak, mixed

    def write(n, mixed):
        result = (mixed[:, 0:128] / mixed[:, 128:256]).astype(BF16)
        for s in range(8):
            out[n, :, s * HD : (s + 1) * HD] = result[s * 64 : (s + 1) * 64]

    def leave(n):
        return pltpu.make_async_copy(out.at[n], out_hbm.at[n], sem.at[3 + n])

    get_q.wait()
    for n in range(4):
        pltpu.make_async_copy(kv.at[n], kv.at[n], sem.at[7 + n]).wait()
        peak, mixed = attend(n, 0, 8, None)
        peaks[n] = jnp.broadcast_to(peak, (512, 128))
        mixes[n] = mixed
        write(n, mixed)
        leave(n).start()
        if n == 1:
            fetched.wait()
            moved.start()

    def deep(n, carry):
        @pl.when(picks[n, 127] > 8)
        def _():
            def more(t, inner):
                for k in range(4):
                    pltpu.make_async_copy(page(n, 8 + 4 * t + k), extra.at[k], sem.at[11]).start()
                pltpu.make_async_copy(extra, extra, sem.at[11]).wait()
                peak, mixed = attend(n, 8 + 4 * t, 4, (peaks[n][:, 0:1], mixes[n]))
                peaks[n] = jnp.broadcast_to(peak, (512, 128))
                mixes[n] = mixed
                return inner

            lax.fori_loop(0, (picks[n, 127] - 5) // 4, more, 0)
            leave(n).wait()
            write(n, mixes[n])
            leave(n).start()

        return carry

    lax.fori_loop(0, 4, deep, 0)
    for n in range(4):
        leave(n).wait()
    moved.wait()


def prefill_call(q, kv, picks, dec):
    hbm = pl.BlockSpec(memory_space=pl.ANY)
    smem = pl.BlockSpec(memory_space=pltpu.SMEM)
    return pl.pallas_call(
        prefill_kernel,
        out_shape=(
            jax.ShapeDtypeStruct((4, PAGE, 1024), BF16),
            jax.ShapeDtypeStruct(dec.shape, BF16),
        ),
        in_specs=[hbm, hbm, smem, hbm],
        out_specs=(hbm, hbm),
        scratch_shapes=[
            pltpu.VMEM((4, PAGE, 1024), BF16),
            pltpu.VMEM((4, 8, 2, PAGE, HD), BF16),
            pltpu.VMEM((4, 2, PAGE, HD), BF16),
            pltpu.VMEM(dec.shape, BF16),
            pltpu.VMEM((4, PAGE, 1024), BF16),
            pltpu.VMEM((4, 512, 128), F32),
            pltpu.VMEM((4, 512, 256), F32),
            pltpu.SemaphoreType.DMA((12,)),
        ],
        compiler_params=pltpu.CompilerParams(vmem_limit_bytes=62 * 1024 * 1024),
        name="prefill",
    )(q, kv, picks, dec)


def per_device(
    prefill_query, prefill_key, prefill_value, tree_mask, pages, cache_len,
    dec_in, norm_gain, w_query, w_keyval, w_out,
):
    kv, picks, dec = layer_call(
        prefill_key, prefill_value, tree_mask, pages.T, cache_len,
        dec_in.reshape(4, 16, 16, 512), norm_gain.reshape(4, 128), w_query,
        w_keyval.reshape(1024, 128), w_out,
    )
    prefill_out, dec_out = prefill_call(
        prefill_query.reshape(4, PAGE, 1024), kv.reshape(16, 2, 4, PAGE, HD), picks, dec
    )
    return prefill_out.reshape(256, 1024), dec_out.reshape(4, 256, 512)


def solution(mesh):
    return jax.shard_map(
        per_device,
        mesh=mesh,
        in_specs=(
            P("ctx", "head"), P("ctx", "head"), P("ctx", "head"), P(), P(), P(),
            P(None, None, "ctx"), P("ctx"), P("ctx", "head"), P("ctx", None, "head"),
            P("head", "ctx"),
        ),
        out_specs=(P("ctx", "head"), P(None, None, "ctx")),
        check_vma=False,
    )
```

```python
import jax
import jax.numpy as jnp
from jax import lax
from jax.experimental import pallas as pl
from jax.experimental.pallas import tpu as pltpu
from jax.sharding import PartitionSpec as P

D = 8192
HD = 128
PAGE = 64
STEPS = 4
SCALE = HD ** (-0.5)
NEG = -1e30
F32 = jnp.float32
BF16 = jnp.bfloat16
MESH = pl.DeviceIdType.MESH

NCH = 4
TS = STEPS // NCH
RB = 16 * TS

KV0 = 0
SQ0 = 12
PART0 = 17
M_CORE, M_X, M_Z, M_HO, M_Y, M_ZL, M_FO = 0, 1, 5, 6, 15, 19, 20
PART_MSGS = 24
NMSG = PART0 + NCH * PART_MSGS


ORDER = (
    "p0.other", "p1.other", "all.sq", "p0.own", "kv.r", "p2.other", "kv.l", "p1.own", "p0.xr2",
    "p3.other", "p0.xr0", "kv.f", "p2.own", "p3.own", "all.sq1", "p1.xr2", "p1.xr0", "p2.xr2",
    "kv.m", "kv.z", "p0.xsum", "kv.s", "p2.xr0", "all.mask", "p3.xr0", "kv.o", "all.sq2",
    "p3.xr2", "p1.xsum", "p2.xsum", "kv.fin", "all.take", "p0.att", "p3.xsum", "p1.att",
    "p2.att", "p0.hz", "p1.hz", "p3.att", "p2.hz", "p1.hl", "p1.hr", "p0.hl", "p0.hr", "p3.hz",
    "p2.hl", "p1.hf", "p2.hr", "p0.hf", "p1.out", "p3.hr", "p3.hl", "p2.hf", "p0.out", "p1.yr0",
    "p1.yr2", "p3.hf", "p2.out", "p0.yr0", "p0.yr2", "p3.out", "p1.ysum", "p2.yr0", "p2.yr2",
    "p0.ysum", "p3.yr0", "p3.yr2", "all.list", "p1.add", "p2.ysum", "p0.add", "p3.ysum",
    "p1.f1", "p1.f2", "p2.add", "all.pf0", "p3.add", "p0.f1", "p0.f2", "p1.f5", "p2.f1",
    "p2.f2", "all.pf1", "p3.f1", "p3.f2", "all.pf2", "p2.f5", "all.pf3", "p0.f5", "p3.f5",
)


def rdot(a, b):
    return lax.dot_general(a, b, (((1,), (1,)), ((), ())), preferred_element_type=F32)


def mdot(a, b):
    return lax.dot_general(a, b, (((1,), (0,)), ((), ())), preferred_element_type=F32)


def first_pages(q_node, keys, values, count):
    q = jnp.concatenate([q_node[:, s * HD : (s + 1) * HD] for s in range(8)], axis=0)
    values = jnp.concatenate([values, jnp.ones((8 * PAGE, 128), BF16)], axis=1)
    j_id = lax.broadcasted_iota(jnp.int32, (1, 8 * PAGE), 1)
    s = rdot(q, keys) * SCALE + jnp.where(j_id < count * PAGE, 0.0, NEG)
    i_id = lax.broadcasted_iota(jnp.int32, (512, 128), 0)
    j_id = lax.broadcasted_iota(jnp.int32, (512, 128), 1)
    seen = (j_id >= PAGE) | (j_id <= lax.rem(i_id, PAGE))
    s = jnp.concatenate([jnp.where(seen, s[:, :128], NEG), s[:, 128:]], axis=1)
    peak = jnp.max(s, axis=1, keepdims=True)
    return peak, mdot(jnp.exp(s - peak).astype(BF16), values)


def write_heads(out, n, mixed):
    result = (mixed[:, 0:128] / mixed[:, 128:256]).astype(BF16)
    for s in range(8):
        out[n, :, s * HD : (s + 1) * HD] = result[s * 64 : (s + 1) * 64]


def layer_kernel(
    q_hbm, key_ref, val_ref, mask_hbm, pages_hbm, clen_hbm, x_ref, gain_hbm, wq_ref, wkv_ref, wo_ref,
    kv_out, picks, pout, out,
    qb, spots, pb, ob, mask_ref, pages_ref, clen_ref, gain_ref,
    kv, xb, wb, wkvb, wkvf, wob, xs, sqs, sqc, sqx, sqn, sqz, sqr, gs, gr, g, prelay, pleft, pright, zs, zr, rf,
    pr, nk, nv, bias, chosen, pool_k, pool_v, sb, ho, o, orelay, oleft, oright, ozs, ozr,
    lsem, ssem, rsem,
):
    c = lax.axis_index("ctx")
    h = lax.axis_index("head")
    core = lax.rem(c, 2)
    zh = lax.rem(c // 2, 2)
    x = c // 4
    y = lax.rem(h, 4)
    zl = h // 4

    def cidx(xi, zi, ci):
        return xi * 4 + zi * 2 + ci

    def hidx(yi, zi):
        return zi * 4 + yi

    xr, xl, xo = lax.rem(x + 1, 4), lax.rem(x + 3, 4), lax.rem(x + 2, 4)
    yr, yl, yo = lax.rem(y + 1, 4), lax.rem(y + 3, 4), lax.rem(y + 2, 4)
    d_xr = (cidx(xr, zh, core), h)
    d_xl = (cidx(xl, zh, core), h)
    d_z = (cidx(x, 1 - zh, core), h)
    d_c = (cidx(x, zh, 1 - core), h)
    d_yr = (c, hidx(yr, zl))
    d_yl = (c, hidx(yl, zl))
    d_zl = (c, hidx(y, 1 - zl))
    d_xo = (cidx(xo, zh, core), h)

    def msg(i, src, dst, dev):
        return pltpu.make_async_remote_copy(
            src_ref=src, dst_ref=dst, send_sem=ssem.at[i], recv_sem=rsem.at[i],
            device_id=dev, device_id_type=MESH,
        )

    barrier = pltpu.get_barrier_semaphore()

    for dev in (d_xr, d_xl, d_z, d_c, d_yr, d_yl, d_zl, d_xo):
        pl.semaphore_signal(barrier, inc=1, device_id=dev, device_id_type=MESH)

    loads = [
        pltpu.make_async_copy(key_ref, kv.at[x, core, zh, 0], lsem.at[0]),
        pltpu.make_async_copy(val_ref, kv.at[x, core, zh, 1], lsem.at[1]),
        pltpu.make_async_copy(x_ref, xb, lsem.at[2]),
        pltpu.make_async_copy(wkv_ref, wkvb, lsem.at[3]),
    ]
    for j in range(4):
        loads.append(
            pltpu.make_async_copy(wq_ref.at[:, pl.ds(256 * j, 256)], wb.at[j], lsem.at[4 + j])
        )
    for j in range(2):
        loads.append(
            pltpu.make_async_copy(wo_ref.at[:, pl.ds(256 * j, 256)], wob.at[j], lsem.at[8 + j])
        )
    for i, (src, dst) in enumerate(
        ((gain_hbm, gain_ref), (mask_hbm, mask_ref), (pages_hbm, pages_ref), (clen_hbm, clen_ref))
    ):
        loads.append(pltpu.make_async_copy(src, dst, lsem.at[11 + i]))
    loads.append(pltpu.make_async_copy(q_hbm, qb, lsem.at[15 + NCH]))
    for copy in loads:
        copy.start()

    pl.semaphore_wait(barrier, 8)

    sent = []

    def send(i, src, dst, dev):
        m = msg(i, src, dst, dev)
        m.start()
        sent.append(m)
        return m

    def drain(left):
        while len(sent) > left:
            sent.pop(0).wait_send()

    def pass_to(msgs, base, k, ref, dev):
        msgs[k] = send(base + k, ref, ref, dev)

    kvm = {}

    def kv_start():
        own = kv.at[x, core, zh]
        pass_to(kvm, KV0, 1, own, d_xr)
        pass_to(kvm, KV0, 2, own, d_xl)
        pass_to(kvm, KV0, 0, own, d_z)

    def kv_pass(what):
        if what == "l":
            kvm[1].wait_recv()
            pass_to(kvm, KV0, 3, kv.at[xl, core, zh, 0], d_xr)
            pass_to(kvm, KV0, 5, kv.at[xl, core, zh], d_z)
        elif what == "r":
            kvm[2].wait_recv()
            pass_to(kvm, KV0, 4, kv.at[xr, core, zh, 1], d_xl)
            pass_to(kvm, KV0, 6, kv.at[xr, core, zh], d_z)
        elif what == "f":
            kvm[3].wait_recv()
            kvm[4].wait_recv()
            pass_to(kvm, KV0, 7, kv.at[xo, core, zh], d_z)
        else:
            waited, given, place = {"z": (0, 8, x), "m": (5, 9, xl), "s": (6, 10, xr), "o": (7, 11, xo)}[
                what
            ]
            kvm[waited].wait_recv()
            pass_to(kvm, KV0, given, kv.at[place, core], d_c)

    class Gather:
        def __init__(self, base, pair):
            self.base, self.pair, self.m = base, pair, {}

        def put(self, k, ref, dev):
            pass_to(self.m, self.base, k, ref, dev)

        def start(self):
            self.put(0, self.pair(x).at[zh], d_z)

        def take(self, which):
            if which == "z":
                self.m[0].wait_recv()
                self.put(1, self.pair(x), d_xr)
                self.put(2, self.pair(x), d_xl)
                self.put(5, self.pair(x), d_c)
            elif which == "l":
                self.m[1].wait_recv()
                self.put(3, self.pair(xl).at[0], d_xr)
                self.put(6, self.pair(xl), d_c)
            elif which == "r":
                self.m[2].wait_recv()
                self.put(4, self.pair(xr).at[1], d_xl)
                self.put(7, self.pair(xr), d_c)
            else:
                self.m[3].wait_recv()
                self.m[4].wait_recv()
                self.put(8, self.pair(xo), d_c)

        def finish(self):
            for k in range(5, 9):
                self.m[k].wait_recv()

    loads[0].wait()
    loads[1].wait()
    kv_start()

    loads[2].wait()
    loads[10].wait()
    row_id = lax.broadcasted_iota(jnp.int32, (64, 128), 0)
    lane_id = lax.broadcasted_iota(jnp.int32, (64, 128), 1)
    eye = row_id == lane_id
    gain4 = gain_ref[...].astype(F32)
    gain = jnp.concatenate([gain4[i : i + 1] for i in range(4)], axis=1)

    def scale_rows(p, side):
        steps = pl.ds(p.k * TS, TS)

        def body(i, carry):
            raw = xb[steps, 2 * i + side].astype(F32).reshape(RB, 512)
            xs[p.k, side, i] = (raw * gain).astype(BF16)
            return carry

        lax.fori_loop(0, 8, body, 0, unroll=True)

    def squares(d, carry):
        raw = xb[:, d].astype(F32).reshape(64, 512)
        part = jnp.sum(raw * raw, axis=1, keepdims=True)
        flat = jnp.sum(jnp.where(eye, part, 0.0), axis=0, keepdims=True)
        sqs[lax.rem(d, 2), d // 4, lax.rem(d // 2, 2)] = jnp.broadcast_to(flat, (8, 128))
        return carry

    first = pl.ds(0, 5)
    second = pl.ds(5, 5)

    class Part:
        pass

    parts = []
    for k in range(NCH):
        p = Part()
        p.k = k
        p.base = PART0 + k * PART_MSGS
        p.px, p.oy = {}, {}
        p.hog = Gather(p.base + M_HO, lambda a, k=k: ho.at[k, a, core])
        parts.append(p)

    def other_rows(p):
        k = p.k

        rows = xs[k, 1 - core].reshape(8 * RB, 512)
        for j in range(5):
            res = mdot(rows, wb[j]).astype(BF16)
            gs[k, 2 * j] = res[:, :128].reshape(4, 2, RB, 128)
            gs[k, 2 * j + 1] = res[:, 128:].reshape(4, 2, RB, 128)
        p.core = send(p.base + M_CORE, gs.at[k], gr.at[k], d_c)

    def own_rows(p):
        k, px = p.k, p.px
        p.core.wait_recv()
        rows = xs[k, core].reshape(8 * RB, 512)

        def body(j):
            res = mdot(rows, wb[j])
            for i in range(2):
                both = res[:, 128 * i : 128 * i + 128].reshape(4, 2, RB, 128) + gr[
                    k, 2 * j + i
                ].astype(F32)
                g[k, :, 2 * j + i] = both.astype(BF16)

        for j in range(3):
            body(j)
        px[0] = send(p.base + M_X, g.at[k, xo, first], prelay.at[k, 0], d_xr)
        for j in range(3, 5):
            body(j)
        px[1] = send(p.base + M_X + 1, g.at[k, xo, second], prelay.at[k, 1], d_xl)

    def x_relay(p, side):
        k, px = p.k, p.px
        which, to, dev, into = ((first, xr, d_xr, pleft), (second, xl, d_xl, pright))[side]
        px[side].wait_recv()
        g[k, to, which] = (g[k, to, which].astype(F32) + prelay[k, side].astype(F32)).astype(BF16)
        px[2 + side] = send(p.base + M_X + 2 + side, g.at[k, to], into.at[k], dev)

    def x_sum(p):
        k, px = p.k, p.px
        px[2].wait_recv()
        px[3].wait_recv()

        def three(s, z):
            return (
                g[k, x, s, z].astype(F32)
                + pleft[k, s, z].astype(F32)
                + pright[k, s, z].astype(F32)
            )

        for s in range(10):
            zs[k, s] = three(s, 1 - zh).astype(BF16)
        p.zp = send(p.base + M_Z, zs.at[k], zr.at[k], d_z)

        for s in range(10):
            rf[k, s] = three(s, zh)

    def attend(p, inverse):
        k = p.k
        nrow = 8 * RB
        nnew = (k + 1) * RB
        inv = inverse[k * RB : (k + 1) * RB]
        p.zp.wait_recv()

        for s in range(10):
            pr[k, s] = ((rf[k, s] + zr[k, s].astype(F32)) * inv).astype(BF16)
        nk[k * RB : (k + 1) * RB] = pr[k, 8]
        nv[k * RB : (k + 1) * RB, 0:128] = pr[k, 9]

        q = pr[k, 0:8].reshape(nrow, HD)
        i_id = lax.broadcasted_iota(jnp.int32, (nrow, nnew), 0)
        j_id = lax.broadcasted_iota(jnp.int32, (nrow, nnew), 1)
        seen = (lax.rem(i_id, 16) == lax.rem(j_id, 16)) & (
            j_id // 16 <= k * TS + lax.rem(i_id // 16, TS)
        )
        s_new = jnp.where(seen, rdot(q, nk[0:nnew]) * SCALE, NEG)
        peak = None
        for b in range(8):
            s = rdot(q, pool_k[256 * b : 256 * b + 256]) * SCALE
            s = (s.reshape(nrow // 16, 16, 256) + bias[b][None]).reshape(nrow, 256)
            sb[b] = s
            here = jnp.maximum(s[:, :128], s[:, 128:])
            peak = here if peak is None else jnp.maximum(peak, here)
        top = jnp.maximum(
            jnp.max(peak, axis=1, keepdims=True), jnp.max(s_new, axis=1, keepdims=True)
        )
        w_new = jnp.exp(s_new - top)
        mixed = mdot(w_new.astype(BF16), nv[0:nnew])
        for b in range(8):
            w = jnp.exp(sb[b] - top).astype(BF16)
            mixed = mixed + mdot(w, pool_v[256 * b : 256 * b + 256])
        head_out = (mixed[:, 0:128] / mixed[:, 128:256]).astype(BF16)
        for s in range(8):
            ho[k, x, core, zh, s // 4, :, (s % 4) * HD : (s % 4 + 1) * HD] = head_out[s * RB : (s + 1) * RB]
        p.hog.start()

    def out_rows(p):
        k, oy = p.k, p.oy
        p.hog.finish()
        lhs = [ho[k, :, :, :, f].reshape(16 * RB, 512) for f in range(2)]
        for n in range(2):
            res = mdot(lhs[0], wob[n, 0:512]) + mdot(lhs[1], wob[n, 512:1024])
            o[k, :, :, :, :, n * 256 : (n + 1) * 256] = res.astype(BF16).reshape(4, 2, 2, RB, 256)
        oy[0] = send(p.base + M_Y, o.at[k, yo, 0], orelay.at[k, 0], d_yr)
        oy[1] = send(p.base + M_Y + 1, o.at[k, yo, 1], orelay.at[k, 1], d_yl)

    def y_relay(p, side):
        k, oy = p.k, p.oy
        to, dev, into = ((yr, d_yr, oleft), (yl, d_yl, oright))[side]
        oy[side].wait_recv()
        o[k, to, side] = (o[k, to, side].astype(F32) + orelay[k, side].astype(F32)).astype(BF16)
        oy[2 + side] = send(p.base + M_Y + 2 + side, o.at[k, to], into.at[k], dev)

    def y_sum(p):
        k, oy = p.k, p.oy
        oy[2].wait_recv()
        oy[3].wait_recv()

        for i in range(2):
            ozs[k, i] = (
                o[k, y, i].astype(F32) + oleft[k, i].astype(F32) + oright[k, i].astype(F32)
            ).astype(BF16)
        p.oz = send(p.base + M_ZL, ozs.at[k], ozr.at[k], d_zl)

    def add_input(p):
        k = p.k
        p.oz.wait_recv()
        steps = pl.ds(k * TS, TS)
        for z in range(2):
            for i in range(2):
                full = ozs[k, i, z].astype(F32) + ozr[k, i, z].astype(F32)
                hidden = xb[steps, cidx(y, z, i)].astype(F32)
                ob[steps, 2 * y + z, pl.ds(16 * i, 16), :] = (
                    hidden + full.reshape(TS, 16, 512)
                ).astype(BF16)
        own = ob.at[steps, pl.ds(2 * y, 2)]
        p.fo = {
            1: send(p.base + M_FO, own, own, d_yr),
            2: send(p.base + M_FO + 1, own, own, d_yl),
        }

    def pass_on(p, k):
        steps = pl.ds(p.k * TS, TS)
        if k == 1:
            p.fo[1].wait_recv()
            part = ob.at[steps, 2 * yl]
            p.fo[5] = send(p.base + M_FO + 2, part, part, d_yr)
        elif k == 2:
            p.fo[2].wait_recv()
            part = ob.at[steps, 2 * yr + 1]
            p.fo[6] = send(p.base + M_FO + 3, part, part, d_yl)
        else:
            p.fo[5].wait_recv()
            p.fo[6].wait_recv()
            p.done = pltpu.make_async_copy(ob.at[steps], out.at[steps], lsem.at[15 + p.k])
            p.done.start()

    def load_weights():
        for k in range(3, 8):
            loads[k].wait()
        wkvf[...] = wkvb[...].astype(F32)
        wb[4, :, 0:128] = wkvf[pl.ds(0, 512, stride=2), :].astype(BF16)
        wb[4, :, 128:256] = wkvf[pl.ds(1, 512, stride=2), :].astype(BF16)

    def sum_squares():
        lax.fori_loop(0, 16, squares, 0, unroll=4)
        return [send(SQ0, sqs.at[1 - core], sqc, d_c)]

    def sum_squares_x(before):
        before[0].wait_recv()
        sqx[...] = sqs[core] + sqc[...]
        return [
            send(SQ0 + 1, sqx.at[xr], sqn.at[0], d_xr),
            send(SQ0 + 2, sqx.at[xl], sqn.at[1], d_xl),
            send(SQ0 + 3, sqx.at[xo], sqn.at[2], d_xo),
        ]

    def sum_squares_z(before):
        for m in before:
            m.wait_recv()
        sqz[...] = sqx[x] + sqn[0] + sqn[1] + sqn[2]
        return [send(SQ0 + 4, sqz.at[1 - zh], sqr, d_z)]

    def inverse_rms(before):
        before[0].wait_recv()
        flat = (sqz[zh] + sqr[...])[0:1, :]
        row_sq = jnp.sum(jnp.where(eye, flat, 0.0), axis=1, keepdims=True)
        return lax.rsqrt(row_sq / D + 1e-05)

    def choose_pages():
        loads[12].wait()
        loads[13].wait()
        pick = (
            lax.broadcasted_iota(jnp.int32, (16, 256), 1)
            == lax.broadcasted_iota(jnp.int32, (16, 256), 0) + 16 * c
        )
        own_pages = rdot(pick.astype(BF16), pages_ref[...].astype(BF16)).astype(jnp.int32)
        r_id = lax.broadcasted_iota(jnp.int32, (16, 256), 0)
        s_id = lax.broadcasted_iota(jnp.int32, (16, 256), 1)
        lens = jnp.zeros((16, 256), jnp.int32)
        for r in range(16):
            lens = jnp.where(r_id == r, clen_ref[c * 16 + r], lens)
        in_page = lax.rem(s_id, PAGE)
        page_id = lax.broadcasted_iota(jnp.int32, (16, 64), 1)
        named = jnp.zeros((16, 64), F32)
        for slot in range(8):
            named = jnp.where(own_pages[:, slot : slot + 1] == page_id, 1.0, named)
        present = jnp.broadcast_to(jnp.max(named, axis=0, keepdims=True), (16, 64))
        a_id = lax.broadcasted_iota(jnp.int32, (64, 64), 0)
        b_id = lax.broadcasted_iota(jnp.int32, (64, 64), 1)
        ahead = (a_id // 4 == b_id // 4) & (a_id < b_id)
        rank = mdot(present.astype(BF16), ahead.astype(BF16))
        code = jnp.where(present > 0.5, rank + 1.0, 0.0).astype(BF16)
        node_id = lax.broadcasted_iota(jnp.int32, (64, 256), 0)
        node_of = lax.broadcasted_iota(jnp.int32, (64, 256), 1) // PAGE
        to_id = lax.broadcasted_iota(jnp.int32, (128, 256), 0)
        from_id = lax.broadcasted_iota(jnp.int32, (128, 256), 1)
        same = lax.rem(to_id, PAGE) == lax.rem(from_id, PAGE)
        want = jnp.where(same, (to_id // PAGE + 1).astype(F32), -1.0)
        last = [
            (own_pages[:, slot : slot + 1], lens - slot * PAGE, s_id // PAGE)
            for slot in range(8)
        ]

        def choose(b):
            live = jnp.zeros((16, 256), F32)
            for named_page, upto, page in last:
                hit = (named_page - 4 * b == page) & (in_page < upto)
                live = jnp.where(hit, 1.0, live)
            spread = mdot(code, (node_id == node_of + 4 * b).astype(BF16))
            sel = jnp.where(spread[0:1] == want, 1.0, 0.0).astype(BF16)
            chosen[b] = sel
            return jnp.where(rdot(live.astype(BF16), sel) > 0.5, 0.0, NEG)

        def choose_two(i, carry):
            bias[i, :, 0:128] = choose(2 * i)
            bias[i, :, 128:256] = choose(2 * i + 1)
            return carry

        lax.fori_loop(0, 8, choose_two, 0, unroll=2)

    def take_pages():
        pool_v[:, 128:256] = jnp.ones((2048, 128), BF16)
        nv[:, 128:256] = jnp.ones((64, 128), BF16)

        def take(b, carry):
            rows = pl.ds(pl.multiple_of(128 * b, 128), 128)
            block = (b // 4, lax.rem(b, 2), lax.rem(b // 2, 2))
            pool_k[rows] = mdot(chosen[b], kv[block + (0,)].reshape(256, HD)).astype(BF16)
            pool_v[rows, 0:128] = mdot(chosen[b], kv[block + (1,)].reshape(256, HD)).astype(BF16)
            return carry

        lax.fori_loop(0, 16, take, 0, unroll=8)

    def list_pages():
        loads[11].wait()
        a_id = lax.broadcasted_iota(jnp.int32, (64, 64), 0)
        b_id = lax.broadcasted_iota(jnp.int32, (64, 64), 1)
        col_id = lax.broadcasted_iota(jnp.int32, (64, 128), 1)
        p_id = lax.broadcasted_iota(jnp.int32, (64, 128), 0)
        spot = (p_id // 16) * 16 + lax.rem(p_id // 4, 2) * 8 + lax.rem(p_id // 8, 2) * 4
        spot = (spot + lax.rem(p_id, 4)).astype(F32)
        rows = []
        for n in range(4):
            a = 4 * c + n
            line = mask_ref[pl.ds(a, 1), :].astype(F32)
            readable = jnp.sum(jnp.where(a_id == b_id, line, 0.0), axis=1, keepdims=True)
            readable = jnp.where((readable > 0.5) & (p_id < a), 1.0, 0.0)
            before = mdot((b_id < a_id).astype(BF16), readable.astype(BF16))
            place = jnp.where(p_id == a, 0.0, before + 1.0).astype(jnp.int32)
            hit = (place == col_id) & ((readable > 0.5) | (p_id == a))
            line = jnp.sum(jnp.where(hit, spot, 0.0), axis=0, keepdims=True)
            count = jnp.sum(readable, axis=0, keepdims=True) + 1.0
            rows.append(jnp.where(col_id[0:1] == 127, count, line))
        picks[...] = jnp.concatenate(rows + rows, axis=0).astype(jnp.int32)
        listed.start()

    def prefill_node(n):
        if n == 0:
            listed.wait()
            loads[14].wait()
        pages = []
        for i in range(8):
            spot = jnp.minimum(jnp.maximum(spots[n, i], 0), 63)
            pages.append(
                (spot // 16, lax.rem(spot // 8, 2), lax.rem(spot // 4, 2), lax.rem(spot, 4))
            )
        keys = jnp.concatenate([kv[a, b, d, 0, i] for a, b, d, i in pages], axis=0)
        values = jnp.concatenate([kv[a, b, d, 1, i] for a, b, d, i in pages], axis=0)
        mixed = first_pages(qb[n], keys, values, spots[n, 127])[1]
        write_heads(pb, n, mixed)
        prefilled[n].start()

    listed = pltpu.make_async_copy(picks, spots, lsem.at[16 + NCH])
    prefilled = [
        pltpu.make_async_copy(pb.at[n], pout.at[n], lsem.at[17 + NCH + n]) for n in range(4)
    ]

    keep = pltpu.make_async_copy(kv, kv_out, lsem.at[10])
    rms, squared = [], []
    late = [loads[8], loads[9]]

    def step(event):
        who, what = event.split(".")
        if who == "kv":
            if what == "fin":
                for k in range(8, 12):
                    kvm[k].wait_recv()
                keep.start()
            else:
                kv_pass(what)
            return
        if who == "all":
            if what[:2] == "sq":
                stage = {"sq": sum_squares, "sq1": sum_squares_x, "sq2": sum_squares_z}[what]
                squared[:] = stage(squared) if squared else stage()
            else:
                if what[:2] == "pf":
                    prefill_node(int(what[2]))
                else:
                    {"mask": choose_pages, "take": take_pages, "list": list_pages}[what]()
            return
        p = parts[int(who[1])]
        if what == "other":
            scale_rows(p, 1 - core)
            if p.k == 0:
                load_weights()
            other_rows(p)
        elif what == "own":
            scale_rows(p, core)
            own_rows(p)
        elif what[0] == "x":
            if what == "xsum":
                x_sum(p)
            else:
                x_relay(p, int(what[2]) // 2)
        elif what == "att":
            if not rms:
                rms.append(inverse_rms(squared))
            attend(p, rms[0])
        elif what[0] == "h":
            p.hog.take(what[1])
        elif what == "out":
            while late:
                late.pop().wait()
            out_rows(p)
        elif what == "ysum":
            drain(10)
            y_sum(p)
        elif what[0] == "y":
            y_relay(p, int(what[2]) // 2)
        elif what == "add":
            add_input(p)
        else:
            drain(6)
            pass_on(p, int(what[1]))

    for event in ORDER:
        step(event)
    keep.wait()
    for copy in prefilled:
        copy.wait()
    drain(0)
    for p in parts:
        p.done.wait()


def layer_call(*args):
    hbm = pl.BlockSpec(memory_space=pl.ANY)
    vmem = pl.BlockSpec(memory_space=pltpu.VMEM)
    return pl.pallas_call(
        layer_kernel,
        out_shape=(
            jax.ShapeDtypeStruct((4, 2, 2, 2, 4, PAGE, HD), BF16),
            jax.ShapeDtypeStruct((8, 128), jnp.int32),
            jax.ShapeDtypeStruct((4, PAGE, 1024), BF16),
            jax.ShapeDtypeStruct((4, 8, 32, 512), BF16),
        ),
        in_specs=[hbm] * 11,
        out_specs=(hbm, vmem, hbm, hbm),
        scratch_shapes=[
            pltpu.VMEM((4, PAGE, 1024), BF16),
            pltpu.SMEM((8, 128), jnp.int32),
            pltpu.VMEM((4, PAGE, 1024), BF16),
            pltpu.VMEM((4, 8, 32, 512), BF16),
            pltpu.VMEM((64, 64), jnp.int32),
            pltpu.VMEM((8, 256), jnp.int32),
            pltpu.SMEM((256,), jnp.int32),
            pltpu.VMEM((4, 128), BF16),
            pltpu.VMEM((4, 2, 2, 2, 4, PAGE, HD), BF16),
            pltpu.VMEM((4, 16, 16, 512), BF16),
            pltpu.VMEM((5, 512, 256), BF16),
            pltpu.VMEM((1024, 128), BF16),
            pltpu.VMEM((1024, 128), F32),
            pltpu.VMEM((2, 1024, 256), BF16),
            pltpu.VMEM((NCH, 2, 8, RB, 512), BF16),
            pltpu.VMEM((2, 4, 2, 8, 128), F32),
            pltpu.VMEM((4, 2, 8, 128), F32),
            pltpu.VMEM((4, 2, 8, 128), F32),
            pltpu.VMEM((3, 2, 8, 128), F32),
            pltpu.VMEM((2, 8, 128), F32),
            pltpu.VMEM((8, 128), F32),
            pltpu.VMEM((NCH, 10, 4, 2, RB, 128), BF16),
            pltpu.VMEM((NCH, 10, 4, 2, RB, 128), BF16),
            pltpu.VMEM((NCH, 4, 10, 2, RB, 128), BF16),
            pltpu.VMEM((NCH, 2, 5, 2, RB, 128), BF16),
            pltpu.VMEM((NCH, 10, 2, RB, 128), BF16),
            pltpu.VMEM((NCH, 10, 2, RB, 128), BF16),
            pltpu.VMEM((NCH, 10, RB, 128), BF16),
            pltpu.VMEM((NCH, 10, RB, 128), BF16),
            pltpu.VMEM((NCH, 10, RB, 128), F32),
            pltpu.VMEM((NCH, 10, RB, 128), BF16),
            pltpu.VMEM((64, 128), BF16),
            pltpu.VMEM((64, 256), BF16),
            pltpu.VMEM((8, 16, 256), F32),
            pltpu.VMEM((16, 128, 256), BF16),
            pltpu.VMEM((2048, HD), BF16),
            pltpu.VMEM((2048, 2 * HD), BF16),
            pltpu.VMEM((8, 8 * RB, 256), F32),
            pltpu.VMEM((NCH, 4, 2, 2, 2, RB, 512), BF16),
            pltpu.VMEM((NCH, 4, 2, 2, RB, 512), BF16),
            pltpu.VMEM((NCH, 2, 2, RB, 512), BF16),
            pltpu.VMEM((NCH, 2, 2, RB, 512), BF16),
            pltpu.VMEM((NCH, 2, 2, RB, 512), BF16),
            pltpu.VMEM((NCH, 2, 2, RB, 512), BF16),
            pltpu.VMEM((NCH, 2, 2, RB, 512), BF16),
            pltpu.SemaphoreType.DMA((21 + NCH,)),
            pltpu.SemaphoreType.DMA((NMSG,)),
            pltpu.SemaphoreType.DMA((NMSG,)),
        ],
        compiler_params=pltpu.CompilerParams(
            collective_id=0, has_side_effects=True, vmem_limit_bytes=56 * 1024 * 1024
        ),
        name="layer",
    )(*args)


def finish_kernel(
    q_hbm, kv_ref, picks, pre_ref, dec_ref, out_hbm, dec_out, q, kv, extra, stage, out, peak, mix, sem
):
    get_dec = [pltpu.make_async_copy(dec_ref.at[t], stage.at[t], sem.at[t]) for t in range(4)]
    put_dec = [pltpu.make_async_copy(stage.at[t], dec_out.at[t], sem.at[4 + t]) for t in range(4)]
    get_pre = pltpu.make_async_copy(pre_ref, out, sem.at[8])
    put_pre = pltpu.make_async_copy(out, out_hbm, sem.at[9])
    get_pre.start()
    for copy in get_dec:
        copy.start()

    def page(n, k):
        spot = picks[n, k]
        return kv_ref.at[spot // 4, :, lax.rem(spot, 4)]

    get_pre.wait()

    def deep(n, carry):
        @pl.when(picks[n, 127] > 8)
        def _():
            pltpu.make_async_copy(q_hbm.at[n], q, sem.at[10]).start()
            for k in range(8):
                pltpu.make_async_copy(page(n, k), kv.at[k], sem.at[11]).start()
            pltpu.make_async_copy(q, q, sem.at[10]).wait()
            pltpu.make_async_copy(kv, kv, sem.at[11]).wait()
            top, mixed = first_pages(
                q[...], kv[:, 0].reshape(512, HD), kv[:, 1].reshape(512, HD), picks[n, 127]
            )
            peak[...] = jnp.broadcast_to(top, (512, 128))
            mix[...] = mixed

            def more(t, inner):
                for k in range(4):
                    pltpu.make_async_copy(page(n, 8 + 4 * t + k), extra.at[k], sem.at[12]).start()
                pltpu.make_async_copy(extra, extra, sem.at[12]).wait()
                rows = jnp.concatenate([q[:, s * HD : (s + 1) * HD] for s in range(8)], axis=0)
                j_id = lax.broadcasted_iota(jnp.int32, (1, 4 * PAGE), 1)
                hidden = jnp.where(j_id < (picks[n, 127] - 8 - 4 * t) * PAGE, 0.0, NEG)
                s = rdot(rows, extra[:, 0].reshape(4 * PAGE, HD)) * SCALE + hidden
                before = peak[:, 0:1]
                top = jnp.maximum(jnp.max(s, axis=1, keepdims=True), before)
                values = jnp.concatenate(
                    [extra[:, 1].reshape(4 * PAGE, HD), jnp.ones((4 * PAGE, 128), BF16)], axis=1
                )
                mix[...] = mix[...] * jnp.exp(before - top) + mdot(
                    jnp.exp(s - top).astype(BF16), values
                )
                peak[...] = jnp.broadcast_to(top, (512, 128))
                return inner

            lax.fori_loop(0, (picks[n, 127] - 5) // 4, more, 0)
            write_heads(out, n, mix[...])

        return carry

    lax.fori_loop(0, 4, deep, 0)
    put_pre.start()
    for t in range(4):
        get_dec[t].wait()
        put_dec[t].start()
    put_pre.wait()
    for t in range(4):
        put_dec[t].wait()


def finish_call(q, kv, picks, pre, dec):
    hbm = pl.BlockSpec(memory_space=pl.ANY)
    smem = pl.BlockSpec(memory_space=pltpu.SMEM)
    return pl.pallas_call(
        finish_kernel,
        out_shape=(
            jax.ShapeDtypeStruct((4, PAGE, 1024), BF16),
            jax.ShapeDtypeStruct(dec.shape, BF16),
        ),
        in_specs=[hbm, hbm, smem, hbm, hbm],
        out_specs=(hbm, hbm),
        scratch_shapes=[
            pltpu.VMEM((PAGE, 1024), BF16),
            pltpu.VMEM((8, 2, PAGE, HD), BF16),
            pltpu.VMEM((4, 2, PAGE, HD), BF16),
            pltpu.VMEM(dec.shape, BF16),
            pltpu.VMEM((4, PAGE, 1024), BF16),
            pltpu.VMEM((512, 128), F32),
            pltpu.VMEM((512, 256), F32),
            pltpu.SemaphoreType.DMA((13,)),
        ],
        compiler_params=pltpu.CompilerParams(vmem_limit_bytes=62 * 1024 * 1024),
        name="finish",
    )(q, kv, picks, pre, dec)


def per_device(
    prefill_query, prefill_key, prefill_value, tree_mask, pages, cache_len,
    dec_in, norm_gain, w_query, w_keyval, w_out,
):
    query = prefill_query.reshape(4, PAGE, 1024)
    kv, picks, pre, dec = layer_call(
        query, prefill_key.reshape(4, PAGE, HD), prefill_value.reshape(4, PAGE, HD), tree_mask,
        pages.T, cache_len, dec_in.reshape(4, 16, 16, 512), norm_gain.reshape(4, 128), w_query,
        w_keyval.reshape(1024, 128), w_out,
    )
    prefill_out, dec_out = finish_call(
        query, kv.reshape(16, 2, 4, PAGE, HD), picks, pre, dec
    )
    return prefill_out.reshape(256, 1024), dec_out.reshape(4, 256, 512)


def solution(mesh):
    return jax.shard_map(
        per_device,
        mesh=mesh,
        in_specs=(
            P("ctx", "head"), P("ctx", "head"), P("ctx", "head"), P(), P(), P(),
            P(None, None, "ctx"), P("ctx"), P("ctx", "head"), P("ctx", None, "head"),
            P("head", "ctx"),
        ),
        out_specs=(P("ctx", "head"), P(None, None, "ctx")),
        check_vma=False,
    )
```

```python
import jax
import jax.numpy as jnp
from jax import lax
from jax.experimental import pallas as pl
from jax.experimental.pallas import tpu as pltpu
from jax.sharding import PartitionSpec as P

D = 8192
HD = 128
PAGE = 64
STEPS = 4
SCALE = HD ** (-0.5)
NEG = -1e30
F32 = jnp.float32
BF16 = jnp.bfloat16
MESH = pl.DeviceIdType.MESH

NCH = 4
TS = STEPS // NCH
RB = 16 * TS

KV0 = 0
SQ0 = 12
PART0 = 17
M_CORE, M_X, M_Z, M_HO, M_Y, M_ZL, M_FO = 0, 1, 5, 6, 15, 19, 20
PART_MSGS = 24
NMSG = PART0 + NCH * PART_MSGS


ORDER = (
    "p0.other", "p1.other", "p2.other", "p0.own", "all.pick", "kv.r", "kv.l", "kv.z", "p1.own",
    "all.sq", "p0.xr2", "p0.xr0", "p2.own", "p3.other", "kv.f", "p1.xr0", "p1.xr2", "all.sq1",
    "p3.own", "p2.xr0", "kv.s", "p2.xr2", "kv.m", "p0.xsum", "all.sq2", "kv.o", "all.mask",
    "p3.xr2", "p1.xsum", "kv.fin", "p3.xr0", "p2.xsum", "p0.att", "p1.att", "p3.xsum", "p2.att",
    "p0.hz", "p1.hz", "p3.att", "p0.hl", "p0.hr", "p2.hz", "p1.hl", "all.list", "p3.hz",
    "p0.hf", "p1.hr", "p2.hl", "p2.hr", "p0.out", "p3.hr", "p3.hl", "p1.hf", "all.pf0", "p2.hf",
    "p0.yr0", "p0.yr2", "p3.hf", "p1.out", "p3.out", "p2.out", "p1.yr2", "p1.yr0", "p0.ysum",
    "p3.yr2", "p3.yr0", "p2.yr0", "p2.yr2", "all.pf1", "p1.ysum", "all.pf2", "p3.ysum",
    "p0.add", "p2.ysum", "p1.add", "p3.add", "p2.add", "p0.f2", "all.pf3", "p0.f1", "p1.f1",
    "p1.f2", "p3.f1", "p3.f2", "p2.f1", "p2.f2", "p1.f5", "p0.f5", "p3.f5", "p2.f5",
)


def rdot(a, b):
    return lax.dot_general(a, b, (((1,), (1,)), ((), ())), preferred_element_type=F32)


def mdot(a, b):
    return lax.dot_general(a, b, (((1,), (0,)), ((), ())), preferred_element_type=F32)


def first_pages(q_node, keys, values, count):
    q = jnp.concatenate([q_node[:, s * HD : (s + 1) * HD] for s in range(8)], axis=0)
    values = jnp.concatenate([values, jnp.ones((8 * PAGE, 128), BF16)], axis=1)
    j_id = lax.broadcasted_iota(jnp.int32, (1, 8 * PAGE), 1)
    s = rdot(q, keys) * SCALE + jnp.where(j_id < count * PAGE, 0.0, NEG)
    i_id = lax.broadcasted_iota(jnp.int32, (512, 128), 0)
    j_id = lax.broadcasted_iota(jnp.int32, (512, 128), 1)
    seen = (j_id >= PAGE) | (j_id <= lax.rem(i_id, PAGE))
    s = jnp.concatenate([jnp.where(seen, s[:, :128], NEG), s[:, 128:]], axis=1)
    peak = jnp.max(s, axis=1, keepdims=True)
    return peak, mdot(jnp.exp(s - peak).astype(BF16), values)


def write_heads(out, n, mixed):
    result = (mixed[:, 0:128] / mixed[:, 128:256]).astype(BF16)
    for s in range(8):
        out[n, :, s * HD : (s + 1) * HD] = result[s * 64 : (s + 1) * 64]


def layer_kernel(
    q_hbm, key_ref, val_ref, mask_hbm, pages_hbm, clen_hbm, x_ref, gain_hbm, wq_ref, wkv_ref, wo_ref,
    kv_out, picks, pout, out,
    qb, spots, pb, ob, mask_ref, pages_ref, clen_ref, gain_ref,
    kv, xb, wb, wkvb, wkvf, wob, xs, sqs, sqc, sqx, sqn, sqz, sqr, gs, gr, g, prelay, pleft, pright, zs, zr, rf,
    pr, nk, nv, bias, two, two_s, sb, ho, o, orelay, oleft, oright, ozs, ozr,
    lsem, ssem, rsem,
):
    c = lax.axis_index("ctx")
    h = lax.axis_index("head")
    core = lax.rem(c, 2)
    zh = lax.rem(c // 2, 2)
    x = c // 4
    y = lax.rem(h, 4)
    zl = h // 4

    def cidx(xi, zi, ci):
        return xi * 4 + zi * 2 + ci

    def hidx(yi, zi):
        return zi * 4 + yi

    up, down = 1 + 2 * core, 3 - 2 * core
    xr, xl, xo = lax.rem(x + up, 4), lax.rem(x + down, 4), lax.rem(x + 2, 4)
    yr, yl, yo = lax.rem(y + up, 4), lax.rem(y + down, 4), lax.rem(y + 2, 4)
    d_xr = (cidx(xr, zh, core), h)
    d_xl = (cidx(xl, zh, core), h)
    d_z = (cidx(x, 1 - zh, core), h)
    d_c = (cidx(x, zh, 1 - core), h)
    d_yr = (c, hidx(yr, zl))
    d_yl = (c, hidx(yl, zl))
    d_zl = (c, hidx(y, 1 - zl))
    d_xo = (cidx(xo, zh, core), h)

    def msg(i, src, dst, dev):
        return pltpu.make_async_remote_copy(
            src_ref=src, dst_ref=dst, send_sem=ssem.at[i], recv_sem=rsem.at[i],
            device_id=dev, device_id_type=MESH,
        )

    barrier = pltpu.get_barrier_semaphore()

    for dev in (d_xr, d_xl, d_z, d_c, d_yr, d_yl, d_zl, d_xo):
        pl.semaphore_signal(barrier, inc=1, device_id=dev, device_id_type=MESH)

    loads = [
        pltpu.make_async_copy(key_ref, kv.at[x, core, zh, 0], lsem.at[0]),
        pltpu.make_async_copy(val_ref, kv.at[x, core, zh, 1], lsem.at[1]),
        pltpu.make_async_copy(x_ref, xb, lsem.at[2]),
        pltpu.make_async_copy(wkv_ref, wkvb, lsem.at[3]),
    ]
    for j in range(4):
        loads.append(
            pltpu.make_async_copy(wq_ref.at[:, pl.ds(256 * j, 256)], wb.at[j], lsem.at[4 + j])
        )
    for j in range(2):
        loads.append(
            pltpu.make_async_copy(wo_ref.at[:, pl.ds(256 * j, 256)], wob.at[j], lsem.at[8 + j])
        )
    for i, (src, dst) in enumerate(
        ((gain_hbm, gain_ref), (mask_hbm, mask_ref), (pages_hbm, pages_ref), (clen_hbm, clen_ref))
    ):
        loads.append(pltpu.make_async_copy(src, dst, lsem.at[11 + i]))
    loads.append(pltpu.make_async_copy(q_hbm, qb, lsem.at[15 + NCH]))
    for copy in loads:
        copy.start()

    pl.semaphore_wait(barrier, 8)

    sent = []

    def send(i, src, dst, dev):
        m = msg(i, src, dst, dev)
        m.start()
        sent.append(m)
        return m

    def drain(left):
        while len(sent) > left:
            sent.pop(0).wait_send()

    def pass_to(msgs, base, k, ref, dev):
        msgs[k] = send(base + k, ref, ref, dev)

    kvm = {}

    def kv_start():
        own = kv.at[x, core, zh]
        pass_to(kvm, KV0, 1, own, d_xr)
        pass_to(kvm, KV0, 2, own, d_xl)
        pass_to(kvm, KV0, 0, own, d_z)

    def kv_pass(what):
        if what == "l":
            kvm[1].wait_recv()
            pass_to(kvm, KV0, 3, kv.at[xl, core, zh, 0], d_xr)
            pass_to(kvm, KV0, 5, kv.at[xl, core, zh], d_z)
        elif what == "r":
            kvm[2].wait_recv()
            pass_to(kvm, KV0, 4, kv.at[xr, core, zh, 1], d_xl)
            pass_to(kvm, KV0, 6, kv.at[xr, core, zh], d_z)
        elif what == "f":
            kvm[3].wait_recv()
            kvm[4].wait_recv()
            pass_to(kvm, KV0, 7, kv.at[xo, core, zh], d_z)
        else:
            waited, given, place = {"z": (0, 8, x), "m": (5, 9, xl), "s": (6, 10, xr), "o": (7, 11, xo)}[
                what
            ]
            kvm[waited].wait_recv()
            pass_to(kvm, KV0, given, kv.at[place, core], d_c)

    class Gather:
        def __init__(self, base, pair):
            self.base, self.pair, self.m = base, pair, {}

        def put(self, k, ref, dev):
            pass_to(self.m, self.base, k, ref, dev)

        def start(self):
            self.put(0, self.pair(x).at[zh], d_z)

        def take(self, which):
            if which == "z":
                self.m[0].wait_recv()
                self.put(1, self.pair(x), d_xr)
                self.put(2, self.pair(x), d_xl)
                self.put(5, self.pair(x), d_c)
            elif which == "l":
                self.m[1].wait_recv()
                self.put(3, self.pair(xl).at[0], d_xr)
                self.put(6, self.pair(xl), d_c)
            elif which == "r":
                self.m[2].wait_recv()
                self.put(4, self.pair(xr).at[1], d_xl)
                self.put(7, self.pair(xr), d_c)
            else:
                self.m[3].wait_recv()
                self.m[4].wait_recv()
                self.put(8, self.pair(xo), d_c)

        def finish(self):
            for k in range(5, 9):
                self.m[k].wait_recv()

    loads[0].wait()
    loads[1].wait()
    kv_start()

    loads[2].wait()
    loads[10].wait()
    row_id = lax.broadcasted_iota(jnp.int32, (64, 128), 0)
    lane_id = lax.broadcasted_iota(jnp.int32, (64, 128), 1)
    eye = row_id == lane_id
    gain4 = gain_ref[...].astype(F32)
    gain = jnp.concatenate([gain4[i : i + 1] for i in range(4)], axis=1)

    def scale_rows(p, side):
        steps = pl.ds(p.k * TS, TS)

        def body(i, carry):
            raw = xb[steps, 2 * i + side].astype(F32).reshape(RB, 512)
            xs[p.k, side, i] = (raw * gain).astype(BF16)
            return carry

        lax.fori_loop(0, 8, body, 0, unroll=True)

    def squares(d, carry):
        raw = xb[:, d].astype(F32).reshape(64, 512)
        part = jnp.sum(raw * raw, axis=1, keepdims=True)
        flat = jnp.sum(jnp.where(eye, part, 0.0), axis=0, keepdims=True)
        sqs[lax.rem(d, 2), d // 4, lax.rem(d // 2, 2)] = jnp.broadcast_to(flat, (8, 128))
        return carry

    first = pl.ds(0, 5)
    second = pl.ds(5, 5)

    class Part:
        pass

    parts = []
    for k in range(NCH):
        p = Part()
        p.k = k
        p.base = PART0 + k * PART_MSGS
        p.px, p.oy = {}, {}
        p.hog = Gather(p.base + M_HO, lambda a, k=k: ho.at[k, a, core])
        parts.append(p)

    def other_rows(p):
        k = p.k

        rows = xs[k, 1 - core].reshape(8 * RB, 512)
        for j in range(5):
            res = mdot(rows, wb[j]).astype(BF16)
            gs[k, 2 * j] = res[:, :128].reshape(4, 2, RB, 128)
            gs[k, 2 * j + 1] = res[:, 128:].reshape(4, 2, RB, 128)
        p.core = send(p.base + M_CORE, gs.at[k], gr.at[k], d_c)

    def own_rows(p):
        k, px = p.k, p.px
        p.core.wait_recv()
        rows = xs[k, core].reshape(8 * RB, 512)

        def body(j):
            res = mdot(rows, wb[j])
            for i in range(2):
                both = res[:, 128 * i : 128 * i + 128].reshape(4, 2, RB, 128) + gr[
                    k, 2 * j + i
                ].astype(F32)
                g[k, :, 2 * j + i] = both.astype(BF16)

        for j in range(3):
            body(j)
        px[0] = send(p.base + M_X, g.at[k, xo, first], prelay.at[k, 0], d_xr)
        for j in range(3, 5):
            body(j)
        px[1] = send(p.base + M_X + 1, g.at[k, xo, second], prelay.at[k, 1], d_xl)

    def x_relay(p, side):
        k, px = p.k, p.px
        which, to, dev, into = ((first, xr, d_xr, pleft), (second, xl, d_xl, pright))[side]
        px[side].wait_recv()
        g[k, to, which] = (g[k, to, which].astype(F32) + prelay[k, side].astype(F32)).astype(BF16)
        px[2 + side] = send(p.base + M_X + 2 + side, g.at[k, to], into.at[k], dev)

    def x_sum(p):
        k, px = p.k, p.px
        px[2].wait_recv()
        px[3].wait_recv()

        def three(s, z):
            return (
                g[k, x, s, z].astype(F32)
                + pleft[k, s, z].astype(F32)
                + pright[k, s, z].astype(F32)
            )

        for s in range(10):
            zs[k, s] = three(s, 1 - zh).astype(BF16)
        p.zp = send(p.base + M_Z, zs.at[k], zr.at[k], d_z)

        for s in range(10):
            rf[k, s] = three(s, zh)

    def attend(p, inverse):
        k = p.k
        nrow = 8 * RB
        nnew = (k + 1) * RB
        inv = inverse[k * RB : (k + 1) * RB]
        p.zp.wait_recv()

        for s in range(10):
            pr[k, s] = ((rf[k, s] + zr[k, s].astype(F32)) * inv).astype(BF16)
        nk[k * RB : (k + 1) * RB] = pr[k, 8]
        nv[k * RB : (k + 1) * RB] = pr[k, 9]

        q = pr[k, 0:8].reshape(nrow, HD)
        i_id = lax.broadcasted_iota(jnp.int32, (nrow, nnew), 0)
        j_id = lax.broadcasted_iota(jnp.int32, (nrow, nnew), 1)
        seen = (lax.rem(i_id, 16) == lax.rem(j_id, 16)) & (
            j_id // 16 <= k * TS + lax.rem(i_id // 16, TS)
        )
        s_new = jnp.where(seen, rdot(q, nk[0:nnew]) * SCALE, NEG)
        peak = None
        for b in range(8):
            s = rdot(q, pool(b, 0)) * SCALE
            s = (s.reshape(nrow // 16, 16, 256) + bias[b][None]).reshape(nrow, 256)
            sb[b] = s
            here = jnp.maximum(s[:, :128], s[:, 128:])
            peak = here if peak is None else jnp.maximum(peak, here)
        top = jnp.maximum(
            jnp.max(peak, axis=1, keepdims=True), jnp.max(s_new, axis=1, keepdims=True)
        )
        w_new = jnp.exp(s_new - top)
        ones = jnp.ones((256, HD), BF16)
        mixed = mdot(
            w_new.astype(BF16), jnp.concatenate([nv[0:nnew], ones[0:nnew]], axis=1)
        )
        for b in range(8):
            w = jnp.exp(sb[b] - top).astype(BF16)
            mixed = mixed + mdot(w, jnp.concatenate([pool(b, 1), ones], axis=1))
        head_out = (mixed[:, 0:128] / mixed[:, 128:256]).astype(BF16)
        for s in range(8):
            ho[k, x, core, zh, s // 4, :, (s % 4) * HD : (s % 4 + 1) * HD] = head_out[s * RB : (s + 1) * RB]
        p.hog.start()

    def out_rows(p):
        k, oy = p.k, p.oy
        p.hog.finish()
        lhs = [ho[k, :, :, :, f].reshape(16 * RB, 512) for f in range(2)]
        for n in range(2):
            res = mdot(lhs[0], wob[n, 0:512]) + mdot(lhs[1], wob[n, 512:1024])
            o[k, :, :, :, :, n * 256 : (n + 1) * 256] = res.astype(BF16).reshape(4, 2, 2, RB, 256)
        oy[0] = send(p.base + M_Y, o.at[k, yo, 0], orelay.at[k, 0], d_yr)
        oy[1] = send(p.base + M_Y + 1, o.at[k, yo, 1], orelay.at[k, 1], d_yl)

    def y_relay(p, side):
        k, oy = p.k, p.oy
        to, dev, into = ((yr, d_yr, oleft), (yl, d_yl, oright))[side]
        oy[side].wait_recv()
        o[k, to, side] = (o[k, to, side].astype(F32) + orelay[k, side].astype(F32)).astype(BF16)
        oy[2 + side] = send(p.base + M_Y + 2 + side, o.at[k, to], into.at[k], dev)

    def y_sum(p):
        k, oy = p.k, p.oy
        oy[2].wait_recv()
        oy[3].wait_recv()

        for i in range(2):
            ozs[k, i] = (
                o[k, y, i].astype(F32) + oleft[k, i].astype(F32) + oright[k, i].astype(F32)
            ).astype(BF16)
        p.oz = send(p.base + M_ZL, ozs.at[k], ozr.at[k], d_zl)

    def add_input(p):
        k = p.k
        p.oz.wait_recv()
        steps = pl.ds(k * TS, TS)
        for z in range(2):
            for i in range(2):
                full = ozs[k, i, z].astype(F32) + ozr[k, i, z].astype(F32)
                hidden = xb[steps, cidx(y, z, i)].astype(F32)
                ob[steps, 2 * y + z, pl.ds(16 * i, 16), :] = (
                    hidden + full.reshape(TS, 16, 512)
                ).astype(BF16)
        own = ob.at[steps, pl.ds(2 * y, 2)]
        p.fo = {
            1: send(p.base + M_FO, own, own, d_yr),
            2: send(p.base + M_FO + 1, own, own, d_yl),
        }

    def pass_on(p, k):
        steps = pl.ds(p.k * TS, TS)
        if k == 1:
            p.fo[1].wait_recv()
            part = ob.at[steps, 2 * yl]
            p.fo[5] = send(p.base + M_FO + 2, part, part, d_yr)
        elif k == 2:
            p.fo[2].wait_recv()
            part = ob.at[steps, 2 * yr + 1]
            p.fo[6] = send(p.base + M_FO + 3, part, part, d_yl)
        else:
            p.fo[5].wait_recv()
            p.fo[6].wait_recv()
            p.done = pltpu.make_async_copy(ob.at[steps], out.at[steps], lsem.at[15 + p.k])
            p.done.start()

    def load_weights():
        for k in range(3, 8):
            loads[k].wait()
        wkvf[...] = wkvb[...].astype(F32)
        wb[4, :, 0:128] = wkvf[pl.ds(0, 512, stride=2), :].astype(BF16)
        wb[4, :, 128:256] = wkvf[pl.ds(1, 512, stride=2), :].astype(BF16)

    def sum_squares():
        lax.fori_loop(0, 16, squares, 0, unroll=4)
        return [send(SQ0, sqs.at[1 - core], sqc, d_c)]

    def sum_squares_x(before):
        before[0].wait_recv()
        sqx[...] = sqs[core] + sqc[...]
        return [
            send(SQ0 + 1, sqx.at[xr], sqn.at[0], d_xr),
            send(SQ0 + 2, sqx.at[xl], sqn.at[1], d_xl),
            send(SQ0 + 3, sqx.at[xo], sqn.at[2], d_xo),
        ]

    def sum_squares_z(before):
        for m in before:
            m.wait_recv()
        sqz[...] = sqx[x] + sqn[0] + sqn[1] + sqn[2]
        return [send(SQ0 + 4, sqz.at[1 - zh], sqr, d_z)]

    def inverse_rms(before):
        before[0].wait_recv()
        flat = (sqz[zh] + sqr[...])[0:1, :]
        row_sq = jnp.sum(jnp.where(eye, flat, 0.0), axis=1, keepdims=True)
        return lax.rsqrt(row_sq / D + 1e-05)

    def own_rows_pages():
        pick = (
            lax.broadcasted_iota(jnp.int32, (16, 256), 1)
            == lax.broadcasted_iota(jnp.int32, (16, 256), 0) + 16 * c
        )
        return rdot(pick.astype(BF16), pages_ref[...].astype(BF16))

    def pick_pages():
        loads[12].wait()
        loads[13].wait()
        own_pages = own_rows_pages()
        page_id = lax.broadcasted_iota(jnp.int32, (16, 64), 1)
        block_id = lax.broadcasted_iota(jnp.int32, (16, 64), 0)
        named = jnp.zeros((16, 64), F32)
        for slot in range(8):
            named = jnp.where(own_pages[:, slot : slot + 1] == page_id.astype(F32), 1.0, named)
        present = jnp.max(named, axis=0, keepdims=True) > 0.5
        here = present & (page_id // 4 == block_id)
        place = lax.rem(page_id, 4).astype(F32)
        low = jnp.min(jnp.where(here, place, 9.0), axis=1, keepdims=True)
        high = jnp.max(jnp.where(here, place, -1.0), axis=1, keepdims=True)
        column = lax.broadcasted_iota(jnp.int32, (16, 128), 1)
        two[...] = jnp.where(column == 0, low, high).astype(jnp.int32)
        paired.start()

    paired = pltpu.make_async_copy(two, two_s, lsem.at[21 + NCH])

    def chosen(b, i):
        return jnp.minimum(jnp.maximum(two_s[b, i], 0), 3)

    def mask_pages():
        paired.wait()
        own_pages = own_rows_pages().astype(jnp.int32)
        r_id = lax.broadcasted_iota(jnp.int32, (16, 128), 0)
        s_id = lax.broadcasted_iota(jnp.int32, (16, 128), 1)
        lens = jnp.zeros((16, 128), jnp.int32)
        for r in range(16):
            lens = jnp.where(r_id == r, clen_ref[c * 16 + r], lens)
        named = [jnp.broadcast_to(own_pages[:, slot : slot + 1], (16, 128)) for slot in range(8)]
        upto = [lens - slot * PAGE for slot in range(8)]
        in_page = lax.rem(s_id, PAGE)
        for b in range(16):
            page = 4 * b + jnp.where(s_id < PAGE, chosen(b, 0), chosen(b, 1))
            end = jnp.zeros((16, 128), jnp.int32)
            for slot in range(8):
                end = jnp.where(named[slot] == page, upto[slot], end)
            bias[b // 2, :, 128 * (b % 2) : 128 * (b % 2) + 128] = jnp.where(in_page < end, 0.0, NEG)

    def pool(t, f):
        pages = []
        for b in (2 * t, 2 * t + 1):
            for i in range(2):
                pages.append(kv[b // 4, b % 2, (b // 2) % 2, f, chosen(b, i)])
        return jnp.concatenate(pages, axis=0)

    def list_pages():
        loads[11].wait()
        a_id = lax.broadcasted_iota(jnp.int32, (64, 64), 0)
        b_id = lax.broadcasted_iota(jnp.int32, (64, 64), 1)
        col_id = lax.broadcasted_iota(jnp.int32, (64, 128), 1)
        p_id = lax.broadcasted_iota(jnp.int32, (64, 128), 0)
        spot = (p_id // 16) * 16 + lax.rem(p_id // 4, 2) * 8 + lax.rem(p_id // 8, 2) * 4
        spot = (spot + lax.rem(p_id, 4)).astype(F32)
        rows = []
        for n in range(4):
            a = 4 * c + n
            line = mask_ref[pl.ds(a, 1), :].astype(F32)
            readable = jnp.sum(jnp.where(a_id == b_id, line, 0.0), axis=1, keepdims=True)
            readable = jnp.where((readable > 0.5) & (p_id < a), 1.0, 0.0)
            before = mdot((b_id < a_id).astype(BF16), readable.astype(BF16))
            place = jnp.where(p_id == a, 0.0, before + 1.0).astype(jnp.int32)
            hit = (place == col_id) & ((readable > 0.5) | (p_id == a))
            line = jnp.sum(jnp.where(hit, spot, 0.0), axis=0, keepdims=True)
            count = jnp.sum(readable, axis=0, keepdims=True) + 1.0
            rows.append(jnp.where(col_id[0:1] == 127, count, line))
        picks[...] = jnp.concatenate(rows + rows, axis=0).astype(jnp.int32)
        listed.start()

    def prefill_node(n):
        if n == 0:
            listed.wait()
            loads[14].wait()
        pages = []
        for i in range(8):
            spot = jnp.minimum(jnp.maximum(spots[n, i], 0), 63)
            pages.append(
                (spot // 16, lax.rem(spot // 8, 2), lax.rem(spot // 4, 2), lax.rem(spot, 4))
            )
        keys = jnp.concatenate([kv[a, b, d, 0, i] for a, b, d, i in pages], axis=0)
        values = jnp.concatenate([kv[a, b, d, 1, i] for a, b, d, i in pages], axis=0)
        mixed = first_pages(qb[n], keys, values, spots[n, 127])[1]
        write_heads(pb, n, mixed)
        prefilled[n].start()

    listed = pltpu.make_async_copy(picks, spots, lsem.at[16 + NCH])
    prefilled = [
        pltpu.make_async_copy(pb.at[n], pout.at[n], lsem.at[17 + NCH + n]) for n in range(4)
    ]

    keep = pltpu.make_async_copy(kv, kv_out, lsem.at[10])
    rms, squared = [], []
    late = [loads[8], loads[9]]

    def step(event):
        who, what = event.split(".")
        if who == "kv":
            if what == "fin":
                for k in range(8, 12):
                    kvm[k].wait_recv()
                keep.start()
            else:
                kv_pass(what)
            return
        if who == "all":
            if what[:2] == "sq":
                stage = {"sq": sum_squares, "sq1": sum_squares_x, "sq2": sum_squares_z}[what]
                squared[:] = stage(squared) if squared else stage()
            else:
                if what[:2] == "pf":
                    prefill_node(int(what[2]))
                else:
                    {"pick": pick_pages, "mask": mask_pages, "list": list_pages}[what]()
            return
        p = parts[int(who[1])]
        if what == "other":
            scale_rows(p, 1 - core)
            if p.k == 0:
                load_weights()
            other_rows(p)
        elif what == "own":
            scale_rows(p, core)
            own_rows(p)
        elif what[0] == "x":
            if what == "xsum":
                x_sum(p)
            else:
                x_relay(p, int(what[2]) // 2)
        elif what == "att":
            if not rms:
                rms.append(inverse_rms(squared))
            attend(p, rms[0])
        elif what[0] == "h":
            p.hog.take(what[1])
        elif what == "out":
            while late:
                late.pop().wait()
            out_rows(p)
        elif what == "ysum":
            drain(10)
            y_sum(p)
        elif what[0] == "y":
            y_relay(p, int(what[2]) // 2)
        elif what == "add":
            add_input(p)
        else:
            drain(6)
            pass_on(p, int(what[1]))

    for event in ORDER:
        step(event)
    keep.wait()
    for copy in prefilled:
        copy.wait()
    drain(0)
    for p in parts:
        p.done.wait()


def layer_call(*args):
    hbm = pl.BlockSpec(memory_space=pl.ANY)
    vmem = pl.BlockSpec(memory_space=pltpu.VMEM)
    return pl.pallas_call(
        layer_kernel,
        out_shape=(
            jax.ShapeDtypeStruct((4, 2, 2, 2, 4, PAGE, HD), BF16),
            jax.ShapeDtypeStruct((8, 128), jnp.int32),
            jax.ShapeDtypeStruct((4, PAGE, 1024), BF16),
            jax.ShapeDtypeStruct((4, 8, 32, 512), BF16),
        ),
        in_specs=[hbm] * 11,
        out_specs=(hbm, vmem, hbm, hbm),
        scratch_shapes=[
            pltpu.VMEM((4, PAGE, 1024), BF16),
            pltpu.SMEM((8, 128), jnp.int32),
            pltpu.VMEM((4, PAGE, 1024), BF16),
            pltpu.VMEM((4, 8, 32, 512), BF16),
            pltpu.VMEM((64, 64), jnp.int32),
            pltpu.VMEM((8, 256), jnp.int32),
            pltpu.SMEM((256,), jnp.int32),
            pltpu.VMEM((4, 128), BF16),
            pltpu.VMEM((4, 2, 2, 2, 4, PAGE, HD), BF16),
            pltpu.VMEM((4, 16, 16, 512), BF16),
            pltpu.VMEM((5, 512, 256), BF16),
            pltpu.VMEM((1024, 128), BF16),
            pltpu.VMEM((1024, 128), F32),
            pltpu.VMEM((2, 1024, 256), BF16),
            pltpu.VMEM((NCH, 2, 8, RB, 512), BF16),
            pltpu.VMEM((2, 4, 2, 8, 128), F32),
            pltpu.VMEM((4, 2, 8, 128), F32),
            pltpu.VMEM((4, 2, 8, 128), F32),
            pltpu.VMEM((3, 2, 8, 128), F32),
            pltpu.VMEM((2, 8, 128), F32),
            pltpu.VMEM((8, 128), F32),
            pltpu.VMEM((NCH, 10, 4, 2, RB, 128), BF16),
            pltpu.VMEM((NCH, 10, 4, 2, RB, 128), BF16),
            pltpu.VMEM((NCH, 4, 10, 2, RB, 128), BF16),
            pltpu.VMEM((NCH, 2, 5, 2, RB, 128), BF16),
            pltpu.VMEM((NCH, 10, 2, RB, 128), BF16),
            pltpu.VMEM((NCH, 10, 2, RB, 128), BF16),
            pltpu.VMEM((NCH, 10, RB, 128), BF16),
            pltpu.VMEM((NCH, 10, RB, 128), BF16),
            pltpu.VMEM((NCH, 10, RB, 128), F32),
            pltpu.VMEM((NCH, 10, RB, 128), BF16),
            pltpu.VMEM((64, 128), BF16),
            pltpu.VMEM((64, 128), BF16),
            pltpu.VMEM((8, 16, 256), F32),
            pltpu.VMEM((16, 128), jnp.int32),
            pltpu.SMEM((16, 128), jnp.int32),
            pltpu.VMEM((8, 8 * RB, 256), F32),
            pltpu.VMEM((NCH, 4, 2, 2, 2, RB, 512), BF16),
            pltpu.VMEM((NCH, 4, 2, 2, RB, 512), BF16),
            pltpu.VMEM((NCH, 2, 2, RB, 512), BF16),
            pltpu.VMEM((NCH, 2, 2, RB, 512), BF16),
            pltpu.VMEM((NCH, 2, 2, RB, 512), BF16),
            pltpu.VMEM((NCH, 2, 2, RB, 512), BF16),
            pltpu.VMEM((NCH, 2, 2, RB, 512), BF16),
            pltpu.SemaphoreType.DMA((22 + NCH,)),
            pltpu.SemaphoreType.DMA((NMSG,)),
            pltpu.SemaphoreType.DMA((NMSG,)),
        ],
        compiler_params=pltpu.CompilerParams(
            collective_id=0, has_side_effects=True, vmem_limit_bytes=56 * 1024 * 1024
        ),
        name="layer",
    )(*args)


def finish_kernel(
    q_hbm, kv_ref, picks, pre_ref, dec_ref, out_hbm, dec_out, q, kv, extra, stage, out, peak, mix, sem
):
    get_dec = [pltpu.make_async_copy(dec_ref.at[t], stage.at[t], sem.at[t]) for t in range(4)]
    put_dec = [pltpu.make_async_copy(stage.at[t], dec_out.at[t], sem.at[4 + t]) for t in range(4)]
    get_pre = pltpu.make_async_copy(pre_ref, out, sem.at[8])
    put_pre = pltpu.make_async_copy(out, out_hbm, sem.at[9])
    get_pre.start()
    for copy in get_dec:
        copy.start()

    def page(n, k):
        spot = picks[n, k]
        return kv_ref.at[spot // 4, :, lax.rem(spot, 4)]

    get_pre.wait()

    def deep(n, carry):
        @pl.when(picks[n, 127] > 8)
        def _():
            pltpu.make_async_copy(q_hbm.at[n], q, sem.at[10]).start()
            for k in range(8):
                pltpu.make_async_copy(page(n, k), kv.at[k], sem.at[11]).start()
            pltpu.make_async_copy(q, q, sem.at[10]).wait()
            pltpu.make_async_copy(kv, kv, sem.at[11]).wait()
            top, mixed = first_pages(
                q[...], kv[:, 0].reshape(512, HD), kv[:, 1].reshape(512, HD), picks[n, 127]
            )
            peak[...] = jnp.broadcast_to(top, (512, 128))
            mix[...] = mixed

            def more(t, inner):
                for k in range(4):
                    pltpu.make_async_copy(page(n, 8 + 4 * t + k), extra.at[k], sem.at[12]).start()
                pltpu.make_async_copy(extra, extra, sem.at[12]).wait()
                rows = jnp.concatenate([q[:, s * HD : (s + 1) * HD] for s in range(8)], axis=0)
                j_id = lax.broadcasted_iota(jnp.int32, (1, 4 * PAGE), 1)
                hidden = jnp.where(j_id < (picks[n, 127] - 8 - 4 * t) * PAGE, 0.0, NEG)
                s = rdot(rows, extra[:, 0].reshape(4 * PAGE, HD)) * SCALE + hidden
                before = peak[:, 0:1]
                top = jnp.maximum(jnp.max(s, axis=1, keepdims=True), before)
                values = jnp.concatenate(
                    [extra[:, 1].reshape(4 * PAGE, HD), jnp.ones((4 * PAGE, 128), BF16)], axis=1
                )
                mix[...] = mix[...] * jnp.exp(before - top) + mdot(
                    jnp.exp(s - top).astype(BF16), values
                )
                peak[...] = jnp.broadcast_to(top, (512, 128))
                return inner

            lax.fori_loop(0, (picks[n, 127] - 5) // 4, more, 0)
            write_heads(out, n, mix[...])

        return carry

    lax.fori_loop(0, 4, deep, 0)
    put_pre.start()
    for t in range(4):
        get_dec[t].wait()
        put_dec[t].start()
    put_pre.wait()
    for t in range(4):
        put_dec[t].wait()


def finish_call(q, kv, picks, pre, dec):
    hbm = pl.BlockSpec(memory_space=pl.ANY)
    smem = pl.BlockSpec(memory_space=pltpu.SMEM)
    return pl.pallas_call(
        finish_kernel,
        out_shape=(
            jax.ShapeDtypeStruct((4, PAGE, 1024), BF16),
            jax.ShapeDtypeStruct(dec.shape, BF16),
        ),
        in_specs=[hbm, hbm, smem, hbm, hbm],
        out_specs=(hbm, hbm),
        scratch_shapes=[
            pltpu.VMEM((PAGE, 1024), BF16),
            pltpu.VMEM((8, 2, PAGE, HD), BF16),
            pltpu.VMEM((4, 2, PAGE, HD), BF16),
            pltpu.VMEM(dec.shape, BF16),
            pltpu.VMEM((4, PAGE, 1024), BF16),
            pltpu.VMEM((512, 128), F32),
            pltpu.VMEM((512, 256), F32),
            pltpu.SemaphoreType.DMA((13,)),
        ],
        compiler_params=pltpu.CompilerParams(vmem_limit_bytes=62 * 1024 * 1024),
        name="finish",
    )(q, kv, picks, pre, dec)


def per_device(
    prefill_query, prefill_key, prefill_value, tree_mask, pages, cache_len,
    dec_in, norm_gain, w_query, w_keyval, w_out,
):
    query = prefill_query.reshape(4, PAGE, 1024)
    kv, picks, pre, dec = layer_call(
        query, prefill_key.reshape(4, PAGE, HD), prefill_value.reshape(4, PAGE, HD), tree_mask,
        pages.T, cache_len, dec_in.reshape(4, 16, 16, 512), norm_gain.reshape(4, 128), w_query,
        w_keyval.reshape(1024, 128), w_out,
    )
    prefill_out, dec_out = finish_call(
        query, kv.reshape(16, 2, 4, PAGE, HD), picks, pre, dec
    )
    return prefill_out.reshape(256, 1024), dec_out.reshape(4, 256, 512)


def solution(mesh):
    return jax.shard_map(
        per_device,
        mesh=mesh,
        in_specs=(
            P("ctx", "head"), P("ctx", "head"), P("ctx", "head"), P(), P(), P(),
            P(None, None, "ctx"), P("ctx"), P("ctx", "head"), P("ctx", None, "head"),
            P("head", "ctx"),
        ),
        out_specs=(P("ctx", "head"), P(None, None, "ctx")),
        check_vma=False,
    )
```

```python
import jax
import jax.numpy as jnp
from jax import lax
from jax.experimental import pallas as pl
from jax.experimental.pallas import tpu as pltpu
from jax.sharding import PartitionSpec as P

D = 8192
HD = 128
PAGE = 64
STEPS = 4
SCALE = HD ** (-0.5)
NEG = -1e30
F32 = jnp.float32
BF16 = jnp.bfloat16
MESH = pl.DeviceIdType.MESH

NCH = 4
TS = STEPS // NCH
RB = 16 * TS
NEAR = 12

KV0 = 0
SQ0 = 12
PART0 = 17
M_CORE, M_X, M_Z, M_HO, M_Y, M_ZL, M_FO = 0, 1, 5, 6, 15, 19, 20
PART_MSGS = 24
NMSG = PART0 + NCH * PART_MSGS


ORDER = (
    "p0.other", "p1.other", "p2.other", "p0.own", "all.pick", "kv.r", "kv.l", "kv.z", "p1.own",
    "all.sq", "p0.xr2", "p0.xr0", "p2.own", "p3.other", "kv.f", "p1.xr0", "p1.xr2", "all.sq1",
    "p3.own", "p2.xr0", "kv.s", "p2.xr2", "kv.m", "p0.xsum", "all.sq2", "kv.o", "all.mask",
    "p3.xr2", "p1.xsum", "kv.fin", "p3.xr0", "p2.xsum", "p0.att", "p1.att", "p3.xsum", "p2.att",
    "p0.hz", "p1.hz", "p3.att", "p0.hl", "p0.hr", "p2.hz", "p1.hl", "all.list", "p3.hz",
    "p0.hf", "p1.hr", "p2.hl", "p2.hr", "p0.out", "p3.hr", "p3.hl", "p1.hf", "all.pf0", "p2.hf",
    "p0.yr0", "p0.yr2", "p3.hf", "p1.out", "p3.out", "p2.out", "p1.yr2", "p1.yr0", "p0.ysum",
    "p3.yr2", "p3.yr0", "p2.yr0", "p2.yr2", "all.pf1", "p1.ysum", "all.pf2", "p3.ysum",
    "p0.add", "p2.ysum", "p1.add", "p3.add", "p2.add", "p0.f2", "all.pf3", "p0.f1", "p1.f1",
    "p1.f2", "p3.f1", "p3.f2", "p2.f1", "p2.f2", "p1.f5", "p0.f5", "p3.f5", "p2.f5",
)


def rdot(a, b):
    return lax.dot_general(a, b, (((1,), (1,)), ((), ())), preferred_element_type=F32)


def mdot(a, b):
    return lax.dot_general(a, b, (((1,), (0,)), ((), ())), preferred_element_type=F32)


def first_pages(q_node, keys, values, count):
    q = jnp.concatenate([q_node[:, s * HD : (s + 1) * HD] for s in range(8)], axis=0)
    values = jnp.concatenate([values, jnp.ones((NEAR * PAGE, 128), BF16)], axis=1)
    j_id = lax.broadcasted_iota(jnp.int32, (1, NEAR * PAGE), 1)
    s = rdot(q, keys) * SCALE + jnp.where(j_id < count * PAGE, 0.0, NEG)
    i_id = lax.broadcasted_iota(jnp.int32, (512, 128), 0)
    j_id = lax.broadcasted_iota(jnp.int32, (512, 128), 1)
    seen = (j_id >= PAGE) | (j_id <= lax.rem(i_id, PAGE))
    s = jnp.concatenate([jnp.where(seen, s[:, :128], NEG), s[:, 128:]], axis=1)
    peak = jnp.max(s, axis=1, keepdims=True)
    return peak, mdot(jnp.exp(s - peak).astype(BF16), values)


def write_heads(out, n, mixed):
    result = (mixed[:, 0:128] / mixed[:, 128:256]).astype(BF16)
    for s in range(8):
        out[n, :, s * HD : (s + 1) * HD] = result[s * 64 : (s + 1) * 64]


def layer_kernel(
    q_hbm, key_ref, val_ref, mask_hbm, pages_hbm, clen_hbm, x_ref, gain_hbm, wq_ref, wkv_ref, wo_ref,
    kv_out, picks_out, pout, out,
    picks, qb, spots, pb, ob, mask_ref, pages_ref, clen_ref, gain_ref,
    kv, xb, wb, wkvb, wkvf, wob, xs, sqs, sqc, sqx, sqn, sqz, sqr, gs, gr, g, prelay, pleft, pright, zs, zr, rf,
    pr, nk, nv, bias, two, two_s, sb, ho, o, orelay, oleft, oright, ozs, ozr,
    lsem, ssem, rsem,
):
    c = lax.axis_index("ctx")
    h = lax.axis_index("head")
    core = lax.rem(c, 2)
    zh = lax.rem(c // 2, 2)
    x = c // 4
    y = lax.rem(h, 4)
    zl = h // 4

    def cidx(xi, zi, ci):
        return xi * 4 + zi * 2 + ci

    def hidx(yi, zi):
        return zi * 4 + yi

    up, down = 1 + 2 * core, 3 - 2 * core
    xr, xl, xo = lax.rem(x + up, 4), lax.rem(x + down, 4), lax.rem(x + 2, 4)
    yr, yl, yo = lax.rem(y + up, 4), lax.rem(y + down, 4), lax.rem(y + 2, 4)
    d_xr = (cidx(xr, zh, core), h)
    d_xl = (cidx(xl, zh, core), h)
    d_z = (cidx(x, 1 - zh, core), h)
    d_c = (cidx(x, zh, 1 - core), h)
    d_yr = (c, hidx(yr, zl))
    d_yl = (c, hidx(yl, zl))
    d_zl = (c, hidx(y, 1 - zl))
    d_xo = (cidx(xo, zh, core), h)

    def msg(i, src, dst, dev):
        return pltpu.make_async_remote_copy(
            src_ref=src, dst_ref=dst, send_sem=ssem.at[i], recv_sem=rsem.at[i],
            device_id=dev, device_id_type=MESH,
        )

    barrier = pltpu.get_barrier_semaphore()

    for dev in (d_xr, d_xl, d_z, d_c, d_yr, d_yl, d_zl, d_xo):
        pl.semaphore_signal(barrier, inc=1, device_id=dev, device_id_type=MESH)

    loads = [
        pltpu.make_async_copy(key_ref, kv.at[x, core, zh, 0], lsem.at[0]),
        pltpu.make_async_copy(val_ref, kv.at[x, core, zh, 1], lsem.at[1]),
        pltpu.make_async_copy(x_ref, xb, lsem.at[2]),
        pltpu.make_async_copy(wkv_ref, wkvb, lsem.at[3]),
    ]
    for j in range(4):
        loads.append(
            pltpu.make_async_copy(wq_ref.at[:, pl.ds(256 * j, 256)], wb.at[j], lsem.at[4 + j])
        )
    for j in range(2):
        loads.append(
            pltpu.make_async_copy(wo_ref.at[:, pl.ds(256 * j, 256)], wob.at[j], lsem.at[8 + j])
        )
    for i, (src, dst) in enumerate(
        ((gain_hbm, gain_ref), (mask_hbm, mask_ref), (pages_hbm, pages_ref), (clen_hbm, clen_ref))
    ):
        loads.append(pltpu.make_async_copy(src, dst, lsem.at[11 + i]))
    loads.append(pltpu.make_async_copy(q_hbm, qb, lsem.at[15 + NCH]))
    for copy in loads:
        copy.start()

    pl.semaphore_wait(barrier, 8)

    sent = []

    def send(i, src, dst, dev):
        m = msg(i, src, dst, dev)
        m.start()
        sent.append(m)
        return m

    def drain(left):
        while len(sent) > left:
            sent.pop(0).wait_send()

    def pass_to(msgs, base, k, ref, dev):
        msgs[k] = send(base + k, ref, ref, dev)

    kvm = {}

    def kv_start():
        own = kv.at[x, core, zh]
        pass_to(kvm, KV0, 1, own, d_xr)
        pass_to(kvm, KV0, 2, own, d_xl)
        pass_to(kvm, KV0, 0, own, d_z)

    def kv_pass(what):
        if what == "l":
            kvm[1].wait_recv()
            pass_to(kvm, KV0, 3, kv.at[xl, core, zh, 0], d_xr)
            pass_to(kvm, KV0, 5, kv.at[xl, core, zh], d_z)
        elif what == "r":
            kvm[2].wait_recv()
            pass_to(kvm, KV0, 4, kv.at[xr, core, zh, 1], d_xl)
            pass_to(kvm, KV0, 6, kv.at[xr, core, zh], d_z)
        elif what == "f":
            kvm[3].wait_recv()
            kvm[4].wait_recv()
            pass_to(kvm, KV0, 7, kv.at[xo, core, zh], d_z)
        else:
            waited, given, place = {"z": (0, 8, x), "m": (5, 9, xl), "s": (6, 10, xr), "o": (7, 11, xo)}[
                what
            ]
            kvm[waited].wait_recv()
            pass_to(kvm, KV0, given, kv.at[place, core], d_c)

    class Gather:
        def __init__(self, base, pair):
            self.base, self.pair, self.m = base, pair, {}

        def put(self, k, ref, dev):
            pass_to(self.m, self.base, k, ref, dev)

        def start(self):
            self.put(0, self.pair(x).at[zh], d_z)

        def take(self, which):
            if which == "z":
                self.m[0].wait_recv()
                self.put(1, self.pair(x), d_xr)
                self.put(2, self.pair(x), d_xl)
                self.put(5, self.pair(x), d_c)
            elif which == "l":
                self.m[1].wait_recv()
                self.put(3, self.pair(xl).at[0], d_xr)
                self.put(6, self.pair(xl), d_c)
            elif which == "r":
                self.m[2].wait_recv()
                self.put(4, self.pair(xr).at[1], d_xl)
                self.put(7, self.pair(xr), d_c)
            else:
                self.m[3].wait_recv()
                self.m[4].wait_recv()
                self.put(8, self.pair(xo), d_c)

        def finish(self):
            for k in range(5, 9):
                self.m[k].wait_recv()

    loads[0].wait()
    loads[1].wait()
    kv_start()

    loads[2].wait()
    loads[10].wait()
    row_id = lax.broadcasted_iota(jnp.int32, (64, 128), 0)
    lane_id = lax.broadcasted_iota(jnp.int32, (64, 128), 1)
    eye = row_id == lane_id
    gain4 = gain_ref[...].astype(F32)
    gain = jnp.concatenate([gain4[i : i + 1] for i in range(4)], axis=1)

    def scale_rows(p, side):
        steps = pl.ds(p.k * TS, TS)

        def body(i, carry):
            raw = xb[steps, 2 * i + side].astype(F32).reshape(RB, 512)
            xs[p.k, side, i] = (raw * gain).astype(BF16)
            return carry

        lax.fori_loop(0, 8, body, 0, unroll=True)

    def squares(d, carry):
        raw = xb[:, d].astype(F32).reshape(64, 512)
        part = jnp.sum(raw * raw, axis=1, keepdims=True)
        flat = jnp.sum(jnp.where(eye, part, 0.0), axis=0, keepdims=True)
        sqs[lax.rem(d, 2), d // 4, lax.rem(d // 2, 2)] = jnp.broadcast_to(flat, (8, 128))
        return carry

    first = pl.ds(0, 5)
    second = pl.ds(5, 5)

    class Part:
        pass

    parts = []
    for k in range(NCH):
        p = Part()
        p.k = k
        p.base = PART0 + k * PART_MSGS
        p.px, p.oy = {}, {}
        p.hog = Gather(p.base + M_HO, lambda a, k=k: ho.at[k, a, core])
        parts.append(p)

    def other_rows(p):
        k = p.k

        rows = xs[k, 1 - core].reshape(8 * RB, 512)
        for j in range(5):
            res = mdot(rows, wb[j]).astype(BF16)
            gs[k, 2 * j] = res[:, :128].reshape(4, 2, RB, 128)
            gs[k, 2 * j + 1] = res[:, 128:].reshape(4, 2, RB, 128)
        p.core = send(p.base + M_CORE, gs.at[k], gr.at[k], d_c)

    def own_rows(p):
        k, px = p.k, p.px
        p.core.wait_recv()
        rows = xs[k, core].reshape(8 * RB, 512)

        def body(j):
            res = mdot(rows, wb[j])
            for i in range(2):
                both = res[:, 128 * i : 128 * i + 128].reshape(4, 2, RB, 128) + gr[
                    k, 2 * j + i
                ].astype(F32)
                g[k, :, 2 * j + i] = both.astype(BF16)

        for j in range(3):
            body(j)
        px[0] = send(p.base + M_X, g.at[k, xo, first], prelay.at[k, 0], d_xr)
        for j in range(3, 5):
            body(j)
        px[1] = send(p.base + M_X + 1, g.at[k, xo, second], prelay.at[k, 1], d_xl)

    def x_relay(p, side):
        k, px = p.k, p.px
        which, to, dev, into = ((first, xr, d_xr, pleft), (second, xl, d_xl, pright))[side]
        px[side].wait_recv()
        g[k, to, which] = (g[k, to, which].astype(F32) + prelay[k, side].astype(F32)).astype(BF16)
        px[2 + side] = send(p.base + M_X + 2 + side, g.at[k, to], into.at[k], dev)

    def x_sum(p):
        k, px = p.k, p.px
        px[2].wait_recv()
        px[3].wait_recv()

        def three(s, z):
            return (
                g[k, x, s, z].astype(F32)
                + pleft[k, s, z].astype(F32)
                + pright[k, s, z].astype(F32)
            )

        for s in range(10):
            zs[k, s] = three(s, 1 - zh).astype(BF16)
        p.zp = send(p.base + M_Z, zs.at[k], zr.at[k], d_z)

        for s in range(10):
            rf[k, s] = three(s, zh)

    def attend(p, inverse):
        k = p.k
        nrow = 8 * RB
        nnew = (k + 1) * RB
        inv = inverse[k * RB : (k + 1) * RB]
        p.zp.wait_recv()

        for s in range(10):
            pr[k, s] = ((rf[k, s] + zr[k, s].astype(F32)) * inv).astype(BF16)
        nk[k * RB : (k + 1) * RB] = pr[k, 8]
        nv[k * RB : (k + 1) * RB] = pr[k, 9]

        q = pr[k, 0:8].reshape(nrow, HD)
        i_id = lax.broadcasted_iota(jnp.int32, (nrow, nnew), 0)
        j_id = lax.broadcasted_iota(jnp.int32, (nrow, nnew), 1)
        seen = (lax.rem(i_id, 16) == lax.rem(j_id, 16)) & (
            j_id // 16 <= k * TS + lax.rem(i_id // 16, TS)
        )
        s_new = jnp.where(seen, rdot(q, nk[0:nnew]) * SCALE, NEG)
        peak = None
        for b in range(8):
            s = rdot(q, pool(b, 0)) * SCALE
            s = (s.reshape(nrow // 16, 16, 256) + bias[b][None]).reshape(nrow, 256)
            sb[b] = s
            here = jnp.maximum(s[:, :128], s[:, 128:])
            peak = here if peak is None else jnp.maximum(peak, here)
        top = jnp.maximum(
            jnp.max(peak, axis=1, keepdims=True), jnp.max(s_new, axis=1, keepdims=True)
        )
        w_new = jnp.exp(s_new - top)
        mixed = mdot(w_new.astype(BF16), nv[0:nnew])
        part = None
        for b in range(8):
            w = jnp.exp(sb[b] - top)
            here = w[:, :128] + w[:, 128:]
            part = here if part is None else part + here
            mixed = mixed + mdot(w.astype(BF16), pool(b, 1))
        total = jnp.sum(part, axis=1, keepdims=True) + jnp.sum(w_new, axis=1, keepdims=True)
        head_out = (mixed / total).astype(BF16)
        for s in range(8):
            ho[k, x, core, zh, s // 4, :, (s % 4) * HD : (s % 4 + 1) * HD] = head_out[s * RB : (s + 1) * RB]
        p.hog.start()

    def out_rows(p):
        k, oy = p.k, p.oy
        p.hog.finish()
        lhs = [ho[k, :, :, :, f].reshape(16 * RB, 512) for f in range(2)]
        for n in range(2):
            res = mdot(lhs[0], wob[n, 0:512]) + mdot(lhs[1], wob[n, 512:1024])
            o[k, :, :, :, :, n * 256 : (n + 1) * 256] = res.astype(BF16).reshape(4, 2, 2, RB, 256)
        oy[0] = send(p.base + M_Y, o.at[k, yo, 0], orelay.at[k, 0], d_yr)
        oy[1] = send(p.base + M_Y + 1, o.at[k, yo, 1], orelay.at[k, 1], d_yl)

    def y_relay(p, side):
        k, oy = p.k, p.oy
        to, dev, into = ((yr, d_yr, oleft), (yl, d_yl, oright))[side]
        oy[side].wait_recv()
        o[k, to, side] = (o[k, to, side].astype(F32) + orelay[k, side].astype(F32)).astype(BF16)
        oy[2 + side] = send(p.base + M_Y + 2 + side, o.at[k, to], into.at[k], dev)

    def y_sum(p):
        k, oy = p.k, p.oy
        oy[2].wait_recv()
        oy[3].wait_recv()

        for i in range(2):
            ozs[k, i] = (
                o[k, y, i].astype(F32) + oleft[k, i].astype(F32) + oright[k, i].astype(F32)
            ).astype(BF16)
        p.oz = send(p.base + M_ZL, ozs.at[k], ozr.at[k], d_zl)

    def add_input(p):
        k = p.k
        p.oz.wait_recv()
        steps = pl.ds(k * TS, TS)
        for z in range(2):
            for i in range(2):
                full = ozs[k, i, z].astype(F32) + ozr[k, i, z].astype(F32)
                hidden = xb[steps, cidx(y, z, i)].astype(F32)
                ob[steps, 2 * y + z, pl.ds(16 * i, 16), :] = (
                    hidden + full.reshape(TS, 16, 512)
                ).astype(BF16)
        own = ob.at[steps, pl.ds(2 * y, 2)]
        p.fo = {
            1: send(p.base + M_FO, own, own, d_yr),
            2: send(p.base + M_FO + 1, own, own, d_yl),
        }

    def pass_on(p, k):
        steps = pl.ds(p.k * TS, TS)
        if k == 1:
            p.fo[1].wait_recv()
            part = ob.at[steps, 2 * yl]
            p.fo[5] = send(p.base + M_FO + 2, part, part, d_yr)
        elif k == 2:
            p.fo[2].wait_recv()
            part = ob.at[steps, 2 * yr + 1]
            p.fo[6] = send(p.base + M_FO + 3, part, part, d_yl)
        else:
            p.fo[5].wait_recv()
            p.fo[6].wait_recv()
            p.done = pltpu.make_async_copy(ob.at[steps], out.at[steps], lsem.at[15 + p.k])
            p.done.start()

    def load_weights():
        for k in range(3, 8):
            loads[k].wait()
        wkvf[...] = wkvb[...].astype(F32)
        wb[4, :, 0:128] = wkvf[pl.ds(0, 512, stride=2), :].astype(BF16)
        wb[4, :, 128:256] = wkvf[pl.ds(1, 512, stride=2), :].astype(BF16)

    def sum_squares():
        lax.fori_loop(0, 16, squares, 0, unroll=4)
        return [send(SQ0, sqs.at[1 - core], sqc, d_c)]

    def sum_squares_x(before):
        before[0].wait_recv()
        sqx[...] = sqs[core] + sqc[...]
        return [
            send(SQ0 + 1, sqx.at[xr], sqn.at[0], d_xr),
            send(SQ0 + 2, sqx.at[xl], sqn.at[1], d_xl),
            send(SQ0 + 3, sqx.at[xo], sqn.at[2], d_xo),
        ]

    def sum_squares_z(before):
        for m in before:
            m.wait_recv()
        sqz[...] = sqx[x] + sqn[0] + sqn[1] + sqn[2]
        return [send(SQ0 + 4, sqz.at[1 - zh], sqr, d_z)]

    def inverse_rms(before):
        before[0].wait_recv()
        flat = (sqz[zh] + sqr[...])[0:1, :]
        row_sq = jnp.sum(jnp.where(eye, flat, 0.0), axis=1, keepdims=True)
        return lax.rsqrt(row_sq / D + 1e-05)

    def own_rows_pages():
        pick = (
            lax.broadcasted_iota(jnp.int32, (16, 256), 1)
            == lax.broadcasted_iota(jnp.int32, (16, 256), 0) + 16 * c
        )
        return rdot(pick.astype(BF16), pages_ref[...].astype(BF16))

    def pick_pages():
        loads[12].wait()
        loads[13].wait()
        own_pages = own_rows_pages()
        page_id = lax.broadcasted_iota(jnp.int32, (16, 64), 1)
        block_id = lax.broadcasted_iota(jnp.int32, (16, 64), 0)
        named = jnp.zeros((16, 64), F32)
        for slot in range(8):
            named = jnp.where(own_pages[:, slot : slot + 1] == page_id.astype(F32), 1.0, named)
        present = jnp.max(named, axis=0, keepdims=True) > 0.5
        here = present & (page_id // 4 == block_id)
        place = lax.rem(page_id, 4).astype(F32)
        low = jnp.min(jnp.where(here, place, 9.0), axis=1, keepdims=True)
        high = jnp.max(jnp.where(here, place, -1.0), axis=1, keepdims=True)
        column = lax.broadcasted_iota(jnp.int32, (16, 128), 1)
        two[...] = jnp.where(column == 0, low, high).astype(jnp.int32)
        paired.start()

    paired = pltpu.make_async_copy(two, two_s, lsem.at[21 + NCH])

    def chosen(b, i):
        return jnp.minimum(jnp.maximum(two_s[b, i], 0), 3)

    def mask_pages():
        paired.wait()
        own_pages = own_rows_pages().astype(jnp.int32)
        r_id = lax.broadcasted_iota(jnp.int32, (16, 128), 0)
        s_id = lax.broadcasted_iota(jnp.int32, (16, 128), 1)
        lens = jnp.zeros((16, 128), jnp.int32)
        for r in range(16):
            lens = jnp.where(r_id == r, clen_ref[c * 16 + r], lens)
        named = [jnp.broadcast_to(own_pages[:, slot : slot + 1], (16, 128)) for slot in range(8)]
        upto = [lens - slot * PAGE for slot in range(8)]
        in_page = lax.rem(s_id, PAGE)
        for b in range(16):
            page = 4 * b + jnp.where(s_id < PAGE, chosen(b, 0), chosen(b, 1))
            end = jnp.zeros((16, 128), jnp.int32)
            for slot in range(8):
                end = jnp.where(named[slot] == page, upto[slot], end)
            bias[b // 2, :, 128 * (b % 2) : 128 * (b % 2) + 128] = jnp.where(in_page < end, 0.0, NEG)

    def pool(t, f):
        pages = []
        for b in (2 * t, 2 * t + 1):
            for i in range(2):
                pages.append(kv[b // 4, b % 2, (b // 2) % 2, f, chosen(b, i)])
        return jnp.concatenate(pages, axis=0)

    def list_pages():
        loads[11].wait()
        a_id = lax.broadcasted_iota(jnp.int32, (64, 64), 0)
        b_id = lax.broadcasted_iota(jnp.int32, (64, 64), 1)
        col_id = lax.broadcasted_iota(jnp.int32, (64, 128), 1)
        p_id = lax.broadcasted_iota(jnp.int32, (64, 128), 0)
        spot = (p_id // 16) * 16 + lax.rem(p_id // 4, 2) * 8 + lax.rem(p_id // 8, 2) * 4
        spot = (spot + lax.rem(p_id, 4)).astype(F32)
        rows = []
        for n in range(4):
            a = 4 * c + n
            line = mask_ref[pl.ds(a, 1), :].astype(F32)
            readable = jnp.sum(jnp.where(a_id == b_id, line, 0.0), axis=1, keepdims=True)
            readable = jnp.where((readable > 0.5) & (p_id < a), 1.0, 0.0)
            before = mdot((b_id < a_id).astype(BF16), readable.astype(BF16))
            place = jnp.where(p_id == a, 0.0, before + 1.0).astype(jnp.int32)
            hit = (place == col_id) & ((readable > 0.5) | (p_id == a))
            line = jnp.sum(jnp.where(hit, spot, 0.0), axis=0, keepdims=True)
            count = jnp.sum(readable, axis=0, keepdims=True) + 1.0
            rows.append(jnp.where(col_id[0:1] == 127, count, line))
        picks[...] = jnp.concatenate(rows + rows, axis=0).astype(jnp.int32)
        listed.start()
        told.start()

    def prefill_node(n):
        if n == 0:
            listed.wait()
            loads[14].wait()
        pages = []
        for i in range(NEAR):
            spot = jnp.minimum(jnp.maximum(spots[n, i], 0), 63)
            pages.append(
                (spot // 16, lax.rem(spot // 8, 2), lax.rem(spot // 4, 2), lax.rem(spot, 4))
            )
        keys = jnp.concatenate([kv[a, b, d, 0, i] for a, b, d, i in pages], axis=0)
        values = jnp.concatenate([kv[a, b, d, 1, i] for a, b, d, i in pages], axis=0)
        mixed = first_pages(qb[n], keys, values, spots[n, 127])[1]
        write_heads(pb, n, mixed)
        prefilled[n].start()

    listed = pltpu.make_async_copy(picks, spots, lsem.at[16 + NCH])
    told = pltpu.make_async_copy(picks, picks_out, lsem.at[22 + NCH])
    prefilled = [
        pltpu.make_async_copy(pb.at[n], pout.at[n], lsem.at[17 + NCH + n]) for n in range(4)
    ]

    keep = pltpu.make_async_copy(kv, kv_out, lsem.at[10])
    rms, squared = [], []
    late = [loads[8], loads[9]]

    def step(event):
        who, what = event.split(".")
        if who == "kv":
            if what == "fin":
                for k in range(8, 12):
                    kvm[k].wait_recv()
                keep.start()
            else:
                kv_pass(what)
            return
        if who == "all":
            if what[:2] == "sq":
                stage = {"sq": sum_squares, "sq1": sum_squares_x, "sq2": sum_squares_z}[what]
                squared[:] = stage(squared) if squared else stage()
            else:
                if what[:2] == "pf":
                    prefill_node(int(what[2]))
                else:
                    {"pick": pick_pages, "mask": mask_pages, "list": list_pages}[what]()
            return
        p = parts[int(who[1])]
        if what == "other":
            scale_rows(p, 1 - core)
            if p.k == 0:
                load_weights()
            other_rows(p)
        elif what == "own":
            scale_rows(p, core)
            own_rows(p)
        elif what[0] == "x":
            if what == "xsum":
                x_sum(p)
            else:
                x_relay(p, int(what[2]) // 2)
        elif what == "att":
            if not rms:
                rms.append(inverse_rms(squared))
            attend(p, rms[0])
        elif what[0] == "h":
            p.hog.take(what[1])
        elif what == "out":
            while late:
                late.pop().wait()
            out_rows(p)
        elif what == "ysum":
            drain(10)
            y_sum(p)
        elif what[0] == "y":
            y_relay(p, int(what[2]) // 2)
        elif what == "add":
            add_input(p)
        else:
            drain(6)
            pass_on(p, int(what[1]))

    for event in ORDER:
        step(event)
    keep.wait()
    told.wait()
    for copy in prefilled:
        copy.wait()
    drain(0)
    for p in parts:
        p.done.wait()


def layer_call(*args):
    hbm = pl.BlockSpec(memory_space=pl.ANY)
    return pl.pallas_call(
        layer_kernel,
        out_shape=(
            jax.ShapeDtypeStruct((4, 2, 2, 2, 4, PAGE, HD), BF16),
            jax.ShapeDtypeStruct((8, 128), jnp.int32),
            jax.ShapeDtypeStruct((4, PAGE, 1024), BF16),
            jax.ShapeDtypeStruct((4, 8, 32, 512), BF16),
        ),
        in_specs=[hbm] * 11,
        out_specs=(hbm, hbm, hbm, hbm),
        scratch_shapes=[
            pltpu.VMEM((8, 128), jnp.int32),
            pltpu.VMEM((4, PAGE, 1024), BF16),
            pltpu.SMEM((8, 128), jnp.int32),
            pltpu.VMEM((4, PAGE, 1024), BF16),
            pltpu.VMEM((4, 8, 32, 512), BF16),
            pltpu.VMEM((64, 64), jnp.int32),
            pltpu.VMEM((8, 256), jnp.int32),
            pltpu.SMEM((256,), jnp.int32),
            pltpu.VMEM((4, 128), BF16),
            pltpu.VMEM((4, 2, 2, 2, 4, PAGE, HD), BF16),
            pltpu.VMEM((4, 16, 16, 512), BF16),
            pltpu.VMEM((5, 512, 256), BF16),
            pltpu.VMEM((1024, 128), BF16),
            pltpu.VMEM((1024, 128), F32),
            pltpu.VMEM((2, 1024, 256), BF16),
            pltpu.VMEM((NCH, 2, 8, RB, 512), BF16),
            pltpu.VMEM((2, 4, 2, 8, 128), F32),
            pltpu.VMEM((4, 2, 8, 128), F32),
            pltpu.VMEM((4, 2, 8, 128), F32),
            pltpu.VMEM((3, 2, 8, 128), F32),
            pltpu.VMEM((2, 8, 128), F32),
            pltpu.VMEM((8, 128), F32),
            pltpu.VMEM((NCH, 10, 4, 2, RB, 128), BF16),
            pltpu.VMEM((NCH, 10, 4, 2, RB, 128), BF16),
            pltpu.VMEM((NCH, 4, 10, 2, RB, 128), BF16),
            pltpu.VMEM((NCH, 2, 5, 2, RB, 128), BF16),
            pltpu.VMEM((NCH, 10, 2, RB, 128), BF16),
            pltpu.VMEM((NCH, 10, 2, RB, 128), BF16),
            pltpu.VMEM((NCH, 10, RB, 128), BF16),
            pltpu.VMEM((NCH, 10, RB, 128), BF16),
            pltpu.VMEM((NCH, 10, RB, 128), F32),
            pltpu.VMEM((NCH, 10, RB, 128), BF16),
            pltpu.VMEM((64, 128), BF16),
            pltpu.VMEM((64, 128), BF16),
            pltpu.VMEM((8, 16, 256), F32),
            pltpu.VMEM((16, 128), jnp.int32),
            pltpu.SMEM((16, 128), jnp.int32),
            pltpu.VMEM((8, 8 * RB, 256), F32),
            pltpu.VMEM((NCH, 4, 2, 2, 2, RB, 512), BF16),
            pltpu.VMEM((NCH, 4, 2, 2, RB, 512), BF16),
            pltpu.VMEM((NCH, 2, 2, RB, 512), BF16),
            pltpu.VMEM((NCH, 2, 2, RB, 512), BF16),
            pltpu.VMEM((NCH, 2, 2, RB, 512), BF16),
            pltpu.VMEM((NCH, 2, 2, RB, 512), BF16),
            pltpu.VMEM((NCH, 2, 2, RB, 512), BF16),
            pltpu.SemaphoreType.DMA((23 + NCH,)),
            pltpu.SemaphoreType.DMA((NMSG,)),
            pltpu.SemaphoreType.DMA((NMSG,)),
        ],
        compiler_params=pltpu.CompilerParams(
            collective_id=0, has_side_effects=True, vmem_limit_bytes=56 * 1024 * 1024
        ),
        name="layer",
    )(*args)


def finish_kernel(
    q_hbm, kv_ref, picks_hbm, pre_ref, dec_ref, out_hbm, dec_out,
    picks, q, kv, extra, stage, out, peak, mix, sem,
):
    get_dec = [pltpu.make_async_copy(dec_ref.at[t], stage.at[t], sem.at[t]) for t in range(4)]
    put_dec = [pltpu.make_async_copy(stage.at[t], dec_out.at[t], sem.at[4 + t]) for t in range(4)]
    get_pre = pltpu.make_async_copy(pre_ref, out, sem.at[8])
    put_pre = pltpu.make_async_copy(out, out_hbm, sem.at[9])
    get_picks = pltpu.make_async_copy(picks_hbm, picks, sem.at[13])
    get_picks.start()
    get_pre.start()
    for copy in get_dec:
        copy.start()

    def page(n, k):
        spot = picks[n, k]
        return kv_ref.at[spot // 4, :, lax.rem(spot, 4)]

    get_picks.wait()
    get_pre.wait()
    for t in range(4):
        get_dec[t].wait()
        put_dec[t].start()

    def deep(n, carry):
        @pl.when(picks[n, 127] > NEAR)
        def _():
            pltpu.make_async_copy(q_hbm.at[n], q, sem.at[10]).start()
            for k in range(NEAR):
                pltpu.make_async_copy(page(n, k), kv.at[k], sem.at[11]).start()
            pltpu.make_async_copy(q, q, sem.at[10]).wait()
            pltpu.make_async_copy(kv, kv, sem.at[11]).wait()
            top, mixed = first_pages(
                q[...],
                kv[:, 0].reshape(NEAR * PAGE, HD),
                kv[:, 1].reshape(NEAR * PAGE, HD),
                picks[n, 127],
            )
            peak[...] = jnp.broadcast_to(top, (512, 128))
            mix[...] = mixed

            def more(t, inner):
                for k in range(4):
                    pltpu.make_async_copy(
                        page(n, NEAR + 4 * t + k), extra.at[k], sem.at[12]
                    ).start()
                pltpu.make_async_copy(extra, extra, sem.at[12]).wait()
                rows = jnp.concatenate([q[:, s * HD : (s + 1) * HD] for s in range(8)], axis=0)
                j_id = lax.broadcasted_iota(jnp.int32, (1, 4 * PAGE), 1)
                hidden = jnp.where(j_id < (picks[n, 127] - NEAR - 4 * t) * PAGE, 0.0, NEG)
                s = rdot(rows, extra[:, 0].reshape(4 * PAGE, HD)) * SCALE + hidden
                before = peak[:, 0:1]
                top = jnp.maximum(jnp.max(s, axis=1, keepdims=True), before)
                values = jnp.concatenate(
                    [extra[:, 1].reshape(4 * PAGE, HD), jnp.ones((4 * PAGE, 128), BF16)], axis=1
                )
                mix[...] = mix[...] * jnp.exp(before - top) + mdot(
                    jnp.exp(s - top).astype(BF16), values
                )
                peak[...] = jnp.broadcast_to(top, (512, 128))
                return inner

            lax.fori_loop(0, (picks[n, 127] - NEAR + 3) // 4, more, 0)
            write_heads(out, n, mix[...])

        return carry

    lax.fori_loop(0, 4, deep, 0)
    put_pre.start()
    put_pre.wait()
    for t in range(4):
        put_dec[t].wait()


def finish_call(q, kv, picks, pre, dec):
    hbm = pl.BlockSpec(memory_space=pl.ANY)
    return pl.pallas_call(
        finish_kernel,
        out_shape=(
            jax.ShapeDtypeStruct((4, PAGE, 1024), BF16),
            jax.ShapeDtypeStruct(dec.shape, BF16),
        ),
        in_specs=[hbm] * 5,
        out_specs=(hbm, hbm),
        scratch_shapes=[
            pltpu.SMEM((8, 128), jnp.int32),
            pltpu.VMEM((PAGE, 1024), BF16),
            pltpu.VMEM((NEAR, 2, PAGE, HD), BF16),
            pltpu.VMEM((4, 2, PAGE, HD), BF16),
            pltpu.VMEM(dec.shape, BF16),
            pltpu.VMEM((4, PAGE, 1024), BF16),
            pltpu.VMEM((512, 128), F32),
            pltpu.VMEM((512, 256), F32),
            pltpu.SemaphoreType.DMA((14,)),
        ],
        compiler_params=pltpu.CompilerParams(vmem_limit_bytes=62 * 1024 * 1024),
        name="finish",
    )(q, kv, picks, pre, dec)


def per_device(
    prefill_query, prefill_key, prefill_value, tree_mask, pages, cache_len,
    dec_in, norm_gain, w_query, w_keyval, w_out,
):
    query = prefill_query.reshape(4, PAGE, 1024)
    kv, picks, pre, dec = layer_call(
        query, prefill_key.reshape(4, PAGE, HD), prefill_value.reshape(4, PAGE, HD), tree_mask,
        pages.T, cache_len, dec_in.reshape(4, 16, 16, 512), norm_gain.reshape(4, 128), w_query,
        w_keyval.reshape(1024, 128), w_out,
    )
    prefill_out, dec_out = finish_call(
        query, kv.reshape(16, 2, 4, PAGE, HD), picks, pre, dec
    )
    return prefill_out.reshape(256, 1024), dec_out.reshape(4, 256, 512)


def solution(mesh):
    return jax.shard_map(
        per_device,
        mesh=mesh,
        in_specs=(
            P("ctx", "head"), P("ctx", "head"), P("ctx", "head"), P(), P(), P(),
            P(None, None, "ctx"), P("ctx"), P("ctx", "head"), P("ctx", None, "head"),
            P("head", "ctx"),
        ),
        out_specs=(P("ctx", "head"), P(None, None, "ctx")),
        check_vma=False,
    )
```

```python
import jax
import jax.numpy as jnp
from jax import lax
from jax.experimental import pallas as pl
from jax.experimental.pallas import tpu as pltpu
from jax.sharding import PartitionSpec as P

D = 8192
HD = 128
PAGE = 64
STEPS = 4
SCALE = HD ** (-0.5)
NEG = -1e30
F32 = jnp.float32
BF16 = jnp.bfloat16
MESH = pl.DeviceIdType.MESH

NCH = 4
TS = STEPS // NCH
RB = 16 * TS
NEAR = 12

KV0 = 0
SQ0 = 12
PART0 = 17
M_CORE, M_X, M_Z, M_HO, M_Y, M_ZL, M_FO = 0, 1, 5, 6, 15, 19, 20
PART_MSGS = 24
NMSG = PART0 + NCH * PART_MSGS


ORDER = (
    "p0.other", "p1.other", "p2.other", "all.sq", "kv.r", "p0.own", "all.pick", "p3.other",
    "kv.l", "p1.own", "p0.xr2", "p0.xr0", "all.sq1", "kv.f", "p2.own", "p3.own", "p1.xr0",
    "all.sq2", "p1.xr2", "p0.xsum", "kv.m", "all.mask", "p2.xr2", "kv.z", "p2.xr0", "kv.o",
    "p3.xr2", "kv.s", "p3.xr0", "p1.xsum", "all.list", "kv.fin", "p0.att", "p2.xsum", "p1.att",
    "p3.xsum", "p0.hz", "p2.att", "p1.hz", "p0.hl", "p0.hr", "p3.att", "p2.hz", "p1.hl",
    "p1.hr", "all.pf0", "p0.hf", "p3.hz", "p2.hr", "p2.hl", "p1.hf", "p0.out", "p1.out",
    "p2.hf", "p3.hl", "p3.hr", "p0.yr2", "p0.yr0", "p2.out", "p3.hf", "p1.yr0", "p1.yr2",
    "p3.out", "p0.ysum", "p2.yr0", "p2.yr2", "p1.ysum", "p3.yr0", "p3.yr2", "p0.add", "p2.ysum",
    "p1.add", "p3.ysum", "all.pf1", "p0.f2", "p2.add", "p3.add", "p0.f1", "p1.f2", "p1.f1",
    "all.pf2", "p2.f2", "p2.f1", "p3.f1", "p3.f2", "all.pf3", "p1.f5", "p0.f5", "p2.f5",
    "p3.f5",
)


def rdot(a, b):
    return lax.dot_general(a, b, (((1,), (1,)), ((), ())), preferred_element_type=F32)


def mdot(a, b):
    return lax.dot_general(a, b, (((1,), (0,)), ((), ())), preferred_element_type=F32)


def first_pages(q_node, keys, values, count):
    q = jnp.concatenate([q_node[:, s * HD : (s + 1) * HD] for s in range(8)], axis=0)
    values = jnp.concatenate([values, jnp.ones((NEAR * PAGE, 128), BF16)], axis=1)
    j_id = lax.broadcasted_iota(jnp.int32, (1, NEAR * PAGE), 1)
    s = rdot(q, keys) * SCALE + jnp.where(j_id < count * PAGE, 0.0, NEG)
    i_id = lax.broadcasted_iota(jnp.int32, (512, 128), 0)
    j_id = lax.broadcasted_iota(jnp.int32, (512, 128), 1)
    seen = (j_id >= PAGE) | (j_id <= lax.rem(i_id, PAGE))
    s = jnp.concatenate([jnp.where(seen, s[:, :128], NEG), s[:, 128:]], axis=1)
    peak = jnp.max(s, axis=1, keepdims=True)
    return peak, mdot(jnp.exp(s - peak).astype(BF16), values)


def write_heads(out, n, mixed):
    result = (mixed[:, 0:128] / mixed[:, 128:256]).astype(BF16)
    for s in range(8):
        out[n, :, s * HD : (s + 1) * HD] = result[s * 64 : (s + 1) * 64]


def layer_kernel(
    q_hbm, key_ref, val_ref, mask_hbm, pages_hbm, clen_hbm, x_ref, gain_hbm, wq_ref, wkv_ref, wo_ref,
    kv_out, picks_out, pout, out,
    picks, qb, spots, pb, ob, mask_ref, pages_ref, clen_ref, gain_ref,
    kv, xb, wb, wkvb, wkvf, wob, xs, sqs, sqc, sqx, sqn, sqz, sqr, gs, gr, g, prelay, pleft, pright, zs, zr, rf,
    pr, nk, nv, bias, two, two_s, sb, ho, o, orelay, oleft, oright, ozs, ozr,
    lsem, ssem, rsem,
):
    c = lax.axis_index("ctx")
    h = lax.axis_index("head")
    core = lax.rem(c, 2)
    zh = lax.rem(c // 2, 2)
    x = c // 4
    y = lax.rem(h, 4)
    zl = h // 4

    def cidx(xi, zi, ci):
        return xi * 4 + zi * 2 + ci

    def hidx(yi, zi):
        return zi * 4 + yi

    up, down = 1 + 2 * core, 3 - 2 * core
    xr, xl, xo = lax.rem(x + up, 4), lax.rem(x + down, 4), lax.rem(x + 2, 4)
    yr, yl, yo = lax.rem(y + up, 4), lax.rem(y + down, 4), lax.rem(y + 2, 4)
    d_xr = (cidx(xr, zh, core), h)
    d_xl = (cidx(xl, zh, core), h)
    d_z = (cidx(x, 1 - zh, core), h)
    d_c = (cidx(x, zh, 1 - core), h)
    d_yr = (c, hidx(yr, zl))
    d_yl = (c, hidx(yl, zl))
    d_zl = (c, hidx(y, 1 - zl))
    d_xo = (cidx(xo, zh, core), h)

    def msg(i, src, dst, dev):
        return pltpu.make_async_remote_copy(
            src_ref=src, dst_ref=dst, send_sem=ssem.at[i], recv_sem=rsem.at[i],
            device_id=dev, device_id_type=MESH,
        )

    barrier = pltpu.get_barrier_semaphore()

    for dev in (d_xr, d_xl, d_z, d_c, d_yr, d_yl, d_zl, d_xo):
        pl.semaphore_signal(barrier, inc=1, device_id=dev, device_id_type=MESH)

    loads = {}

    def load(name, src, dst):
        loads[name] = pltpu.make_async_copy(src, dst, lsem.at[len(loads)])
        loads[name].start()

    waited = set()

    def need(name):
        if name not in waited:
            waited.add(name)
            loads[name].wait()

    load("key", key_ref, kv.at[x, core, zh, 0])
    load("value", val_ref, kv.at[x, core, zh, 1])
    load("gain", gain_hbm, gain_ref)
    load("x0", x_ref.at[0], xb.at[0])
    load("wkv", wkv_ref, wkvb)
    for j in range(4):
        load(f"wq{j}", wq_ref.at[:, pl.ds(256 * j, 256)], wb.at[j])
    for t in range(1, 4):
        load(f"x{t}", x_ref.at[t], xb.at[t])

    def load_rest():
        load("pages", pages_hbm, pages_ref)
        load("lens", clen_hbm, clen_ref)
        load("mask", mask_hbm, mask_ref)
        for j in range(2):
            load(f"wo{j}", wo_ref.at[:, pl.ds(256 * j, 256)], wob.at[j])
        load("query", q_hbm, qb)

    pl.semaphore_wait(barrier, 8)

    sent = []

    def send(i, src, dst, dev):
        m = msg(i, src, dst, dev)
        m.start()
        sent.append(m)
        return m

    def drain(left):
        while len(sent) > left:
            sent.pop(0).wait_send()

    def pass_to(msgs, base, k, ref, dev):
        msgs[k] = send(base + k, ref, ref, dev)

    kvm = {}

    def kv_start():
        own = kv.at[x, core, zh]
        pass_to(kvm, KV0, 0, own, d_z)
        pass_to(kvm, KV0, 1, own, d_xr)
        pass_to(kvm, KV0, 2, own, d_xl)

    def kv_pass(what):
        if what == "l":
            kvm[1].wait_recv()
            pass_to(kvm, KV0, 3, kv.at[xl, core, zh, 0], d_xr)
            pass_to(kvm, KV0, 5, kv.at[xl, core, zh], d_z)
        elif what == "r":
            kvm[2].wait_recv()
            pass_to(kvm, KV0, 4, kv.at[xr, core, zh, 1], d_xl)
            pass_to(kvm, KV0, 6, kv.at[xr, core, zh], d_z)
        elif what == "f":
            kvm[3].wait_recv()
            kvm[4].wait_recv()
            pass_to(kvm, KV0, 7, kv.at[xo, core, zh], d_z)
        else:
            waited, given, place = {"z": (0, 8, x), "m": (5, 9, xl), "s": (6, 10, xr), "o": (7, 11, xo)}[
                what
            ]
            kvm[waited].wait_recv()
            pass_to(kvm, KV0, given, kv.at[place, core], d_c)

    class Gather:
        def __init__(self, base, pair):
            self.base, self.pair, self.m = base, pair, {}

        def put(self, k, ref, dev):
            pass_to(self.m, self.base, k, ref, dev)

        def start(self):
            self.put(0, self.pair(x).at[zh], d_z)

        def take(self, which):
            if which == "z":
                self.m[0].wait_recv()
                self.put(1, self.pair(x), d_xr)
                self.put(2, self.pair(x), d_xl)
                self.put(5, self.pair(x), d_c)
            elif which == "l":
                self.m[1].wait_recv()
                self.put(3, self.pair(xl).at[0], d_xr)
                self.put(6, self.pair(xl), d_c)
            elif which == "r":
                self.m[2].wait_recv()
                self.put(4, self.pair(xr).at[1], d_xl)
                self.put(7, self.pair(xr), d_c)
            else:
                self.m[3].wait_recv()
                self.m[4].wait_recv()
                self.put(8, self.pair(xo), d_c)

        def finish(self):
            for k in range(5, 9):
                self.m[k].wait_recv()

    need("key")
    need("value")
    kv_start()

    need("gain")
    row_id = lax.broadcasted_iota(jnp.int32, (64, 128), 0)
    lane_id = lax.broadcasted_iota(jnp.int32, (64, 128), 1)
    eye = row_id == lane_id
    gain4 = gain_ref[...].astype(F32)
    gain = jnp.concatenate([gain4[i : i + 1] for i in range(4)], axis=1)

    def scale_rows(p, side):
        steps = pl.ds(p.k * TS, TS)
        for t in range(p.k * TS, p.k * TS + TS):
            need(f"x{t}")

        def body(i, carry):
            raw = xb[steps, 2 * i + side].astype(F32).reshape(RB, 512)
            xs[p.k, side, i] = (raw * gain).astype(BF16)
            return carry

        lax.fori_loop(0, 8, body, 0, unroll=True)

    def squares(d, carry):
        raw = xb[:, d].astype(F32).reshape(64, 512)
        part = jnp.sum(raw * raw, axis=1, keepdims=True)
        flat = jnp.sum(jnp.where(eye, part, 0.0), axis=0, keepdims=True)
        sqs[lax.rem(d, 2), d // 4, lax.rem(d // 2, 2)] = jnp.broadcast_to(flat, (8, 128))
        return carry

    first = pl.ds(0, 5)
    second = pl.ds(5, 5)

    class Part:
        pass

    parts = []
    for k in range(NCH):
        p = Part()
        p.k = k
        p.base = PART0 + k * PART_MSGS
        p.px, p.oy = {}, {}
        p.hog = Gather(p.base + M_HO, lambda a, k=k: ho.at[k, a, core])
        parts.append(p)

    def other_rows(p):
        k = p.k

        rows = xs[k, 1 - core].reshape(8 * RB, 512)
        for j in range(5):
            res = mdot(rows, weights(j)).astype(BF16)
            gs[k, 2 * j] = res[:, :128].reshape(4, 2, RB, 128)
            gs[k, 2 * j + 1] = res[:, 128:].reshape(4, 2, RB, 128)
        p.core = send(p.base + M_CORE, gs.at[k], gr.at[k], d_c)

    def own_rows(p):
        k, px = p.k, p.px
        p.core.wait_recv()
        rows = xs[k, core].reshape(8 * RB, 512)

        def body(j):
            res = mdot(rows, wb[j])
            for i in range(2):
                both = res[:, 128 * i : 128 * i + 128].reshape(4, 2, RB, 128) + gr[
                    k, 2 * j + i
                ].astype(F32)
                g[k, :, 2 * j + i] = both.astype(BF16)

        for j in range(3):
            body(j)
        px[0] = send(p.base + M_X, g.at[k, xo, first], prelay.at[k, 0], d_xr)
        for j in range(3, 5):
            body(j)
        px[1] = send(p.base + M_X + 1, g.at[k, xo, second], prelay.at[k, 1], d_xl)

    def x_relay(p, side):
        k, px = p.k, p.px
        which, to, dev, into = ((first, xr, d_xr, pleft), (second, xl, d_xl, pright))[side]
        px[side].wait_recv()
        g[k, to, which] = (g[k, to, which].astype(F32) + prelay[k, side].astype(F32)).astype(BF16)
        px[2 + side] = send(p.base + M_X + 2 + side, g.at[k, to], into.at[k], dev)

    def x_sum(p):
        k, px = p.k, p.px
        px[2].wait_recv()
        px[3].wait_recv()

        def three(s, z):
            return (
                g[k, x, s, z].astype(F32)
                + pleft[k, s, z].astype(F32)
                + pright[k, s, z].astype(F32)
            )

        for s in range(10):
            zs[k, s] = three(s, 1 - zh).astype(BF16)
        p.zp = send(p.base + M_Z, zs.at[k], zr.at[k], d_z)

        for s in range(10):
            rf[k, s] = three(s, zh)

    def attend(p, inverse):
        k = p.k
        nrow = 8 * RB
        nnew = (k + 1) * RB
        inv = inverse[k * RB : (k + 1) * RB]
        p.zp.wait_recv()

        for s in range(10):
            pr[k, s] = ((rf[k, s] + zr[k, s].astype(F32)) * inv).astype(BF16)
        nk[k * RB : (k + 1) * RB] = pr[k, 8]
        nv[k * RB : (k + 1) * RB] = pr[k, 9]

        q = pr[k, 0:8].reshape(nrow, HD)
        i_id = lax.broadcasted_iota(jnp.int32, (nrow, nnew), 0)
        j_id = lax.broadcasted_iota(jnp.int32, (nrow, nnew), 1)
        seen = (lax.rem(i_id, 16) == lax.rem(j_id, 16)) & (
            j_id // 16 <= k * TS + lax.rem(i_id // 16, TS)
        )
        s_new = jnp.where(seen, rdot(q, nk[0:nnew]) * SCALE, NEG)
        peak = None
        for b in range(8):
            s = rdot(q, pool(b, 0)) * SCALE
            s = (s.reshape(nrow // 16, 16, 256) + bias[b][None]).reshape(nrow, 256)
            sb[b] = s
            here = jnp.maximum(s[:, :128], s[:, 128:])
            peak = here if peak is None else jnp.maximum(peak, here)
        top = jnp.maximum(
            jnp.max(peak, axis=1, keepdims=True), jnp.max(s_new, axis=1, keepdims=True)
        )
        w_new = jnp.exp(s_new - top)
        mixed = mdot(w_new.astype(BF16), nv[0:nnew])
        part = None
        for b in range(8):
            w = jnp.exp(sb[b] - top)
            here = w[:, :128] + w[:, 128:]
            part = here if part is None else part + here
            mixed = mixed + mdot(w.astype(BF16), pool(b, 1))
        total = jnp.sum(part, axis=1, keepdims=True) + jnp.sum(w_new, axis=1, keepdims=True)
        head_out = (mixed / total).astype(BF16)
        for s in range(8):
            ho[k, x, core, zh, s // 4, :, (s % 4) * HD : (s % 4 + 1) * HD] = head_out[s * RB : (s + 1) * RB]
        p.hog.start()

    def out_rows(p):
        k, oy = p.k, p.oy
        p.hog.finish()
        lhs = [ho[k, :, :, :, f].reshape(16 * RB, 512) for f in range(2)]
        for n in range(2):
            res = mdot(lhs[0], wob[n, 0:512]) + mdot(lhs[1], wob[n, 512:1024])
            o[k, :, :, :, :, n * 256 : (n + 1) * 256] = res.astype(BF16).reshape(4, 2, 2, RB, 256)
        oy[0] = send(p.base + M_Y, o.at[k, yo, 0], orelay.at[k, 0], d_yr)
        oy[1] = send(p.base + M_Y + 1, o.at[k, yo, 1], orelay.at[k, 1], d_yl)

    def y_relay(p, side):
        k, oy = p.k, p.oy
        to, dev, into = ((yr, d_yr, oleft), (yl, d_yl, oright))[side]
        oy[side].wait_recv()
        o[k, to, side] = (o[k, to, side].astype(F32) + orelay[k, side].astype(F32)).astype(BF16)
        oy[2 + side] = send(p.base + M_Y + 2 + side, o.at[k, to], into.at[k], dev)

    def y_sum(p):
        k, oy = p.k, p.oy
        oy[2].wait_recv()
        oy[3].wait_recv()

        for i in range(2):
            ozs[k, i] = (
                o[k, y, i].astype(F32) + oleft[k, i].astype(F32) + oright[k, i].astype(F32)
            ).astype(BF16)
        p.oz = send(p.base + M_ZL, ozs.at[k], ozr.at[k], d_zl)

    def add_input(p):
        k = p.k
        p.oz.wait_recv()
        steps = pl.ds(k * TS, TS)
        for z in range(2):
            for i in range(2):
                full = ozs[k, i, z].astype(F32) + ozr[k, i, z].astype(F32)
                hidden = xb[steps, cidx(y, z, i)].astype(F32)
                ob[steps, 2 * y + z, pl.ds(16 * i, 16), :] = (
                    hidden + full.reshape(TS, 16, 512)
                ).astype(BF16)
        own = ob.at[steps, pl.ds(2 * y, 2)]
        p.fo = {
            1: send(p.base + M_FO, own, own, d_yr),
            2: send(p.base + M_FO + 1, own, own, d_yl),
        }

    def pass_on(p, k):
        steps = pl.ds(p.k * TS, TS)
        if k == 1:
            p.fo[1].wait_recv()
            part = ob.at[steps, 2 * yl]
            p.fo[5] = send(p.base + M_FO + 2, part, part, d_yr)
        elif k == 2:
            p.fo[2].wait_recv()
            part = ob.at[steps, 2 * yr + 1]
            p.fo[6] = send(p.base + M_FO + 3, part, part, d_yl)
        else:
            p.fo[5].wait_recv()
            p.fo[6].wait_recv()
            p.done = pltpu.make_async_copy(ob.at[steps], out.at[steps], lsem.at[19 + p.k])
            p.done.start()

    def weights(j):
        if j < 4:
            need(f"wq{j}")
        elif "wkv" not in waited:
            need("wkv")
            wkvf[...] = wkvb[...].astype(F32)
            wb[4, :, 0:128] = wkvf[pl.ds(0, 512, stride=2), :].astype(BF16)
            wb[4, :, 128:256] = wkvf[pl.ds(1, 512, stride=2), :].astype(BF16)
        return wb[j]

    def sum_squares():
        for t in range(4):
            need(f"x{t}")
        lax.fori_loop(0, 16, squares, 0, unroll=4)
        return [send(SQ0, sqs.at[1 - core], sqc, d_c)]

    def sum_squares_x(before):
        before[0].wait_recv()
        sqx[...] = sqs[core] + sqc[...]
        return [
            send(SQ0 + 1, sqx.at[xr], sqn.at[0], d_xr),
            send(SQ0 + 2, sqx.at[xl], sqn.at[1], d_xl),
            send(SQ0 + 3, sqx.at[xo], sqn.at[2], d_xo),
        ]

    def sum_squares_z(before):
        for m in before:
            m.wait_recv()
        sqz[...] = sqx[x] + sqn[0] + sqn[1] + sqn[2]
        return [send(SQ0 + 4, sqz.at[1 - zh], sqr, d_z)]

    def inverse_rms(before):
        before[0].wait_recv()
        flat = (sqz[zh] + sqr[...])[0:1, :]
        row_sq = jnp.sum(jnp.where(eye, flat, 0.0), axis=1, keepdims=True)
        return lax.rsqrt(row_sq / D + 1e-05)

    def own_rows_pages():
        pick = (
            lax.broadcasted_iota(jnp.int32, (16, 256), 1)
            == lax.broadcasted_iota(jnp.int32, (16, 256), 0) + 16 * c
        )
        return rdot(pick.astype(BF16), pages_ref[...].astype(BF16))

    def pick_pages():
        need("pages")
        need("lens")
        own_pages = own_rows_pages()
        page_id = lax.broadcasted_iota(jnp.int32, (16, 64), 1)
        block_id = lax.broadcasted_iota(jnp.int32, (16, 64), 0)
        named = jnp.zeros((16, 64), F32)
        for slot in range(8):
            named = jnp.where(own_pages[:, slot : slot + 1] == page_id.astype(F32), 1.0, named)
        present = jnp.max(named, axis=0, keepdims=True) > 0.5
        here = present & (page_id // 4 == block_id)
        place = lax.rem(page_id, 4).astype(F32)
        low = jnp.min(jnp.where(here, place, 9.0), axis=1, keepdims=True)
        high = jnp.max(jnp.where(here, place, -1.0), axis=1, keepdims=True)
        column = lax.broadcasted_iota(jnp.int32, (16, 128), 1)
        two[...] = jnp.where(column == 0, low, high).astype(jnp.int32)
        paired.start()

    paired = pltpu.make_async_copy(two, two_s, lsem.at[24 + NCH])

    def chosen(b, i):
        return jnp.minimum(jnp.maximum(two_s[b, i], 0), 3)

    def mask_pages():
        paired.wait()
        own_pages = own_rows_pages().astype(jnp.int32)
        r_id = lax.broadcasted_iota(jnp.int32, (16, 128), 0)
        s_id = lax.broadcasted_iota(jnp.int32, (16, 128), 1)
        lens = jnp.zeros((16, 128), jnp.int32)
        for r in range(16):
            lens = jnp.where(r_id == r, clen_ref[c * 16 + r], lens)
        named = [jnp.broadcast_to(own_pages[:, slot : slot + 1], (16, 128)) for slot in range(8)]
        upto = [lens - slot * PAGE for slot in range(8)]
        in_page = lax.rem(s_id, PAGE)
        for b in range(16):
            page = 4 * b + jnp.where(s_id < PAGE, chosen(b, 0), chosen(b, 1))
            end = jnp.zeros((16, 128), jnp.int32)
            for slot in range(8):
                end = jnp.where(named[slot] == page, upto[slot], end)
            bias[b // 2, :, 128 * (b % 2) : 128 * (b % 2) + 128] = jnp.where(in_page < end, 0.0, NEG)

    def pool(t, f):
        pages = []
        for b in (2 * t, 2 * t + 1):
            for i in range(2):
                pages.append(kv[b // 4, b % 2, (b // 2) % 2, f, chosen(b, i)])
        return jnp.concatenate(pages, axis=0)

    def list_pages():
        need("mask")
        a_id = lax.broadcasted_iota(jnp.int32, (64, 64), 0)
        b_id = lax.broadcasted_iota(jnp.int32, (64, 64), 1)
        col_id = lax.broadcasted_iota(jnp.int32, (64, 128), 1)
        p_id = lax.broadcasted_iota(jnp.int32, (64, 128), 0)
        spot = (p_id // 16) * 16 + lax.rem(p_id // 4, 2) * 8 + lax.rem(p_id // 8, 2) * 4
        spot = (spot + lax.rem(p_id, 4)).astype(F32)
        rows = []
        for n in range(4):
            a = 4 * c + n
            line = mask_ref[pl.ds(a, 1), :].astype(F32)
            readable = jnp.sum(jnp.where(a_id == b_id, line, 0.0), axis=1, keepdims=True)
            readable = jnp.where((readable > 0.5) & (p_id < a), 1.0, 0.0)
            before = mdot((b_id < a_id).astype(BF16), readable.astype(BF16))
            place = jnp.where(p_id == a, 0.0, before + 1.0).astype(jnp.int32)
            hit = (place == col_id) & ((readable > 0.5) | (p_id == a))
            line = jnp.sum(jnp.where(hit, spot, 0.0), axis=0, keepdims=True)
            count = jnp.sum(readable, axis=0, keepdims=True) + 1.0
            rows.append(jnp.where(col_id[0:1] == 127, count, line))
        picks[...] = jnp.concatenate(rows + rows, axis=0).astype(jnp.int32)
        listed.start()
        told.start()

    def prefill_node(n):
        if n == 0:
            listed.wait()
            need("query")
        pages = []
        for i in range(NEAR):
            spot = jnp.minimum(jnp.maximum(spots[n, i], 0), 63)
            pages.append(
                (spot // 16, lax.rem(spot // 8, 2), lax.rem(spot // 4, 2), lax.rem(spot, 4))
            )
        keys = jnp.concatenate([kv[a, b, d, 0, i] for a, b, d, i in pages], axis=0)
        values = jnp.concatenate([kv[a, b, d, 1, i] for a, b, d, i in pages], axis=0)
        mixed = first_pages(qb[n], keys, values, spots[n, 127])[1]
        write_heads(pb, n, mixed)
        prefilled[n].start()

    listed = pltpu.make_async_copy(picks, spots, lsem.at[19 + NCH])
    told = pltpu.make_async_copy(picks, picks_out, lsem.at[25 + NCH])
    prefilled = [
        pltpu.make_async_copy(pb.at[n], pout.at[n], lsem.at[20 + NCH + n]) for n in range(4)
    ]

    keep = pltpu.make_async_copy(kv, kv_out, lsem.at[18])
    rms, squared = [], []

    def step(event):
        who, what = event.split(".")
        if who == "kv":
            if what == "fin":
                for k in range(8, 12):
                    kvm[k].wait_recv()
                keep.start()
            else:
                kv_pass(what)
            return
        if who == "all":
            if what[:2] == "sq":
                stage = {"sq": sum_squares, "sq1": sum_squares_x, "sq2": sum_squares_z}[what]
                squared[:] = stage(squared) if squared else stage()
            else:
                if what[:2] == "pf":
                    prefill_node(int(what[2]))
                else:
                    {"pick": pick_pages, "mask": mask_pages, "list": list_pages}[what]()
            return
        p = parts[int(who[1])]
        if what == "other":
            scale_rows(p, 1 - core)
            other_rows(p)
            if p.k == 0:
                load_rest()
        elif what == "own":
            scale_rows(p, core)
            own_rows(p)
        elif what[0] == "x":
            if what == "xsum":
                x_sum(p)
            else:
                x_relay(p, int(what[2]) // 2)
        elif what == "att":
            if not rms:
                rms.append(inverse_rms(squared))
            attend(p, rms[0])
        elif what[0] == "h":
            p.hog.take(what[1])
        elif what == "out":
            need("wo0")
            need("wo1")
            out_rows(p)
        elif what == "ysum":
            drain(10)
            y_sum(p)
        elif what[0] == "y":
            y_relay(p, int(what[2]) // 2)
        elif what == "add":
            add_input(p)
        else:
            drain(6)
            pass_on(p, int(what[1]))

    for event in ORDER:
        step(event)
    keep.wait()
    told.wait()
    for copy in prefilled:
        copy.wait()
    drain(0)
    for p in parts:
        p.done.wait()


def layer_call(*args):
    hbm = pl.BlockSpec(memory_space=pl.ANY)
    return pl.pallas_call(
        layer_kernel,
        out_shape=(
            jax.ShapeDtypeStruct((4, 2, 2, 2, 4, PAGE, HD), BF16),
            jax.ShapeDtypeStruct((8, 128), jnp.int32),
            jax.ShapeDtypeStruct((4, PAGE, 1024), BF16),
            jax.ShapeDtypeStruct((4, 8, 32, 512), BF16),
        ),
        in_specs=[hbm] * 11,
        out_specs=(hbm, hbm, hbm, hbm),
        scratch_shapes=[
            pltpu.VMEM((8, 128), jnp.int32),
            pltpu.VMEM((4, PAGE, 1024), BF16),
            pltpu.SMEM((8, 128), jnp.int32),
            pltpu.VMEM((4, PAGE, 1024), BF16),
            pltpu.VMEM((4, 8, 32, 512), BF16),
            pltpu.VMEM((64, 64), jnp.int32),
            pltpu.VMEM((8, 256), jnp.int32),
            pltpu.SMEM((256,), jnp.int32),
            pltpu.VMEM((4, 128), BF16),
            pltpu.VMEM((4, 2, 2, 2, 4, PAGE, HD), BF16),
            pltpu.VMEM((4, 16, 16, 512), BF16),
            pltpu.VMEM((5, 512, 256), BF16),
            pltpu.VMEM((1024, 128), BF16),
            pltpu.VMEM((1024, 128), F32),
            pltpu.VMEM((2, 1024, 256), BF16),
            pltpu.VMEM((NCH, 2, 8, RB, 512), BF16),
            pltpu.VMEM((2, 4, 2, 8, 128), F32),
            pltpu.VMEM((4, 2, 8, 128), F32),
            pltpu.VMEM((4, 2, 8, 128), F32),
            pltpu.VMEM((3, 2, 8, 128), F32),
            pltpu.VMEM((2, 8, 128), F32),
            pltpu.VMEM((8, 128), F32),
            pltpu.VMEM((NCH, 10, 4, 2, RB, 128), BF16),
            pltpu.VMEM((NCH, 10, 4, 2, RB, 128), BF16),
            pltpu.VMEM((NCH, 4, 10, 2, RB, 128), BF16),
            pltpu.VMEM((NCH, 2, 5, 2, RB, 128), BF16),
            pltpu.VMEM((NCH, 10, 2, RB, 128), BF16),
            pltpu.VMEM((NCH, 10, 2, RB, 128), BF16),
            pltpu.VMEM((NCH, 10, RB, 128), BF16),
            pltpu.VMEM((NCH, 10, RB, 128), BF16),
            pltpu.VMEM((NCH, 10, RB, 128), F32),
            pltpu.VMEM((NCH, 10, RB, 128), BF16),
            pltpu.VMEM((64, 128), BF16),
            pltpu.VMEM((64, 128), BF16),
            pltpu.VMEM((8, 16, 256), F32),
            pltpu.VMEM((16, 128), jnp.int32),
            pltpu.SMEM((16, 128), jnp.int32),
            pltpu.VMEM((8, 8 * RB, 256), F32),
            pltpu.VMEM((NCH, 4, 2, 2, 2, RB, 512), BF16),
            pltpu.VMEM((NCH, 4, 2, 2, RB, 512), BF16),
            pltpu.VMEM((NCH, 2, 2, RB, 512), BF16),
            pltpu.VMEM((NCH, 2, 2, RB, 512), BF16),
            pltpu.VMEM((NCH, 2, 2, RB, 512), BF16),
            pltpu.VMEM((NCH, 2, 2, RB, 512), BF16),
            pltpu.VMEM((NCH, 2, 2, RB, 512), BF16),
            pltpu.SemaphoreType.DMA((26 + NCH,)),
            pltpu.SemaphoreType.DMA((NMSG,)),
            pltpu.SemaphoreType.DMA((NMSG,)),
        ],
        compiler_params=pltpu.CompilerParams(
            collective_id=0, has_side_effects=True, vmem_limit_bytes=56 * 1024 * 1024
        ),
        name="layer",
    )(*args)


def finish_kernel(
    q_hbm, kv_ref, picks_hbm, pre_ref, dec_ref, out_hbm, dec_out,
    picks, q, kv, extra, stage, out, peak, mix, sem,
):
    get_dec = [pltpu.make_async_copy(dec_ref.at[t], stage.at[t], sem.at[t]) for t in range(4)]
    put_dec = [pltpu.make_async_copy(stage.at[t], dec_out.at[t], sem.at[4 + t]) for t in range(4)]
    get_pre = pltpu.make_async_copy(pre_ref, out, sem.at[8])
    put_pre = pltpu.make_async_copy(out, out_hbm, sem.at[9])
    get_picks = pltpu.make_async_copy(picks_hbm, picks, sem.at[13])
    get_picks.start()
    get_pre.start()
    for copy in get_dec:
        copy.start()

    def page(n, k):
        spot = picks[n, k]
        return kv_ref.at[spot // 4, :, lax.rem(spot, 4)]

    get_picks.wait()
    get_pre.wait()
    for t in range(4):
        get_dec[t].wait()
        put_dec[t].start()

    def deep(n, carry):
        @pl.when(picks[n, 127] > NEAR)
        def _():
            pltpu.make_async_copy(q_hbm.at[n], q, sem.at[10]).start()
            for k in range(NEAR):
                pltpu.make_async_copy(page(n, k), kv.at[k], sem.at[11]).start()
            pltpu.make_async_copy(q, q, sem.at[10]).wait()
            pltpu.make_async_copy(kv, kv, sem.at[11]).wait()
            top, mixed = first_pages(
                q[...],
                kv[:, 0].reshape(NEAR * PAGE, HD),
                kv[:, 1].reshape(NEAR * PAGE, HD),
                picks[n, 127],
            )
            peak[...] = jnp.broadcast_to(top, (512, 128))
            mix[...] = mixed

            def more(t, inner):
                for k in range(4):
                    pltpu.make_async_copy(
                        page(n, NEAR + 4 * t + k), extra.at[k], sem.at[12]
                    ).start()
                pltpu.make_async_copy(extra, extra, sem.at[12]).wait()
                rows = jnp.concatenate([q[:, s * HD : (s + 1) * HD] for s in range(8)], axis=0)
                j_id = lax.broadcasted_iota(jnp.int32, (1, 4 * PAGE), 1)
                hidden = jnp.where(j_id < (picks[n, 127] - NEAR - 4 * t) * PAGE, 0.0, NEG)
                s = rdot(rows, extra[:, 0].reshape(4 * PAGE, HD)) * SCALE + hidden
                before = peak[:, 0:1]
                top = jnp.maximum(jnp.max(s, axis=1, keepdims=True), before)
                values = jnp.concatenate(
                    [extra[:, 1].reshape(4 * PAGE, HD), jnp.ones((4 * PAGE, 128), BF16)], axis=1
                )
                mix[...] = mix[...] * jnp.exp(before - top) + mdot(
                    jnp.exp(s - top).astype(BF16), values
                )
                peak[...] = jnp.broadcast_to(top, (512, 128))
                return inner

            lax.fori_loop(0, (picks[n, 127] - NEAR + 3) // 4, more, 0)
            write_heads(out, n, mix[...])

        return carry

    lax.fori_loop(0, 4, deep, 0)
    put_pre.start()
    put_pre.wait()
    for t in range(4):
        put_dec[t].wait()


def finish_call(q, kv, picks, pre, dec):
    hbm = pl.BlockSpec(memory_space=pl.ANY)
    return pl.pallas_call(
        finish_kernel,
        out_shape=(
            jax.ShapeDtypeStruct((4, PAGE, 1024), BF16),
            jax.ShapeDtypeStruct(dec.shape, BF16),
        ),
        in_specs=[hbm] * 5,
        out_specs=(hbm, hbm),
        scratch_shapes=[
            pltpu.SMEM((8, 128), jnp.int32),
            pltpu.VMEM((PAGE, 1024), BF16),
            pltpu.VMEM((NEAR, 2, PAGE, HD), BF16),
            pltpu.VMEM((4, 2, PAGE, HD), BF16),
            pltpu.VMEM(dec.shape, BF16),
            pltpu.VMEM((4, PAGE, 1024), BF16),
            pltpu.VMEM((512, 128), F32),
            pltpu.VMEM((512, 256), F32),
            pltpu.SemaphoreType.DMA((14,)),
        ],
        compiler_params=pltpu.CompilerParams(vmem_limit_bytes=62 * 1024 * 1024),
        name="finish",
    )(q, kv, picks, pre, dec)


def per_device(
    prefill_query, prefill_key, prefill_value, tree_mask, pages, cache_len,
    dec_in, norm_gain, w_query, w_keyval, w_out,
):
    query = prefill_query.reshape(4, PAGE, 1024)
    kv, picks, pre, dec = layer_call(
        query, prefill_key.reshape(4, PAGE, HD), prefill_value.reshape(4, PAGE, HD), tree_mask,
        pages.T, cache_len, dec_in.reshape(4, 16, 16, 512), norm_gain.reshape(4, 128), w_query,
        w_keyval.reshape(1024, 128), w_out,
    )
    prefill_out, dec_out = finish_call(
        query, kv.reshape(16, 2, 4, PAGE, HD), picks, pre, dec
    )
    return prefill_out.reshape(256, 1024), dec_out.reshape(4, 256, 512)


def solution(mesh):
    return jax.shard_map(
        per_device,
        mesh=mesh,
        in_specs=(
            P("ctx", "head"), P("ctx", "head"), P("ctx", "head"), P(), P(), P(),
            P(None, None, "ctx"), P("ctx"), P("ctx", "head"), P("ctx", None, "head"),
            P("head", "ctx"),
        ),
        out_specs=(P("ctx", "head"), P(None, None, "ctx")),
        check_vma=False,
    )
```

```python
import jax
import jax.numpy as jnp
from jax import lax
from jax.experimental import pallas as pl
from jax.experimental.pallas import tpu as pltpu
from jax.sharding import PartitionSpec as P

D = 8192
HD = 128
PAGE = 64
STEPS = 4
SCALE = HD ** (-0.5)
NEG = -1e30
F32 = jnp.float32
BF16 = jnp.bfloat16
MESH = pl.DeviceIdType.MESH

NCH = 4
TS = STEPS // NCH
RB = 16 * TS
NEAR = 12

KV0 = 0
SQ0 = 12
PART0 = 17
M_CORE, M_X, M_Z, M_HO, M_Y, M_ZL, M_FO = 0, 1, 5, 6, 15, 19, 20
PART_MSGS = 24
NMSG = PART0 + NCH * PART_MSGS


ORDER = (
    "p0.other", "p1.other", "p2.other", "p0.own", "all.pick", "kv.r", "kv.l", "kv.z", "p1.own",
    "all.sq", "p0.xr2", "p0.xr0", "p2.own", "p3.other", "kv.f", "p1.xr0", "p1.xr2", "all.sq1",
    "p3.own", "p2.xr0", "kv.s", "p2.xr2", "kv.m", "p0.xsum", "all.sq2", "kv.o", "all.mask",
    "p3.xr2", "p1.xsum", "kv.fin", "p3.xr0", "p2.xsum", "p0.att", "p1.att", "p3.xsum", "p2.att",
    "p0.hz", "p1.hz", "p3.att", "p0.hl", "p0.hr", "p2.hz", "p1.hl", "all.list", "p3.hz",
    "p0.hf", "p1.hr", "p2.hl", "p2.hr", "p0.out", "p3.hr", "p3.hl", "p1.hf", "all.pf0", "p2.hf",
    "p0.yr0", "p0.yr2", "p3.hf", "p1.out", "p3.out", "p2.out", "p1.yr2", "p1.yr0", "p0.ysum",
    "p3.yr2", "p3.yr0", "p2.yr0", "p2.yr2", "all.pf1", "p1.ysum", "all.pf2", "p3.ysum",
    "p0.add", "p2.ysum", "p1.add", "p3.add", "p2.add", "p0.f2", "all.pf3", "p0.f1", "p1.f1",
    "p1.f2", "p3.f1", "p3.f2", "p2.f1", "p2.f2", "p1.f5", "p0.f5", "p3.f5", "p2.f5",
)


def rdot(a, b):
    return lax.dot_general(a, b, (((1,), (1,)), ((), ())), preferred_element_type=F32)


def mdot(a, b):
    return lax.dot_general(a, b, (((1,), (0,)), ((), ())), preferred_element_type=F32)


def first_pages(q_node, keys, values, count):
    q = jnp.concatenate([q_node[:, s * HD : (s + 1) * HD] for s in range(8)], axis=0)
    values = jnp.concatenate([values, jnp.ones((NEAR * PAGE, 128), BF16)], axis=1)
    j_id = lax.broadcasted_iota(jnp.int32, (1, NEAR * PAGE), 1)
    s = rdot(q, keys) * SCALE + jnp.where(j_id < count * PAGE, 0.0, NEG)
    i_id = lax.broadcasted_iota(jnp.int32, (512, 128), 0)
    j_id = lax.broadcasted_iota(jnp.int32, (512, 128), 1)
    seen = (j_id >= PAGE) | (j_id <= lax.rem(i_id, PAGE))
    s = jnp.concatenate([jnp.where(seen, s[:, :128], NEG), s[:, 128:]], axis=1)
    peak = jnp.max(s, axis=1, keepdims=True)
    return peak, mdot(jnp.exp(s - peak).astype(BF16), values)


def write_heads(out, n, mixed):
    result = (mixed[:, 0:128] / mixed[:, 128:256]).astype(BF16)
    for s in range(8):
        out[n, :, s * HD : (s + 1) * HD] = result[s * 64 : (s + 1) * 64]


def layer_kernel(
    q_hbm, key_ref, val_ref, mask_hbm, pages_hbm, clen_hbm, x_ref, gain_hbm, wq_ref, wkv_ref, wo_ref,
    kv_out, picks_out, pout, out,
    picks, qb, spots, pb, ob, mask_ref, pages_ref, clen_ref, gain_ref,
    kv, xb, wb, wkvb, wkvf, wob, xs, sqs, sqc, sqx, sqn, sqz, sqr, gs, gr, g, prelay, pleft, pright, zs, zr, rf,
    pr, nk, nv, bias, two, two_s, sb, ho, o, orelay, oleft, oright, ozs, ozr,
    lsem, ssem, rsem,
):
    c = lax.axis_index("ctx")
    h = lax.axis_index("head")
    core = lax.rem(c, 2)
    zh = lax.rem(c // 2, 2)
    x = c // 4
    y = lax.rem(h, 4)
    zl = h // 4

    def cidx(xi, zi, ci):
        return xi * 4 + zi * 2 + ci

    def hidx(yi, zi):
        return zi * 4 + yi

    up, down = 1 + 2 * core, 3 - 2 * core
    xr, xl, xo = lax.rem(x + up, 4), lax.rem(x + down, 4), lax.rem(x + 2, 4)
    yr, yl, yo = lax.rem(y + up, 4), lax.rem(y + down, 4), lax.rem(y + 2, 4)
    d_xr = (cidx(xr, zh, core), h)
    d_xl = (cidx(xl, zh, core), h)
    d_z = (cidx(x, 1 - zh, core), h)
    d_c = (cidx(x, zh, 1 - core), h)
    d_yr = (c, hidx(yr, zl))
    d_yl = (c, hidx(yl, zl))
    d_zl = (c, hidx(y, 1 - zl))
    d_xo = (cidx(xo, zh, core), h)

    def msg(i, src, dst, dev):
        return pltpu.make_async_remote_copy(
            src_ref=src, dst_ref=dst, send_sem=ssem.at[i], recv_sem=rsem.at[i],
            device_id=dev, device_id_type=MESH,
        )

    barrier = pltpu.get_barrier_semaphore()

    for dev in (d_xr, d_xl, d_z, d_c, d_yr, d_yl, d_zl, d_xo):
        pl.semaphore_signal(barrier, inc=1, device_id=dev, device_id_type=MESH)

    loads = {}

    def load(name, src, dst):
        loads[name] = pltpu.make_async_copy(src, dst, lsem.at[len(loads)])
        loads[name].start()

    waited = set()

    def need(name):
        if name not in waited:
            waited.add(name)
            loads[name].wait()

    load("key", key_ref, kv.at[x, core, zh, 0])
    load("value", val_ref, kv.at[x, core, zh, 1])
    load("gain", gain_hbm, gain_ref)
    load("x0", x_ref.at[0], xb.at[0])
    load("wkv", wkv_ref, wkvb)
    for j in range(4):
        load(f"wq{j}", wq_ref.at[:, pl.ds(256 * j, 256)], wb.at[j])
    for t in range(1, 4):
        load(f"x{t}", x_ref.at[t], xb.at[t])

    def load_rest():
        load("pages", pages_hbm, pages_ref)
        load("lens", clen_hbm, clen_ref)
        load("mask", mask_hbm, mask_ref)
        for j in range(2):
            load(f"wo{j}", wo_ref.at[:, pl.ds(256 * j, 256)], wob.at[j])
        load("query", q_hbm, qb)

    pl.semaphore_wait(barrier, 8)

    sent = []

    def send(i, src, dst, dev):
        m = msg(i, src, dst, dev)
        m.start()
        sent.append(m)
        return m

    def drain(left):
        while len(sent) > left:
            sent.pop(0).wait_send()

    def pass_to(msgs, base, k, ref, dev):
        msgs[k] = send(base + k, ref, ref, dev)

    kvm = {}

    def kv_start():
        own = kv.at[x, core, zh]
        pass_to(kvm, KV0, 0, own, d_z)
        pass_to(kvm, KV0, 1, own, d_xr)
        pass_to(kvm, KV0, 2, own, d_xl)

    def kv_pass(what):
        if what == "l":
            kvm[1].wait_recv()
            pass_to(kvm, KV0, 3, kv.at[xl, core, zh, 0], d_xr)
            pass_to(kvm, KV0, 5, kv.at[xl, core, zh], d_z)
        elif what == "r":
            kvm[2].wait_recv()
            pass_to(kvm, KV0, 4, kv.at[xr, core, zh, 1], d_xl)
            pass_to(kvm, KV0, 6, kv.at[xr, core, zh], d_z)
        elif what == "f":
            kvm[3].wait_recv()
            kvm[4].wait_recv()
            pass_to(kvm, KV0, 7, kv.at[xo, core, zh], d_z)
        else:
            waited, given, place = {"z": (0, 8, x), "m": (5, 9, xl), "s": (6, 10, xr), "o": (7, 11, xo)}[
                what
            ]
            kvm[waited].wait_recv()
            pass_to(kvm, KV0, given, kv.at[place, core], d_c)

    class Gather:
        def __init__(self, base, pair):
            self.base, self.pair, self.m = base, pair, {}

        def put(self, k, ref, dev):
            pass_to(self.m, self.base, k, ref, dev)

        def start(self):
            self.put(0, self.pair(x).at[zh], d_z)

        def take(self, which):
            if which == "z":
                self.m[0].wait_recv()
                self.put(1, self.pair(x), d_xr)
                self.put(2, self.pair(x), d_xl)
                self.put(5, self.pair(x), d_c)
            elif which == "l":
                self.m[1].wait_recv()
                self.put(3, self.pair(xl).at[0], d_xr)
                self.put(6, self.pair(xl), d_c)
            elif which == "r":
                self.m[2].wait_recv()
                self.put(4, self.pair(xr).at[1], d_xl)
                self.put(7, self.pair(xr), d_c)
            else:
                self.m[3].wait_recv()
                self.m[4].wait_recv()
                self.put(8, self.pair(xo), d_c)

        def finish(self):
            for k in range(5, 9):
                self.m[k].wait_recv()

    need("key")
    need("value")
    kv_start()

    need("gain")
    row_id = lax.broadcasted_iota(jnp.int32, (64, 128), 0)
    lane_id = lax.broadcasted_iota(jnp.int32, (64, 128), 1)
    eye = row_id == lane_id
    gain4 = gain_ref[...].astype(F32)
    gain = jnp.concatenate([gain4[i : i + 1] for i in range(4)], axis=1)

    def scale_rows(p, side):
        steps = pl.ds(p.k * TS, TS)
        for t in range(p.k * TS, p.k * TS + TS):
            need(f"x{t}")

        def body(i, carry):
            raw = xb[steps, 2 * i + side].astype(F32).reshape(RB, 512)
            xs[p.k, side, i] = (raw * gain).astype(BF16)
            return carry

        lax.fori_loop(0, 8, body, 0, unroll=True)

    def squares(d, carry):
        raw = xb[:, d].astype(F32).reshape(64, 512)
        part = jnp.sum(raw * raw, axis=1, keepdims=True)
        flat = jnp.sum(jnp.where(eye, part, 0.0), axis=0, keepdims=True)
        sqs[lax.rem(d, 2), d // 4, lax.rem(d // 2, 2)] = jnp.broadcast_to(flat, (8, 128))
        return carry

    first = pl.ds(0, 5)
    second = pl.ds(5, 5)

    class Part:
        pass

    parts = []
    for k in range(NCH):
        p = Part()
        p.k = k
        p.base = PART0 + k * PART_MSGS
        p.px, p.oy = {}, {}
        p.hog = Gather(p.base + M_HO, lambda a, k=k: ho.at[k, a, core])
        parts.append(p)

    def other_rows(p):
        k = p.k

        rows = xs[k, 1 - core].reshape(8 * RB, 512)
        for j in range(5):
            res = mdot(rows, weights(j)).astype(BF16)
            gs[k, 2 * j] = res[:, :128].reshape(4, 2, RB, 128)
            gs[k, 2 * j + 1] = res[:, 128:].reshape(4, 2, RB, 128)
        p.core = send(p.base + M_CORE, gs.at[k], gr.at[k], d_c)

    def own_rows(p):
        k, px = p.k, p.px
        p.core.wait_recv()
        rows = xs[k, core].reshape(8 * RB, 512)

        def body(j):
            res = mdot(rows, wb[j])
            for i in range(2):
                both = res[:, 128 * i : 128 * i + 128].reshape(4, 2, RB, 128) + gr[
                    k, 2 * j + i
                ].astype(F32)
                g[k, :, 2 * j + i] = both.astype(BF16)

        for j in range(3):
            body(j)
        px[0] = send(p.base + M_X, g.at[k, xo, first], prelay.at[k, 0], d_xr)
        for j in range(3, 5):
            body(j)
        px[1] = send(p.base + M_X + 1, g.at[k, xo, second], prelay.at[k, 1], d_xl)

    def x_relay(p, side):
        k, px = p.k, p.px
        which, to, dev, into = ((first, xr, d_xr, pleft), (second, xl, d_xl, pright))[side]
        px[side].wait_recv()
        g[k, to, which] = (g[k, to, which].astype(F32) + prelay[k, side].astype(F32)).astype(BF16)
        px[2 + side] = send(p.base + M_X + 2 + side, g.at[k, to], into.at[k], dev)

    def x_sum(p):
        k, px = p.k, p.px
        px[2].wait_recv()
        px[3].wait_recv()

        def three(s, z):
            return (
                g[k, x, s, z].astype(F32)
                + pleft[k, s, z].astype(F32)
                + pright[k, s, z].astype(F32)
            )

        for s in range(10):
            zs[k, s] = three(s, 1 - zh).astype(BF16)
        p.zp = send(p.base + M_Z, zs.at[k], zr.at[k], d_z)

        for s in range(10):
            rf[k, s] = three(s, zh)

    def attend(p, inverse):
        k = p.k
        nrow = 8 * RB
        nnew = (k + 1) * RB
        inv = inverse[k * RB : (k + 1) * RB]
        p.zp.wait_recv()

        for s in range(10):
            pr[k, s] = ((rf[k, s] + zr[k, s].astype(F32)) * inv).astype(BF16)
        nk[k * RB : (k + 1) * RB] = pr[k, 8]
        nv[k * RB : (k + 1) * RB] = pr[k, 9]

        q = pr[k, 0:8].reshape(nrow, HD)
        i_id = lax.broadcasted_iota(jnp.int32, (nrow, nnew), 0)
        j_id = lax.broadcasted_iota(jnp.int32, (nrow, nnew), 1)
        seen = (lax.rem(i_id, 16) == lax.rem(j_id, 16)) & (
            j_id // 16 <= k * TS + lax.rem(i_id // 16, TS)
        )
        s_new = jnp.where(seen, rdot(q, nk[0:nnew]) * SCALE, NEG)
        peak = None
        for b in range(8):
            s = rdot(q, pool(b, 0)) * SCALE
            s = (s.reshape(nrow // 16, 16, 256) + bias[b][None]).reshape(nrow, 256)
            sb[b] = s
            here = jnp.maximum(s[:, :128], s[:, 128:])
            peak = here if peak is None else jnp.maximum(peak, here)
        top = jnp.maximum(
            jnp.max(peak, axis=1, keepdims=True), jnp.max(s_new, axis=1, keepdims=True)
        )
        w_new = jnp.exp(s_new - top)
        mixed = mdot(w_new.astype(BF16), nv[0:nnew])
        part = None
        for b in range(8):
            w = jnp.exp(sb[b] - top)
            here = w[:, :128] + w[:, 128:]
            part = here if part is None else part + here
            mixed = mixed + mdot(w.astype(BF16), pool(b, 1))
        total = jnp.sum(part, axis=1, keepdims=True) + jnp.sum(w_new, axis=1, keepdims=True)
        head_out = (mixed / total).astype(BF16)
        for s in range(8):
            ho[k, x, core, zh, s // 4, :, (s % 4) * HD : (s % 4 + 1) * HD] = head_out[s * RB : (s + 1) * RB]
        p.hog.start()

    def out_rows(p):
        k, oy = p.k, p.oy
        p.hog.finish()
        lhs = [ho[k, :, :, :, f].reshape(16 * RB, 512) for f in range(2)]
        for n in range(2):
            res = mdot(lhs[0], wob[n, 0:512]) + mdot(lhs[1], wob[n, 512:1024])
            o[k, :, :, :, :, n * 256 : (n + 1) * 256] = res.astype(BF16).reshape(4, 2, 2, RB, 256)
        oy[0] = send(p.base + M_Y, o.at[k, yo, 0], orelay.at[k, 0], d_yr)
        oy[1] = send(p.base + M_Y + 1, o.at[k, yo, 1], orelay.at[k, 1], d_yl)

    def y_relay(p, side):
        k, oy = p.k, p.oy
        to, dev, into = ((yr, d_yr, oleft), (yl, d_yl, oright))[side]
        oy[side].wait_recv()
        o[k, to, side] = (o[k, to, side].astype(F32) + orelay[k, side].astype(F32)).astype(BF16)
        oy[2 + side] = send(p.base + M_Y + 2 + side, o.at[k, to], into.at[k], dev)

    def y_sum(p):
        k, oy = p.k, p.oy
        oy[2].wait_recv()
        oy[3].wait_recv()

        for i in range(2):
            ozs[k, i] = (
                o[k, y, i].astype(F32) + oleft[k, i].astype(F32) + oright[k, i].astype(F32)
            ).astype(BF16)
        p.oz = send(p.base + M_ZL, ozs.at[k], ozr.at[k], d_zl)

    def add_input(p):
        k = p.k
        p.oz.wait_recv()
        steps = pl.ds(k * TS, TS)
        for z in range(2):
            for i in range(2):
                full = ozs[k, i, z].astype(F32) + ozr[k, i, z].astype(F32)
                hidden = xb[steps, cidx(y, z, i)].astype(F32)
                ob[steps, 2 * y + z, pl.ds(16 * i, 16), :] = (
                    hidden + full.reshape(TS, 16, 512)
                ).astype(BF16)
        own = ob.at[steps, pl.ds(2 * y, 2)]
        p.fo = {
            1: send(p.base + M_FO, own, own, d_yr),
            2: send(p.base + M_FO + 1, own, own, d_yl),
        }

    def pass_on(p, k):
        steps = pl.ds(p.k * TS, TS)
        if k == 1:
            p.fo[1].wait_recv()
            part = ob.at[steps, 2 * yl]
            p.fo[5] = send(p.base + M_FO + 2, part, part, d_yr)
        elif k == 2:
            p.fo[2].wait_recv()
            part = ob.at[steps, 2 * yr + 1]
            p.fo[6] = send(p.base + M_FO + 3, part, part, d_yl)
        else:
            p.fo[5].wait_recv()
            p.fo[6].wait_recv()
            p.done = pltpu.make_async_copy(ob.at[steps], out.at[steps], lsem.at[19 + p.k])
            p.done.start()

    def weights(j):
        if j < 4:
            need(f"wq{j}")
        elif "wkv" not in waited:
            need("wkv")
            wkvf[...] = wkvb[...].astype(F32)
            wb[4, :, 0:128] = wkvf[pl.ds(0, 512, stride=2), :].astype(BF16)
            wb[4, :, 128:256] = wkvf[pl.ds(1, 512, stride=2), :].astype(BF16)
        return wb[j]

    def sum_squares():
        for t in range(4):
            need(f"x{t}")
        lax.fori_loop(0, 16, squares, 0, unroll=4)
        return [send(SQ0, sqs.at[1 - core], sqc, d_c)]

    def sum_squares_x(before):
        before[0].wait_recv()
        sqx[...] = sqs[core] + sqc[...]
        return [
            send(SQ0 + 1, sqx.at[xr], sqn.at[0], d_xr),
            send(SQ0 + 2, sqx.at[xl], sqn.at[1], d_xl),
            send(SQ0 + 3, sqx.at[xo], sqn.at[2], d_xo),
        ]

    def sum_squares_z(before):
        for m in before:
            m.wait_recv()
        sqz[...] = sqx[x] + sqn[0] + sqn[1] + sqn[2]
        return [send(SQ0 + 4, sqz.at[1 - zh], sqr, d_z)]

    def inverse_rms(before):
        before[0].wait_recv()
        flat = (sqz[zh] + sqr[...])[0:1, :]
        row_sq = jnp.sum(jnp.where(eye, flat, 0.0), axis=1, keepdims=True)
        return lax.rsqrt(row_sq / D + 1e-05)

    def own_rows_pages():
        pick = (
            lax.broadcasted_iota(jnp.int32, (16, 256), 1)
            == lax.broadcasted_iota(jnp.int32, (16, 256), 0) + 16 * c
        )
        return rdot(pick.astype(BF16), pages_ref[...].astype(BF16))

    def pick_pages():
        need("pages")
        need("lens")
        own_pages = own_rows_pages()
        page_id = lax.broadcasted_iota(jnp.int32, (16, 64), 1)
        block_id = lax.broadcasted_iota(jnp.int32, (16, 64), 0)
        named = jnp.zeros((16, 64), F32)
        for slot in range(8):
            named = jnp.where(own_pages[:, slot : slot + 1] == page_id.astype(F32), 1.0, named)
        present = jnp.max(named, axis=0, keepdims=True) > 0.5
        here = present & (page_id // 4 == block_id)
        place = lax.rem(page_id, 4).astype(F32)
        low = jnp.min(jnp.where(here, place, 9.0), axis=1, keepdims=True)
        high = jnp.max(jnp.where(here, place, -1.0), axis=1, keepdims=True)
        column = lax.broadcasted_iota(jnp.int32, (16, 128), 1)
        two[...] = jnp.where(column == 0, low, high).astype(jnp.int32)
        paired.start()

    paired = pltpu.make_async_copy(two, two_s, lsem.at[24 + NCH])

    def chosen(b, i):
        return jnp.minimum(jnp.maximum(two_s[b, i], 0), 3)

    def mask_pages():
        paired.wait()
        own_pages = own_rows_pages().astype(jnp.int32)
        r_id = lax.broadcasted_iota(jnp.int32, (16, 128), 0)
        s_id = lax.broadcasted_iota(jnp.int32, (16, 128), 1)
        lens = jnp.zeros((16, 128), jnp.int32)
        for r in range(16):
            lens = jnp.where(r_id == r, clen_ref[c * 16 + r], lens)
        named = [jnp.broadcast_to(own_pages[:, slot : slot + 1], (16, 128)) for slot in range(8)]
        upto = [lens - slot * PAGE for slot in range(8)]
        in_page = lax.rem(s_id, PAGE)
        for b in range(16):
            page = 4 * b + jnp.where(s_id < PAGE, chosen(b, 0), chosen(b, 1))
            end = jnp.zeros((16, 128), jnp.int32)
            for slot in range(8):
                end = jnp.where(named[slot] == page, upto[slot], end)
            bias[b // 2, :, 128 * (b % 2) : 128 * (b % 2) + 128] = jnp.where(in_page < end, 0.0, NEG)

    def pool(t, f):
        pages = []
        for b in (2 * t, 2 * t + 1):
            for i in range(2):
                pages.append(kv[b // 4, b % 2, (b // 2) % 2, f, chosen(b, i)])
        return jnp.concatenate(pages, axis=0)

    def list_pages():
        need("mask")
        a_id = lax.broadcasted_iota(jnp.int32, (64, 64), 0)
        b_id = lax.broadcasted_iota(jnp.int32, (64, 64), 1)
        col_id = lax.broadcasted_iota(jnp.int32, (64, 128), 1)
        p_id = lax.broadcasted_iota(jnp.int32, (64, 128), 0)
        spot = (p_id // 16) * 16 + lax.rem(p_id // 4, 2) * 8 + lax.rem(p_id // 8, 2) * 4
        spot = (spot + lax.rem(p_id, 4)).astype(F32)
        rows = []
        for n in range(4):
            a = 4 * c + n
            line = mask_ref[pl.ds(a, 1), :].astype(F32)
            readable = jnp.sum(jnp.where(a_id == b_id, line, 0.0), axis=1, keepdims=True)
            readable = jnp.where((readable > 0.5) & (p_id < a), 1.0, 0.0)
            before = mdot((b_id < a_id).astype(BF16), readable.astype(BF16))
            place = jnp.where(p_id == a, 0.0, before + 1.0).astype(jnp.int32)
            hit = (place == col_id) & ((readable > 0.5) | (p_id == a))
            line = jnp.sum(jnp.where(hit, spot, 0.0), axis=0, keepdims=True)
            count = jnp.sum(readable, axis=0, keepdims=True) + 1.0
            rows.append(jnp.where(col_id[0:1] == 127, count, line))
        picks[...] = jnp.concatenate(rows + rows, axis=0).astype(jnp.int32)
        listed.start()
        told.start()

    def prefill_node(n):
        if n == 0:
            listed.wait()
            need("query")
        pages = []
        for i in range(NEAR):
            spot = jnp.minimum(jnp.maximum(spots[n, i], 0), 63)
            pages.append(
                (spot // 16, lax.rem(spot // 8, 2), lax.rem(spot // 4, 2), lax.rem(spot, 4))
            )
        keys = jnp.concatenate([kv[a, b, d, 0, i] for a, b, d, i in pages], axis=0)
        values = jnp.concatenate([kv[a, b, d, 1, i] for a, b, d, i in pages], axis=0)
        mixed = first_pages(qb[n], keys, values, spots[n, 127])[1]
        write_heads(pb, n, mixed)
        prefilled[n].start()

    listed = pltpu.make_async_copy(picks, spots, lsem.at[19 + NCH])
    told = pltpu.make_async_copy(picks, picks_out, lsem.at[25 + NCH])
    prefilled = [
        pltpu.make_async_copy(pb.at[n], pout.at[n], lsem.at[20 + NCH + n]) for n in range(4)
    ]

    keep = pltpu.make_async_copy(kv, kv_out, lsem.at[18])
    rms, squared = [], []

    def step(event):
        who, what = event.split(".")
        if who == "kv":
            if what == "fin":
                for k in range(8, 12):
                    kvm[k].wait_recv()
                keep.start()
            else:
                kv_pass(what)
            return
        if who == "all":
            if what[:2] == "sq":
                stage = {"sq": sum_squares, "sq1": sum_squares_x, "sq2": sum_squares_z}[what]
                squared[:] = stage(squared) if squared else stage()
            else:
                if what[:2] == "pf":
                    prefill_node(int(what[2]))
                else:
                    {"pick": pick_pages, "mask": mask_pages, "list": list_pages}[what]()
            return
        p = parts[int(who[1])]
        if what == "other":
            scale_rows(p, 1 - core)
            other_rows(p)
            if p.k == 0:
                load_rest()
        elif what == "own":
            scale_rows(p, core)
            own_rows(p)
        elif what[0] == "x":
            if what == "xsum":
                x_sum(p)
            else:
                x_relay(p, int(what[2]) // 2)
        elif what == "att":
            if not rms:
                rms.append(inverse_rms(squared))
            attend(p, rms[0])
        elif what[0] == "h":
            p.hog.take(what[1])
        elif what == "out":
            need("wo0")
            need("wo1")
            out_rows(p)
        elif what == "ysum":
            drain(10)
            y_sum(p)
        elif what[0] == "y":
            y_relay(p, int(what[2]) // 2)
        elif what == "add":
            add_input(p)
        else:
            drain(6)
            pass_on(p, int(what[1]))

    for event in ORDER:
        step(event)
    keep.wait()
    told.wait()
    for copy in prefilled:
        copy.wait()
    drain(0)
    for p in parts:
        p.done.wait()


def layer_call(*args):
    hbm = pl.BlockSpec(memory_space=pl.ANY)
    return pl.pallas_call(
        layer_kernel,
        out_shape=(
            jax.ShapeDtypeStruct((4, 2, 2, 2, 4, PAGE, HD), BF16),
            jax.ShapeDtypeStruct((8, 128), jnp.int32),
            jax.ShapeDtypeStruct((4, PAGE, 1024), BF16),
            jax.ShapeDtypeStruct((4, 8, 32, 512), BF16),
        ),
        in_specs=[hbm] * 11,
        out_specs=(hbm, hbm, hbm, hbm),
        scratch_shapes=[
            pltpu.VMEM((8, 128), jnp.int32),
            pltpu.VMEM((4, PAGE, 1024), BF16),
            pltpu.SMEM((8, 128), jnp.int32),
            pltpu.VMEM((4, PAGE, 1024), BF16),
            pltpu.VMEM((4, 8, 32, 512), BF16),
            pltpu.VMEM((64, 64), jnp.int32),
            pltpu.VMEM((8, 256), jnp.int32),
            pltpu.SMEM((256,), jnp.int32),
            pltpu.VMEM((4, 128), BF16),
            pltpu.VMEM((4, 2, 2, 2, 4, PAGE, HD), BF16),
            pltpu.VMEM((4, 16, 16, 512), BF16),
            pltpu.VMEM((5, 512, 256), BF16),
            pltpu.VMEM((1024, 128), BF16),
            pltpu.VMEM((1024, 128), F32),
            pltpu.VMEM((2, 1024, 256), BF16),
            pltpu.VMEM((NCH, 2, 8, RB, 512), BF16),
            pltpu.VMEM((2, 4, 2, 8, 128), F32),
            pltpu.VMEM((4, 2, 8, 128), F32),
            pltpu.VMEM((4, 2, 8, 128), F32),
            pltpu.VMEM((3, 2, 8, 128), F32),
            pltpu.VMEM((2, 8, 128), F32),
            pltpu.VMEM((8, 128), F32),
            pltpu.VMEM((NCH, 10, 4, 2, RB, 128), BF16),
            pltpu.VMEM((NCH, 10, 4, 2, RB, 128), BF16),
            pltpu.VMEM((NCH, 4, 10, 2, RB, 128), BF16),
            pltpu.VMEM((NCH, 2, 5, 2, RB, 128), BF16),
            pltpu.VMEM((NCH, 10, 2, RB, 128), BF16),
            pltpu.VMEM((NCH, 10, 2, RB, 128), BF16),
            pltpu.VMEM((NCH, 10, RB, 128), BF16),
            pltpu.VMEM((NCH, 10, RB, 128), BF16),
            pltpu.VMEM((NCH, 10, RB, 128), F32),
            pltpu.VMEM((NCH, 10, RB, 128), BF16),
            pltpu.VMEM((64, 128), BF16),
            pltpu.VMEM((64, 128), BF16),
            pltpu.VMEM((8, 16, 256), F32),
            pltpu.VMEM((16, 128), jnp.int32),
            pltpu.SMEM((16, 128), jnp.int32),
            pltpu.VMEM((8, 8 * RB, 256), F32),
            pltpu.VMEM((NCH, 4, 2, 2, 2, RB, 512), BF16),
            pltpu.VMEM((NCH, 4, 2, 2, RB, 512), BF16),
            pltpu.VMEM((NCH, 2, 2, RB, 512), BF16),
            pltpu.VMEM((NCH, 2, 2, RB, 512), BF16),
            pltpu.VMEM((NCH, 2, 2, RB, 512), BF16),
            pltpu.VMEM((NCH, 2, 2, RB, 512), BF16),
            pltpu.VMEM((NCH, 2, 2, RB, 512), BF16),
            pltpu.SemaphoreType.DMA((26 + NCH,)),
            pltpu.SemaphoreType.DMA((NMSG,)),
            pltpu.SemaphoreType.DMA((NMSG,)),
        ],
        compiler_params=pltpu.CompilerParams(
            collective_id=0, has_side_effects=True, vmem_limit_bytes=56 * 1024 * 1024
        ),
        name="layer",
    )(*args)


def finish_kernel(
    q_hbm, kv_ref, picks_hbm, pre_ref, dec_ref, out_hbm, dec_out,
    picks, q, kv, extra, stage, out, peak, mix, sem,
):
    get_dec = [pltpu.make_async_copy(dec_ref.at[t], stage.at[t], sem.at[t]) for t in range(4)]
    put_dec = [pltpu.make_async_copy(stage.at[t], dec_out.at[t], sem.at[4 + t]) for t in range(4)]
    get_pre = pltpu.make_async_copy(pre_ref, out, sem.at[8])
    put_pre = pltpu.make_async_copy(out, out_hbm, sem.at[9])
    get_picks = pltpu.make_async_copy(picks_hbm, picks, sem.at[13])
    get_picks.start()
    get_pre.start()
    for copy in get_dec:
        copy.start()

    def page(n, k):
        spot = picks[n, k]
        return kv_ref.at[spot // 4, :, lax.rem(spot, 4)]

    get_picks.wait()
    get_pre.wait()
    for t in range(4):
        get_dec[t].wait()
        put_dec[t].start()

    def deep(n, carry):
        @pl.when(picks[n, 127] > NEAR)
        def _():
            pltpu.make_async_copy(q_hbm.at[n], q, sem.at[10]).start()
            for k in range(NEAR):
                pltpu.make_async_copy(page(n, k), kv.at[k], sem.at[11]).start()
            pltpu.make_async_copy(q, q, sem.at[10]).wait()
            pltpu.make_async_copy(kv, kv, sem.at[11]).wait()
            top, mixed = first_pages(
                q[...],
                kv[:, 0].reshape(NEAR * PAGE, HD),
                kv[:, 1].reshape(NEAR * PAGE, HD),
                picks[n, 127],
            )
            peak[...] = jnp.broadcast_to(top, (512, 128))
            mix[...] = mixed

            def more(t, inner):
                for k in range(4):
                    pltpu.make_async_copy(
                        page(n, NEAR + 4 * t + k), extra.at[k], sem.at[12]
                    ).start()
                pltpu.make_async_copy(extra, extra, sem.at[12]).wait()
                rows = jnp.concatenate([q[:, s * HD : (s + 1) * HD] for s in range(8)], axis=0)
                j_id = lax.broadcasted_iota(jnp.int32, (1, 4 * PAGE), 1)
                hidden = jnp.where(j_id < (picks[n, 127] - NEAR - 4 * t) * PAGE, 0.0, NEG)
                s = rdot(rows, extra[:, 0].reshape(4 * PAGE, HD)) * SCALE + hidden
                before = peak[:, 0:1]
                top = jnp.maximum(jnp.max(s, axis=1, keepdims=True), before)
                values = jnp.concatenate(
                    [extra[:, 1].reshape(4 * PAGE, HD), jnp.ones((4 * PAGE, 128), BF16)], axis=1
                )
                mix[...] = mix[...] * jnp.exp(before - top) + mdot(
                    jnp.exp(s - top).astype(BF16), values
                )
                peak[...] = jnp.broadcast_to(top, (512, 128))
                return inner

            lax.fori_loop(0, (picks[n, 127] - NEAR + 3) // 4, more, 0)
            write_heads(out, n, mix[...])

        return carry

    lax.fori_loop(0, 4, deep, 0)
    put_pre.start()
    put_pre.wait()
    for t in range(4):
        put_dec[t].wait()


def finish_call(q, kv, picks, pre, dec):
    hbm = pl.BlockSpec(memory_space=pl.ANY)
    return pl.pallas_call(
        finish_kernel,
        out_shape=(
            jax.ShapeDtypeStruct((4, PAGE, 1024), BF16),
            jax.ShapeDtypeStruct(dec.shape, BF16),
        ),
        in_specs=[hbm] * 5,
        out_specs=(hbm, hbm),
        scratch_shapes=[
            pltpu.SMEM((8, 128), jnp.int32),
            pltpu.VMEM((PAGE, 1024), BF16),
            pltpu.VMEM((NEAR, 2, PAGE, HD), BF16),
            pltpu.VMEM((4, 2, PAGE, HD), BF16),
            pltpu.VMEM(dec.shape, BF16),
            pltpu.VMEM((4, PAGE, 1024), BF16),
            pltpu.VMEM((512, 128), F32),
            pltpu.VMEM((512, 256), F32),
            pltpu.SemaphoreType.DMA((14,)),
        ],
        compiler_params=pltpu.CompilerParams(vmem_limit_bytes=62 * 1024 * 1024),
        name="finish",
    )(q, kv, picks, pre, dec)


def per_device(
    prefill_query, prefill_key, prefill_value, tree_mask, pages, cache_len,
    dec_in, norm_gain, w_query, w_keyval, w_out,
):
    query = prefill_query.reshape(4, PAGE, 1024)
    kv, picks, pre, dec = layer_call(
        query, prefill_key.reshape(4, PAGE, HD), prefill_value.reshape(4, PAGE, HD), tree_mask,
        pages.T, cache_len, dec_in.reshape(4, 16, 16, 512), norm_gain.reshape(4, 128), w_query,
        w_keyval.reshape(1024, 128), w_out,
    )
    prefill_out, dec_out = finish_call(
        query, kv.reshape(16, 2, 4, PAGE, HD), picks, pre, dec
    )
    return prefill_out.reshape(256, 1024), dec_out.reshape(4, 256, 512)


def solution(mesh):
    return jax.shard_map(
        per_device,
        mesh=mesh,
        in_specs=(
            P("ctx", "head"), P("ctx", "head"), P("ctx", "head"), P(), P(), P(),
            P(None, None, "ctx"), P("ctx"), P("ctx", "head"), P("ctx", None, "head"),
            P("head", "ctx"),
        ),
        out_specs=(P("ctx", "head"), P(None, None, "ctx")),
        check_vma=False,
    )
```

```python
import jax
import jax.numpy as jnp
from jax import lax
from jax.experimental import pallas as pl
from jax.experimental.pallas import tpu as pltpu
from jax.sharding import PartitionSpec as P

D = 8192
HD = 128
PAGE = 64
STEPS = 4
SCALE = HD ** (-0.5)
NEG = -1e30
F32 = jnp.float32
BF16 = jnp.bfloat16
MESH = pl.DeviceIdType.MESH

NCH = 4
TS = STEPS // NCH
RB = 16 * TS
NEAR = 12

KV0 = 0
SQ0 = 12
PART0 = 17
M_CORE, M_X, M_Z, M_HO, M_Y, M_ZL, M_FO = 0, 1, 5, 6, 15, 19, 20
PART_MSGS = 24
NMSG = PART0 + NCH * PART_MSGS


ORDER = (
    "p0.other", "p1.other", "p2.other", "p0.own", "all.pick", "kv.r", "kv.l", "kv.z", "p1.own",
    "all.sq", "p0.xr2", "p0.xr0", "p2.own", "p3.other", "kv.f", "p1.xr0", "p1.xr2", "all.sq1",
    "p3.own", "p2.xr0", "kv.s", "p2.xr2", "kv.m", "p0.xsum", "all.sq2", "kv.o", "all.mask",
    "p3.xr2", "p1.xsum", "kv.fin", "p3.xr0", "p2.xsum", "p0.att", "p1.att", "p3.xsum", "p2.att",
    "p0.hz", "p1.hz", "p3.att", "p0.hl", "p0.hr", "p2.hz", "p1.hl", "all.list", "p3.hz",
    "p0.hf", "p1.hr", "p2.hl", "p2.hr", "p0.out", "p3.hr", "p3.hl", "p1.hf", "all.pf0", "p2.hf",
    "p0.yr0", "p0.yr2", "p3.hf", "p1.out", "p3.out", "p2.out", "p1.yr2", "p1.yr0", "p0.ysum",
    "p3.yr2", "p3.yr0", "p2.yr0", "p2.yr2", "all.pf1", "p1.ysum", "all.pf2", "p3.ysum",
    "p0.add", "p2.ysum", "p1.add", "p3.add", "p2.add", "p0.f2", "all.pf3", "p0.f1", "p1.f1",
    "p1.f2", "p3.f1", "p3.f2", "p2.f1", "p2.f2", "p1.f5", "p0.f5", "p3.f5", "p2.f5",
)


def rdot(a, b):
    return lax.dot_general(a, b, (((1,), (1,)), ((), ())), preferred_element_type=F32)


def mdot(a, b):
    return lax.dot_general(a, b, (((1,), (0,)), ((), ())), preferred_element_type=F32)


def first_pages(q_node, keys, values, count):
    q = jnp.concatenate([q_node[:, s * HD : (s + 1) * HD] for s in range(8)], axis=0)
    values = jnp.concatenate([values, jnp.ones((NEAR * PAGE, 128), BF16)], axis=1)
    j_id = lax.broadcasted_iota(jnp.int32, (1, NEAR * PAGE), 1)
    s = rdot(q, keys) * SCALE + jnp.where(j_id < count * PAGE, 0.0, NEG)
    i_id = lax.broadcasted_iota(jnp.int32, (512, 128), 0)
    j_id = lax.broadcasted_iota(jnp.int32, (512, 128), 1)
    seen = (j_id >= PAGE) | (j_id <= lax.rem(i_id, PAGE))
    s = jnp.concatenate([jnp.where(seen, s[:, :128], NEG), s[:, 128:]], axis=1)
    peak = jnp.max(s, axis=1, keepdims=True)
    return peak, mdot(jnp.exp(s - peak).astype(BF16), values)


def write_heads(out, n, mixed):
    result = (mixed[:, 0:128] / mixed[:, 128:256]).astype(BF16)
    for s in range(8):
        out[n, :, s * HD : (s + 1) * HD] = result[s * 64 : (s + 1) * 64]


def layer_kernel(
    q_hbm, key_ref, val_ref, mask_hbm, pages_hbm, clen_hbm, x_ref, gain_hbm, wq_ref, wkv_ref, wo_ref,
    kv_out, picks_out, pout, out,
    picks, qb, spots, pb, ob, mask_ref, pages_ref, clen_ref, gain_ref,
    kv, xb, wb, wkvb, wkvf, wob, xs, sqs, sqc, sqx, sqn, sqz, sqr, gs, gr, g, prelay, pleft, pright, zs, zr, rf,
    pr, nk, nv, bias, two, two_s, sb, ho, o, orelay, oleft, oright, ozs, ozr,
    lsem, ssem, rsem,
):
    c = lax.axis_index("ctx")
    h = lax.axis_index("head")
    core = lax.rem(c, 2)
    zh = lax.rem(c // 2, 2)
    x = c // 4
    y = lax.rem(h, 4)
    zl = h // 4

    def cidx(xi, zi, ci):
        return xi * 4 + zi * 2 + ci

    def hidx(yi, zi):
        return zi * 4 + yi

    up, down = 1 + 2 * core, 3 - 2 * core
    xr, xl, xo = lax.rem(x + up, 4), lax.rem(x + down, 4), lax.rem(x + 2, 4)
    yr, yl, yo = lax.rem(y + up, 4), lax.rem(y + down, 4), lax.rem(y + 2, 4)
    d_xr = (cidx(xr, zh, core), h)
    d_xl = (cidx(xl, zh, core), h)
    d_z = (cidx(x, 1 - zh, core), h)
    d_c = (cidx(x, zh, 1 - core), h)
    d_yr = (c, hidx(yr, zl))
    d_yl = (c, hidx(yl, zl))
    d_zl = (c, hidx(y, 1 - zl))
    d_xo = (cidx(xo, zh, core), h)

    def msg(i, src, dst, dev):
        return pltpu.make_async_remote_copy(
            src_ref=src, dst_ref=dst, send_sem=ssem.at[i], recv_sem=rsem.at[i],
            device_id=dev, device_id_type=MESH,
        )

    barrier = pltpu.get_barrier_semaphore()

    for dev in (d_xr, d_xl, d_z, d_c, d_yr, d_yl, d_zl, d_xo):
        pl.semaphore_signal(barrier, inc=1, device_id=dev, device_id_type=MESH)

    loads = {}

    def load(name, src, dst):
        loads[name] = pltpu.make_async_copy(src, dst, lsem.at[len(loads)])
        loads[name].start()

    waited = set()

    def need(name):
        if name not in waited:
            waited.add(name)
            loads[name].wait()

    load("key", key_ref, kv.at[x, core, zh, 0])
    load("value", val_ref, kv.at[x, core, zh, 1])
    load("gain", gain_hbm, gain_ref)
    load("x0", x_ref.at[0], xb.at[0])
    load("wkv", wkv_ref, wkvb)
    for j in range(4):
        load(f"wq{j}", wq_ref.at[:, pl.ds(256 * j, 256)], wb.at[j])
    for t in range(1, 4):
        load(f"x{t}", x_ref.at[t], xb.at[t])

    def load_rest():
        load("pages", pages_hbm, pages_ref)
        load("lens", clen_hbm, clen_ref)
        load("mask", mask_hbm, mask_ref)
        for j in range(2):
            load(f"wo{j}", wo_ref.at[:, pl.ds(256 * j, 256)], wob.at[j])
        load("query", q_hbm, qb)

    pl.semaphore_wait(barrier, 8)

    sent = []

    def send(i, src, dst, dev):
        m = msg(i, src, dst, dev)
        m.start()
        sent.append(m)
        return m

    def drain(left):
        while len(sent) > left:
            sent.pop(0).wait_send()

    def pass_to(msgs, base, k, ref, dev):
        msgs[k] = send(base + k, ref, ref, dev)

    kvm = {}

    def kv_start():
        own = kv.at[x, core, zh]
        pass_to(kvm, KV0, 0, own, d_z)
        pass_to(kvm, KV0, 1, own, d_xr)
        pass_to(kvm, KV0, 2, own, d_xl)

    def kv_pass(what):
        if what == "l":
            kvm[1].wait_recv()
            pass_to(kvm, KV0, 3, kv.at[xl, core, zh, 0], d_xr)
            pass_to(kvm, KV0, 5, kv.at[xl, core, zh], d_z)
        elif what == "r":
            kvm[2].wait_recv()
            pass_to(kvm, KV0, 4, kv.at[xr, core, zh, 1], d_xl)
            pass_to(kvm, KV0, 6, kv.at[xr, core, zh], d_z)
        elif what == "f":
            kvm[3].wait_recv()
            kvm[4].wait_recv()
            pass_to(kvm, KV0, 7, kv.at[xo, core, zh], d_z)
        else:
            waited, given, place = {"z": (0, 8, x), "m": (5, 9, xl), "s": (6, 10, xr), "o": (7, 11, xo)}[
                what
            ]
            kvm[waited].wait_recv()
            pass_to(kvm, KV0, given, kv.at[place, core], d_c)

    class Gather:
        def __init__(self, base, pair):
            self.base, self.pair, self.m = base, pair, {}

        def put(self, k, ref, dev):
            pass_to(self.m, self.base, k, ref, dev)

        def start(self):
            self.put(0, self.pair(x).at[zh], d_z)

        def take(self, which):
            if which == "z":
                self.m[0].wait_recv()
                self.put(1, self.pair(x), d_xr)
                self.put(2, self.pair(x), d_xl)
                self.put(5, self.pair(x), d_c)
            elif which == "l":
                self.m[1].wait_recv()
                self.put(3, self.pair(xl).at[0], d_xr)
                self.put(6, self.pair(xl), d_c)
            elif which == "r":
                self.m[2].wait_recv()
                self.put(4, self.pair(xr).at[1], d_xl)
                self.put(7, self.pair(xr), d_c)
            else:
                self.m[3].wait_recv()
                self.m[4].wait_recv()
                self.put(8, self.pair(xo), d_c)

        def finish(self):
            for k in range(5, 9):
                self.m[k].wait_recv()

    need("key")
    need("value")
    kv_start()

    need("gain")
    row_id = lax.broadcasted_iota(jnp.int32, (64, 128), 0)
    lane_id = lax.broadcasted_iota(jnp.int32, (64, 128), 1)
    eye = row_id == lane_id
    gain4 = gain_ref[...].astype(F32)
    gain = jnp.concatenate([gain4[i : i + 1] for i in range(4)], axis=1)

    def scale_rows(p, side):
        steps = pl.ds(p.k * TS, TS)
        for t in range(p.k * TS, p.k * TS + TS):
            need(f"x{t}")

        def body(i, carry):
            raw = xb[steps, 2 * i + side].astype(F32).reshape(RB, 512)
            xs[p.k, side, i] = (raw * gain).astype(BF16)
            return carry

        lax.fori_loop(0, 8, body, 0, unroll=True)

    def squares(d, carry):
        raw = xb[:, d].astype(F32).reshape(64, 512)
        part = jnp.sum(raw * raw, axis=1, keepdims=True)
        flat = jnp.sum(jnp.where(eye, part, 0.0), axis=0, keepdims=True)
        sqs[lax.rem(d, 2), d // 4, lax.rem(d // 2, 2)] = jnp.broadcast_to(flat, (8, 128))
        return carry

    first = pl.ds(0, 5)
    second = pl.ds(5, 5)

    class Part:
        pass

    parts = []
    for k in range(NCH):
        p = Part()
        p.k = k
        p.base = PART0 + k * PART_MSGS
        p.px, p.oy = {}, {}
        p.hog = Gather(p.base + M_HO, lambda a, k=k: ho.at[k, a, core])
        parts.append(p)

    def other_rows(p):
        k = p.k

        rows = xs[k, 1 - core].reshape(8 * RB, 512)
        for j in range(5):
            res = mdot(rows, weights(j)).astype(BF16)
            gs[k, 2 * j] = res[:, :128].reshape(4, 2, RB, 128)
            gs[k, 2 * j + 1] = res[:, 128:].reshape(4, 2, RB, 128)
        p.core = send(p.base + M_CORE, gs.at[k], gr.at[k], d_c)

    def own_rows(p):
        k, px = p.k, p.px
        p.core.wait_recv()
        rows = xs[k, core].reshape(8 * RB, 512)

        def body(j):
            res = mdot(rows, wb[j])
            for i in range(2):
                both = res[:, 128 * i : 128 * i + 128].reshape(4, 2, RB, 128) + gr[
                    k, 2 * j + i
                ].astype(F32)
                g[k, :, 2 * j + i] = both.astype(BF16)

        for j in range(3):
            body(j)
        px[0] = send(p.base + M_X, g.at[k, xo, first], prelay.at[k, 0], d_xr)
        for j in range(3, 5):
            body(j)
        px[1] = send(p.base + M_X + 1, g.at[k, xo, second], prelay.at[k, 1], d_xl)

    def x_relay(p, side):
        k, px = p.k, p.px
        which, to, dev, into = ((first, xr, d_xr, pleft), (second, xl, d_xl, pright))[side]
        px[side].wait_recv()
        g[k, to, which] = (g[k, to, which].astype(F32) + prelay[k, side].astype(F32)).astype(BF16)
        px[2 + side] = send(p.base + M_X + 2 + side, g.at[k, to], into.at[k], dev)

    def x_sum(p):
        k, px = p.k, p.px
        px[2].wait_recv()
        px[3].wait_recv()

        def three(s, z):
            return (
                g[k, x, s, z].astype(F32)
                + pleft[k, s, z].astype(F32)
                + pright[k, s, z].astype(F32)
            )

        for s in range(10):
            zs[k, s] = three(s, 1 - zh).astype(BF16)
        p.zp = send(p.base + M_Z, zs.at[k], zr.at[k], d_z)

        for s in range(10):
            rf[k, s] = three(s, zh)

    def attend(p, inverse):
        k = p.k
        nrow = 8 * RB
        nnew = (k + 1) * RB
        inv = inverse[k * RB : (k + 1) * RB]
        p.zp.wait_recv()

        for s in range(10):
            pr[k, s] = ((rf[k, s] + zr[k, s].astype(F32)) * inv).astype(BF16)
        nk[k * RB : (k + 1) * RB] = pr[k, 8]
        nv[k * RB : (k + 1) * RB] = pr[k, 9]

        q = pr[k, 0:8].reshape(nrow, HD)
        i_id = lax.broadcasted_iota(jnp.int32, (nrow, nnew), 0)
        j_id = lax.broadcasted_iota(jnp.int32, (nrow, nnew), 1)
        seen = (lax.rem(i_id, 16) == lax.rem(j_id, 16)) & (
            j_id // 16 <= k * TS + lax.rem(i_id // 16, TS)
        )
        s_new = jnp.where(seen, rdot(q, nk[0:nnew]) * SCALE, NEG)
        peak = None
        for b in range(8):
            s = rdot(q, pool(b, 0)) * SCALE
            s = (s.reshape(nrow // 16, 16, 256) + bias[b][None]).reshape(nrow, 256)
            sb[b] = s
            here = jnp.maximum(s[:, :128], s[:, 128:])
            peak = here if peak is None else jnp.maximum(peak, here)
        top = jnp.maximum(
            jnp.max(peak, axis=1, keepdims=True), jnp.max(s_new, axis=1, keepdims=True)
        )
        w_new = jnp.exp(s_new - top)
        mixed = mdot(w_new.astype(BF16), nv[0:nnew])
        part = None
        for b in range(8):
            w = jnp.exp(sb[b] - top)
            here = w[:, :128] + w[:, 128:]
            part = here if part is None else part + here
            mixed = mixed + mdot(w.astype(BF16), pool(b, 1))
        total = jnp.sum(part, axis=1, keepdims=True) + jnp.sum(w_new, axis=1, keepdims=True)
        head_out = (mixed / total).astype(BF16)
        for s in range(8):
            ho[k, x, core, zh, s // 4, :, (s % 4) * HD : (s % 4 + 1) * HD] = head_out[s * RB : (s + 1) * RB]
        p.hog.start()

    def out_rows(p):
        k, oy = p.k, p.oy
        p.hog.finish()
        lhs = [ho[k, :, :, :, f].reshape(16 * RB, 512) for f in range(2)]
        for n in range(2):
            res = mdot(lhs[0], wob[n, 0:512]) + mdot(lhs[1], wob[n, 512:1024])
            o[k, :, :, :, :, n * 256 : (n + 1) * 256] = res.astype(BF16).reshape(4, 2, 2, RB, 256)
        oy[0] = send(p.base + M_Y, o.at[k, yo, 0], orelay.at[k, 0], d_yr)
        oy[1] = send(p.base + M_Y + 1, o.at[k, yo, 1], orelay.at[k, 1], d_yl)

    def y_relay(p, side):
        k, oy = p.k, p.oy
        to, dev, into = ((yr, d_yr, oleft), (yl, d_yl, oright))[side]
        oy[side].wait_recv()
        o[k, to, side] = (o[k, to, side].astype(F32) + orelay[k, side].astype(F32)).astype(BF16)
        oy[2 + side] = send(p.base + M_Y + 2 + side, o.at[k, to], into.at[k], dev)

    def y_sum(p):
        k, oy = p.k, p.oy
        oy[2].wait_recv()
        oy[3].wait_recv()

        for i in range(2):
            ozs[k, i] = (
                o[k, y, i].astype(F32) + oleft[k, i].astype(F32) + oright[k, i].astype(F32)
            ).astype(BF16)
        p.oz = send(p.base + M_ZL, ozs.at[k], ozr.at[k], d_zl)

    def add_input(p):
        k = p.k
        p.oz.wait_recv()
        steps = pl.ds(k * TS, TS)
        for z in range(2):
            for i in range(2):
                full = ozs[k, i, z].astype(F32) + ozr[k, i, z].astype(F32)
                hidden = xb[steps, cidx(y, z, i)].astype(F32)
                ob[steps, 2 * y + z, pl.ds(16 * i, 16), :] = (
                    hidden + full.reshape(TS, 16, 512)
                ).astype(BF16)
        own = ob.at[steps, pl.ds(2 * y, 2)]
        p.fo = {
            1: send(p.base + M_FO, own, own, d_yr),
            2: send(p.base + M_FO + 1, own, own, d_yl),
        }

    def pass_on(p, k):
        steps = pl.ds(p.k * TS, TS)
        if k == 1:
            p.fo[1].wait_recv()
            part = ob.at[steps, 2 * yl]
            p.fo[5] = send(p.base + M_FO + 2, part, part, d_yr)
        elif k == 2:
            p.fo[2].wait_recv()
            part = ob.at[steps, 2 * yr + 1]
            p.fo[6] = send(p.base + M_FO + 3, part, part, d_yl)
        else:
            p.fo[5].wait_recv()
            p.fo[6].wait_recv()
            p.done = pltpu.make_async_copy(ob.at[steps], out.at[steps], lsem.at[19 + p.k])
            p.done.start()

    def weights(j):
        if j < 4:
            need(f"wq{j}")
        elif "wkv" not in waited:
            need("wkv")
            wkvf[...] = wkvb[...].astype(F32)
            wb[4, :, 0:128] = wkvf[pl.ds(0, 512, stride=2), :].astype(BF16)
            wb[4, :, 128:256] = wkvf[pl.ds(1, 512, stride=2), :].astype(BF16)
        return wb[j]

    def sum_squares():
        for t in range(4):
            need(f"x{t}")
        lax.fori_loop(0, 16, squares, 0, unroll=4)
        return [send(SQ0, sqs.at[1 - core], sqc, d_c)]

    def sum_squares_x(before):
        before[0].wait_recv()
        sqx[...] = sqs[core] + sqc[...]
        return [
            send(SQ0 + 1, sqx.at[xr], sqn.at[0], d_xr),
            send(SQ0 + 2, sqx.at[xl], sqn.at[1], d_xl),
            send(SQ0 + 3, sqx.at[xo], sqn.at[2], d_xo),
        ]

    def sum_squares_z(before):
        for m in before:
            m.wait_recv()
        sqz[...] = sqx[x] + sqn[0] + sqn[1] + sqn[2]
        return [send(SQ0 + 4, sqz.at[1 - zh], sqr, d_z)]

    def inverse_rms(before):
        before[0].wait_recv()
        flat = (sqz[zh] + sqr[...])[0:1, :]
        row_sq = jnp.sum(jnp.where(eye, flat, 0.0), axis=1, keepdims=True)
        return lax.rsqrt(row_sq / D + 1e-05)

    def own_rows_pages():
        pick = (
            lax.broadcasted_iota(jnp.int32, (16, 256), 1)
            == lax.broadcasted_iota(jnp.int32, (16, 256), 0) + 16 * c
        )
        return rdot(pick.astype(BF16), pages_ref[...].astype(BF16))

    def pick_pages():
        need("pages")
        need("lens")
        own_pages = own_rows_pages()
        page_id = lax.broadcasted_iota(jnp.int32, (16, 64), 1)
        block_id = lax.broadcasted_iota(jnp.int32, (16, 64), 0)
        named = jnp.zeros((16, 64), F32)
        for slot in range(8):
            named = jnp.where(own_pages[:, slot : slot + 1] == page_id.astype(F32), 1.0, named)
        present = jnp.max(named, axis=0, keepdims=True) > 0.5
        here = present & (page_id // 4 == block_id)
        place = lax.rem(page_id, 4).astype(F32)
        low = jnp.min(jnp.where(here, place, 9.0), axis=1, keepdims=True)
        high = jnp.max(jnp.where(here, place, -1.0), axis=1, keepdims=True)
        column = lax.broadcasted_iota(jnp.int32, (16, 128), 1)
        two[...] = jnp.where(column == 0, low, high).astype(jnp.int32)
        paired.start()

    paired = pltpu.make_async_copy(two, two_s, lsem.at[24 + NCH])

    def chosen(b, i):
        return jnp.minimum(jnp.maximum(two_s[b, i], 0), 3)

    def mask_pages():
        paired.wait()
        own_pages = own_rows_pages().astype(jnp.int32)
        r_id = lax.broadcasted_iota(jnp.int32, (16, 128), 0)
        s_id = lax.broadcasted_iota(jnp.int32, (16, 128), 1)
        lens = jnp.zeros((16, 128), jnp.int32)
        for r in range(16):
            lens = jnp.where(r_id == r, clen_ref[c * 16 + r], lens)
        named = [jnp.broadcast_to(own_pages[:, slot : slot + 1], (16, 128)) for slot in range(8)]
        upto = [lens - slot * PAGE for slot in range(8)]
        in_page = lax.rem(s_id, PAGE)
        for b in range(16):
            page = 4 * b + jnp.where(s_id < PAGE, chosen(b, 0), chosen(b, 1))
            end = jnp.zeros((16, 128), jnp.int32)
            for slot in range(8):
                end = jnp.where(named[slot] == page, upto[slot], end)
            bias[b // 2, :, 128 * (b % 2) : 128 * (b % 2) + 128] = jnp.where(in_page < end, 0.0, NEG)

    def pool(t, f):
        pages = []
        for b in (2 * t, 2 * t + 1):
            for i in range(2):
                pages.append(kv[b // 4, b % 2, (b // 2) % 2, f, chosen(b, i)])
        return jnp.concatenate(pages, axis=0)

    def list_pages():
        need("mask")
        a_id = lax.broadcasted_iota(jnp.int32, (64, 64), 0)
        b_id = lax.broadcasted_iota(jnp.int32, (64, 64), 1)
        col_id = lax.broadcasted_iota(jnp.int32, (64, 128), 1)
        p_id = lax.broadcasted_iota(jnp.int32, (64, 128), 0)
        spot = (p_id // 16) * 16 + lax.rem(p_id // 4, 2) * 8 + lax.rem(p_id // 8, 2) * 4
        spot = (spot + lax.rem(p_id, 4)).astype(F32)
        rows = []
        for n in range(4):
            a = 4 * c + n
            line = mask_ref[pl.ds(a, 1), :].astype(F32)
            readable = jnp.sum(jnp.where(a_id == b_id, line, 0.0), axis=1, keepdims=True)
            readable = jnp.where((readable > 0.5) & (p_id < a), 1.0, 0.0)
            before = mdot((b_id < a_id).astype(BF16), readable.astype(BF16))
            place = jnp.where(p_id == a, 0.0, before + 1.0).astype(jnp.int32)
            hit = (place == col_id) & ((readable > 0.5) | (p_id == a))
            line = jnp.sum(jnp.where(hit, spot, 0.0), axis=0, keepdims=True)
            count = jnp.sum(readable, axis=0, keepdims=True) + 1.0
            rows.append(jnp.where(col_id[0:1] == 127, count, line))
        picks[...] = jnp.concatenate(rows + rows, axis=0).astype(jnp.int32)
        listed.start()
        told.start()

    def prefill_node(n):
        if n == 0:
            listed.wait()
            need("query")
        pages = []
        for i in range(NEAR):
            spot = jnp.minimum(jnp.maximum(spots[n, i], 0), 63)
            pages.append(
                (spot // 16, lax.rem(spot // 8, 2), lax.rem(spot // 4, 2), lax.rem(spot, 4))
            )
        keys = jnp.concatenate([kv[a, b, d, 0, i] for a, b, d, i in pages], axis=0)
        values = jnp.concatenate([kv[a, b, d, 1, i] for a, b, d, i in pages], axis=0)
        mixed = first_pages(qb[n], keys, values, spots[n, 127])[1]
        write_heads(pb, n, mixed)
        prefilled[n].start()

    listed = pltpu.make_async_copy(picks, spots, lsem.at[19 + NCH])
    told = pltpu.make_async_copy(picks, picks_out, lsem.at[25 + NCH])
    prefilled = [
        pltpu.make_async_copy(pb.at[n], pout.at[n], lsem.at[20 + NCH + n]) for n in range(4)
    ]

    keep = pltpu.make_async_copy(kv, kv_out, lsem.at[18])
    rms, squared = [], []

    def step(event):
        who, what = event.split(".")
        if who == "kv":
            if what == "fin":
                for k in range(8, 12):
                    kvm[k].wait_recv()
                keep.start()
            else:
                kv_pass(what)
            return
        if who == "all":
            if what[:2] == "sq":
                stage = {"sq": sum_squares, "sq1": sum_squares_x, "sq2": sum_squares_z}[what]
                squared[:] = stage(squared) if squared else stage()
            else:
                if what[:2] == "pf":
                    prefill_node(int(what[2]))
                else:
                    {"pick": pick_pages, "mask": mask_pages, "list": list_pages}[what]()
            return
        p = parts[int(who[1])]
        if what == "other":
            scale_rows(p, 1 - core)
            other_rows(p)
            if p.k == 0:
                load_rest()
        elif what == "own":
            scale_rows(p, core)
            own_rows(p)
        elif what[0] == "x":
            if what == "xsum":
                x_sum(p)
            else:
                x_relay(p, int(what[2]) // 2)
        elif what == "att":
            if not rms:
                rms.append(inverse_rms(squared))
            attend(p, rms[0])
        elif what[0] == "h":
            p.hog.take(what[1])
        elif what == "out":
            need("wo0")
            need("wo1")
            out_rows(p)
        elif what == "ysum":
            drain(30)
            y_sum(p)
        elif what[0] == "y":
            y_relay(p, int(what[2]) // 2)
        elif what == "add":
            add_input(p)
        else:
            drain(16)
            pass_on(p, int(what[1]))

    for event in ORDER:
        step(event)
    keep.wait()
    told.wait()
    for copy in prefilled:
        copy.wait()
    drain(0)
    for p in parts:
        p.done.wait()


def layer_call(*args):
    hbm = pl.BlockSpec(memory_space=pl.ANY)
    return pl.pallas_call(
        layer_kernel,
        out_shape=(
            jax.ShapeDtypeStruct((4, 2, 2, 2, 4, PAGE, HD), BF16),
            jax.ShapeDtypeStruct((8, 128), jnp.int32),
            jax.ShapeDtypeStruct((4, PAGE, 1024), BF16),
            jax.ShapeDtypeStruct((4, 8, 32, 512), BF16),
        ),
        in_specs=[hbm] * 11,
        out_specs=(hbm, hbm, hbm, hbm),
        scratch_shapes=[
            pltpu.VMEM((8, 128), jnp.int32),
            pltpu.VMEM((4, PAGE, 1024), BF16),
            pltpu.SMEM((8, 128), jnp.int32),
            pltpu.VMEM((4, PAGE, 1024), BF16),
            pltpu.VMEM((4, 8, 32, 512), BF16),
            pltpu.VMEM((64, 64), jnp.int32),
            pltpu.VMEM((8, 256), jnp.int32),
            pltpu.SMEM((256,), jnp.int32),
            pltpu.VMEM((4, 128), BF16),
            pltpu.VMEM((4, 2, 2, 2, 4, PAGE, HD), BF16),
            pltpu.VMEM((4, 16, 16, 512), BF16),
            pltpu.VMEM((5, 512, 256), BF16),
            pltpu.VMEM((1024, 128), BF16),
            pltpu.VMEM((1024, 128), F32),
            pltpu.VMEM((2, 1024, 256), BF16),
            pltpu.VMEM((NCH, 2, 8, RB, 512), BF16),
            pltpu.VMEM((2, 4, 2, 8, 128), F32),
            pltpu.VMEM((4, 2, 8, 128), F32),
            pltpu.VMEM((4, 2, 8, 128), F32),
            pltpu.VMEM((3, 2, 8, 128), F32),
            pltpu.VMEM((2, 8, 128), F32),
            pltpu.VMEM((8, 128), F32),
            pltpu.VMEM((NCH, 10, 4, 2, RB, 128), BF16),
            pltpu.VMEM((NCH, 10, 4, 2, RB, 128), BF16),
            pltpu.VMEM((NCH, 4, 10, 2, RB, 128), BF16),
            pltpu.VMEM((NCH, 2, 5, 2, RB, 128), BF16),
            pltpu.VMEM((NCH, 10, 2, RB, 128), BF16),
            pltpu.VMEM((NCH, 10, 2, RB, 128), BF16),
            pltpu.VMEM((NCH, 10, RB, 128), BF16),
            pltpu.VMEM((NCH, 10, RB, 128), BF16),
            pltpu.VMEM((NCH, 10, RB, 128), F32),
            pltpu.VMEM((NCH, 10, RB, 128), BF16),
            pltpu.VMEM((64, 128), BF16),
            pltpu.VMEM((64, 128), BF16),
            pltpu.VMEM((8, 16, 256), F32),
            pltpu.VMEM((16, 128), jnp.int32),
            pltpu.SMEM((16, 128), jnp.int32),
            pltpu.VMEM((8, 8 * RB, 256), F32),
            pltpu.VMEM((NCH, 4, 2, 2, 2, RB, 512), BF16),
            pltpu.VMEM((NCH, 4, 2, 2, RB, 512), BF16),
            pltpu.VMEM((NCH, 2, 2, RB, 512), BF16),
            pltpu.VMEM((NCH, 2, 2, RB, 512), BF16),
            pltpu.VMEM((NCH, 2, 2, RB, 512), BF16),
            pltpu.VMEM((NCH, 2, 2, RB, 512), BF16),
            pltpu.VMEM((NCH, 2, 2, RB, 512), BF16),
            pltpu.SemaphoreType.DMA((26 + NCH,)),
            pltpu.SemaphoreType.DMA((NMSG,)),
            pltpu.SemaphoreType.DMA((NMSG,)),
        ],
        compiler_params=pltpu.CompilerParams(
            collective_id=0, has_side_effects=True, vmem_limit_bytes=56 * 1024 * 1024
        ),
        name="layer",
    )(*args)


def finish_kernel(
    q_hbm, kv_ref, picks_hbm, pre_ref, dec_ref, out_hbm, dec_out,
    picks, q, kv, extra, stage, out, peak, mix, sem,
):
    get_dec = [pltpu.make_async_copy(dec_ref.at[t], stage.at[t], sem.at[t]) for t in range(4)]
    put_dec = [pltpu.make_async_copy(stage.at[t], dec_out.at[t], sem.at[4 + t]) for t in range(4)]
    get_pre = pltpu.make_async_copy(pre_ref, out, sem.at[8])
    put_pre = pltpu.make_async_copy(out, out_hbm, sem.at[9])
    get_picks = pltpu.make_async_copy(picks_hbm, picks, sem.at[13])
    get_picks.start()
    get_pre.start()
    for copy in get_dec:
        copy.start()

    def page(n, k):
        spot = picks[n, k]
        return kv_ref.at[spot // 4, :, lax.rem(spot, 4)]

    get_picks.wait()
    get_pre.wait()
    for t in range(4):
        get_dec[t].wait()
        put_dec[t].start()

    def deep(n, carry):
        @pl.when(picks[n, 127] > NEAR)
        def _():
            pltpu.make_async_copy(q_hbm.at[n], q, sem.at[10]).start()
            for k in range(NEAR):
                pltpu.make_async_copy(page(n, k), kv.at[k], sem.at[11]).start()
            pltpu.make_async_copy(q, q, sem.at[10]).wait()
            pltpu.make_async_copy(kv, kv, sem.at[11]).wait()
            top, mixed = first_pages(
                q[...],
                kv[:, 0].reshape(NEAR * PAGE, HD),
                kv[:, 1].reshape(NEAR * PAGE, HD),
                picks[n, 127],
            )
            peak[...] = jnp.broadcast_to(top, (512, 128))
            mix[...] = mixed

            def more(t, inner):
                for k in range(4):
                    pltpu.make_async_copy(
                        page(n, NEAR + 4 * t + k), extra.at[k], sem.at[12]
                    ).start()
                pltpu.make_async_copy(extra, extra, sem.at[12]).wait()
                rows = jnp.concatenate([q[:, s * HD : (s + 1) * HD] for s in range(8)], axis=0)
                j_id = lax.broadcasted_iota(jnp.int32, (1, 4 * PAGE), 1)
                hidden = jnp.where(j_id < (picks[n, 127] - NEAR - 4 * t) * PAGE, 0.0, NEG)
                s = rdot(rows, extra[:, 0].reshape(4 * PAGE, HD)) * SCALE + hidden
                before = peak[:, 0:1]
                top = jnp.maximum(jnp.max(s, axis=1, keepdims=True), before)
                values = jnp.concatenate(
                    [extra[:, 1].reshape(4 * PAGE, HD), jnp.ones((4 * PAGE, 128), BF16)], axis=1
                )
                mix[...] = mix[...] * jnp.exp(before - top) + mdot(
                    jnp.exp(s - top).astype(BF16), values
                )
                peak[...] = jnp.broadcast_to(top, (512, 128))
                return inner

            lax.fori_loop(0, (picks[n, 127] - NEAR + 3) // 4, more, 0)
            write_heads(out, n, mix[...])

        return carry

    lax.fori_loop(0, 4, deep, 0)
    put_pre.start()
    put_pre.wait()
    for t in range(4):
        put_dec[t].wait()


def finish_call(q, kv, picks, pre, dec):
    hbm = pl.BlockSpec(memory_space=pl.ANY)
    return pl.pallas_call(
        finish_kernel,
        out_shape=(
            jax.ShapeDtypeStruct((4, PAGE, 1024), BF16),
            jax.ShapeDtypeStruct(dec.shape, BF16),
        ),
        in_specs=[hbm] * 5,
        out_specs=(hbm, hbm),
        scratch_shapes=[
            pltpu.SMEM((8, 128), jnp.int32),
            pltpu.VMEM((PAGE, 1024), BF16),
            pltpu.VMEM((NEAR, 2, PAGE, HD), BF16),
            pltpu.VMEM((4, 2, PAGE, HD), BF16),
            pltpu.VMEM(dec.shape, BF16),
            pltpu.VMEM((4, PAGE, 1024), BF16),
            pltpu.VMEM((512, 128), F32),
            pltpu.VMEM((512, 256), F32),
            pltpu.SemaphoreType.DMA((14,)),
        ],
        compiler_params=pltpu.CompilerParams(vmem_limit_bytes=62 * 1024 * 1024),
        name="finish",
    )(q, kv, picks, pre, dec)


def per_device(
    prefill_query, prefill_key, prefill_value, tree_mask, pages, cache_len,
    dec_in, norm_gain, w_query, w_keyval, w_out,
):
    query = prefill_query.reshape(4, PAGE, 1024)
    kv, picks, pre, dec = layer_call(
        query, prefill_key.reshape(4, PAGE, HD), prefill_value.reshape(4, PAGE, HD), tree_mask,
        pages.T, cache_len, dec_in.reshape(4, 16, 16, 512), norm_gain.reshape(4, 128), w_query,
        w_keyval.reshape(1024, 128), w_out,
    )
    prefill_out, dec_out = finish_call(
        query, kv.reshape(16, 2, 4, PAGE, HD), picks, pre, dec
    )
    return prefill_out.reshape(256, 1024), dec_out.reshape(4, 256, 512)


def solution(mesh):
    return jax.shard_map(
        per_device,
        mesh=mesh,
        in_specs=(
            P("ctx", "head"), P("ctx", "head"), P("ctx", "head"), P(), P(), P(),
            P(None, None, "ctx"), P("ctx"), P("ctx", "head"), P("ctx", None, "head"),
            P("head", "ctx"),
        ),
        out_specs=(P("ctx", "head"), P(None, None, "ctx")),
        check_vma=False,
    )
```
